32 devices in a mesh: dp: 8 (over y, x, core), mp: 4 (over z).
Axes of the slice: x: 2, y: 2, z: 4, core: 2. Of those that a mesh axis runs over, the one named last changes fastest.
Arguments:
- tokens: bfloat16 [96, 160, 768], P('dp', 'mp'), may hold values from -6 to 6
- word_len: int32 [96], P('dp'), may hold values from 1 to 60, as said below
- region_count: int32 [96], P('dp'), may hold values from 10 to 100, as said below
- w_qkv: bfloat16 [3, 768, 768], P(None, None, 'mp'), may hold values from -0.3125 to 0.3125
- qv_bias: bfloat16 [2, 768], P(None, 'mp'), may hold values from -3 to 3
- w_out: bfloat16 [768, 768], P('mp'), may hold values from -0.625 to 0.625
- out_bias: bfloat16 [768], replicated, may hold values from -3 to 3
- norm1_gain: bfloat16 [768], replicated, may hold values from 0.5 to 1.5
- norm1_bias: bfloat16 [768], replicated, may hold values from -3 to 3
- w_in: bfloat16 [768, 3072], P(None, 'mp'), may hold values from -0.21875 to 0.21875
- in_bias: bfloat16 [3072], P('mp'), may hold values from -3 to 3
- w_down: bfloat16 [3072, 768], P('mp'), may hold values from -0.15625 to 0.15625
- down_bias: bfloat16 [768], replicated, may hold values from -3 to 3
- norm2_gain: bfloat16 [768], replicated, may hold values from 0.5 to 1.5
- norm2_bias: bfloat16 [768], replicated, may hold values from -3 to 3
- cotangent: bfloat16 [96, 160, 768], P('dp', 'mp'), may hold values from -6 to 6
Outputs:
- layer_out: bfloat16 [96, 160, 768], P('dp', 'mp')
- grad_input: float32 [96, 160, 768], P('dp', 'mp')
- grad_qkv: float32 [3, 768, 768], P(None, None, 'mp')
- grad_qv_bias: float32 [2, 768], P(None, 'mp')
- grad_out: float32 [768, 768], P('mp')
- grad_out_bias: float32 [768], replicated
- grad_norm1_gain: float32 [768], replicated
- grad_norm1_bias: float32 [768], replicated
- grad_in: float32 [768, 3072], P(None, 'mp')
- grad_in_bias: float32 [3072], P('mp')
- grad_down: float32 [3072, 768], P('mp')
- grad_down_bias: float32 [768], replicated
- grad_norm2_gain: float32 [768], replicated
- grad_norm2_bias: float32 [768], replicated
The draws below stay inside these ranges and needn't reach their ends.
Inputs may be any that keep to these rules, and one draw needn't show every extreme that they name: `word_len`: words of a pair; in each aligned block of 12 pairs one pair, chosen at random, has 60 words and 100 regions. `region_count`: regions of a pair.
All inputs are finite; a program needn't handle non-finite values.
Results may differ from the reference program's by a relative error of at most 0.014.
The reference program's roundings to bfloat16 on the way count: a program that leaves them out, or rounds other values in their place, can miss the bound.
Values may be sent and summed in bfloat16 or wider, within the bound.
No kernel may reach another device: no remote copies, remote signals or barrier semaphores. Data moves between devices by JAX's collectives and lax.ppermute only.
A program may use at most 128 MiB of HBM per device.

```python
import math
import jax
import jax.numpy as jnp
from jax import lax

D = 768
HEADS = 12
HEAD = 64
FF = 3072
WORDS = 60
REGIONS = 100
PAIRS_DEV = 12
HH = 768
SLOTS = 160
PAIRS = 96


def filled_pairs(key):
    blocks = PAIRS // PAIRS_DEV
    chosen = jax.random.randint(jax.random.fold_in(key, 11), (blocks,), 0, PAIRS_DEV)
    within = jnp.arange(PAIRS) % PAIRS_DEV
    return within == jnp.repeat(chosen, PAIRS_DEV, total_repeat_length=PAIRS)


def draw_word_len(key, part):
    filled = filled_pairs(key)
    key = jax.random.fold_in(key, 1)
    drawn = jax.random.randint(key, (PAIRS,), 1, WORDS + 1)
    return jnp.where(filled, WORDS, drawn).astype(jnp.int32)


def draw_region_count(key, part):
    filled = filled_pairs(key)
    key = jax.random.fold_in(key, 2)
    lowest = max(1, REGIONS // 10)
    drawn = jax.random.randint(key, (PAIRS,), lowest, REGIONS + 1)
    return jnp.where(filled, REGIONS, drawn).astype(jnp.int32)


def shard_levels(rng, extent, split, least, top_value):
    factor_of = 1.0
    for dim, shards_of in split:
        draws = jax.random.uniform(jax.random.fold_in(jax.random.fold_in(rng, 6), dim), (shards_of,), jnp.float32, least / len(split), top_value / len(split))
        factor_of = factor_of * jnp.repeat(jnp.exp(draws), extent[dim] // shards_of).reshape((-1,) + (1,) * (len(extent) - 1 - dim))
    return factor_of


def centred(key, extent, width, most, split=(), kind=jnp.bfloat16):
    factor_of = shard_levels(key, extent, split, -0.22, 0.18) if split else 1.0
    values = jax.random.normal(key, extent, jnp.float32) * width * factor_of
    return jnp.minimum(jnp.maximum(values, -most), most).astype(kind)


def setup_inputs(seed: int = 0) -> dict:
    keys = jax.random.split(jax.random.key(seed), 17)
    return {
        "tokens": centred(keys[0], (PAIRS, SLOTS, D), 1.0, 6.0, ((0, 8), (1, 4))),
        "word_len": draw_word_len(jax.random.fold_in(keys[16], 71), 0),
        "region_count": draw_region_count(jax.random.fold_in(keys[16], 71), 0),
        "w_qkv": centred(keys[3], (3, D, HH), (D // 2) ** -0.5, 0.3125, ((2, 4),)),
        "qv_bias": centred(keys[4], (2, HH), 0.5, 3.0, ((1, 4),)),
        "w_out": centred(keys[5], (HH, D), (HH // 8) ** -0.5, 0.625, ((0, 4),)),
        "out_bias": centred(keys[6], (D,), 0.5, 3.0),
        "norm1_gain": jnp.clip(1.0 + 0.1 * jax.random.normal(keys[7], (D,), jnp.float32), 0.5, 1.5).astype(jnp.bfloat16),
        "norm1_bias": centred(keys[8], (D,), 0.5, 3.0),
        "w_in": centred(keys[9], (D, FF), D ** -0.5, 0.21875, ((1, 4),)),
        "in_bias": centred(keys[10], (FF,), 0.5, 3.0, ((0, 4),)),
        "w_down": centred(keys[11], (FF, D), (FF // 2) ** -0.5, 0.15625, ((0, 4),)),
        "down_bias": centred(keys[12], (D,), 0.5, 3.0),
        "norm2_gain": jnp.clip(1.0 + 0.1 * jax.random.normal(keys[13], (D,), jnp.float32), 0.5, 1.5).astype(jnp.bfloat16),
        "norm2_bias": centred(keys[14], (D,), 0.5, 3.0),
        "cotangent": centred(keys[15], (PAIRS, SLOTS, D), 1.0, 6.0, ((0, 8), (1, 4))),
    }


EPSILON = 1e-05

@jax.custom_vjp
def low(v):
    return lax.optimization_barrier(v.astype(jnp.bfloat16)).astype(jnp.float32)

@jax.custom_vjp
def low_back(v):
    return v

def low_keep(v):
    return (low(v), None)

def low_pass(kept, grad):
    return (grad,)

def back_keep(v):
    return (v, None)

def back_low(kept, grad):
    return (low(grad),)
low.defvjp(low_keep, low_pass)
low_back.defvjp(back_keep, back_low)

def rounded(tensor):
    return low(low_back(tensor))

def layer_norm(total, gain, shift):
    centered = total - lax.optimization_barrier(jnp.mean(total, axis=-1, keepdims=True))
    inv_scale = lax.rsqrt(lax.optimization_barrier(jnp.mean(centered * centered, axis=-1, keepdims=True)) + EPSILON)
    return centered * inv_scale * gain + shift

def attend(block_in):
    queries, key_heads, values, key_valid = block_in
    scores = jnp.einsum('pqhd,pkhd->phqk', queries, key_heads, precision=lax.Precision.HIGHEST) * HEAD ** (-0.5)
    scores = jnp.where(key_valid[:, None, None, :], scores, -1e+30)
    weights = low(jax.nn.softmax(low_back(scores), axis=-1))
    return jnp.einsum('phqk,pkhd->pqhd', weights, values, precision=lax.Precision.HIGHEST)

def reference(tokens, word_len, region_count, w_qkv, qv_bias, w_out, out_bias, norm1_gain, norm1_bias, w_in, in_bias, w_down, down_bias, norm2_gain, norm2_bias, cotangent):
    slot_index = jnp.arange(SLOTS, dtype=jnp.int32)
    key_valid = jnp.where(slot_index[None, :] < WORDS, slot_index[None, :] < word_len[:, None], slot_index[None, :] - WORDS < region_count[:, None])
    group_size = math.gcd(PAIRS, 16)
    group_count = PAIRS // group_size
    highest = lax.Precision.HIGHEST

    def forward(inputs, qkv_weight, bias_pair, out_weight, bias_out, gain_one, shift_one, in_weight, bias_in, down_weight, bias_down, gain_two, shift_two):
        projected = jnp.einsum('psd,jdc->jpsc', inputs, qkv_weight, precision=highest)
        queries = rounded(projected[0] + bias_pair[0])
        key_heads = rounded(projected[1])
        values = rounded(projected[2] + bias_pair[1])
        head_shape = (group_count, group_size, SLOTS, HEADS, HEAD)
        context = lax.map(jax.checkpoint(attend), (queries.reshape(head_shape), key_heads.reshape(head_shape), values.reshape(head_shape), key_valid.reshape(group_count, group_size, SLOTS)))
        context = rounded(context.reshape(PAIRS, SLOTS, HH))
        first_sum = low_back(jnp.einsum('psc,cd->psd', context, out_weight, precision=highest)) + bias_out + inputs
        hidden = layer_norm(first_sum, gain_one, shift_one)
        pre_act = low_back(jnp.einsum('psd,df->psf', low(hidden), in_weight, precision=highest) + bias_in)
        activation = low(jax.nn.gelu(pre_act, approximate=False))
        second = low_back(jnp.einsum('psf,fd->psd', activation, down_weight, precision=highest)) + bias_down + hidden
        return layer_norm(second, gain_two, shift_two)
    arrays = [item.astype(jnp.float32) for item in (tokens, w_qkv, qv_bias, w_out, out_bias, norm1_gain, norm1_bias, w_in, in_bias, w_down, down_bias, norm2_gain, norm2_bias)]
    layer_out, pull = jax.vjp(forward, *arrays)
    grads = pull(cotangent.astype(jnp.float32))
    return (layer_out.astype(jnp.bfloat16), grads[0], grads[1], grads[2], grads[3], grads[4], grads[5], grads[6], grads[7], grads[8], grads[9], grads[10], grads[11], grads[12])
```

```python
from functools import partial

import jax
import jax.numpy as jnp
from jax import lax
from jax.sharding import PartitionSpec as P

HEAD = 64
WORDS = 60
EPSILON = 1e-05
F32 = jnp.float32
BF16 = jnp.bfloat16


def normalize(total, gain, shift):
    centered = total - jnp.mean(total, axis=-1, keepdims=True)
    inv_scale = lax.rsqrt(jnp.mean(centered * centered, axis=-1, keepdims=True) + EPSILON)
    normed = centered * inv_scale
    return (normed * gain + shift, normed, inv_scale)


def normalize_back(upstream, normed, inv_scale, gain):
    scaled_up = upstream * gain
    mean_one = jnp.mean(scaled_up, axis=-1, keepdims=True)
    mean_two = jnp.mean(scaled_up * normed, axis=-1, keepdims=True)
    return inv_scale * (scaled_up - mean_one - normed * mean_two)


def flip(array, axis, bit):
    size = lax.axis_size(axis)
    return lax.ppermute(array, axis, [(i, i ^ bit) for i in range(size)])


def tie(*arrays):
    return lax.optimization_barrier(arrays)


def dp_bits():
    size = lax.axis_size("dp")
    bits = size.bit_length() - 1
    return bits


def pick(array, axis, index):
    return lax.dynamic_index_in_dim(array, index, axis, keepdims=False)


def gather_steps(halves):
    bits = dp_bits()
    me = lax.axis_index("dp")
    outer = list(range(1, bits))
    orders = [outer, outer[::-1]]
    held = [h.reshape((1,) * bits + h.shape) for h in halves]
    for step in range(len(outer)):
        held = list(tie(*held))
        got = [flip(h, "dp", 1 << order[step]) for h, order in zip(held, orders)]
        got = list(tie(*got))
        for side, order in enumerate(orders):
            bit = order[step]
            axis = bits - 1 - bit
            mine = ((me >> bit) & 1) == 0
            held[side] = jnp.concatenate(
                [jnp.where(mine, held[side], got[side]), jnp.where(mine, got[side], held[side])],
                axis=axis,
            )
    both = jnp.concatenate(held, axis=bits + 1)
    other = flip(both, "dp", 1)
    mine = (me & 1) == 0
    full = jnp.concatenate(
        [jnp.where(mine, both, other), jnp.where(mine, other, both)], axis=bits - 1
    )
    return full.reshape((lax.axis_size("dp"),) + full.shape[bits:])


def gather_dp(pieces):
    n, rows, cols = pieces.shape
    half = rows // 2
    full = gather_steps([pieces[:, :half], pieces[:, half:]])
    return full.transpose(1, 0, 2, 3).reshape(n, -1, cols)


def add_low(one, two):
    return (one.astype(F32) + two.astype(F32)).astype(BF16)


def reduce_dp(packs):
    bits = dp_bits()
    me = lax.axis_index("dp")
    shards_, rows, cols = packs.shape
    part = rows // lax.axis_size("dp")
    array = packs.reshape((shards_,) + (2,) * bits + (part, cols))
    low = me & 1
    other = flip(pick(array, bits, 1 - low), "dp", 1)
    array = add_low(pick(array, bits, low), other)
    half = shards_ // 2
    held = [array[:half], array[half:]]
    outer = list(range(1, bits))
    orders = [outer, outer[::-1]]
    left = [list(reversed(outer)) for _ in orders]
    for step in range(len(outer)):
        sends = []
        for side, order in enumerate(orders):
            bit = order[step]
            axis = 1 + left[side].index(bit)
            sends.append(pick(held[side], axis, 1 - ((me >> bit) & 1)))
        sends = tie(*sends)
        got = [flip(s, "dp", 1 << order[step]) for s, order in zip(sends, orders)]
        got = tie(*got)
        for side, order in enumerate(orders):
            bit = order[step]
            axis = 1 + left[side].index(bit)
            held[side] = add_low(pick(held[side], axis, (me >> bit) & 1), got[side])
            left[side].remove(bit)
    return jnp.concatenate(held, axis=0)


def reduce_mp(parts):
    sends = tie(*[parts[k] for k in range(1, parts.shape[0])])
    got = [flip(s, "mp", k + 1) for k, s in enumerate(sends)]
    got = tie(*got)
    total = parts[0].astype(F32)
    for g in got:
        total = total + g.astype(F32)
    return total.astype(BF16)


def exchange_rows(array):
    size = lax.axis_size("mp")
    me = lax.axis_index("mp")
    blocks = array.reshape((size, array.shape[0] // size) + array.shape[1:])
    sends = tie(*[pick(blocks, 0, me ^ k) for k in range(size)])
    got = [sends[0]] + [flip(sends[k], "mp", k) for k in range(1, size)]
    return jnp.concatenate(got, axis=1)


def return_rows(array):
    size = lax.axis_size("mp")
    me = lax.axis_index("mp")
    pairs, slots, cols = array.shape
    rows = slots // size
    sends = [array[:, k * rows : (k + 1) * rows] for k in range(size)]
    sends = tie(*sends)
    got = jnp.stack([sends[0]] + [flip(sends[k], "mp", k) for k in range(1, size)])
    got = jnp.take(got, jnp.arange(size) ^ me, axis=0)
    return got.reshape(size * pairs, rows, cols)


def shards(
    tokens,
    word_len,
    region_count,
    w_qkv,
    qv_bias,
    w_out,
    out_bias,
    norm1_gain,
    norm1_bias,
    w_in,
    in_bias,
    w_down,
    down_bias,
    norm2_gain,
    norm2_bias,
    cotangent,
):
    mp = lax.axis_size("mp")
    dp = lax.axis_size("dp")
    mi = lax.axis_index("mp")
    di = lax.axis_index("dp")
    width = tokens.shape[2]
    rows_local = tokens.shape[1]
    slot_total = rows_local * mp
    pair_count = tokens.shape[0] // mp
    cols = w_qkv.shape[2]
    units = w_in.shape[1]
    heads = cols // HEAD
    head_scale = HEAD ** (-0.5)
    order = jnp.arange(mp) ^ mi

    att_own = jnp.concatenate([w_qkv.transpose(0, 2, 1).reshape(3 * cols, width), w_out], axis=0)
    att_rows = att_own.shape[0]
    att_part = att_rows // dp
    in_own = w_in.T
    in_part = units // dp
    piece = lax.dynamic_slice_in_dim(att_own, di * att_part, att_part, 0)
    in_piece = lax.dynamic_slice_in_dim(in_own, di * in_part, in_part, 0)
    down_piece = lax.dynamic_slice_in_dim(w_down, di * in_part, in_part, 0)

    small = jnp.concatenate([qv_bias.reshape(-1), in_bias])
    small_rows = -(-small.shape[0] // width)
    pad_rows = -(-small_rows // 8) * 8
    small = jnp.pad(small, (0, pad_rows * width - small.shape[0])).reshape(pad_rows, width)
    payload = jnp.concatenate([piece, small], axis=0)

    x = exchange_rows(tokens)
    payload, x = tie(payload, x)
    got = tie(*[flip(payload, "mp", k) for k in range(1, mp)])
    w_in_all = lax.all_gather(in_piece, ("mp", "dp"), axis=0, tiled=True)
    w_down_all = lax.all_gather(down_piece, ("mp", "dp"), axis=0, tiled=True)
    smalls = jnp.stack([small] + [g[att_part:] for g in got]).reshape(mp, -1)
    qv_all = smalls[:, : 2 * cols].reshape(mp, 2, cols)
    in_bias_all = jnp.take(smalls[:, 2 * cols : 2 * cols + units], order, axis=0).reshape(-1)
    others = gather_dp(jnp.stack([g[:att_part] for g in got]))
    att_all = jnp.concatenate([att_own[None], others], axis=0)
    qkv_all = att_all[:, : 3 * cols].reshape(mp, 3, cols, width)
    out_all = att_all[:, 3 * cols :]

    words = lax.dynamic_slice_in_dim(word_len, mi * pair_count, pair_count, 0)
    regions = lax.dynamic_slice_in_dim(region_count, mi * pair_count, pair_count, 0)
    slot_index = (order[:, None] * rows_local + jnp.arange(rows_local)[None, :]).reshape(-1)
    key_valid = jnp.where(
        slot_index[None, :] < WORDS,
        slot_index[None, :] < words[:, None],
        slot_index[None, :] - WORDS < regions[:, None],
    )
    gain_one = norm1_gain.astype(F32)
    gain_two = norm2_gain.astype(F32)
    head_shape = (mp, pair_count, slot_total, heads, HEAD)
    projected = jnp.einsum("psd,kjcd->jkpsc", x, qkv_all, preferred_element_type=F32)
    queries = (projected[0] + qv_all[:, 0][:, None, None]).astype(BF16).reshape(head_shape)
    key_heads = projected[1].astype(BF16).reshape(head_shape)
    values = (projected[2] + qv_all[:, 1][:, None, None]).astype(BF16).reshape(head_shape)

    def masked_scores():
        raw_scores = (
            jnp.einsum("kpqhd,kpthd->kphqt", queries, key_heads, preferred_element_type=F32)
            * head_scale
        )
        return jnp.where(key_valid[None, :, None, None, :], raw_scores, -1e30)

    masked = masked_scores()
    row_max = jnp.max(masked, axis=-1, keepdims=True)
    exp_scores = jnp.exp(masked - row_max)
    weights = exp_scores / jnp.sum(exp_scores, axis=-1, keepdims=True)
    prob_low = weights.astype(BF16)
    context = jnp.einsum("kphqt,kpthd->kpqhd", prob_low, values, preferred_element_type=F32)
    context = context.astype(BF16).reshape(mp, pair_count, slot_total, cols)
    branch = jnp.einsum("kpsc,kcd->psd", context, out_all, preferred_element_type=F32)
    first_sum = branch + out_bias + x
    hidden, normed_one, scale_one = normalize(first_sum, gain_one, norm1_bias.astype(F32))
    hidden_low = hidden.astype(BF16)

    cot = exchange_rows(tie(cotangent, hidden_low)[0])

    pre_act = jnp.einsum("psd,fd->psf", hidden_low, w_in_all, preferred_element_type=F32)
    pre_act = pre_act + in_bias_all
    activation, gelu_back = jax.vjp(partial(jax.nn.gelu, approximate=False), pre_act)
    act_low = activation.astype(BF16)
    ffn_term = jnp.einsum("psf,fd->psd", act_low, w_down_all, preferred_element_type=F32)
    second = ffn_term + down_bias + hidden
    output, normed_two, scale_two = normalize(second, gain_two, norm2_bias.astype(F32))
    upstream = cot.astype(F32)
    grad_norm2_gain = jnp.sum(upstream * normed_two, axis=(0, 1))
    grad_norm2_bias = jnp.sum(upstream, axis=(0, 1))
    delta_ffn = normalize_back(upstream, normed_two, scale_two, gain_two)
    grad_down_bias = jnp.sum(delta_ffn, axis=(0, 1))
    ffn_low = delta_ffn.astype(BF16)

    grad_down = jnp.einsum("psf,psd->fd", act_low, ffn_low, preferred_element_type=F32)
    act_grad = jnp.einsum("psd,fd->psf", ffn_low, w_down_all, preferred_element_type=F32)
    pre_grad = gelu_back(act_grad)[0].astype(BF16)
    grad_in = jnp.einsum("psf,psd->fd", pre_grad, hidden_low, preferred_element_type=F32)
    grad_in_bias = jnp.sum(pre_grad.astype(F32), axis=(0, 1))
    ffn_pack = jnp.stack(
        [grad_in.astype(BF16).reshape(mp, units, width), grad_down.astype(BF16).reshape(mp, units, width)],
        axis=1,
    )
    ffn_pack = jnp.take(ffn_pack, order, axis=0).reshape(2 * mp, units, width)
    ffn_part = reduce_dp(ffn_pack)
    ffn_part = reduce_mp(ffn_part.reshape(mp, 2 * in_part, width))
    ffn_grads = gather_dp(ffn_part.reshape(2, in_part, width))

    back_term = jnp.einsum("psf,fd->psd", pre_grad, w_in_all, preferred_element_type=F32)
    hidden_grad = back_term + delta_ffn
    grad_norm1_gain = jnp.sum(hidden_grad * normed_one, axis=(0, 1))
    grad_norm1_bias = jnp.sum(hidden_grad, axis=(0, 1))
    delta_attn = normalize_back(hidden_grad, normed_one, scale_one, gain_one)
    grad_out_bias = jnp.sum(delta_attn, axis=(0, 1))
    attn_low = delta_attn.astype(BF16)
    grad_out = jnp.einsum("kpsc,psd->kcd", context, attn_low, preferred_element_type=F32)
    context_grad = jnp.einsum("psd,kcd->kpsc", attn_low, out_all, preferred_element_type=F32)
    context_grad = context_grad.astype(BF16).reshape(head_shape)
    prob_grad = jnp.einsum("kpqhd,kpthd->kphqt", context_grad, values, preferred_element_type=F32)
    inner_sum = jnp.sum(prob_grad * weights, axis=-1, keepdims=True)
    score_grad = (weights * (prob_grad - inner_sum)).astype(BF16)
    value_grad = jnp.einsum(
        "kphqt,kpqhd->kpthd", prob_low, context_grad, preferred_element_type=F32
    ).astype(BF16)
    query_grad = (
        jnp.einsum("kphqt,kpthd->kpqhd", score_grad, key_heads, preferred_element_type=F32)
        * head_scale
    ).astype(BF16)
    key_grad = (
        jnp.einsum("kphqt,kpqhd->kpthd", score_grad, queries, preferred_element_type=F32)
        * head_scale
    ).astype(BF16)
    stacked = jnp.stack([query_grad, key_grad, value_grad], axis=1).reshape(
        mp, 3, pair_count, slot_total, cols
    )
    grad_qkv = jnp.einsum("kjpsc,psd->kjcd", stacked, x, preferred_element_type=F32)
    att_pack = jnp.concatenate(
        [grad_qkv.astype(BF16).reshape(mp, 3 * cols, width), grad_out.astype(BF16)], axis=1
    )
    att_part_sum = reduce_mp(reduce_dp(att_pack))
    att_grads = gather_dp(att_part_sum[None])[0]
    sums_qv = jnp.stack(
        [
            jnp.sum(query_grad.astype(F32), axis=(1, 2)).reshape(mp, cols),
            jnp.sum(value_grad.astype(F32), axis=(1, 2)).reshape(mp, cols),
        ],
        axis=1,
    )
    input_term = jnp.einsum("kjpsc,kjcd->psd", stacked, qkv_all, preferred_element_type=F32)
    grad_rows = (input_term + delta_attn).astype(BF16)

    layer_out = return_rows(output.astype(BF16))
    grad_input = return_rows(grad_rows).astype(F32)

    flat = jnp.concatenate(
        [
            grad_out_bias,
            grad_norm1_gain,
            grad_norm1_bias,
            grad_down_bias,
            grad_norm2_gain,
            grad_norm2_bias,
            grad_in_bias,
            jnp.take(sums_qv, order, axis=0).reshape(-1),
        ]
    )
    flat = lax.psum(flat, ("dp", "mp"))
    vectors = flat[: 6 * width].reshape(6, width)
    sum_in_bias = lax.dynamic_slice_in_dim(flat, 6 * width + mi * units, units, 0)
    sum_qv = lax.dynamic_slice_in_dim(
        flat, 6 * width + mp * units + mi * 2 * cols, 2 * cols, 0
    ).reshape(2, cols)

    grad_qkv_own = att_grads[: 3 * cols].reshape(3, cols, width).astype(F32).transpose(0, 2, 1)
    grad_out_own = att_grads[3 * cols :].astype(F32)
    grad_in_own = ffn_grads[0].astype(F32).T
    grad_down_own = ffn_grads[1].astype(F32)
    return (
        layer_out,
        grad_input,
        grad_qkv_own,
        sum_qv,
        grad_out_own,
        vectors[0],
        vectors[1],
        vectors[2],
        grad_in_own,
        sum_in_bias,
        grad_down_own,
        vectors[3],
        vectors[4],
        vectors[5],
    )


def solution(mesh):
    in_specs = (
        P("dp", "mp", None),
        P("dp"),
        P("dp"),
        P(None, None, "mp"),
        P(None, "mp"),
        P("mp", None),
        P(),
        P(),
        P(),
        P(None, "mp"),
        P("mp"),
        P("mp", None),
        P(),
        P(),
        P(),
        P("dp", "mp", None),
    )
    out_specs = (
        P("dp", "mp", None),
        P("dp", "mp", None),
        P(None, None, "mp"),
        P(None, "mp"),
        P("mp", None),
        P(),
        P(),
        P(),
        P(None, "mp"),
        P("mp"),
        P("mp", None),
        P(),
        P(),
        P(),
    )
    return jax.shard_map(shards, mesh=mesh, in_specs=in_specs, out_specs=out_specs, check_vma=False)
```

```python
from functools import partial

import jax
import jax.numpy as jnp
from jax import lax
from jax.experimental import pallas as pl
from jax.experimental.pallas import tpu as pltpu
from jax.sharding import PartitionSpec as P

HEAD = 64
WORDS = 60
EPSILON = 1e-05
SQRT_HALF = 0.7071067811865476
DENSITY = 0.3989422804014327
F32 = jnp.float32
BF16 = jnp.bfloat16
VMEM_BYTES = 58 * 1024 * 1024
SMALL_VMEM_BYTES = 16 * 1024 * 1024


def dot(one, two, one_axis, two_axis):
    return lax.dot_general(
        one, two, (((one_axis,), (two_axis,)), ((), ())), preferred_element_type=F32
    )


def normalize(total, gain, shift):
    centered = total - jnp.mean(total, axis=-1, keepdims=True)
    inv_scale = lax.rsqrt(jnp.mean(centered * centered, axis=-1, keepdims=True) + EPSILON)
    normed = centered * inv_scale
    return normed * gain + shift, normed, inv_scale


def normalize_back(upstream, normed, inv_scale, gain):
    scaled_up = upstream * gain
    mean_one = jnp.mean(scaled_up, axis=-1, keepdims=True)
    mean_two = jnp.mean(scaled_up * normed, axis=-1, keepdims=True)
    return inv_scale * (scaled_up - mean_one - normed * mean_two)


def column_sum(array):
    return jnp.sum(array, axis=0, keepdims=True)


def head_stack(array, heads):
    head = lax.broadcasted_iota(jnp.int32, array.shape, 1) // HEAD
    zero = jnp.zeros_like(array)
    return jnp.concatenate([jnp.where(head == h, array, zero) for h in range(heads)], axis=0)


def head_pick(stacked, heads):
    rows = stacked.shape[0] // heads
    head = lax.broadcasted_iota(jnp.int32, (rows, stacked.shape[1]), 1) // HEAD
    total = stacked[:rows]
    for h in range(1, heads):
        total = jnp.where(head == h, stacked[h * rows : (h + 1) * rows], total)
    return total


def attention_kernel(
    pairs, x_ref, qk_ref, vo_ref, small_ref, valid_ref, vectors_ref,
    q_ref, k_ref, v_ref, weights_ref, context_ref, low_ref, normed_ref, scale_ref, total_ref,
):
    step = pl.program_id(0)
    cols = q_ref.shape[2]
    heads = cols // HEAD
    slots = x_ref.shape[0] // pairs
    x = x_ref[...]
    q_ref[0] = (dot(x, qk_ref[0, :cols], 1, 1) + small_ref[0, 0:1, :cols]).astype(BF16)
    k_ref[0] = dot(x, qk_ref[0, cols:], 1, 1).astype(BF16)
    v_ref[0] = (dot(x, vo_ref[0, :cols], 1, 1) + small_ref[0, 1:2, :cols]).astype(BF16)
    for p in range(pairs):
        rows = slice(p * slots, (p + 1) * slots)
        scores = dot(head_stack(q_ref[0, rows], heads), k_ref[0, rows], 1, 1) * HEAD ** (-0.5)
        scores = jnp.where(valid_ref[p] > 0.5, scores, -1e30)
        exp_scores = jnp.exp(scores - jnp.max(scores, axis=-1, keepdims=True))
        weights = exp_scores / jnp.sum(exp_scores, axis=-1, keepdims=True)
        weights_ref[0, p] = weights
        mixed = dot(weights.astype(BF16), v_ref[0, rows], 1, 0)
        context_ref[0, rows] = head_pick(mixed, heads).astype(BF16)
    branch = dot(context_ref[0], vo_ref[0, cols:], 1, 0)

    @pl.when(step == 0)
    def _():
        total_ref[...] = branch

    @pl.when(step > 0)
    def _():
        total_ref[...] += branch

    @pl.when(step == pl.num_programs(0) - 1)
    def _():
        first_sum = total_ref[...] + vectors_ref[0:1] + x.astype(F32)
        hidden, normed, scale = normalize(first_sum, vectors_ref[1:2], vectors_ref[2:3])
        low_ref[...] = hidden.astype(BF16)
        normed_ref[...] = normed
        scale_ref[...] = scale


def unit_rows(one, two, start, stop):
    half = one.shape[1]
    parts = []
    if start < half:
        parts.append(one[0, start : min(stop, half)])
    if stop > half:
        parts.append(two[0, max(start - half, 0) : stop - half])
    return parts[0] if len(parts) == 1 else jnp.concatenate(parts, axis=0)


def blocks_of(units):
    size = min(256, units)
    return [(start, start + size) for start in range(0, units, size)]


def by_owner(step, body, own, others):
    @pl.when(step == 0)
    def _():
        body(True, *own)

    @pl.when(step > 0)
    def _():
        body(False, *others)


def ffn_kernel(
    here_ref, low_ref, normed_ref, own_in_one, own_in_two, in_one, in_two, own_down_one, own_down_two, down_one,
    down_two, bias_one, bias_two, cot_ref, vectors_ref,
    act_ref, slope_ref, out_ref, delta_ref, ffn_low_ref, sums_ref, total_ref,
):
    step = pl.program_id(0)
    low = low_ref[...]
    half = in_one.shape[1]

    def body(first, w_in_one, w_in_two, w_down_one, w_down_two):
        bias = jnp.concatenate([bias_one[0, 2:3], bias_two[0, 2:3]], axis=1)
        branch = None
        for start, stop in blocks_of(2 * half):
            pre_act = dot(low, unit_rows(w_in_one, w_in_two, start, stop), 1, 1) + bias[:, start:stop]
            share = 0.5 * (1.0 + lax.erf(pre_act * SQRT_HALF))
            act = (pre_act * share).astype(BF16)
            act_ref[0, :, start:stop] = act
            slope_ref[0, :, start:stop] = share + pre_act * (DENSITY * jnp.exp(-0.5 * pre_act * pre_act))
            term = dot(act, unit_rows(w_down_one, w_down_two, start, stop), 1, 0)
            branch = term if branch is None else branch + term
        if first:
            total_ref[...] = branch
        else:
            total_ref[...] += branch

    by_owner(
        step,
        body,
        (own_in_one, own_in_two, own_down_one, own_down_two),
        (in_one, in_two, down_one, down_two),
    )

    @pl.when(step == pl.num_programs(0) - 1)
    def _():
        hidden = normed_ref[...] * vectors_ref[1:2] + vectors_ref[2:3]
        second = total_ref[...] + vectors_ref[3:4] + hidden
        gain = vectors_ref[4:5]
        output, normed, scale = normalize(second, gain, vectors_ref[5:6])
        out_ref[...] = output.astype(BF16)
        upstream = cot_ref[...].astype(F32)
        delta = normalize_back(upstream, normed, scale, gain)
        delta_ref[...] = delta
        ffn_low_ref[...] = delta.astype(BF16)
        sums_ref[...] = jnp.zeros_like(sums_ref)
        sums_ref[0:1] = column_sum(upstream * normed)
        sums_ref[1:2] = column_sum(upstream)
        sums_ref[2:3] = column_sum(delta)


def down_grad_kernel(act_ref, ffn_low_ref, keep_ref, send_ref):
    half = keep_ref.shape[1]
    low = ffn_low_ref[...]
    send_ref[0] = dot(act_ref[0, :, half:], low, 0, 0).astype(BF16)
    keep_ref[0] = dot(act_ref[0, :, :half], low, 0, 0).astype(BF16)


def in_grad_kernel(
    here_ref, ffn_low_ref, low_ref, slope_ref, own_down_one, own_down_two, down_one, down_two,
    keep_ref, send_ref, pre_grad_ref, sum_in_ref,
):
    core = here_ref[0]
    half = keep_ref.shape[1]
    ffn_low = ffn_low_ref[...]

    def body(first, w_down_one, w_down_two):
        for start, stop in blocks_of(2 * half):
            act_grad = dot(ffn_low, unit_rows(w_down_one, w_down_two, start, stop), 1, 1)
            pre_grad_ref[0, :, start:stop] = (act_grad * slope_ref[0, :, start:stop]).astype(BF16)

    by_owner(pl.program_id(0), body, (own_down_one, own_down_two), (down_one, down_two))
    low = low_ref[...]
    one, two = pre_grad_ref[0, :, :half], pre_grad_ref[0, :, half:]
    sum_in_ref[0, :, pl.ds(pl.multiple_of(core * half, half), half)] = column_sum(one.astype(F32))
    sum_in_ref[0, :, pl.ds(pl.multiple_of((1 - core) * half, half), half)] = column_sum(two.astype(F32))
    send_ref[0] = dot(two, low, 0, 0).astype(BF16)
    keep_ref[0] = dot(one, low, 0, 0).astype(BF16)


def ffn_back_kernel(
    here_ref, pre_grad_ref, own_in_one, own_in_two, in_one, in_two, delta_ref, normed_ref, scale_ref, vectors_ref,
    delta_attn_ref, attn_low_ref, sums_ref, total_ref,
):
    step = pl.program_id(0)
    units = pre_grad_ref.shape[2]

    def body(first, w_in_one, w_in_two):
        branch = None
        for start, stop in blocks_of(units):
            term = dot(pre_grad_ref[0, :, start:stop], unit_rows(w_in_one, w_in_two, start, stop), 1, 0)
            branch = term if branch is None else branch + term
        if first:
            total_ref[...] = branch
        else:
            total_ref[...] += branch

    by_owner(step, body, (own_in_one, own_in_two), (in_one, in_two))

    @pl.when(step == pl.num_programs(0) - 1)
    def _():
        hidden_grad = total_ref[...] + delta_ref[...]
        normed = normed_ref[...]
        delta = normalize_back(hidden_grad, normed, scale_ref[...], vectors_ref[1:2])
        delta_attn_ref[...] = delta
        attn_low_ref[...] = delta.astype(BF16)
        sums_ref[...] = jnp.zeros_like(sums_ref)
        sums_ref[0:1] = column_sum(delta)
        sums_ref[1:2] = column_sum(hidden_grad * normed)
        sums_ref[2:3] = column_sum(hidden_grad)


def attention_back_kernel(
    pairs, here_ref, x_ref, attn_low_ref, delta_ref, qk_ref, vo_ref, q_ref, k_ref, v_ref, weights_ref, context_ref,
    sums_one_ref, sums_two_ref, sum_in_ref,
    qk_keep_ref, vo_keep_ref, send_ref, sums_ref, rows_ref, dq_ref, dk_ref, dv_ref, total_ref,
):
    step = pl.program_id(0)
    core = here_ref[0]
    cols = q_ref.shape[2]
    heads = cols // HEAD
    slots = x_ref.shape[0] // pairs
    scale = HEAD ** (-0.5)
    x = x_ref[...]
    attn_low = attn_low_ref[...]
    context_grad = dot(attn_low, vo_ref[0, cols:], 1, 1).astype(BF16)
    grad_out = dot(context_ref[0], attn_low, 0, 0).astype(BF16)
    for p in range(pairs):
        rows = slice(p * slots, (p + 1) * slots)
        up = head_stack(context_grad[rows], heads)
        weights = weights_ref[0, p]
        prob_grad = dot(up, v_ref[0, rows], 1, 1)
        inner = jnp.sum(prob_grad * weights, axis=-1, keepdims=True)
        score_grad = (weights * (prob_grad - inner)).astype(BF16)
        dv_ref[rows] = dot(weights.astype(BF16), up, 0, 0).astype(BF16)
        query_grad = head_pick(dot(score_grad, k_ref[0, rows], 1, 0), heads)
        dq_ref[rows] = (query_grad * scale).astype(BF16)
        key_grad = dot(score_grad, head_stack(q_ref[0, rows], heads), 0, 0)
        dk_ref[rows] = (key_grad * scale).astype(BF16)
    dq, dk, dv = dq_ref[...], dk_ref[...], dv_ref[...]
    shards_ = pl.num_programs(0)

    @pl.when(step == 0)
    def _():
        sums_ref[...] = jnp.zeros_like(sums_ref)
        sums_ref[0:8] = sums_one_ref[...]
        sums_ref[8:16] = sums_two_ref[...]
        for j in range(sum_in_ref.shape[0]):
            sums_ref[16 + j : 17 + j] = sum_in_ref[j]

    row = pl.ds(16 + shards_ + (step ^ here_ref[1]), 1)
    sums_ref[row, :cols] = column_sum(dq.astype(F32))
    sums_ref[row, 2 * cols : 3 * cols] = column_sum(dv.astype(F32))
    grad_q = dot(dq, x, 0, 0).astype(BF16)
    grad_k = dot(dk, x, 0, 0).astype(BF16)
    grad_v = dot(dv, x, 0, 0).astype(BF16)

    @pl.when(core == 0)
    def _():
        qk_keep_ref[0], send_ref[0, 0] = grad_q, grad_k
        vo_keep_ref[0], send_ref[1, 0] = grad_v, grad_out

    @pl.when(core != 0)
    def _():
        qk_keep_ref[0], send_ref[0, 0] = grad_k, grad_q
        vo_keep_ref[0], send_ref[1, 0] = grad_out, grad_v

    branch = dot(dq, qk_ref[0, :cols], 1, 0) + dot(dk, qk_ref[0, cols:], 1, 0)
    branch = branch + dot(dv, vo_ref[0, :cols], 1, 0)

    @pl.when(step == 0)
    def _():
        total_ref[...] = branch + delta_ref[...]

    @pl.when(step > 0)
    def _():
        total_ref[...] += branch

    @pl.when(step == pl.num_programs(0) - 1)
    def _():
        rows_ref[...] = total_ref[...].astype(BF16)


def whole(array):
    return pl.BlockSpec(array.shape, lambda *_: (0,) * len(array.shape))


def per_step(array):
    return pl.BlockSpec((1,) + array.shape[1:], lambda s, *_: (s,) + (0,) * (len(array.shape) - 1))


def call(kernel, steps, name, inputs, outputs, scratch, scalar=None):
    spec = pltpu.PrefetchScalarGridSpec(
        num_scalar_prefetch=0 if scalar is None else 1,
        grid=(steps,),
        in_specs=[make if isinstance(make, pl.BlockSpec) else make(a) for make, a in inputs],
        out_specs=[make if isinstance(make, pl.BlockSpec) else make(a) for make, a in outputs],
        scratch_shapes=scratch,
    )
    return pl.pallas_call(
        kernel,
        grid_spec=spec,
        out_shape=[a for _, a in outputs],
        name=name,
        cost_estimate=pl.CostEstimate(flops=0, bytes_accessed=0, transcendentals=0),
        compiler_params=pltpu.CompilerParams(vmem_limit_bytes=VMEM_BYTES),
    )(*(() if scalar is None else (scalar,)), *[a for _, a in inputs])


def shape(dims, dtype):
    return jax.ShapeDtypeStruct(dims, dtype)


def add_kernel(count, *refs):
    total = refs[1][...].astype(F32)
    for ref in refs[2 : 1 + count]:
        total = total + ref[...].astype(F32)
    refs[1 + count][...] = total.astype(BF16)


def add_terms(terms, me, fixed):
    first, bits = terms[0]
    left = [b for b in bits if b not in fixed]
    n, _, rows, cols = first.shape

    def place(own_bits):
        def index(g, me_ref):
            at = 0
            for b in own_bits:
                if b in fixed:
                    value = (me_ref[0] >> b) & 1
                    value = value if fixed[b] else 1 - value
                else:
                    value = (g >> (len(left) - 1 - left.index(b))) & 1
                at = at * 2 + value
            return (0, at, 0, 0)

        return index

    spec = pltpu.PrefetchScalarGridSpec(
        num_scalar_prefetch=1,
        grid=(1 << len(left),),
        in_specs=[pl.BlockSpec((n, 1, rows, cols), place(b)) for _, b in terms],
        out_specs=pl.BlockSpec((n, 1, rows, cols), lambda g, _: (0, g, 0, 0)),
    )
    out = pl.pallas_call(
        partial(add_kernel, len(terms)),
        grid_spec=spec,
        out_shape=shape((n, 1 << len(left), rows, cols), BF16),
        name="add",
        cost_estimate=pl.CostEstimate(flops=0, bytes_accessed=0, transcendentals=0),
        compiler_params=pltpu.CompilerParams(vmem_limit_bytes=SMALL_VMEM_BYTES),
    )(me, *[a for a, _ in terms])
    return out, left


def flip(array, axis, mask):
    size = lax.axis_size(axis)
    return lax.ppermute(array, axis, [(i, i ^ mask) for i in range(size)])


def tie(*arrays):
    return lax.optimization_barrier(arrays)


def pick(array, axis, index):
    return lax.dynamic_index_in_dim(array, index, axis, keepdims=False)


def outer_bits():
    bits = list(range(1, lax.axis_size("dp").bit_length() - 1))
    return bits, (bits, bits[::-1])


def share_of():
    me = lax.axis_index("dp")
    return (me & 1) * (lax.axis_size("dp") // 2) + (me >> 1)


class Gather:
    def __init__(self, pair):
        self.bits, self.orders = outer_bits()
        self.steps = len(self.bits)
        self.n, _, self.cols = pair[0].shape
        self.held = [
            a.reshape((self.n,) + (1,) * self.steps + a.shape[1:]) for a in pair
        ]

    def send(self, step):
        return [flip(h, "dp", 1 << order[step]) for h, order in zip(self.held, self.orders)]

    def take(self, step, got):
        me = lax.axis_index("dp")
        merged = []
        for mine, theirs, order in zip(self.held, got, self.orders):
            bit = order[step]
            low = ((me >> bit) & 1) == 0
            parts = [jnp.where(low, mine, theirs), jnp.where(low, theirs, mine)]
            merged.append(jnp.concatenate(parts, axis=1 + self.steps - bit))
        self.held = merged

    def send_core(self):
        self.halves = jnp.stack([h.reshape(self.n, -1, self.cols) for h in self.held])
        return flip(self.halves, "dp", 1)

    def finish(self, got):
        low = (lax.axis_index("dp") & 1) == 0
        one, two = jnp.where(low, self.halves, got), jnp.where(low, got, self.halves)
        return [jnp.concatenate([one[i], two[i]], axis=1) for i in range(2)]


class Reduce:
    def __init__(self, keeps, gots):
        self.bits, self.orders = outer_bits()
        self.steps = len(self.bits)
        self.me = lax.axis_index("dp").astype(jnp.int32).reshape(1)
        high_first = self.bits[::-1]
        n, rows, cols = keeps[0].shape
        form = (n, 1 << self.steps, rows >> self.steps, cols)
        self.terms = [
            [(k.reshape(form), high_first), (g.reshape(form), high_first)]
            for k, g in zip(keeps, gots)
        ]
        self.left = [None, None]

    def pack(self, step):
        sends = []
        for side, order in enumerate(self.orders):
            fixed = {b: True for b in order[:step]}
            fixed[order[step]] = False
            out, self.left[side] = add_terms(self.terms[side], self.me, fixed)
            sends.append(out)
        return sends

    def send(self, step, packs):
        return [flip(p, "dp", 1 << order[step]) for p, order in zip(packs, self.orders)]

    def take(self, got):
        for side in range(2):
            self.terms[side].append((got[side], self.left[side]))

    def finish(self):
        fixed = {b: True for b in self.bits}
        return [add_terms(t, self.me, fixed)[0][:, 0] for t in self.terms]


def add_parts(*parts):
    total = parts[0].astype(F32)
    for part in parts[1:]:
        total = total + part.astype(F32)
    return total.astype(BF16)


def shards(
    tokens,
    word_len,
    region_count,
    w_qkv,
    qv_bias,
    w_out,
    out_bias,
    norm1_gain,
    norm1_bias,
    w_in,
    in_bias,
    w_down,
    down_bias,
    norm2_gain,
    norm2_bias,
    cotangent,
):
    mp = lax.axis_size("mp")
    dp = lax.axis_size("dp")
    mi = lax.axis_index("mp")
    width = tokens.shape[2]
    rows_local = tokens.shape[1]
    slots = rows_local * mp
    pairs = tokens.shape[0] // mp
    rows = pairs * slots
    cols = w_qkv.shape[2]
    units = w_in.shape[1]
    half_units = units // 2
    order = jnp.arange(mp) ^ mi
    here = jnp.stack([lax.axis_index("dp") & 1, mi]).astype(jnp.int32)
    share = share_of()

    turned = w_qkv.transpose(0, 2, 1)
    own = {
        "qk": turned[:2].reshape(2 * cols, width),
        "vo": jnp.concatenate([turned[2], w_out], axis=0),
        "in": w_in.T,
        "down": w_down,
    }

    def piece(name):
        part = own[name].shape[0] // dp
        return lax.dynamic_slice_in_dim(own[name], share * part, part, 0)

    def row_blocks(array):
        blocks = array.reshape((mp, pairs) + array.shape[1:])
        return [pick(blocks, 0, mi ^ k) for k in range(mp)]

    def join(blocks):
        return jnp.concatenate(blocks, axis=1).reshape(rows, width)

    fill = lambda v: jnp.pad(v, ((0, 0), (0, width - v.shape[1])))
    small = jnp.concatenate([fill(qv_bias), in_bias.reshape(1, units), jnp.zeros((5, width), BF16)])
    att_part, ffn_part = 2 * cols // dp, units // dp
    att_send = jnp.concatenate([piece("qk"), piece("vo"), small], axis=0)
    ffn_send = jnp.concatenate([piece("in"), piece("down")], axis=0)
    tok = row_blocks(tokens)
    cot = row_blocks(cotangent)
    vectors = jnp.stack(
        [out_bias, norm1_gain, norm1_bias, down_bias, norm2_gain, norm2_bias, out_bias, out_bias]
    ).astype(F32)
    words = lax.dynamic_slice_in_dim(word_len, mi * pairs, pairs, 0)
    regions = lax.dynamic_slice_in_dim(region_count, mi * pairs, pairs, 0)
    slot_index = (order[:, None] * rows_local + jnp.arange(rows_local)[None, :]).reshape(-1)
    key_valid = jnp.where(
        slot_index[None, :] < WORDS,
        slot_index[None, :] < words[:, None],
        slot_index[None, :] - WORDS < regions[:, None],
    ).astype(F32)[:, None, :]

    att_two = flip(att_send, "mp", 2)
    att_two, ffn_send, tok, vectors, key_valid = tie(att_two, ffn_send, tok, vectors, key_valid)
    att_odd = flip(jnp.stack([att_send, att_two]), "mp", 1)
    ffn_two = flip(ffn_send, "mp", 2)
    att_odd, ffn_two = tie(att_odd, ffn_two)
    att_got = [att_odd[0], att_two, att_odd[1]]
    att = Gather(
        [
            jnp.stack([g[:att_part] for g in att_got]),
            jnp.stack([g[att_part : 2 * att_part] for g in att_got]),
        ]
    )
    ffn_odd = flip(jnp.stack([ffn_send, ffn_two]), "mp", 1)
    got = att.send(0)
    smalls = jnp.stack([small] + [g[2 * att_part :] for g in att_got]).astype(F32)
    ffn_odd, got, tok, smalls = tie(ffn_odd, got, tok, smalls)
    for step in range(1, att.steps):
        att.take(step - 1, got)
        got = att.send(step)
        if step == 1:
            tok_one, tok_three = flip(tok[1], "mp", 1), flip(tok[3], "mp", 3)
        got, tok_one, tok_three, tok = tie(got, tok_one, tok_three, tok)
    att.take(att.steps - 1, got)
    ffn_got = [ffn_odd[0], ffn_two, ffn_odd[1]]
    ffn = Gather(
        [
            jnp.stack([g[:ffn_part] for g in ffn_got]),
            jnp.stack([g[ffn_part:] for g in ffn_got]),
        ]
    )
    got = ffn.send(0)
    core_got = att.send_core()
    tok_two = flip(tok[2], "mp", 2)
    got, core_got, tok_two, cot = tie(got, core_got, tok_two, cot)
    qk_others, vo_others = att.finish(core_got)
    qk_all = jnp.concatenate([own["qk"][None], qk_others])
    vo_all = jnp.concatenate([own["vo"][None], vo_others])
    x = join([tok[0], tok_one, tok_two, tok_three])
    heads_low = shape((mp, rows, cols), BF16)
    low_shape = shape((rows, width), BF16)
    rows_shape = shape((rows, width), F32)
    sums_shape = shape((8, width), F32)
    for step in range(1, ffn.steps):
        ffn.take(step - 1, got)
        got = ffn.send(step)
        if step == 1:
            cot_one, cot_three = flip(cot[1], "mp", 1), flip(cot[3], "mp", 3)
            got, qk_all, vo_all, x = tie(got, qk_all, vo_all, x) if ffn.steps > 2 else (got, qk_all, vo_all, x)
    q, k, v, weights, context, hidden_low, normed_one, scale_one = call(
        partial(attention_kernel, pairs),
        mp,
        "attention",
        [
            (whole, x),
            (per_step, qk_all),
            (per_step, vo_all),
            (per_step, smalls),
            (whole, key_valid),
            (whole, vectors),
        ],
        [
            (per_step, heads_low),
            (per_step, heads_low),
            (per_step, heads_low),
            (per_step, shape((mp, pairs, cols // HEAD * slots, slots), F32)),
            (per_step, heads_low),
            (whole, low_shape),
            (whole, rows_shape),
            (whole, shape((rows, 1), F32)),
        ],
        [pltpu.VMEM((rows, width), F32)],
    )
    got, hidden_low, cot_one, cot_three, cot = tie(got, hidden_low, cot_one, cot_three, cot)
    ffn.take(ffn.steps - 1, got)
    in_one, down_one = [h.reshape(mp - 1, half_units, width) for h in ffn.held]
    in_two, down_two = flip(in_one, "dp", 1), flip(down_one, "dp", 1)
    cot_two = flip(cot[2], "mp", 2)
    in_two, down_two, cot_two, hidden_low = tie(in_two, down_two, cot_two, hidden_low)
    cot_rows = join([cot[0], cot_one, cot_two, cot_three])

    one_block, two_block = (1, half_units, width), (1, half_units, width)
    mine = pl.BlockSpec(one_block, lambda s, h: (h[0], 0, 0))
    other = pl.BlockSpec(one_block, lambda s, h: (1 - h[0], 0, 0))
    later = pl.BlockSpec(two_block, lambda s, h: (jnp.maximum(s - 1, 0), 0, 0))
    own_in = own["in"].reshape(2, half_units, width)
    own_down = own["down"].reshape(2, half_units, width)
    in_args = [(mine, own_in), (other, own_in), (later, in_one), (later, in_two)]
    down_args = [(mine, own_down), (other, own_down), (later, down_one), (later, down_two)]
    act, slope, output, delta_ffn, ffn_low, sums_two = call(
        ffn_kernel,
        mp,
        "ffn",
        [
            (whole, hidden_low),
            (whole, normed_one),
            *in_args,
            *down_args,
            (pl.BlockSpec((1, 8, half_units), lambda s, h: (s, 0, h[0])), smalls),
            (pl.BlockSpec((1, 8, half_units), lambda s, h: (s, 0, 1 - h[0])), smalls),
            (whole, cot_rows),
            (whole, vectors),
        ],
        [
            (per_step, shape((mp, rows, units), BF16)),
            (per_step, shape((mp, rows, units), F32)),
            (whole, low_shape),
            (whole, rows_shape),
            (whole, low_shape),
            (whole, sums_shape),
        ],
        [pltpu.VMEM((rows, width), F32)],
        here,
    )
    half = shape((mp, half_units, width), BF16)
    down_keep, down_send = call(
        down_grad_kernel,
        mp,
        "down_grad",
        [(per_step, act), (whole, ffn_low)],
        [(per_step, half), (per_step, half)],
        [],
    )
    down_send, ffn_low = tie(down_send, ffn_low)
    down_got = flip(down_send, "dp", 1)
    in_keep, in_send, pre_grad, sum_in = call(
        in_grad_kernel,
        mp,
        "in_grad",
        [(whole, ffn_low), (whole, hidden_low), (per_step, slope), *down_args],
        [
            (per_step, half),
            (per_step, half),
            (per_step, shape((mp, rows, units), BF16)),
            (
                pl.BlockSpec((1, 1, units), lambda s, h: (s ^ h[1], 0, 0)),
                shape((mp, 1, units), F32),
            ),
        ],
        [],
        here,
    )
    out_rows = output.reshape(pairs, mp, rows_local, width)
    out_blocks = [out_rows[:, k] for k in range(mp)]
    down_got, in_send, pre_grad, out_blocks = tie(down_got, in_send, pre_grad, out_blocks)
    in_got = flip(in_send, "dp", 1)
    delta_attn, attn_low, sums_one = call(
        ffn_back_kernel,
        mp,
        "ffn_back",
        [
            (per_step, pre_grad),
            *in_args,
            (whole, delta_ffn),
            (whole, normed_one),
            (whole, scale_one),
            (whole, vectors),
        ],
        [(whole, rows_shape), (whole, low_shape), (whole, sums_shape)],
        [pltpu.VMEM((rows, width), F32)],
        here,
    )
    in_got, attn_low = tie(in_got, attn_low)
    ffn = Reduce([in_keep, down_keep], [in_got, down_got])
    packs = ffn.pack(0)
    packs, attn_low = tie(packs, attn_low)
    got = ffn.send(0, packs)
    out_got = [out_blocks[0]] + [flip(out_blocks[k], "mp", k) for k in range(1, mp)]
    small_half = shape((mp, cols, width), BF16)
    qk_keep, vo_keep, att_send, sums, grad_rows = call(
        partial(attention_back_kernel, pairs),
        mp,
        "attention_back",
        [
            (whole, x),
            (whole, attn_low),
            (whole, delta_attn),
            (per_step, qk_all),
            (per_step, vo_all),
            (per_step, q),
            (per_step, k),
            (per_step, v),
            (per_step, weights),
            (per_step, context),
            (whole, sums_one),
            (whole, sums_two),
            (whole, sum_in),
        ],
        [
            (per_step, small_half),
            (per_step, small_half),
            (
                pl.BlockSpec((2, 1, cols, width), lambda s, h: (0, s, 0, 0)),
                shape((2, mp, cols, width), BF16),
            ),
            (whole, shape((16 + 2 * mp, width), F32)),
            (whole, low_shape),
        ],
        [pltpu.VMEM((rows, cols), BF16)] * 3 + [pltpu.VMEM((rows, width), F32)],
        here,
    )
    grad_rows = grad_rows.reshape(pairs, mp, rows_local, width)
    row_sends = [grad_rows[:, k] for k in range(mp)]
    got, out_got, att_send, row_sends, sums = tie(got, out_got, att_send, row_sends, sums)
    for step in range(1, ffn.steps):
        ffn.take(got)
        packs = ffn.pack(step)
        got = ffn.send(step, packs)
        if step == 1:
            att_got = flip(att_send, "dp", 1)
            sums_got = flip(sums, "dp", 1)
            row_three = flip(row_sends[3], "mp", 3)
        got, att_got, sums_got, row_three, row_sends = tie(got, att_got, sums_got, row_three, row_sends)
    ffn.take(got)
    sums = sums + sums_got
    ffn_parts = ffn.finish()
    ffn_odd = jnp.concatenate([p[1::2] for p in ffn_parts], axis=1)
    ffn_even = jnp.concatenate([p[0::2] for p in ffn_parts], axis=1)
    att = Reduce([qk_keep, vo_keep], [att_got[0], att_got[1]])
    packs = att.pack(0)
    ffn_odd, ffn_even, packs, sums = tie(ffn_odd, ffn_even, packs, sums)
    got = att.send(0, packs)
    ffn_got = flip(ffn_odd, "mp", 1)
    row_one = flip(row_sends[1], "mp", 1)
    sums_got = flip(sums, "dp", 2)
    got, ffn_got, row_one, sums_got = tie(got, ffn_got, row_one, sums_got)
    sums = sums + sums_got
    for mask in [1 << b for b in range(2, dp.bit_length() - 2)]:
        sums = sums + flip(sums, "dp", mask)
    ffn_two = add_parts(ffn_even[1], ffn_got[1])
    for step in range(1, att.steps):
        att.take(got)
        packs = att.pack(step)
        got = att.send(step, packs)
        if step == 1:
            ffn_last = flip(ffn_two, "mp", 2)
            sums_got = flip(sums, "dp", dp // 2)
        got, ffn_last, sums_got, row_sends = tie(got, ffn_last, sums_got, row_sends)
    att.take(got)
    sums = sums + sums_got
    att_parts = att.finish()
    att_odd = jnp.concatenate([p[1::2] for p in att_parts], axis=1)
    att_even = jnp.concatenate([p[0::2] for p in att_parts], axis=1)
    ffn_sum = add_parts(ffn_even[0], ffn_got[0], ffn_last)
    ffn = Gather([ffn_sum[None, :ffn_part], ffn_sum[None, ffn_part:]])
    ffn.held, att_odd, att_even, sums = tie(ffn.held, att_odd, att_even, sums)
    got = ffn.send(0)
    att_got = flip(att_odd, "mp", 1)
    row_two = flip(row_sends[2], "mp", 2)
    sums_got = flip(sums, "mp", 1)
    got, att_got, row_two, sums_got = tie(got, att_got, row_two, sums_got)
    sums = sums + sums_got
    att_two = add_parts(att_even[1], att_got[1])
    for step in range(1, ffn.steps):
        ffn.take(step - 1, got)
        got = ffn.send(step)
        if step == 1:
            att_last = flip(att_two, "mp", 2)
            sums_got = flip(sums, "mp", 2)
        got, att_last, sums_got = tie(got, att_last, sums_got)
    ffn.take(ffn.steps - 1, got)
    sums = sums + sums_got
    att_sum = add_parts(att_even[0], att_got[0], att_last)
    att = Gather([att_sum[None, :att_part], att_sum[None, att_part:]])
    core_got = ffn.send_core()
    got = att.send(0)
    core_got, got = tie(core_got, got)
    grad_in, grad_down = ffn.finish(core_got)
    for step in range(1, att.steps):
        att.take(step - 1, got)
        got = tie(*att.send(step))
    att.take(att.steps - 1, got)
    grad_qk, grad_vo = att.finish(att.send_core())

    def leave(blocks):
        return jnp.take(jnp.stack(blocks), order, axis=0).reshape(mp * pairs, rows_local, width)

    layer_out = leave(out_got)
    grad_input = leave([row_sends[0], row_one, row_two, row_three]).astype(F32)
    sum_in_bias = lax.dynamic_index_in_dim(sums, 16 + mi, 0, keepdims=False)
    sum_qv = lax.dynamic_index_in_dim(sums, 16 + mp + mi, 0, keepdims=False)
    sum_qv = jnp.stack([sum_qv[:cols], sum_qv[2 * cols : 3 * cols]])
    grad_qkv = jnp.concatenate([grad_qk[0], grad_vo[0, :cols]], axis=0).reshape(3, cols, width)
    return (
        layer_out,
        grad_input,
        grad_qkv.astype(F32).transpose(0, 2, 1),
        sum_qv,
        grad_vo[0, cols:].astype(F32),
        sums[0],
        sums[1],
        sums[2],
        grad_in[0].astype(F32).T,
        sum_in_bias,
        grad_down[0].astype(F32),
        sums[10],
        sums[8],
        sums[9],
    )


def solution(mesh):
    in_specs = (
        P("dp", "mp", None),
        P("dp"),
        P("dp"),
        P(None, None, "mp"),
        P(None, "mp"),
        P("mp", None),
        P(),
        P(),
        P(),
        P(None, "mp"),
        P("mp"),
        P("mp", None),
        P(),
        P(),
        P(),
        P("dp", "mp", None),
    )
    out_specs = (
        P("dp", "mp", None),
        P("dp", "mp", None),
        P(None, None, "mp"),
        P(None, "mp"),
        P("mp", None),
        P(),
        P(),
        P(),
        P(None, "mp"),
        P("mp"),
        P("mp", None),
        P(),
        P(),
        P(),
    )
    return jax.shard_map(shards, mesh=mesh, in_specs=in_specs, out_specs=out_specs, check_vma=False)
```

```python
from functools import partial

import jax
import jax.numpy as jnp
from jax import lax
from jax.experimental import pallas as pl
from jax.experimental.pallas import tpu as pltpu
from jax.sharding import PartitionSpec as P

HEAD = 64
WORDS = 60
EPSILON = 1e-05
SQRT_HALF = 0.7071067811865476
DENSITY = 0.3989422804014327
F32 = jnp.float32
BF16 = jnp.bfloat16
MIB = 1024 * 1024


def dot(one, two, one_axis, two_axis):
    return lax.dot_general(
        one, two, (((one_axis,), (two_axis,)), ((), ())), preferred_element_type=F32
    )


def normalize(total, gain, shift):
    centered = total - jnp.mean(total, axis=-1, keepdims=True)
    inv_scale = lax.rsqrt(jnp.mean(centered * centered, axis=-1, keepdims=True) + EPSILON)
    normed = centered * inv_scale
    return normed * gain + shift, normed, inv_scale


def normalize_back(upstream, normed, inv_scale, gain):
    scaled_up = upstream * gain
    mean_one = jnp.mean(scaled_up, axis=-1, keepdims=True)
    mean_two = jnp.mean(scaled_up * normed, axis=-1, keepdims=True)
    return inv_scale * (scaled_up - mean_one - normed * mean_two)


def column_sum(array):
    return jnp.sum(array, axis=0, keepdims=True)


def head_stack(array, heads):
    head = lax.broadcasted_iota(jnp.int32, array.shape, 1) // HEAD
    zero = jnp.zeros_like(array)
    return jnp.concatenate([jnp.where(head == h, array, zero) for h in range(heads)], axis=0)


def head_pick(stacked, heads):
    rows = stacked.shape[0] // heads
    head = lax.broadcasted_iota(jnp.int32, (rows, stacked.shape[1]), 1) // HEAD
    total = stacked[:rows]
    for h in range(1, heads):
        total = jnp.where(head == h, stacked[h * rows : (h + 1) * rows], total)
    return total


def head_weights(here_ref, own_ref, one_ref, two_ref):
    first, low = pl.program_id(0) == 0, here_ref[0] == 0
    half = one_ref.shape[1]
    one, two = one_ref[0], two_ref[0]
    return (
        jnp.where(first, own_ref[:half], jnp.where(low, one, two)),
        jnp.where(first, own_ref[half:], jnp.where(low, two, one)),
    )


def attention_kernel(
    pairs, here_ref, x_ref, own_qk, qk_one, qk_two, own_vo, vo_one, vo_two, small_ref, valid_ref, vectors_ref,
    q_ref, k_ref, v_ref, weights_ref, context_ref, low_ref, normed_ref, scale_ref, total_ref,
):
    step = pl.program_id(0)
    cols = q_ref.shape[2]
    heads = cols // HEAD
    slots = x_ref.shape[0] // pairs
    x = x_ref[...]
    w_q, w_k = head_weights(here_ref, own_qk, qk_one, qk_two)
    w_v, w_o = head_weights(here_ref, own_vo, vo_one, vo_two)
    q_ref[0] = (dot(x, w_q, 1, 1) + small_ref[0, 0:1, :cols]).astype(BF16)
    k_ref[0] = dot(x, w_k, 1, 1).astype(BF16)
    v_ref[0] = (dot(x, w_v, 1, 1) + small_ref[0, 1:2, :cols]).astype(BF16)
    for p in range(pairs):
        rows = slice(p * slots, (p + 1) * slots)
        scores = dot(head_stack(q_ref[0, rows], heads), k_ref[0, rows], 1, 1) * HEAD ** (-0.5)
        scores = jnp.where(valid_ref[p] > 0.5, scores, -1e30)
        exp_scores = jnp.exp(scores - jnp.max(scores, axis=-1, keepdims=True))
        weights = exp_scores / jnp.sum(exp_scores, axis=-1, keepdims=True)
        weights_ref[0, p] = weights
        mixed = dot(weights.astype(BF16), v_ref[0, rows], 1, 0)
        context_ref[0, rows] = head_pick(mixed, heads).astype(BF16)
    branch = dot(context_ref[0], w_o, 1, 0)

    @pl.when(step == 0)
    def _():
        total_ref[...] = branch

    @pl.when(step > 0)
    def _():
        total_ref[...] += branch

    @pl.when(step == pl.num_programs(0) - 1)
    def _():
        first_sum = total_ref[...] + vectors_ref[0:1] + x.astype(F32)
        hidden, normed, scale = normalize(first_sum, vectors_ref[1:2], vectors_ref[2:3])
        low_ref[...] = hidden.astype(BF16)
        normed_ref[...] = normed
        scale_ref[...] = scale


def unit_rows(one, two, start, stop):
    half = one.shape[1]
    parts = []
    if start < half:
        parts.append(one[0, start : min(stop, half)])
    if stop > half:
        parts.append(two[0, max(start - half, 0) : stop - half])
    return parts[0] if len(parts) == 1 else jnp.concatenate(parts, axis=0)


def blocks_of(units):
    size = min(256, units)
    return [(start, start + size) for start in range(0, units, size)]


def ffn_kernel(
    here_ref, low_ref, normed_ref, own_in_one, own_in_two, in_one, in_two, own_down_one, own_down_two, down_one,
    down_two, bias_one, bias_two, cot_ref, vectors_ref,
    out_ref, delta_ref, pre_grad_ref, in_keep_ref, in_send_ref, down_keep_ref, down_send_ref, sum_in_ref, sums_ref,
    act_ref, slope_ref, ffn_low_ref, total_ref,
):
    step = pl.program_id(0)
    shards_ = pl.num_programs(0) // 2
    core = here_ref[0]
    half = in_one.shape[1]

    def down_of(first, slot):
        if first:
            return own_down_one, own_down_two
        other = pl.ds(slot - 1, 1)
        return down_one.at[other], down_two.at[other]

    def forward(first):
        low = low_ref[...]
        bias = jnp.concatenate([bias_one[0, 2:3], bias_two[0, 2:3]], axis=1)
        w_in = (own_in_one, own_in_two) if first else (in_one, in_two)
        w_down = down_of(first, step)
        branch = None
        for start, stop in blocks_of(2 * half):
            pre_act = dot(low, unit_rows(*w_in, start, stop), 1, 1) + bias[:, start:stop]
            share = 0.5 * (1.0 + lax.erf(pre_act * SQRT_HALF))
            act = (pre_act * share).astype(BF16)
            act_ref[step, :, start:stop] = act
            slope_ref[step, :, start:stop] = share + pre_act * (DENSITY * jnp.exp(-0.5 * pre_act * pre_act))
            term = dot(act, unit_rows(*w_down, start, stop), 1, 0)
            branch = term if branch is None else branch + term
        if first:
            total_ref[...] = branch
        else:
            total_ref[...] += branch

    def backward(first):
        slot = 0 if first else step - shards_
        ffn_low = ffn_low_ref[...]
        w_down = down_of(first, slot)
        for start, stop in blocks_of(2 * half):
            act_grad = dot(ffn_low, unit_rows(*w_down, start, stop), 1, 1)
            pre_grad_ref[0, :, start:stop] = (act_grad * slope_ref[slot, :, start:stop]).astype(BF16)
        down_send_ref[0] = dot(act_ref[slot, :, half:], ffn_low, 0, 0).astype(BF16)
        down_keep_ref[0] = dot(act_ref[slot, :, :half], ffn_low, 0, 0).astype(BF16)
        low = low_ref[...]
        one, two = pre_grad_ref[0, :, :half], pre_grad_ref[0, :, half:]
        sum_in_ref[0, :, pl.ds(pl.multiple_of(core * half, half), half)] = column_sum(one.astype(F32))
        sum_in_ref[0, :, pl.ds(pl.multiple_of((1 - core) * half, half), half)] = column_sum(two.astype(F32))
        in_send_ref[0] = dot(two, low, 0, 0).astype(BF16)
        in_keep_ref[0] = dot(one, low, 0, 0).astype(BF16)

    pl.when(step == 0)(partial(forward, True))
    pl.when((step > 0) & (step < shards_))(partial(forward, False))

    @pl.when(step == shards_ - 1)
    def _():
        hidden = normed_ref[...] * vectors_ref[1:2] + vectors_ref[2:3]
        second = total_ref[...] + vectors_ref[3:4] + hidden
        gain = vectors_ref[4:5]
        output, normed, scale = normalize(second, gain, vectors_ref[5:6])
        out_ref[...] = output.astype(BF16)
        upstream = cot_ref[...].astype(F32)
        delta = normalize_back(upstream, normed, scale, gain)
        delta_ref[...] = delta
        ffn_low_ref[...] = delta.astype(BF16)
        sums_ref[...] = jnp.zeros_like(sums_ref)
        sums_ref[0:1] = column_sum(upstream * normed)
        sums_ref[1:2] = column_sum(upstream)
        sums_ref[2:3] = column_sum(delta)

    pl.when(step == shards_)(partial(backward, True))
    pl.when(step > shards_)(partial(backward, False))


def ffn_back_kernel(
    here_ref, pre_grad_ref, own_in_one, own_in_two, in_one, in_two, delta_ref, normed_ref, scale_ref, vectors_ref,
    delta_attn_ref, attn_low_ref, sums_ref, total_ref,
):
    step = pl.program_id(0)
    units = pre_grad_ref.shape[2]

    def body(first, w_in_one, w_in_two):
        branch = None
        for start, stop in blocks_of(units):
            term = dot(pre_grad_ref[0, :, start:stop], unit_rows(w_in_one, w_in_two, start, stop), 1, 0)
            branch = term if branch is None else branch + term
        if first:
            total_ref[...] = branch
        else:
            total_ref[...] += branch

    pl.when(step == 0)(partial(body, True, own_in_one, own_in_two))
    pl.when(step > 0)(partial(body, False, in_one, in_two))

    @pl.when(step == pl.num_programs(0) - 1)
    def _():
        hidden_grad = total_ref[...] + delta_ref[...]
        normed = normed_ref[...]
        delta = normalize_back(hidden_grad, normed, scale_ref[...], vectors_ref[1:2])
        delta_attn_ref[...] = delta
        attn_low_ref[...] = delta.astype(BF16)
        sums_ref[...] = jnp.zeros_like(sums_ref)
        sums_ref[0:1] = column_sum(delta)
        sums_ref[1:2] = column_sum(hidden_grad * normed)
        sums_ref[2:3] = column_sum(hidden_grad)


def attention_back_kernel(
    pairs, here_ref, x_ref, attn_low_ref, delta_ref, own_qk, qk_one, qk_two, own_vo, vo_one, vo_two, q_ref, k_ref, v_ref, weights_ref, context_ref,
    sums_one_ref, sums_two_ref, sum_in_ref,
    qk_keep_ref, vo_keep_ref, send_ref, sums_ref, rows_ref, dq_ref, dk_ref, dv_ref, total_ref,
):
    step = pl.program_id(0)
    core = here_ref[0]
    cols = q_ref.shape[2]
    heads = cols // HEAD
    slots = x_ref.shape[0] // pairs
    scale = HEAD ** (-0.5)
    x = x_ref[...]
    attn_low = attn_low_ref[...]
    w_q, w_k = head_weights(here_ref, own_qk, qk_one, qk_two)
    w_v, w_o = head_weights(here_ref, own_vo, vo_one, vo_two)
    context_grad = dot(attn_low, w_o, 1, 1).astype(BF16)
    grad_out = dot(context_ref[0], attn_low, 0, 0).astype(BF16)
    for p in range(pairs):
        rows = slice(p * slots, (p + 1) * slots)
        up = head_stack(context_grad[rows], heads)
        weights = weights_ref[0, p]
        prob_grad = dot(up, v_ref[0, rows], 1, 1)
        inner = jnp.sum(prob_grad * weights, axis=-1, keepdims=True)
        score_grad = (weights * (prob_grad - inner)).astype(BF16)
        dv_ref[rows] = dot(weights.astype(BF16), up, 0, 0).astype(BF16)
        query_grad = head_pick(dot(score_grad, k_ref[0, rows], 1, 0), heads)
        dq_ref[rows] = (query_grad * scale).astype(BF16)
        key_grad = dot(score_grad, head_stack(q_ref[0, rows], heads), 0, 0)
        dk_ref[rows] = (key_grad * scale).astype(BF16)
    dq, dk, dv = dq_ref[...], dk_ref[...], dv_ref[...]
    shards_ = pl.num_programs(0)

    @pl.when(step == 0)
    def _():
        sums_ref[...] = jnp.zeros_like(sums_ref)
        sums_ref[0:8] = sums_one_ref[...]
        sums_ref[8:16] = sums_two_ref[...]
        for j in range(sum_in_ref.shape[0]):
            sums_ref[16 + j : 17 + j] = sum_in_ref[j]

    row = pl.ds(16 + shards_ + (step ^ here_ref[1]), 1)
    sums_ref[row, :cols] = column_sum(dq.astype(F32))
    sums_ref[row, 2 * cols : 3 * cols] = column_sum(dv.astype(F32))
    grad_q = dot(dq, x, 0, 0).astype(BF16)
    grad_k = dot(dk, x, 0, 0).astype(BF16)
    grad_v = dot(dv, x, 0, 0).astype(BF16)

    @pl.when(core == 0)
    def _():
        qk_keep_ref[0], send_ref[0, 0] = grad_q, grad_k
        vo_keep_ref[0], send_ref[1, 0] = grad_v, grad_out

    @pl.when(core != 0)
    def _():
        qk_keep_ref[0], send_ref[0, 0] = grad_k, grad_q
        vo_keep_ref[0], send_ref[1, 0] = grad_out, grad_v

    branch = dot(dq, w_q, 1, 0) + dot(dk, w_k, 1, 0) + dot(dv, w_v, 1, 0)

    @pl.when(step == 0)
    def _():
        total_ref[...] = branch + delta_ref[...]

    @pl.when(step > 0)
    def _():
        total_ref[...] += branch

    @pl.when(step == pl.num_programs(0) - 1)
    def _():
        rows_ref[...] = total_ref[...].astype(BF16)


def whole(array):
    return pl.BlockSpec(array.shape, lambda *_: (0,) * len(array.shape))


def per_step(array):
    return pl.BlockSpec((1,) + array.shape[1:], lambda s, *_: (s,) + (0,) * (len(array.shape) - 1))


def call(kernel, steps, name, vmem, inputs, outputs, scratch, scalar, kept=()):
    spec = pltpu.PrefetchScalarGridSpec(
        num_scalar_prefetch=1,
        grid=(steps,),
        in_specs=[make if isinstance(make, pl.BlockSpec) else make(a) for make, a in inputs],
        out_specs=[make if isinstance(make, pl.BlockSpec) else make(a) for make, a in outputs],
        scratch_shapes=scratch,
    )
    return pl.pallas_call(
        kernel,
        grid_spec=spec,
        out_shape=[pltpu.HBM(a.shape, a.dtype) if i in kept else a for i, (_, a) in enumerate(outputs)],
        name=name,
        cost_estimate=pl.CostEstimate(flops=0, bytes_accessed=0, transcendentals=0),
        compiler_params=pltpu.CompilerParams(vmem_limit_bytes=vmem * MIB),
    )(scalar, *[a for _, a in inputs])


def shape(dims, dtype):
    return jax.ShapeDtypeStruct(dims, dtype)


def add_kernel(count, *refs):
    total = refs[1][...].astype(F32)
    for ref in refs[2 : 1 + count]:
        total = total + ref[...].astype(F32)
    refs[1 + count][...] = total.astype(BF16)


def add_terms(terms, me, fixed):
    first, bits = terms[0]
    left = [b for b in bits if b not in fixed]
    n, _, rows, cols = first.shape

    def place(own_bits):
        def index(g, me_ref):
            at = 0
            for b in own_bits:
                if b in fixed:
                    value = (me_ref[0] >> b) & 1
                    value = value if fixed[b] else 1 - value
                else:
                    value = (g >> (len(left) - 1 - left.index(b))) & 1
                at = at * 2 + value
            return (0, at, 0, 0)

        return index

    spec = pltpu.PrefetchScalarGridSpec(
        num_scalar_prefetch=1,
        grid=(1 << len(left),),
        in_specs=[pl.BlockSpec((n, 1, rows, cols), place(b)) for _, b in terms],
        out_specs=pl.BlockSpec((n, 1, rows, cols), lambda g, _: (0, g, 0, 0)),
    )
    out = pl.pallas_call(
        partial(add_kernel, len(terms)),
        grid_spec=spec,
        out_shape=shape((n, 1 << len(left), rows, cols), BF16),
        name="add",
        cost_estimate=pl.CostEstimate(flops=0, bytes_accessed=0, transcendentals=0),
        compiler_params=pltpu.CompilerParams(vmem_limit_bytes=16 * MIB),
    )(me, *[a for a, _ in terms])
    return out, left


def flip(array, axis, mask):
    size = lax.axis_size(axis)
    return lax.ppermute(array, axis, [(i, i ^ mask) for i in range(size)])


def tie(*arrays):
    return lax.optimization_barrier(arrays)


def pick(array, axis, index):
    return lax.dynamic_index_in_dim(array, index, axis, keepdims=False)


def outer_bits():
    bits = list(range(1, lax.axis_size("dp").bit_length() - 1))
    return bits, (bits, bits[::-1])


def share_of():
    me = lax.axis_index("dp")
    return (me & 1) * (lax.axis_size("dp") // 2) + (me >> 1)


class Gather:
    def __init__(self, pair):
        self.bits, self.orders = outer_bits()
        self.steps = len(self.bits)
        self.n, _, self.cols = pair[0].shape
        self.held = [
            a.reshape((self.n,) + (1,) * self.steps + a.shape[1:]) for a in pair
        ]

    def send(self, step):
        return [flip(h, "dp", 1 << order[step]) for h, order in zip(self.held, self.orders)]

    def take(self, step, got):
        me = lax.axis_index("dp")
        merged = []
        for mine, theirs, order in zip(self.held, got, self.orders):
            bit = order[step]
            low = ((me >> bit) & 1) == 0
            parts = [jnp.where(low, mine, theirs), jnp.where(low, theirs, mine)]
            merged.append(jnp.concatenate(parts, axis=1 + self.steps - bit))
        self.held = merged

    def halves(self):
        return [h.reshape(self.n, -1, self.cols) for h in self.held]

    def finish(self, halves, got):
        low = (lax.axis_index("dp") & 1) == 0
        return [
            jnp.concatenate([jnp.where(low, h, g), jnp.where(low, g, h)], axis=1)
            for h, g in zip(halves, got)
        ]


class Reduce:
    def __init__(self, keeps, gots):
        self.bits, self.orders = outer_bits()
        self.steps = len(self.bits)
        self.me = lax.axis_index("dp").astype(jnp.int32).reshape(1)
        high_first = self.bits[::-1]
        n, rows, cols = keeps[0].shape
        form = (n, 1 << self.steps, rows >> self.steps, cols)
        self.terms = [
            [(k.reshape(form), high_first), (g.reshape(form), high_first)]
            for k, g in zip(keeps, gots)
        ]
        self.left = [None, None]

    def pack(self, step):
        sends = []
        for side, order in enumerate(self.orders):
            fixed = {b: True for b in order[:step]}
            fixed[order[step]] = False
            out, self.left[side] = add_terms(self.terms[side], self.me, fixed)
            sends.append(out)
        return sends

    def send(self, step, packs):
        return [flip(p, "dp", 1 << order[step]) for p, order in zip(packs, self.orders)]

    def take(self, got):
        for side in range(2):
            self.terms[side].append((got[side], self.left[side]))

    def finish(self):
        fixed = {b: True for b in self.bits}
        return [add_terms(t, self.me, fixed)[0][:, 0] for t in self.terms]


def add_parts(*parts):
    total = parts[0].astype(F32)
    for part in parts[1:]:
        total = total + part.astype(F32)
    return total.astype(BF16)


def shards(
    tokens,
    word_len,
    region_count,
    w_qkv,
    qv_bias,
    w_out,
    out_bias,
    norm1_gain,
    norm1_bias,
    w_in,
    in_bias,
    w_down,
    down_bias,
    norm2_gain,
    norm2_bias,
    cotangent,
):
    mp = lax.axis_size("mp")
    dp = lax.axis_size("dp")
    mi = lax.axis_index("mp")
    width = tokens.shape[2]
    rows_local = tokens.shape[1]
    slots = rows_local * mp
    pairs = tokens.shape[0] // mp
    rows = pairs * slots
    cols = w_qkv.shape[2]
    units = w_in.shape[1]
    half_units = units // 2
    order = jnp.arange(mp) ^ mi
    here = jnp.stack([lax.axis_index("dp") & 1, mi]).astype(jnp.int32)
    share = share_of()

    turned = w_qkv.transpose(0, 2, 1)
    own = {
        "qk": turned[:2].reshape(2 * cols, width),
        "vo": jnp.concatenate([turned[2], w_out], axis=0),
        "in": w_in.T,
        "down": w_down,
    }

    def piece(name):
        part = own[name].shape[0] // dp
        return lax.dynamic_slice_in_dim(own[name], share * part, part, 0)

    def row_blocks(array):
        blocks = array.reshape((mp, pairs) + array.shape[1:])
        return [pick(blocks, 0, mi ^ k) for k in range(mp)]

    def join(blocks):
        return jnp.concatenate(blocks, axis=1).reshape(rows, width)

    fill = lambda v: jnp.pad(v, ((0, 0), (0, width - v.shape[1])))
    small = jnp.concatenate([fill(qv_bias), in_bias.reshape(1, units), jnp.zeros((5, width), BF16)])
    att_part, ffn_part = 2 * cols // dp, units // dp
    att_send = jnp.concatenate([piece("qk"), piece("vo"), small], axis=0)
    ffn_send = jnp.concatenate([piece("in"), piece("down")], axis=0)
    tok = row_blocks(tokens)
    cot = row_blocks(cotangent)
    vectors = jnp.stack(
        [out_bias, norm1_gain, norm1_bias, down_bias, norm2_gain, norm2_bias, out_bias, out_bias]
    ).astype(F32)
    words = lax.dynamic_slice_in_dim(word_len, mi * pairs, pairs, 0)
    regions = lax.dynamic_slice_in_dim(region_count, mi * pairs, pairs, 0)
    slot_index = (order[:, None] * rows_local + jnp.arange(rows_local)[None, :]).reshape(-1)
    key_valid = jnp.where(
        slot_index[None, :] < WORDS,
        slot_index[None, :] < words[:, None],
        slot_index[None, :] - WORDS < regions[:, None],
    ).astype(F32)[:, None, :]

    att_two = flip(att_send, "mp", 2)
    att_two, ffn_send, tok, vectors, key_valid, here, own = tie(
        att_two, ffn_send, tok, vectors, key_valid, here, own
    )
    att_odd = flip(jnp.stack([att_send, att_two]), "mp", 1)
    ffn_two = flip(ffn_send, "mp", 2)
    att_odd, ffn_two = tie(att_odd, ffn_two)
    att_got = [att_odd[0], att_two, att_odd[1]]
    att = Gather(
        [
            jnp.stack([g[:att_part] for g in att_got]),
            jnp.stack([g[att_part : 2 * att_part] for g in att_got]),
        ]
    )
    ffn_odd = flip(jnp.stack([ffn_send, ffn_two]), "mp", 1)
    got = att.send(0)
    smalls = jnp.stack([small] + [g[2 * att_part :] for g in att_got]).astype(F32)
    ffn_odd, got, tok, smalls = tie(ffn_odd, got, tok, smalls)
    for step in range(1, att.steps):
        att.take(step - 1, got)
        got = att.send(step)
        if step == 1:
            tok_one, tok_three = flip(tok[1], "mp", 1), flip(tok[3], "mp", 3)
        got, tok_one, tok_three, tok = tie(got, tok_one, tok_three, tok)
    att.take(att.steps - 1, got)
    ffn_got = [ffn_odd[0], ffn_two, ffn_odd[1]]
    ffn = Gather(
        [
            jnp.stack([g[:ffn_part] for g in ffn_got]),
            jnp.stack([g[ffn_part:] for g in ffn_got]),
        ]
    )
    got = ffn.send(0)
    qk_one, vo_one = att.halves()
    qk_two, vo_two = flip(qk_one, "dp", 1), flip(vo_one, "dp", 1)
    tok_two = flip(tok[2], "mp", 2)
    got, qk_two, vo_two, tok_two, cot = tie(got, qk_two, vo_two, tok_two, cot)
    x = join([tok[0], tok_one, tok_two, tok_three])
    heads_low = shape((mp, rows, cols), BF16)
    low_shape = shape((rows, width), BF16)
    rows_shape = shape((rows, width), F32)
    sums_shape = shape((8, width), F32)
    for step in range(1, ffn.steps):
        ffn.take(step - 1, got)
        got = ffn.send(step)
        if step == 1:
            cot_one, cot_two, cot_three = [flip(cot[k], "mp", k) for k in range(1, mp)]
        if step < ffn.steps - 1:
            got = tie(*got)
    later = lambda a: pl.BlockSpec((1,) + a.shape[1:], lambda s, h: (jnp.clip(s - 1, 0, mp - 2), 0, 0))
    head_args = [
        (whole, own["qk"]),
        (later, qk_one),
        (later, qk_two),
        (whole, own["vo"]),
        (later, vo_one),
        (later, vo_two),
    ]
    q, k, v, weights, context, hidden_low, normed_one, scale_one = call(
        partial(attention_kernel, pairs),
        mp,
        "attention",
        32,
        [
            (whole, x),
            *head_args,
            (per_step, smalls),
            (whole, key_valid),
            (whole, vectors),
        ],
        [
            (per_step, heads_low),
            (per_step, heads_low),
            (per_step, heads_low),
            (per_step, shape((mp, pairs, cols // HEAD * slots, slots), F32)),
            (per_step, heads_low),
            (whole, low_shape),
            (whole, rows_shape),
            (whole, shape((rows, 1), F32)),
        ],
        [pltpu.VMEM((rows, width), F32)],
        here,
        range(5),
    )
    got, hidden_low, cot_one, cot_two, cot_three = tie(got, hidden_low, cot_one, cot_two, cot_three)
    ffn.take(ffn.steps - 1, got)
    in_one, down_one = ffn.halves()
    in_two, down_two = flip(in_one, "dp", 1), flip(down_one, "dp", 1)
    cot_rows = join([cot[0], cot_one, cot_two, cot_three])
    in_two, down_two, hidden_low, cot_rows = tie(in_two, down_two, hidden_low, cot_rows)

    half_block = (1, half_units, width)
    mine = pl.BlockSpec(half_block, lambda s, h: (h[0], 0, 0))
    other = pl.BlockSpec(half_block, lambda s, h: (1 - h[0], 0, 0))
    own_in = own["in"].reshape(2, half_units, width)
    own_down = own["down"].reshape(2, half_units, width)
    in_args = [(mine, own_in), (other, own_in), (later, in_one), (later, in_two)]
    down_args = [(mine, own_down), (other, own_down), (whole, down_one), (whole, down_two)]
    half = shape((mp, half_units, width), BF16)
    bias_block = (1, 8, half_units)
    back_step = lambda s: jnp.maximum(s - mp, 0)
    back = lambda a: pl.BlockSpec((1,) + a.shape[1:], lambda s, h: (back_step(s), 0, 0))
    output, delta_ffn, pre_grad, in_keep, in_send, down_keep, down_send, sum_in, sums_two = call(
        ffn_kernel,
        2 * mp,
        "ffn",
        52,
        [
            (whole, hidden_low),
            (whole, normed_one),
            *in_args,
            *down_args,
            (pl.BlockSpec(bias_block, lambda s, h: (jnp.minimum(s, mp - 1), 0, h[0])), smalls),
            (pl.BlockSpec(bias_block, lambda s, h: (jnp.minimum(s, mp - 1), 0, 1 - h[0])), smalls),
            (whole, cot_rows),
            (whole, vectors),
        ],
        [
            (whole, low_shape),
            (whole, rows_shape),
            (back, shape((mp, rows, units), BF16)),
            (back, half),
            (back, half),
            (back, half),
            (back, half),
            (
                pl.BlockSpec((1, 1, units), lambda s, h: (back_step(s) ^ h[1], 0, 0)),
                shape((mp, 1, units), F32),
            ),
            (whole, sums_shape),
        ],
        [
            pltpu.VMEM((mp, rows, units), BF16),
            pltpu.VMEM((mp, rows, units), F32),
            pltpu.VMEM((rows, width), BF16),
            pltpu.VMEM((rows, width), F32),
        ],
        here,
        range(2, 7),
    )
    in_got, down_got = flip(in_send, "dp", 1), flip(down_send, "dp", 1)
    delta_attn, attn_low, sums_one = call(
        ffn_back_kernel,
        mp,
        "ffn_back",
        24,
        [
            (per_step, pre_grad),
            *in_args,
            (whole, delta_ffn),
            (whole, normed_one),
            (whole, scale_one),
            (whole, vectors),
        ],
        [(whole, rows_shape), (whole, low_shape), (whole, sums_shape)],
        [pltpu.VMEM((rows, width), F32)],
        here,
    )
    out_rows = output.reshape(pairs, mp, rows_local, width)
    out_blocks = [out_rows[:, k] for k in range(mp)]
    in_got, down_got, attn_low, out_blocks = tie(in_got, down_got, attn_low, out_blocks)
    ffn = Reduce([in_keep, down_keep], [in_got, down_got])
    packs = ffn.pack(0)
    packs, attn_low = tie(packs, attn_low)
    got = ffn.send(0, packs)
    out_got = [out_blocks[0]] + [flip(out_blocks[k], "mp", k) for k in range(1, mp)]
    small_half = shape((mp, cols, width), BF16)
    qk_keep, vo_keep, att_send, sums, grad_rows = call(
        partial(attention_back_kernel, pairs),
        mp,
        "attention_back",
        32,
        [
            (whole, x),
            (whole, attn_low),
            (whole, delta_attn),
            *head_args,
            (per_step, q),
            (per_step, k),
            (per_step, v),
            (per_step, weights),
            (per_step, context),
            (whole, sums_one),
            (whole, sums_two),
            (whole, sum_in),
        ],
        [
            (per_step, small_half),
            (per_step, small_half),
            (
                pl.BlockSpec((2, 1, cols, width), lambda s, h: (0, s, 0, 0)),
                shape((2, mp, cols, width), BF16),
            ),
            (whole, shape((16 + 2 * mp, width), F32)),
            (whole, low_shape),
        ],
        [pltpu.VMEM((rows, cols), BF16)] * 3 + [pltpu.VMEM((rows, width), F32)],
        here,
    )
    grad_rows = grad_rows.reshape(pairs, mp, rows_local, width)
    row_sends = [grad_rows[:, k] for k in range(mp)]
    got, out_got, att_send, row_sends, sums = tie(got, out_got, att_send, row_sends, sums)
    for step in range(1, ffn.steps):
        ffn.take(got)
        packs = ffn.pack(step)
        got = ffn.send(step, packs)
        if step == 1:
            att_got = flip(att_send, "dp", 1)
            row_two, row_three = flip(row_sends[2], "mp", 2), flip(row_sends[3], "mp", 3)
        got, att_got, row_two, row_three, row_sends = tie(got, att_got, row_two, row_three, row_sends)
    ffn.take(got)
    ffn_parts = ffn.finish()
    ffn_odd = jnp.concatenate([p[1::2] for p in ffn_parts], axis=1)
    ffn_even = jnp.concatenate([p[0::2] for p in ffn_parts], axis=1)
    att = Reduce([qk_keep, vo_keep], [att_got[0], att_got[1]])
    packs = att.pack(0)
    ffn_odd, ffn_even, packs, sums = tie(ffn_odd, ffn_even, packs, sums)
    got = att.send(0, packs)
    ffn_got = flip(ffn_odd, "mp", 1)
    sums_got = flip(sums, "dp", 1)
    got, ffn_got, sums_got, row_sends, out_got = tie(got, ffn_got, sums_got, row_sends, out_got)
    sums = sums + sums_got
    for mask in [1 << b for b in range(2, dp.bit_length() - 2)]:
        sums = sums + flip(sums, "dp", mask)
    ffn_two = add_parts(ffn_even[1], ffn_got[1])
    for step in range(1, att.steps):
        att.take(got)
        packs = att.pack(step)
        got = att.send(step, packs)
        if step == 1:
            ffn_last = flip(ffn_two, "mp", 2)
            row_one = flip(row_sends[1], "mp", 1)
            sums_got = flip(sums, "dp", 2)
        got, ffn_last, row_one, sums_got = tie(got, ffn_last, row_one, sums_got)
    att.take(got)
    sums = sums + sums_got
    att_parts = att.finish()
    att_odd = jnp.concatenate([p[1::2] for p in att_parts], axis=1)
    att_even = jnp.concatenate([p[0::2] for p in att_parts], axis=1)
    ffn_sum = add_parts(ffn_even[0], ffn_got[0], ffn_last)
    ffn = Gather([ffn_sum[None, :ffn_part], ffn_sum[None, ffn_part:]])
    ffn.held, att_odd, att_even, sums = tie(ffn.held, att_odd, att_even, sums)
    got = ffn.send(0)
    att_got = flip(att_odd, "mp", 1)
    sums_got = flip(sums, "dp", dp // 2)
    got, att_got, sums_got = tie(got, att_got, sums_got)
    sums = sums + sums_got
    att_two = add_parts(att_even[1], att_got[1])
    for step in range(1, ffn.steps):
        ffn.take(step - 1, got)
        got = ffn.send(step)
        if step == 1:
            att_last = flip(att_two, "mp", 2)
            sums_got = flip(sums, "mp", 1)
        got, att_last, sums_got = tie(got, att_last, sums_got)
    ffn.take(ffn.steps - 1, got)
    sums = sums + sums_got
    att_sum = add_parts(att_even[0], att_got[0], att_last)
    att = Gather([att_sum[None, :att_part], att_sum[None, att_part:]])
    ffn_halves = ffn.halves()
    core_got = [flip(h, "dp", 1) for h in ffn_halves]
    got = att.send(0)
    sums_got = flip(sums, "mp", 2)
    core_got, got, sums_got, row_one, row_two, row_three = tie(
        core_got, got, sums_got, row_one, row_two, row_three
    )
    sums = sums + sums_got
    grad_in, grad_down = ffn.finish(ffn_halves, core_got)
    grad_in, grad_down = grad_in[0].astype(F32).T, grad_down[0].astype(F32)
    for step in range(1, att.steps):
        att.take(step - 1, got)
        got = tie(*att.send(step))
    grad_in, grad_down, got, row_one = tie(grad_in, grad_down, got, row_one)
    att.take(att.steps - 1, got)
    att_halves = att.halves()
    grad_qk, grad_vo = att.finish(att_halves, [flip(h, "dp", 1) for h in att_halves])

    def leave(blocks):
        return jnp.take(jnp.stack(blocks), order, axis=0).reshape(mp * pairs, rows_local, width)

    layer_out = leave(out_got)
    grad_input = leave([row_sends[0], row_one, row_two, row_three]).astype(F32)
    sum_in_bias = lax.dynamic_index_in_dim(sums, 16 + mi, 0, keepdims=False)
    sum_qv = lax.dynamic_index_in_dim(sums, 16 + mp + mi, 0, keepdims=False)
    sum_qv = jnp.stack([sum_qv[:cols], sum_qv[2 * cols : 3 * cols]])
    grad_qkv = jnp.concatenate([grad_qk[0], grad_vo[0, :cols]], axis=0).reshape(3, cols, width)
    return (
        layer_out,
        grad_input,
        grad_qkv.astype(F32).transpose(0, 2, 1),
        sum_qv,
        grad_vo[0, cols:].astype(F32),
        sums[0],
        sums[1],
        sums[2],
        grad_in,
        sum_in_bias,
        grad_down,
        sums[10],
        sums[8],
        sums[9],
    )


def solution(mesh):
    in_specs = (
        P("dp", "mp", None),
        P("dp"),
        P("dp"),
        P(None, None, "mp"),
        P(None, "mp"),
        P("mp", None),
        P(),
        P(),
        P(),
        P(None, "mp"),
        P("mp"),
        P("mp", None),
        P(),
        P(),
        P(),
        P("dp", "mp", None),
    )
    out_specs = (
        P("dp", "mp", None),
        P("dp", "mp", None),
        P(None, None, "mp"),
        P(None, "mp"),
        P("mp", None),
        P(),
        P(),
        P(),
        P(None, "mp"),
        P("mp"),
        P("mp", None),
        P(),
        P(),
        P(),
    )
    return jax.shard_map(shards, mesh=mesh, in_specs=in_specs, out_specs=out_specs, check_vma=False)
```

```python
from functools import partial

import jax
import jax.numpy as jnp
from jax import lax
from jax.experimental import pallas as pl
from jax.experimental.pallas import tpu as pltpu
from jax.sharding import PartitionSpec as P

HEAD = 64
WORDS = 60
EPSILON = 1e-05
SQRT_HALF = 0.7071067811865476
DENSITY = 0.3989422804014327
F32 = jnp.float32
BF16 = jnp.bfloat16
MIB = 1024 * 1024


def dot(one, two, one_axis, two_axis):
    return lax.dot_general(
        one, two, (((one_axis,), (two_axis,)), ((), ())), preferred_element_type=F32
    )


def normalize(total, gain, shift):
    centered = total - jnp.mean(total, axis=-1, keepdims=True)
    inv_scale = lax.rsqrt(jnp.mean(centered * centered, axis=-1, keepdims=True) + EPSILON)
    normed = centered * inv_scale
    return normed * gain + shift, normed, inv_scale


def normalize_back(upstream, normed, inv_scale, gain):
    scaled_up = upstream * gain
    mean_one = jnp.mean(scaled_up, axis=-1, keepdims=True)
    mean_two = jnp.mean(scaled_up * normed, axis=-1, keepdims=True)
    return inv_scale * (scaled_up - mean_one - normed * mean_two)


def column_sum(array):
    return jnp.sum(array, axis=0, keepdims=True)


def head_stack(array, heads):
    head = lax.broadcasted_iota(jnp.int32, array.shape, 1) // HEAD
    zero = jnp.zeros_like(array)
    return jnp.concatenate([jnp.where(head == h, array, zero) for h in range(heads)], axis=0)


def head_pick(stacked, heads):
    rows = stacked.shape[0] // heads
    head = lax.broadcasted_iota(jnp.int32, (rows, stacked.shape[1]), 1) // HEAD
    total = stacked[:rows]
    for h in range(1, heads):
        total = jnp.where(head == h, stacked[h * rows : (h + 1) * rows], total)
    return total


def head_weights(first, here_ref, own_ref, one_ref, two_ref):
    low = here_ref[0] == 0
    half = one_ref.shape[1]
    one, two = one_ref[0], two_ref[0]
    return (
        jnp.where(first, own_ref[:half], jnp.where(low, one, two)),
        jnp.where(first, own_ref[half:], jnp.where(low, two, one)),
    )


def attention_kernel(
    pairs, here_ref, x_ref, own_qk, qk_one, qk_two, own_vo, vo_one, vo_two, small_ref, valid_ref, vectors_ref,
    q_ref, k_ref, v_ref, weights_ref, context_ref, low_ref, normed_ref, scale_ref, total_ref,
):
    step = pl.program_id(0)
    cols = q_ref.shape[2]
    heads = cols // HEAD
    slots = x_ref.shape[0] // pairs
    x = x_ref[...]
    w_q, w_k = head_weights(step == 0, here_ref, own_qk, qk_one, qk_two)
    w_v, w_o = head_weights(step == 0, here_ref, own_vo, vo_one, vo_two)
    q_ref[0] = (dot(x, w_q, 1, 1) + small_ref[0, 0:1, :cols]).astype(BF16)
    k_ref[0] = dot(x, w_k, 1, 1).astype(BF16)
    v_ref[0] = (dot(x, w_v, 1, 1) + small_ref[0, 1:2, :cols]).astype(BF16)
    for p in range(pairs):
        rows = slice(p * slots, (p + 1) * slots)
        scores = dot(head_stack(q_ref[0, rows], heads), k_ref[0, rows], 1, 1) * HEAD ** (-0.5)
        scores = jnp.where(valid_ref[p] > 0.5, scores, -1e30)
        exp_scores = jnp.exp(scores - jnp.max(scores, axis=-1, keepdims=True))
        weights = exp_scores / jnp.sum(exp_scores, axis=-1, keepdims=True)
        weights_ref[0, p] = weights
        mixed = dot(weights.astype(BF16), v_ref[0, rows], 1, 0)
        context_ref[0, rows] = head_pick(mixed, heads).astype(BF16)
    branch = dot(context_ref[0], w_o, 1, 0)

    @pl.when(step == 0)
    def _():
        total_ref[...] = branch

    @pl.when(step > 0)
    def _():
        total_ref[...] += branch

    @pl.when(step == pl.num_programs(0) - 1)
    def _():
        first_sum = total_ref[...] + vectors_ref[0:1] + x.astype(F32)
        hidden, normed, scale = normalize(first_sum, vectors_ref[1:2], vectors_ref[2:3])
        low_ref[...] = hidden.astype(BF16)
        normed_ref[...] = normed
        scale_ref[...] = scale


def unit_rows(one, two, start, stop):
    half = one.shape[1]
    parts = []
    if start < half:
        parts.append(one[0, start : min(stop, half)])
    if stop > half:
        parts.append(two[0, max(start - half, 0) : stop - half])
    return parts[0] if len(parts) == 1 else jnp.concatenate(parts, axis=0)


def unit_columns(one, two, start, stop):
    half = one.shape[1]
    parts = []
    if start < half:
        parts.append(one[:, start : min(stop, half)])
    if stop > half:
        parts.append(two[:, max(start - half, 0) : stop - half])
    return parts[0] if len(parts) == 1 else jnp.concatenate(parts, axis=1)


def blocks_of(units):
    size = min(256, units)
    return [(start, start + size) for start in range(0, units, size)]


def join_rows(refs):
    pairs = refs[0].shape[0]
    return jnp.concatenate([ref[p].astype(F32) for p in range(pairs) for ref in refs], axis=0)


def leave_rows(array, refs):
    pairs, rows = refs[0].shape[:2]
    for p in range(pairs):
        for j, ref in enumerate(refs):
            start = (p * len(refs) + j) * rows
            ref[p] = array[start : start + rows].astype(BF16)


def ffn_kernel(
    count, here_ref, low_hbm, normed_hbm, w_in_hbm, in_one_hbm, in_two_hbm, w_down_hbm, down_one_hbm, down_two_hbm,
    small_ref, vectors_ref, *refs,
):
    cot_hbm, out_refs = refs[:count], refs[count : 2 * count]
    (
        delta_hbm, pre_grad_hbm, in_keep_hbm, in_send_hbm, down_keep_hbm, down_send_hbm, sum_in_ref, sums_ref,
        low_ref, normed_ref, w_in_ref, in_one, in_two, w_down_ref, down_one, down_two, cot_ref, act_ref, slope_ref,
        total_ref, delta_ref, pre_grad_ref, in_keep_ref, in_send_ref, down_keep_ref, down_send_ref, sems,
    ) = refs[2 * count :]
    core = here_ref[0]
    half = in_one.shape[1]
    started = [0]

    def start(*pairs):
        copies = []
        for source, target in pairs:
            copies.append(pltpu.make_async_copy(source, target, sems.at[started[0]]))
            copies[-1].start()
            started[0] += 1
        return copies

    def wait(copies):
        for copy in copies:
            copy.wait()

    def shard(slot):
        k = slot - 1
        return start(
            (in_one_hbm.at[k], in_one.at[k]),
            (in_two_hbm.at[k], in_two.at[k]),
            (down_one_hbm.at[k], down_one.at[k]),
            (down_two_hbm.at[k], down_two.at[k]),
        )

    def halves(start_, stop):
        parts = []
        if start_ < half:
            parts.append((0, start_, min(stop, half)))
        if stop > half:
            parts.append((1, max(start_ - half, 0), stop - half))
        return parts

    def own(which, first, last):
        side = core if which == 0 else 1 - core
        return pl.ds(pl.multiple_of(side * half + first, 128), last - first)

    def down_rows(slot, start_, stop):
        if slot == 0:
            parts = [w_down_ref[own(w, a, b)] for w, a, b in halves(start_, stop)]
        else:
            parts = [(down_one, down_two)[w][slot - 1, a:b] for w, a, b in halves(start_, stop)]
        return jnp.concatenate(parts, axis=0)

    def forward(slot):
        low = low_ref[...]
        branch = None
        for first, last in blocks_of(2 * half):
            parts = halves(first, last)
            if slot == 0:
                w_in = jnp.concatenate([w_in_ref[:, own(*p)] for p in parts], axis=1)
                pre_act = dot(low, w_in, 1, 0)
            else:
                w_in = jnp.concatenate([(in_one, in_two)[w][slot - 1, a:b] for w, a, b in parts], axis=0)
                pre_act = dot(low, w_in, 1, 1)
            bias = jnp.concatenate([small_ref[slot, 2:3, own(*p)] for p in parts], axis=1)
            pre_act = pre_act + bias
            share = 0.5 * (1.0 + lax.erf(pre_act * SQRT_HALF))
            act = (pre_act * share).astype(BF16)
            act_ref[slot, :, first:last] = act
            slope_ref[slot, :, first:last] = share + pre_act * (DENSITY * jnp.exp(-0.5 * pre_act * pre_act))
            term = dot(act, down_rows(slot, first, last), 1, 0)
            branch = term if branch is None else branch + term
        if slot == 0:
            total_ref[...] = branch
        else:
            total_ref[...] += branch

    first_copies = start((low_hbm, low_ref), (w_in_hbm, w_in_ref), (w_down_hbm, w_down_ref))
    ahead = shard(1)
    wait(first_copies)
    forward(0)
    for slot in range(1, count):
        copies = ahead
        if slot + 1 < count:
            ahead = shard(slot + 1)
        else:
            ahead = start((normed_hbm, normed_ref), *[(cot_hbm[k], cot_ref.at[k]) for k in range(count)])
        wait(copies)
        forward(slot)
    wait(ahead)

    hidden = normed_ref[...] * vectors_ref[1:2] + vectors_ref[2:3]
    second = total_ref[...] + vectors_ref[3:4] + hidden
    gain = vectors_ref[4:5]
    output, normed, scale = normalize(second, gain, vectors_ref[5:6])
    leave_rows(output, out_refs)
    upstream = join_rows([cot_ref.at[k] for k in range(count)])
    delta = normalize_back(upstream, normed, scale, gain)
    delta_ref[...] = delta
    leaving = start((delta_ref, delta_hbm))
    sums_ref[...] = jnp.zeros_like(sums_ref)
    sums_ref[0:1] = column_sum(upstream * normed)
    sums_ref[1:2] = column_sum(upstream)
    sums_ref[2:3] = column_sum(delta)
    ffn_low = delta.astype(BF16)
    low = low_ref[...]
    for slot in range(count):
        for first, last in blocks_of(2 * half):
            act_grad = dot(ffn_low, down_rows(slot, first, last), 1, 1)
            pre_grad_ref[slot, :, first:last] = (act_grad * slope_ref[slot, :, first:last]).astype(BF16)
        leaving += start((pre_grad_ref.at[slot], pre_grad_hbm.at[slot]))
        down_send_ref[slot] = dot(act_ref[slot, :, half:], ffn_low, 0, 0).astype(BF16)
        leaving += start((down_send_ref.at[slot], down_send_hbm.at[slot]))
        down_keep_ref[slot] = dot(act_ref[slot, :, :half], ffn_low, 0, 0).astype(BF16)
        leaving += start((down_keep_ref.at[slot], down_keep_hbm.at[slot]))
        one, two = pre_grad_ref[slot, :, :half], pre_grad_ref[slot, :, half:]
        in_send_ref[slot] = dot(two, low, 0, 0).astype(BF16)
        leaving += start((in_send_ref.at[slot], in_send_hbm.at[slot]))
        in_keep_ref[slot] = dot(one, low, 0, 0).astype(BF16)
        leaving += start((in_keep_ref.at[slot], in_keep_hbm.at[slot]))
        natural = slot ^ here_ref[1]
        sum_in_ref[natural, :, own(0, 0, half)] = column_sum(one.astype(F32))
        sum_in_ref[natural, :, own(1, 0, half)] = column_sum(two.astype(F32))
    wait(leaving)


def ffn_back_kernel(
    here_ref, pre_grad_ref, own_in_one, own_in_two, in_one, in_two, delta_ref, normed_ref, scale_ref, vectors_ref,
    delta_attn_ref, attn_low_ref, sums_ref, total_ref,
):
    step = pl.program_id(0)

    def body(first):
        branch = None
        for start, stop in blocks_of(pre_grad_ref.shape[2]):
            pre_grad = pre_grad_ref[0, :, start:stop]
            if first:
                term = dot(pre_grad, unit_columns(own_in_one, own_in_two, start, stop), 1, 1)
            else:
                term = dot(pre_grad, unit_rows(in_one, in_two, start, stop), 1, 0)
            branch = term if branch is None else branch + term
        if first:
            total_ref[...] = branch
        else:
            total_ref[...] += branch

    pl.when(step == 0)(partial(body, True))
    pl.when(step > 0)(partial(body, False))

    @pl.when(step == pl.num_programs(0) - 1)
    def _():
        hidden_grad = total_ref[...] + delta_ref[...]
        normed = normed_ref[...]
        delta = normalize_back(hidden_grad, normed, scale_ref[...], vectors_ref[1:2])
        delta_attn_ref[...] = delta
        attn_low_ref[...] = delta.astype(BF16)
        sums_ref[...] = jnp.zeros_like(sums_ref)
        sums_ref[0:1] = column_sum(delta)
        sums_ref[1:2] = column_sum(hidden_grad * normed)
        sums_ref[2:3] = column_sum(hidden_grad)


def attention_back_kernel(
    pairs, here_ref, x_ref, attn_low_ref, delta_ref, own_qk, qk_one, qk_two, own_vo, vo_one, vo_two, q_ref, k_ref,
    v_ref, weights_ref, context_ref, sums_one_ref, sums_two_ref, sum_in_ref,
    qk_keep_ref, vo_keep_ref, send_ref, sums_ref, *refs,
):
    step = pl.program_id(0)
    shards_ = pl.num_programs(0)
    out_refs = refs[:shards_]
    dq_ref, dk_ref, dv_ref, total_ref = refs[shards_:]

    @pl.when(step == 0)
    def _():
        total_ref[...] = delta_ref[...]
        sums_ref[...] = jnp.zeros_like(sums_ref)
        sums_ref[0:8] = sums_one_ref[...]
        sums_ref[8:16] = sums_two_ref[...]
        for j in range(shards_):
            sums_ref[16 + j : 17 + j] = sum_in_ref[j]

    core = here_ref[0]
    cols = q_ref.shape[2]
    heads = cols // HEAD
    slots = x_ref.shape[0] // pairs
    scale = HEAD ** (-0.5)
    x = x_ref[...]
    attn_low = attn_low_ref[...]
    w_q, w_k = head_weights(step == 0, here_ref, own_qk, qk_one, qk_two)
    w_v, w_o = head_weights(step == 0, here_ref, own_vo, vo_one, vo_two)
    context_grad = dot(attn_low, w_o, 1, 1).astype(BF16)
    grad_out = dot(context_ref[0], attn_low, 0, 0).astype(BF16)
    for p in range(pairs):
        rows = slice(p * slots, (p + 1) * slots)
        up = head_stack(context_grad[rows], heads)
        weights = weights_ref[0, p]
        prob_grad = dot(up, v_ref[0, rows], 1, 1)
        inner = jnp.sum(prob_grad * weights, axis=-1, keepdims=True)
        score_grad = (weights * (prob_grad - inner)).astype(BF16)
        dv_ref[rows] = dot(weights.astype(BF16), up, 0, 0).astype(BF16)
        query_grad = head_pick(dot(score_grad, k_ref[0, rows], 1, 0), heads)
        dq_ref[rows] = (query_grad * scale).astype(BF16)
        key_grad = dot(score_grad, head_stack(q_ref[0, rows], heads), 0, 0)
        dk_ref[rows] = (key_grad * scale).astype(BF16)
    dq, dk, dv = dq_ref[...], dk_ref[...], dv_ref[...]
    row = pl.ds(16 + shards_ + (step ^ here_ref[1]), 1)
    sums_ref[row, :cols] = column_sum(dq.astype(F32))
    sums_ref[row, 2 * cols : 3 * cols] = column_sum(dv.astype(F32))
    grad_q = dot(dq, x, 0, 0).astype(BF16)
    grad_k = dot(dk, x, 0, 0).astype(BF16)
    grad_v = dot(dv, x, 0, 0).astype(BF16)

    @pl.when(core == 0)
    def _():
        qk_keep_ref[0], send_ref[0, 0] = grad_q, grad_k
        vo_keep_ref[0], send_ref[1, 0] = grad_v, grad_out

    @pl.when(core != 0)
    def _():
        qk_keep_ref[0], send_ref[0, 0] = grad_k, grad_q
        vo_keep_ref[0], send_ref[1, 0] = grad_out, grad_v

    total_ref[...] += dot(dq, w_q, 1, 0) + dot(dk, w_k, 1, 0) + dot(dv, w_v, 1, 0)

    @pl.when(step == shards_ - 1)
    def _():
        leave_rows(total_ref[...], out_refs)


def place_kernel(pairs, here_ref, *refs):
    out_ref = refs[-1]
    for k, ref in enumerate(refs[:-1]):
        out_ref[pl.ds((here_ref[1] ^ k) * pairs, pairs)] = ref[...].astype(out_ref.dtype)


def head_grads_kernel(here_ref, qk_ref, vo_ref, qk_other, vo_other, grad_qkv_ref, grad_out_ref):
    low = here_ref[0] == 0
    pick_two = lambda a, b: (jnp.where(low, a[0], b[0]), jnp.where(low, b[0], a[0]))
    grad_q, grad_k = pick_two(qk_ref, qk_other)
    grad_v, grad_out = pick_two(vo_ref, vo_other)
    for j, grad in enumerate((grad_q, grad_k, grad_v)):
        grad_qkv_ref[j] = grad.astype(F32)
    grad_out_ref[...] = grad_out.astype(F32)


def unit_grads_kernel(here_ref, in_ref, down_ref, in_other, down_other, grad_in_ref, grad_down_ref):
    half = in_ref.shape[1]
    mine = pl.multiple_of(here_ref[0] * half, half)
    other = pl.multiple_of((1 - here_ref[0]) * half, half)
    grad_in_ref[:, pl.ds(mine, half)] = in_ref[0].astype(F32).T
    grad_in_ref[:, pl.ds(other, half)] = in_other[0].astype(F32).T
    grad_down_ref[pl.ds(mine, half)] = down_ref[0].astype(F32)
    grad_down_ref[pl.ds(other, half)] = down_other[0].astype(F32)


def whole(array):
    return pl.BlockSpec(array.shape, lambda *_: (0,) * len(array.shape))


def per_step(array):
    return pl.BlockSpec((1,) + array.shape[1:], lambda s, *_: (s,) + (0,) * (len(array.shape) - 1))


def in_place(array):
    if array.size * array.dtype.itemsize < MIB:
        return array
    return pltpu.with_memory_space_constraint(array, pltpu.HBM)


def where_it_is(array):
    return pl.BlockSpec(memory_space=pl.ANY)


def call(kernel, steps, name, vmem, inputs, outputs, scratch, scalar, kept=()):
    spec = pltpu.PrefetchScalarGridSpec(
        num_scalar_prefetch=1,
        grid=(steps,),
        in_specs=[make if isinstance(make, pl.BlockSpec) else make(a) for make, a in inputs],
        out_specs=[make if isinstance(make, pl.BlockSpec) else make(a) for make, a in outputs],
        scratch_shapes=scratch,
    )
    return pl.pallas_call(
        kernel,
        grid_spec=spec,
        out_shape=[pltpu.HBM(a.shape, a.dtype) if i in kept else a for i, (_, a) in enumerate(outputs)],
        name=name,
        cost_estimate=pl.CostEstimate(flops=0, bytes_accessed=0, transcendentals=0),
        compiler_params=pltpu.CompilerParams(vmem_limit_bytes=vmem * MIB),
    )(scalar, *[in_place(a) for _, a in inputs])


def shape(dims, dtype):
    return jax.ShapeDtypeStruct(dims, dtype)


def add_kernel(count, *refs):
    total = refs[1][...].astype(F32)
    for ref in refs[2 : 1 + count]:
        total = total + ref[...].astype(F32)
    refs[1 + count][...] = total.astype(BF16)


def add_terms(terms, me, fixed):
    first, bits = terms[0]
    left = [b for b in bits if b not in fixed]
    n, _, rows, cols = first.shape

    def place(own_bits):
        def index(g, me_ref):
            at = 0
            for b in own_bits:
                if b in fixed:
                    value = (me_ref[0] >> b) & 1
                    value = value if fixed[b] else 1 - value
                else:
                    value = (g >> (len(left) - 1 - left.index(b))) & 1
                at = at * 2 + value
            return (0, at, 0, 0)

        return index

    spec = pltpu.PrefetchScalarGridSpec(
        num_scalar_prefetch=1,
        grid=(1 << len(left),),
        in_specs=[pl.BlockSpec((n, 1, rows, cols), place(b)) for _, b in terms],
        out_specs=pl.BlockSpec((n, 1, rows, cols), lambda g, _: (0, g, 0, 0)),
    )
    out = pl.pallas_call(
        partial(add_kernel, len(terms)),
        grid_spec=spec,
        out_shape=shape((n, 1 << len(left), rows, cols), BF16),
        name="add",
        cost_estimate=pl.CostEstimate(flops=0, bytes_accessed=0, transcendentals=0),
        compiler_params=pltpu.CompilerParams(vmem_limit_bytes=16 * MIB),
    )(me, *[a for a, _ in terms])
    return out, left


def flip(array, axis, mask):
    size = lax.axis_size(axis)
    return lax.ppermute(array, axis, [(i, i ^ mask) for i in range(size)])


def tie(*arrays):
    return lax.optimization_barrier(arrays)


def pick(array, axis, index):
    return lax.dynamic_index_in_dim(array, index, axis, keepdims=False)


def outer_bits():
    bits = list(range(1, lax.axis_size("dp").bit_length() - 1))
    return bits, (bits, bits[::-1])


def share_of():
    me = lax.axis_index("dp")
    return (me & 1) * (lax.axis_size("dp") // 2) + (me >> 1)


class Gather:
    def __init__(self, pair):
        self.bits, self.orders = outer_bits()
        self.steps = len(self.bits)
        self.n, _, self.cols = pair[0].shape
        self.held = [
            a.reshape((self.n,) + (1,) * self.steps + a.shape[1:]) for a in pair
        ]

    def send(self, step):
        return [flip(h, "dp", 1 << order[step]) for h, order in zip(self.held, self.orders)]

    def take(self, step, got):
        me = lax.axis_index("dp")
        merged = []
        for mine, theirs, order in zip(self.held, got, self.orders):
            bit = order[step]
            low = ((me >> bit) & 1) == 0
            parts = [jnp.where(low, mine, theirs), jnp.where(low, theirs, mine)]
            merged.append(jnp.concatenate(parts, axis=1 + self.steps - bit))
        self.held = merged

    def halves(self):
        return [h.reshape(self.n, -1, self.cols) for h in self.held]


class Reduce:
    def __init__(self, keeps, gots):
        self.bits, self.orders = outer_bits()
        self.steps = len(self.bits)
        self.me = lax.axis_index("dp").astype(jnp.int32).reshape(1)
        high_first = self.bits[::-1]
        n, rows, cols = keeps[0].shape
        form = (n, 1 << self.steps, rows >> self.steps, cols)
        self.terms = [
            [(k.reshape(form), high_first), (g.reshape(form), high_first)]
            for k, g in zip(keeps, gots)
        ]
        self.left = [None, None]

    def pack(self, step):
        sends = []
        for side, order in enumerate(self.orders):
            fixed = {b: True for b in order[:step]}
            fixed[order[step]] = False
            out, self.left[side] = add_terms(self.terms[side], self.me, fixed)
            sends.append(out)
        return sends

    def send(self, step, packs):
        return [flip(p, "dp", 1 << order[step]) for p, order in zip(packs, self.orders)]

    def take(self, got):
        for side in range(2):
            self.terms[side].append((got[side], self.left[side]))

    def finish(self):
        fixed = {b: True for b in self.bits}
        return [add_terms(t, self.me, fixed)[0][:, 0] for t in self.terms]


def add_parts(*parts):
    total = parts[0].astype(F32)
    for part in parts[1:]:
        total = total + part.astype(F32)
    return total.astype(BF16)


def shards(
    tokens,
    word_len,
    region_count,
    w_qkv,
    qv_bias,
    w_out,
    out_bias,
    norm1_gain,
    norm1_bias,
    w_in,
    in_bias,
    w_down,
    down_bias,
    norm2_gain,
    norm2_bias,
    cotangent,
):
    mp = lax.axis_size("mp")
    dp = lax.axis_size("dp")
    mi = lax.axis_index("mp")
    width = tokens.shape[2]
    rows_local = tokens.shape[1]
    slots = rows_local * mp
    pairs = tokens.shape[0] // mp
    rows = pairs * slots
    cols = w_qkv.shape[2]
    units = w_in.shape[1]
    half_units = units // 2
    order = jnp.arange(mp) ^ mi
    here = jnp.stack([lax.axis_index("dp") & 1, mi]).astype(jnp.int32)
    share = share_of()

    turned = w_qkv.transpose(0, 2, 1)
    own = {
        "qk": turned[:2].reshape(2 * cols, width),
        "vo": jnp.concatenate([turned[2], w_out], axis=0),
        "in": w_in.T,
        "down": w_down,
    }
    own_qk, own_vo = own["qk"], own["vo"]

    def piece(name):
        part = own[name].shape[0] // dp
        return lax.dynamic_slice_in_dim(own[name], share * part, part, 0)

    def row_blocks(array):
        blocks = array.reshape((mp, pairs) + array.shape[1:])
        return [pick(blocks, 0, mi ^ k) for k in range(mp)]

    def join(blocks):
        return jnp.concatenate(blocks, axis=1).reshape(rows, width)

    fill = lambda v: jnp.pad(v, ((0, 0), (0, width - v.shape[1])))
    small = jnp.concatenate([fill(qv_bias), in_bias.reshape(1, units), jnp.zeros((5, width), BF16)])
    att_part, ffn_part = 2 * cols // dp, units // dp
    att_send = jnp.concatenate([piece("qk"), piece("vo"), small], axis=0)
    ffn_send = jnp.concatenate([piece("in"), piece("down")], axis=0)
    tok = row_blocks(tokens)
    cot = row_blocks(cotangent)
    vectors = jnp.stack(
        [out_bias, norm1_gain, norm1_bias, down_bias, norm2_gain, norm2_bias, out_bias, out_bias]
    ).astype(F32)
    words = lax.dynamic_slice_in_dim(word_len, mi * pairs, pairs, 0)
    regions = lax.dynamic_slice_in_dim(region_count, mi * pairs, pairs, 0)
    slot_index = (order[:, None] * rows_local + jnp.arange(rows_local)[None, :]).reshape(-1)
    key_valid = jnp.where(
        slot_index[None, :] < WORDS,
        slot_index[None, :] < words[:, None],
        slot_index[None, :] - WORDS < regions[:, None],
    ).astype(F32)[:, None, :]

    att_got = [flip(att_send, "mp", k) for k in range(1, mp)]
    att_got, ffn_send, tok, vectors, key_valid, here, own_qk, own_vo = tie(
        att_got, ffn_send, tok, vectors, key_valid, here, own_qk, own_vo
    )
    att = Gather(
        [
            jnp.stack([g[:att_part] for g in att_got]),
            jnp.stack([g[att_part : 2 * att_part] for g in att_got]),
        ]
    )
    ffn_two = flip(ffn_send, "mp", 2)
    got = att.send(0)
    tok_one = flip(tok[1], "mp", 1)
    ffn_two, got, tok_one, ffn_send, tok, att_got = tie(ffn_two, got, tok_one, ffn_send, tok, att_got)
    smalls = jnp.stack([small] + [g[2 * att_part :] for g in att_got]).astype(F32)
    for step in range(1, att.steps):
        att.take(step - 1, got)
        got = att.send(step)
        if step == 1:
            ffn_odd = flip(jnp.stack([ffn_send, ffn_two]), "mp", 1)
            tok_three = flip(tok[3], "mp", 3)
        got, ffn_odd, tok_three, tok, smalls = tie(got, ffn_odd, tok_three, tok, smalls)
    att.take(att.steps - 1, got)
    ffn_got = [ffn_odd[0], ffn_two, ffn_odd[1]]
    ffn = Gather(
        [
            jnp.stack([g[:ffn_part] for g in ffn_got]),
            jnp.stack([g[ffn_part:] for g in ffn_got]),
        ]
    )
    got = ffn.send(0)
    qk_one, vo_one = att.halves()
    qk_two, vo_two = flip(qk_one, "dp", 1), flip(vo_one, "dp", 1)
    tok_two = flip(tok[2], "mp", 2)
    got, qk_two, vo_two, tok_two, cot = tie(got, qk_two, vo_two, tok_two, cot)
    heads_low = shape((mp, rows, cols), BF16)
    low_shape = shape((rows, width), BF16)
    rows_shape = shape((rows, width), F32)
    sums_shape = shape((8, width), F32)
    block_shape = shape((pairs, rows_local, width), BF16)
    for step in range(1, ffn.steps):
        ffn.take(step - 1, got)
        got = ffn.send(step)
        if step == 1:
            cot_blocks = [cot[0]] + [flip(cot[k], "mp", k) for k in range(1, mp)]
        if step < ffn.steps - 1:
            got = tie(*got)
    x = join([tok[0], tok_one, tok_two, tok_three])
    later = lambda a: pl.BlockSpec((1,) + a.shape[1:], lambda s, h: (jnp.clip(s - 1, 0, mp - 2), 0, 0))
    head_args = [
        (whole, own_qk),
        (later, qk_one),
        (later, qk_two),
        (whole, own_vo),
        (later, vo_one),
        (later, vo_two),
    ]
    q, k, v, weights, context, hidden_low, normed_one, scale_one = call(
        partial(attention_kernel, pairs),
        mp,
        "attention",
        32,
        [
            (whole, x),
            *head_args,
            (per_step, smalls),
            (whole, key_valid),
            (whole, vectors),
        ],
        [
            (per_step, heads_low),
            (per_step, heads_low),
            (per_step, heads_low),
            (per_step, shape((mp, pairs, cols // HEAD * slots, slots), F32)),
            (per_step, heads_low),
            (whole, low_shape),
            (whole, rows_shape),
            (whole, shape((rows, 1), F32)),
        ],
        [pltpu.VMEM((rows, width), F32)],
        here,
        range(5),
    )
    got, hidden_low, cot_blocks = tie(got, hidden_low, cot_blocks)
    ffn.take(ffn.steps - 1, got)
    in_one, down_one = ffn.halves()
    in_two, down_two = flip(in_one, "dp", 1), flip(down_one, "dp", 1)
    in_two, down_two, hidden_low = tie(in_two, down_two, hidden_low)

    column_mine = pl.BlockSpec((width, half_units), lambda s, h: (0, h[0]))
    column_other = pl.BlockSpec((width, half_units), lambda s, h: (0, 1 - h[0]))
    in_args = [(column_mine, w_in), (column_other, w_in), (later, in_one), (later, in_two)]
    half = shape((mp, half_units, width), BF16)
    pre_shape = shape((mp, rows, units), BF16)
    others = (mp - 1, half_units, width)
    vmem = lambda a: pltpu.VMEM(a.shape, a.dtype)
    results = call(
        partial(ffn_kernel, mp),
        1,
        "ffn",
        52,
        [
            (where_it_is, hidden_low),
            (where_it_is, normed_one),
            (where_it_is, w_in),
            (where_it_is, in_one),
            (where_it_is, in_two),
            (where_it_is, w_down),
            (where_it_is, down_one),
            (where_it_is, down_two),
            (whole, smalls),
            (whole, vectors),
            *[(where_it_is, c) for c in cot_blocks],
        ],
        [
            *[(whole, block_shape)] * mp,
            (where_it_is, rows_shape),
            (where_it_is, pre_shape),
            (where_it_is, half),
            (where_it_is, half),
            (where_it_is, half),
            (where_it_is, half),
            (whole, shape((mp, 1, units), F32)),
            (whole, sums_shape),
        ],
        [
            vmem(low_shape),
            vmem(rows_shape),
            pltpu.VMEM((width, units), BF16),
            pltpu.VMEM(others, BF16),
            pltpu.VMEM(others, BF16),
            pltpu.VMEM((units, width), BF16),
            pltpu.VMEM(others, BF16),
            pltpu.VMEM(others, BF16),
            pltpu.VMEM((mp,) + block_shape.shape, BF16),
            vmem(pre_shape),
            pltpu.VMEM(pre_shape.shape, F32),
            vmem(rows_shape),
            vmem(rows_shape),
            vmem(pre_shape),
            vmem(half),
            vmem(half),
            vmem(half),
            vmem(half),
            pltpu.SemaphoreType.DMA((3 + 4 * (mp - 1) + 1 + mp + 1 + 5 * mp,)),
        ],
        here,
        range(mp, mp + 6),
    )
    out_blocks = results[:mp]
    delta_ffn, pre_grad, in_keep, in_send, down_keep, down_send, sum_in, sums_two = results[mp:]
    in_got, down_got = flip(in_send, "dp", 1), flip(down_send, "dp", 1)
    delta_attn, attn_low, sums_one = call(
        ffn_back_kernel,
        mp,
        "ffn_back",
        32,
        [
            (per_step, pre_grad),
            *in_args,
            (whole, delta_ffn),
            (whole, normed_one),
            (whole, scale_one),
            (whole, vectors),
        ],
        [(whole, rows_shape), (whole, low_shape), (whole, sums_shape)],
        [pltpu.VMEM((rows, width), F32)],
        here,
    )
    in_got, down_got, out_blocks, attn_low = tie(in_got, down_got, out_blocks, attn_low)
    ffn = Reduce([in_keep, down_keep], [in_got, down_got])
    packs = ffn.pack(0)
    packs, attn_low, out_blocks = tie(packs, attn_low, out_blocks)
    got = ffn.send(0, packs)
    out_got = [out_blocks[0]] + [flip(out_blocks[k], "mp", k) for k in range(1, mp)]
    small_half = shape((mp, cols, width), BF16)
    results = call(
        partial(attention_back_kernel, pairs),
        mp,
        "attention_back",
        40,
        [
            (whole, x),
            (whole, attn_low),
            (whole, delta_attn),
            *head_args,
            (per_step, q),
            (per_step, k),
            (per_step, v),
            (per_step, weights),
            (per_step, context),
            (whole, sums_one),
            (whole, sums_two),
            (whole, sum_in),
        ],
        [
            (per_step, small_half),
            (per_step, small_half),
            (
                pl.BlockSpec((2, 1, cols, width), lambda s, h: (0, s, 0, 0)),
                shape((2, mp, cols, width), BF16),
            ),
            (whole, shape((16 + 2 * mp, width), F32)),
            *[(whole, block_shape)] * mp,
        ],
        [pltpu.VMEM((rows, cols), BF16)] * 3 + [pltpu.VMEM((rows, width), F32)],
        here,
        (0, 1, 2) + tuple(range(4, 4 + mp)),
    )
    qk_keep, vo_keep, att_send, sums = results[:4]
    row_sends = results[4:]
    got, out_got, att_send, row_sends, sums = tie(got, out_got, att_send, row_sends, sums)
    for step in range(1, ffn.steps):
        ffn.take(got)
        packs = ffn.pack(step)
        got = ffn.send(step, packs)
        if step == 1:
            att_got = flip(att_send, "dp", 1)
            row_two, row_three = flip(row_sends[2], "mp", 2), flip(row_sends[3], "mp", 3)
        got, att_got, row_two, row_three, row_sends = tie(got, att_got, row_two, row_three, row_sends)
    place = lambda blocks, dtype: call(
        partial(place_kernel, pairs),
        1,
        "place",
        16,
        [(whole, b) for b in blocks],
        [(whole, shape((mp * pairs, rows_local, width), dtype))],
        [],
        here,
    )[0]
    layer_out = place(out_got, BF16)
    ffn.take(got)
    ffn_parts = ffn.finish()
    ffn_odd = jnp.concatenate([p[1::2] for p in ffn_parts], axis=1)
    ffn_even = jnp.concatenate([p[0::2] for p in ffn_parts], axis=1)
    att = Reduce([qk_keep, vo_keep], [att_got[0], att_got[1]])
    ffn_odd, ffn_even, sums = tie(ffn_odd, ffn_even, sums)
    got = att.send(0, att.pack(0))
    ffn_got = flip(ffn_odd, "mp", 1)
    sums_got = flip(sums, "dp", 1)
    got, ffn_got, sums_got, row_sends, layer_out = tie(got, ffn_got, sums_got, row_sends, layer_out)
    sums = sums + sums_got
    for mask in [1 << b for b in range(2, dp.bit_length() - 2)]:
        sums = sums + flip(sums, "dp", mask)
    ffn_two = add_parts(ffn_even[1], ffn_got[1])
    for step in range(1, att.steps):
        att.take(got)
        packs = att.pack(step)
        got = att.send(step, packs)
        if step == 1:
            ffn_last = flip(ffn_two, "mp", 2)
            row_one = flip(row_sends[1], "mp", 1)
            sums_got = flip(sums, "dp", 2)
        got, ffn_last, row_one, sums_got = tie(got, ffn_last, row_one, sums_got)
    att.take(got)
    sums = sums + sums_got
    att_parts = att.finish()
    att_odd = jnp.concatenate([p[1::2] for p in att_parts], axis=1)
    att_even = jnp.concatenate([p[0::2] for p in att_parts], axis=1)
    ffn_sum = add_parts(ffn_even[0], ffn_got[0], ffn_last)
    ffn = Gather([ffn_sum[None, :ffn_part], ffn_sum[None, ffn_part:]])
    ffn.held, att_odd, att_even, sums = tie(ffn.held, att_odd, att_even, sums)
    grad_input = place([row_sends[0], row_one, row_two, row_three], F32)
    got = ffn.send(0)
    att_got = flip(att_odd, "mp", 1)
    sums_got = flip(sums, "dp", dp // 2)
    got, att_got, sums_got, grad_input = tie(got, att_got, sums_got, grad_input)
    sums = sums + sums_got
    att_two = add_parts(att_even[1], att_got[1])
    for step in range(1, ffn.steps):
        ffn.take(step - 1, got)
        got = ffn.send(step)
        if step == 1:
            att_last = flip(att_two, "mp", 2)
            sums_got = flip(sums, "mp", 1)
        got, att_last, sums_got = tie(got, att_last, sums_got)
    ffn.take(ffn.steps - 1, got)
    sums = sums + sums_got
    att_sum = add_parts(att_even[0], att_got[0], att_last)
    att = Gather([att_sum[None, :att_part], att_sum[None, att_part:]])
    ffn_halves = ffn.halves()
    core_got = [flip(h, "dp", 1) for h in ffn_halves]
    got = att.send(0)
    sums_got = flip(sums, "mp", 2)
    core_got, got, sums_got = tie(core_got, got, sums_got)
    sums = sums + sums_got
    grad_in, grad_down = call(
        unit_grads_kernel,
        1,
        "unit_grads",
        24,
        [(whole, a) for a in ffn_halves + core_got],
        [(whole, shape((width, units), F32)), (whole, shape((units, width), F32))],
        [],
        here,
    )
    for step in range(1, att.steps):
        att.take(step - 1, got)
        got = tie(*att.send(step))
    grad_in, grad_down, got = tie(grad_in, grad_down, got)
    att.take(att.steps - 1, got)
    att_halves = att.halves()
    core_got = [flip(h, "dp", 1) for h in att_halves]
    grad_qkv, grad_out = call(
        head_grads_kernel,
        1,
        "head_grads",
        24,
        [(whole, a) for a in att_halves + core_got],
        [(whole, shape((3, cols, width), F32)), (whole, shape((cols, width), F32))],
        [],
        here,
    )
    sum_in_bias = lax.dynamic_index_in_dim(sums, 16 + mi, 0, keepdims=False)
    sum_qv = lax.dynamic_index_in_dim(sums, 16 + mp + mi, 0, keepdims=False)
    sum_qv = jnp.stack([sum_qv[:cols], sum_qv[2 * cols : 3 * cols]])
    return (
        layer_out,
        grad_input,
        grad_qkv.transpose(0, 2, 1),
        sum_qv,
        grad_out,
        sums[0],
        sums[1],
        sums[2],
        grad_in,
        sum_in_bias,
        grad_down,
        sums[10],
        sums[8],
        sums[9],
    )


def solution(mesh):
    in_specs = (
        P("dp", "mp", None),
        P("dp"),
        P("dp"),
        P(None, None, "mp"),
        P(None, "mp"),
        P("mp", None),
        P(),
        P(),
        P(),
        P(None, "mp"),
        P("mp"),
        P("mp", None),
        P(),
        P(),
        P(),
        P("dp", "mp", None),
    )
    out_specs = (
        P("dp", "mp", None),
        P("dp", "mp", None),
        P(None, None, "mp"),
        P(None, "mp"),
        P("mp", None),
        P(),
        P(),
        P(),
        P(None, "mp"),
        P("mp"),
        P("mp", None),
        P(),
        P(),
        P(),
    )
    return jax.shard_map(shards, mesh=mesh, in_specs=in_specs, out_specs=out_specs, check_vma=False)
```

```python
from functools import partial

import jax
import jax.numpy as jnp
from jax import lax
from jax.experimental import pallas as pl
from jax.experimental.pallas import tpu as pltpu
from jax.sharding import PartitionSpec as P

HEAD = 64
WORDS = 60
EPSILON = 1e-05
SQRT_HALF = 0.7071067811865476
DENSITY = 0.3989422804014327
F32 = jnp.float32
BF16 = jnp.bfloat16
MIB = 1024 * 1024


def dot(one, two, one_axis, two_axis):
    return lax.dot_general(
        one, two, (((one_axis,), (two_axis,)), ((), ())), preferred_element_type=F32
    )


def normalize(total, gain, shift):
    centered = total - jnp.mean(total, axis=-1, keepdims=True)
    inv_scale = lax.rsqrt(jnp.mean(centered * centered, axis=-1, keepdims=True) + EPSILON)
    normed = centered * inv_scale
    return normed * gain + shift, normed, inv_scale


def normalize_back(upstream, normed, inv_scale, gain):
    scaled_up = upstream * gain
    mean_one = jnp.mean(scaled_up, axis=-1, keepdims=True)
    mean_two = jnp.mean(scaled_up * normed, axis=-1, keepdims=True)
    return inv_scale * (scaled_up - mean_one - normed * mean_two)


def column_sum(array):
    return jnp.sum(array, axis=0, keepdims=True)


def head_stack(array, heads):
    head = lax.broadcasted_iota(jnp.int32, array.shape, 1) // HEAD
    zero = jnp.zeros_like(array)
    return jnp.concatenate([jnp.where(head == h, array, zero) for h in range(heads)], axis=0)


def head_pick(stacked, heads):
    rows = stacked.shape[0] // heads
    head = lax.broadcasted_iota(jnp.int32, (rows, stacked.shape[1]), 1) // HEAD
    total = stacked[:rows]
    for h in range(1, heads):
        total = jnp.where(head == h, stacked[h * rows : (h + 1) * rows], total)
    return total


def head_weights(first, here_ref, own_ref, one_ref, two_ref):
    low = here_ref[0] == 0
    half = one_ref.shape[1]
    one, two = one_ref[0], two_ref[0]
    return (
        jnp.where(first, own_ref[:half], jnp.where(low, one, two)),
        jnp.where(first, own_ref[half:], jnp.where(low, two, one)),
    )


def attention_kernel(
    pairs, here_ref, x_ref, own_qk, qk_one, qk_two, own_vo, vo_one, vo_two, small_ref, valid_ref, vectors_ref,
    q_ref, k_ref, v_ref, weights_ref, context_ref, low_ref, normed_ref, scale_ref, total_ref,
):
    step = pl.program_id(0)
    cols = q_ref.shape[2]
    heads = cols // HEAD
    slots = x_ref.shape[0] // pairs
    x = x_ref[...]
    w_q, w_k = head_weights(step == 0, here_ref, own_qk, qk_one, qk_two)
    w_v, w_o = head_weights(step == 0, here_ref, own_vo, vo_one, vo_two)
    q_ref[0] = (dot(x, w_q, 1, 1) + small_ref[0, 0:1, :cols]).astype(BF16)
    k_ref[0] = dot(x, w_k, 1, 1).astype(BF16)
    v_ref[0] = (dot(x, w_v, 1, 1) + small_ref[0, 1:2, :cols]).astype(BF16)
    for p in range(pairs):
        rows = slice(p * slots, (p + 1) * slots)
        scores = dot(head_stack(q_ref[0, rows], heads), k_ref[0, rows], 1, 1) * HEAD ** (-0.5)
        scores = jnp.where(valid_ref[p] > 0.5, scores, -1e30)
        exp_scores = jnp.exp(scores - jnp.max(scores, axis=-1, keepdims=True))
        weights = exp_scores / jnp.sum(exp_scores, axis=-1, keepdims=True)
        weights_ref[0, p] = weights
        mixed = dot(weights.astype(BF16), v_ref[0, rows], 1, 0)
        context_ref[0, rows] = head_pick(mixed, heads).astype(BF16)
    branch = dot(context_ref[0], w_o, 1, 0)

    @pl.when(step == 0)
    def _():
        total_ref[...] = branch

    @pl.when(step > 0)
    def _():
        total_ref[...] += branch

    @pl.when(step == pl.num_programs(0) - 1)
    def _():
        first_sum = total_ref[...] + vectors_ref[0:1] + x.astype(F32)
        hidden, normed, scale = normalize(first_sum, vectors_ref[1:2], vectors_ref[2:3])
        low_ref[...] = hidden.astype(BF16)
        normed_ref[...] = normed
        scale_ref[...] = scale


def unit_rows(one, two, start, stop):
    half = one.shape[1]
    parts = []
    if start < half:
        parts.append(one[0, start : min(stop, half)])
    if stop > half:
        parts.append(two[0, max(start - half, 0) : stop - half])
    return parts[0] if len(parts) == 1 else jnp.concatenate(parts, axis=0)


def unit_columns(one, two, start, stop):
    half = one.shape[1]
    parts = []
    if start < half:
        parts.append(one[:, start : min(stop, half)])
    if stop > half:
        parts.append(two[:, max(start - half, 0) : stop - half])
    return parts[0] if len(parts) == 1 else jnp.concatenate(parts, axis=1)


def blocks_of(units):
    size = min(256, units)
    return [(start, start + size) for start in range(0, units, size)]


def join_rows(refs):
    pairs = refs[0].shape[0]
    return jnp.concatenate([ref[p].astype(F32) for p in range(pairs) for ref in refs], axis=0)


def leave_rows(array, refs):
    pairs, rows = refs[0].shape[:2]
    for p in range(pairs):
        for j, ref in enumerate(refs):
            start = (p * len(refs) + j) * rows
            ref[p] = array[start : start + rows].astype(BF16)


def ffn_kernel(
    count, here_ref, low_hbm, normed_hbm, w_in_hbm, in_one, in_two, w_down_hbm, down_one, down_two, small_ref,
    vectors_ref, *refs,
):
    cot_hbm, out_refs = refs[:count], refs[count : 2 * count]
    (
        delta_hbm, pre_grad_hbm, in_keep_hbm, in_send_hbm, down_keep_hbm, down_send_hbm, sum_in_ref, sums_ref,
        low_ref, normed_ref, w_in_ref, w_down_ref, cot_ref, act_ref, slope_ref, total_ref, delta_ref, pre_grad_ref,
        in_keep_ref, in_send_ref, down_keep_ref, down_send_ref, sems,
    ) = refs[2 * count :]
    core = here_ref[0]
    half = in_one.shape[1]
    started = [0]

    def start(*pairs):
        copies = []
        for source, target in pairs:
            copies.append(pltpu.make_async_copy(source, target, sems.at[started[0]]))
            copies[-1].start()
            started[0] += 1
        return copies

    def wait(copies):
        for copy in copies:
            copy.wait()

    def halves(start_, stop):
        parts = []
        if start_ < half:
            parts.append((0, start_, min(stop, half)))
        if stop > half:
            parts.append((1, max(start_ - half, 0), stop - half))
        return parts

    def own(which, first, last):
        side = core if which == 0 else 1 - core
        return pl.ds(pl.multiple_of(side * half + first, 128), last - first)

    def down_rows(slot, start_, stop):
        if slot == 0:
            parts = [w_down_ref[own(w, a, b)] for w, a, b in halves(start_, stop)]
        else:
            parts = [(down_one, down_two)[w][slot - 1, a:b] for w, a, b in halves(start_, stop)]
        return jnp.concatenate(parts, axis=0)

    def forward(slot):
        low = low_ref[...]
        branch = None
        for first, last in blocks_of(2 * half):
            parts = halves(first, last)
            if slot == 0:
                w_in = jnp.concatenate([w_in_ref[:, own(*p)] for p in parts], axis=1)
                pre_act = dot(low, w_in, 1, 0)
            else:
                w_in = jnp.concatenate([(in_one, in_two)[w][slot - 1, a:b] for w, a, b in parts], axis=0)
                pre_act = dot(low, w_in, 1, 1)
            bias = jnp.concatenate([small_ref[slot, 2:3, own(*p)] for p in parts], axis=1)
            pre_act = pre_act + bias
            share = 0.5 * (1.0 + lax.erf(pre_act * SQRT_HALF))
            act = (pre_act * share).astype(BF16)
            act_ref[slot, :, first:last] = act
            slope_ref[slot, :, first:last] = share + pre_act * (DENSITY * jnp.exp(-0.5 * pre_act * pre_act))
            term = dot(act, down_rows(slot, first, last), 1, 0)
            branch = term if branch is None else branch + term
        if slot == 0:
            total_ref[...] = branch
        else:
            total_ref[...] += branch

    first_copies = start((low_hbm, low_ref), (w_in_hbm, w_in_ref), (w_down_hbm, w_down_ref))
    later_copies = start((normed_hbm, normed_ref), *[(cot_hbm[k], cot_ref.at[k]) for k in range(count)])
    wait(first_copies)
    for slot in range(count):
        forward(slot)
    wait(later_copies)

    hidden = normed_ref[...] * vectors_ref[1:2] + vectors_ref[2:3]
    second = total_ref[...] + vectors_ref[3:4] + hidden
    gain = vectors_ref[4:5]
    output, normed, scale = normalize(second, gain, vectors_ref[5:6])
    leave_rows(output, out_refs)
    upstream = join_rows([cot_ref.at[k] for k in range(count)])
    delta = normalize_back(upstream, normed, scale, gain)
    delta_ref[...] = delta
    leaving = start((delta_ref, delta_hbm))
    sums_ref[...] = jnp.zeros_like(sums_ref)
    sums_ref[0:1] = column_sum(upstream * normed)
    sums_ref[1:2] = column_sum(upstream)
    sums_ref[2:3] = column_sum(delta)
    ffn_low = delta.astype(BF16)
    low = low_ref[...]
    for slot in range(count):
        for first, last in blocks_of(2 * half):
            act_grad = dot(ffn_low, down_rows(slot, first, last), 1, 1)
            pre_grad_ref[slot, :, first:last] = (act_grad * slope_ref[slot, :, first:last]).astype(BF16)
        leaving += start((pre_grad_ref.at[slot], pre_grad_hbm.at[slot]))
        down_send_ref[slot] = dot(act_ref[slot, :, half:], ffn_low, 0, 0).astype(BF16)
        leaving += start((down_send_ref.at[slot], down_send_hbm.at[slot]))
        down_keep_ref[slot] = dot(act_ref[slot, :, :half], ffn_low, 0, 0).astype(BF16)
        leaving += start((down_keep_ref.at[slot], down_keep_hbm.at[slot]))
        one, two = pre_grad_ref[slot, :, :half], pre_grad_ref[slot, :, half:]
        in_send_ref[slot] = dot(two, low, 0, 0).astype(BF16)
        leaving += start((in_send_ref.at[slot], in_send_hbm.at[slot]))
        in_keep_ref[slot] = dot(one, low, 0, 0).astype(BF16)
        leaving += start((in_keep_ref.at[slot], in_keep_hbm.at[slot]))
        natural = slot ^ here_ref[1]
        sum_in_ref[natural, :, own(0, 0, half)] = column_sum(one.astype(F32))
        sum_in_ref[natural, :, own(1, 0, half)] = column_sum(two.astype(F32))
    wait(leaving)


def ffn_back_kernel(
    here_ref, pre_grad_ref, own_in_one, own_in_two, in_one, in_two, delta_ref, normed_ref, scale_ref, vectors_ref,
    delta_attn_ref, attn_low_ref, sums_ref, total_ref,
):
    step = pl.program_id(0)

    def body(first):
        branch = None
        for start, stop in blocks_of(pre_grad_ref.shape[2]):
            pre_grad = pre_grad_ref[0, :, start:stop]
            if first:
                term = dot(pre_grad, unit_columns(own_in_one, own_in_two, start, stop), 1, 1)
            else:
                term = dot(pre_grad, unit_rows(in_one, in_two, start, stop), 1, 0)
            branch = term if branch is None else branch + term
        if first:
            total_ref[...] = branch
        else:
            total_ref[...] += branch

    pl.when(step == 0)(partial(body, True))
    pl.when(step > 0)(partial(body, False))

    @pl.when(step == pl.num_programs(0) - 1)
    def _():
        hidden_grad = total_ref[...] + delta_ref[...]
        normed = normed_ref[...]
        delta = normalize_back(hidden_grad, normed, scale_ref[...], vectors_ref[1:2])
        delta_attn_ref[...] = delta
        attn_low_ref[...] = delta.astype(BF16)
        sums_ref[...] = jnp.zeros_like(sums_ref)
        sums_ref[0:1] = column_sum(delta)
        sums_ref[1:2] = column_sum(hidden_grad * normed)
        sums_ref[2:3] = column_sum(hidden_grad)


def attention_back_kernel(
    pairs, here_ref, x_ref, attn_low_ref, delta_ref, own_qk, qk_one, qk_two, own_vo, vo_one, vo_two, q_ref, k_ref,
    v_ref, weights_ref, context_ref, sums_one_ref, sums_two_ref, sum_in_ref,
    qk_keep_ref, vo_keep_ref, send_ref, sums_ref, *refs,
):
    step = pl.program_id(0)
    shards_ = pl.num_programs(0)
    out_refs = refs[:shards_]
    dq_ref, dk_ref, dv_ref, total_ref = refs[shards_:]

    @pl.when(step == 0)
    def _():
        total_ref[...] = delta_ref[...]
        sums_ref[...] = jnp.zeros_like(sums_ref)
        sums_ref[0:8] = sums_one_ref[...]
        sums_ref[8:16] = sums_two_ref[...]
        for j in range(shards_):
            sums_ref[16 + j : 17 + j] = sum_in_ref[j]

    core = here_ref[0]
    cols = q_ref.shape[2]
    heads = cols // HEAD
    slots = x_ref.shape[0] // pairs
    scale = HEAD ** (-0.5)
    x = x_ref[...]
    attn_low = attn_low_ref[...]
    w_q, w_k = head_weights(step == 0, here_ref, own_qk, qk_one, qk_two)
    w_v, w_o = head_weights(step == 0, here_ref, own_vo, vo_one, vo_two)
    context_grad = dot(attn_low, w_o, 1, 1).astype(BF16)
    grad_out = dot(context_ref[0], attn_low, 0, 0).astype(BF16)
    for p in range(pairs):
        rows = slice(p * slots, (p + 1) * slots)
        up = head_stack(context_grad[rows], heads)
        weights = weights_ref[0, p]
        prob_grad = dot(up, v_ref[0, rows], 1, 1)
        inner = jnp.sum(prob_grad * weights, axis=-1, keepdims=True)
        score_grad = (weights * (prob_grad - inner)).astype(BF16)
        dv_ref[rows] = dot(weights.astype(BF16), up, 0, 0).astype(BF16)
        query_grad = head_pick(dot(score_grad, k_ref[0, rows], 1, 0), heads)
        dq_ref[rows] = (query_grad * scale).astype(BF16)
        key_grad = dot(score_grad, head_stack(q_ref[0, rows], heads), 0, 0)
        dk_ref[rows] = (key_grad * scale).astype(BF16)
    dq, dk, dv = dq_ref[...], dk_ref[...], dv_ref[...]
    row = pl.ds(16 + shards_ + (step ^ here_ref[1]), 1)
    sums_ref[row, :cols] = column_sum(dq.astype(F32))
    sums_ref[row, 2 * cols : 3 * cols] = column_sum(dv.astype(F32))
    grad_q = dot(dq, x, 0, 0).astype(BF16)
    grad_k = dot(dk, x, 0, 0).astype(BF16)
    grad_v = dot(dv, x, 0, 0).astype(BF16)

    @pl.when(core == 0)
    def _():
        qk_keep_ref[0], send_ref[0, 0] = grad_q, grad_k
        vo_keep_ref[0], send_ref[1, 0] = grad_v, grad_out

    @pl.when(core != 0)
    def _():
        qk_keep_ref[0], send_ref[0, 0] = grad_k, grad_q
        vo_keep_ref[0], send_ref[1, 0] = grad_out, grad_v

    total_ref[...] += dot(dq, w_q, 1, 0) + dot(dk, w_k, 1, 0) + dot(dv, w_v, 1, 0)

    @pl.when(step == shards_ - 1)
    def _():
        leave_rows(total_ref[...], out_refs)


def place_kernel(pairs, here_ref, *refs):
    out_ref = refs[-1]
    for k, ref in enumerate(refs[:-1]):
        out_ref[pl.ds((here_ref[1] ^ k) * pairs, pairs)] = ref[...].astype(out_ref.dtype)


def head_grads_kernel(indices, here_ref, qk_mine, vo_mine, qk_other, vo_other, grad_qkv_ref, grad_out_ref):
    core, place_here = here_ref[0], here_ref[2]
    for side, qk_ref, vo_ref in ((core, qk_mine, vo_mine), (1 - core, qk_other, vo_other)):
        for k, (qk_index, vo_index) in enumerate(zip(*indices)):
            grad_qkv_ref[side, place_here ^ qk_index] = qk_ref[k].astype(F32)
            place = place_here ^ vo_index
            piece = vo_ref[k].astype(F32)

            @pl.when(side == 0)
            def _():
                grad_qkv_ref[2, place] = piece

            @pl.when(side != 0)
            def _():
                grad_out_ref[place] = piece


def unit_grads_kernel(here_ref, in_ref, down_ref, in_other, down_other, grad_in_ref, grad_down_ref):
    half = in_ref.shape[1]
    mine = pl.multiple_of(here_ref[0] * half, half)
    other = pl.multiple_of((1 - here_ref[0]) * half, half)
    grad_in_ref[:, pl.ds(mine, half)] = in_ref[0].astype(F32).T
    grad_in_ref[:, pl.ds(other, half)] = in_other[0].astype(F32).T
    grad_down_ref[pl.ds(mine, half)] = down_ref[0].astype(F32)
    grad_down_ref[pl.ds(other, half)] = down_other[0].astype(F32)


def whole(array):
    return pl.BlockSpec(array.shape, lambda *_: (0,) * len(array.shape))


def per_step(array):
    return pl.BlockSpec((1,) + array.shape[1:], lambda s, *_: (s,) + (0,) * (len(array.shape) - 1))


def in_place(array):
    if array.size * array.dtype.itemsize < MIB:
        return array
    return pltpu.with_memory_space_constraint(array, pltpu.HBM)


def where_it_is(array):
    return pl.BlockSpec(memory_space=pl.ANY)


def in_vmem(array):
    return pl.BlockSpec(memory_space=pltpu.VMEM)


def call(kernel, steps, name, vmem, inputs, outputs, scratch, scalar, kept=()):
    spec = pltpu.PrefetchScalarGridSpec(
        num_scalar_prefetch=1,
        grid=(steps,),
        in_specs=[make if isinstance(make, pl.BlockSpec) else make(a) for make, a in inputs],
        out_specs=[make if isinstance(make, pl.BlockSpec) else make(a) for make, a in outputs],
        scratch_shapes=scratch,
    )
    return pl.pallas_call(
        kernel,
        grid_spec=spec,
        out_shape=[pltpu.HBM(a.shape, a.dtype) if i in kept else a for i, (_, a) in enumerate(outputs)],
        name=name,
        cost_estimate=pl.CostEstimate(flops=0, bytes_accessed=0, transcendentals=0),
        compiler_params=pltpu.CompilerParams(vmem_limit_bytes=vmem * MIB),
    )(scalar, *[a if make is in_vmem else in_place(a) for make, a in inputs])


def shape(dims, dtype):
    return jax.ShapeDtypeStruct(dims, dtype)


def add_kernel(counts, *refs):
    refs = refs[1:]
    out_refs = refs[sum(counts) :]
    for count, out_ref in zip(counts, out_refs):
        total = refs[0][...].astype(F32)
        for ref in refs[1:count]:
            total = total + ref[...].astype(F32)
        out_ref[...] = total.astype(BF16)
        refs = refs[count:]


def add_terms(sides, me):
    in_specs, out_specs, arrays, outs, lefts = [], [], [], [], []

    def place(own_bits, fixed, left):
        def index(g, me_ref):
            at = 0
            for b in own_bits:
                if b in fixed:
                    value = (me_ref[0] >> b) & 1
                    value = value if fixed[b] else 1 - value
                else:
                    value = (g >> (len(left) - 1 - left.index(b))) & 1
                at = at * 2 + value
            return (0, at, 0, 0)

        return index

    for terms, fixed in sides:
        first, bits = terms[0]
        left = [b for b in bits if b not in fixed]
        n, _, rows, cols = first.shape
        in_specs += [pl.BlockSpec((n, 1, rows, cols), place(b, fixed, left)) for _, b in terms]
        out_specs.append(pl.BlockSpec((n, 1, rows, cols), lambda g, _: (0, g, 0, 0)))
        arrays += [a for a, _ in terms]
        outs.append(shape((n, 1 << len(left), rows, cols), BF16))
        lefts.append(left)
    results = pl.pallas_call(
        partial(add_kernel, [len(terms) for terms, _ in sides]),
        grid_spec=pltpu.PrefetchScalarGridSpec(
            num_scalar_prefetch=1, grid=(1 << len(lefts[0]),), in_specs=in_specs, out_specs=out_specs
        ),
        out_shape=outs,
        name="add",
        cost_estimate=pl.CostEstimate(flops=0, bytes_accessed=0, transcendentals=0),
        compiler_params=pltpu.CompilerParams(vmem_limit_bytes=24 * MIB),
    )(me, *arrays)
    return results, lefts


def flip(array, axis, mask):
    size = lax.axis_size(axis)
    return lax.ppermute(array, axis, [(i, i ^ mask) for i in range(size)])


def tie(*arrays):
    return lax.optimization_barrier(arrays)


def pick(array, axis, index):
    return lax.dynamic_index_in_dim(array, index, axis, keepdims=False)


def outer_bits():
    bits = list(range(1, lax.axis_size("dp").bit_length() - 1))
    return bits, (bits, bits[::-1])


def share_of():
    me = lax.axis_index("dp")
    return (me & 1) * (lax.axis_size("dp") // 2) + (me >> 1)


class Gather:
    def __init__(self, pair):
        self.bits, self.orders = outer_bits()
        self.steps = len(self.bits)
        self.n, _, self.cols = pair[0].shape
        self.held = [
            a.reshape((self.n,) + (1,) * self.steps + a.shape[1:]) for a in pair
        ]

    def send(self, step):
        return [flip(h, "dp", 1 << order[step]) for h, order in zip(self.held, self.orders)]

    def take(self, step, got):
        me = lax.axis_index("dp")
        merged = []
        for mine, theirs, order in zip(self.held, got, self.orders):
            bit = order[step]
            low = ((me >> bit) & 1) == 0
            parts = [jnp.where(low, mine, theirs), jnp.where(low, theirs, mine)]
            merged.append(jnp.concatenate(parts, axis=1 + self.steps - bit))
        self.held = merged

    def halves(self):
        return [h.reshape(self.n, -1, self.cols) for h in self.held]


class Reduce:
    def __init__(self, keeps, gots):
        self.bits, self.orders = outer_bits()
        self.steps = len(self.bits)
        self.me = lax.axis_index("dp").astype(jnp.int32).reshape(1)
        high_first = self.bits[::-1]
        n, rows, cols = keeps[0].shape
        form = (n, 1 << self.steps, rows >> self.steps, cols)
        self.terms = [
            [(k.reshape(form), high_first), (g.reshape(form), high_first)]
            for k, g in zip(keeps, gots)
        ]
        self.left = [None, None]

    def pack(self, step):
        sides = []
        for terms, order in zip(self.terms, self.orders):
            fixed = {b: True for b in order[:step]}
            fixed[order[step]] = False
            sides.append((terms, fixed))
        sends, self.left = add_terms(sides, self.me)
        return sends

    def send(self, step, packs):
        return [flip(p, "dp", 1 << order[step]) for p, order in zip(packs, self.orders)]

    def take(self, got):
        for side in range(2):
            self.terms[side].append((got[side], self.left[side]))

    def finish(self):
        fixed = {b: True for b in self.bits}
        sums, _ = add_terms([(t, fixed) for t in self.terms], self.me)
        return [a[:, 0] for a in sums]


class Pieces:
    def __init__(self, pair):
        self.bits, self.orders = outer_bits()
        self.steps = len(self.bits)
        self.held = [p[None] for p in pair]
        self.indices = [[0], [0]]

    def send(self, step):
        return [flip(h, "dp", 1 << order[step]) for h, order in zip(self.held, self.orders)]

    def take(self, step, got):
        self.held = [jnp.concatenate([h, g]) for h, g in zip(self.held, got)]
        self.indices = [
            index + [i ^ (1 << (order[step] - 1)) for i in index]
            for index, order in zip(self.indices, self.orders)
        ]


def add_parts(*parts):
    total = parts[0].astype(F32)
    for part in parts[1:]:
        total = total + part.astype(F32)
    return total.astype(BF16)


def shards(
    tokens,
    word_len,
    region_count,
    w_qkv,
    qv_bias,
    w_out,
    out_bias,
    norm1_gain,
    norm1_bias,
    w_in,
    in_bias,
    w_down,
    down_bias,
    norm2_gain,
    norm2_bias,
    cotangent,
):
    mp = lax.axis_size("mp")
    dp = lax.axis_size("dp")
    mi = lax.axis_index("mp")
    width = tokens.shape[2]
    rows_local = tokens.shape[1]
    slots = rows_local * mp
    pairs = tokens.shape[0] // mp
    rows = pairs * slots
    cols = w_qkv.shape[2]
    units = w_in.shape[1]
    half_units = units // 2
    order = jnp.arange(mp) ^ mi
    here = jnp.stack([lax.axis_index("dp") & 1, mi, lax.axis_index("dp") >> 1]).astype(jnp.int32)
    share = share_of()

    turned = w_qkv.transpose(0, 2, 1).reshape(3 * cols, width)
    own_qk = turned[: 2 * cols]
    own_vo = jnp.concatenate([turned[2 * cols :], w_out], axis=0)
    att_part, ffn_part = 2 * cols // dp, units // dp
    first = share * att_part
    rows_of = lambda array, start, size: lax.dynamic_slice_in_dim(array, start, size, 0)
    vo_piece = jnp.where(
        first < cols,
        rows_of(turned, 2 * cols + jnp.minimum(first, cols - att_part), att_part),
        rows_of(w_out, jnp.maximum(first - cols, 0), att_part),
    )

    def row_blocks(array):
        blocks = array.reshape((mp, pairs) + array.shape[1:])
        return [pick(blocks, 0, mi ^ k) for k in range(mp)]

    def join(blocks):
        return jnp.concatenate(blocks, axis=1).reshape(rows, width)

    fill = lambda v: jnp.pad(v, ((0, 0), (0, width - v.shape[1])))
    small = jnp.concatenate([fill(qv_bias), in_bias.reshape(1, units), jnp.zeros((5, width), BF16)])
    att_send = jnp.concatenate([rows_of(turned, first, att_part), vo_piece], axis=0)
    ffn_send = jnp.concatenate(
        [rows_of(w_in.T, share * ffn_part, ffn_part), rows_of(w_down, share * ffn_part, ffn_part), small],
        axis=0,
    )
    tok = row_blocks(tokens)
    cot = row_blocks(cotangent)
    vectors = jnp.stack(
        [out_bias, norm1_gain, norm1_bias, down_bias, norm2_gain, norm2_bias, out_bias, out_bias]
    ).astype(F32)
    words = lax.dynamic_slice_in_dim(word_len, mi * pairs, pairs, 0)
    regions = lax.dynamic_slice_in_dim(region_count, mi * pairs, pairs, 0)
    slot_index = (order[:, None] * rows_local + jnp.arange(rows_local)[None, :]).reshape(-1)
    key_valid = jnp.where(
        slot_index[None, :] < WORDS,
        slot_index[None, :] < words[:, None],
        slot_index[None, :] - WORDS < regions[:, None],
    ).astype(F32)[:, None, :]

    att_got = [flip(att_send, "mp", k) for k in range(1, mp)]
    att_got, ffn_send, tok, vectors, key_valid, here, own_qk, own_vo = tie(
        att_got, ffn_send, tok, vectors, key_valid, here, own_qk, own_vo
    )
    att = Gather(
        [
            jnp.stack([g[:att_part] for g in att_got]),
            jnp.stack([g[att_part:] for g in att_got]),
        ]
    )
    ffn_two = flip(ffn_send, "mp", 2)
    got = att.send(0)
    tok_one = flip(tok[1], "mp", 1)
    ffn_two, got, tok_one, ffn_send, tok = tie(ffn_two, got, tok_one, ffn_send, tok)
    for step in range(1, att.steps):
        att.take(step - 1, got)
        got = att.send(step)
        if step == 1:
            ffn_odd = flip(jnp.stack([ffn_send, ffn_two]), "mp", 1)
            tok_three = flip(tok[3], "mp", 3)
        got, ffn_odd, tok_three, tok = tie(got, ffn_odd, tok_three, tok)
    att.take(att.steps - 1, got)
    ffn_got = [ffn_odd[0], ffn_two, ffn_odd[1]]
    ffn = Gather(
        [
            jnp.stack([g[:ffn_part] for g in ffn_got]),
            jnp.stack([g[ffn_part : 2 * ffn_part] for g in ffn_got]),
        ]
    )
    got = ffn.send(0)
    qk_one, vo_one = att.halves()
    qk_two, vo_two = flip(qk_one, "dp", 1), flip(vo_one, "dp", 1)
    tok_two = flip(tok[2], "mp", 2)
    smalls = jnp.stack([small] + [g[2 * ffn_part :] for g in ffn_got]).astype(F32)
    got, qk_two, vo_two, tok_two, cot, smalls = tie(got, qk_two, vo_two, tok_two, cot, smalls)
    heads_low = shape((mp, rows, cols), BF16)
    low_shape = shape((rows, width), BF16)
    rows_shape = shape((rows, width), F32)
    sums_shape = shape((8, width), F32)
    block_shape = shape((pairs, rows_local, width), BF16)
    for step in range(1, ffn.steps):
        ffn.take(step - 1, got)
        got = ffn.send(step)
        if step == 1:
            cot_blocks = [cot[0]] + [flip(cot[k], "mp", k) for k in range(1, mp)]
        if step < ffn.steps - 1:
            got = tie(*got)
    x = join([tok[0], tok_one, tok_two, tok_three])
    later = lambda a: pl.BlockSpec((1,) + a.shape[1:], lambda s, h: (jnp.clip(s - 1, 0, mp - 2), 0, 0))
    head_args = [
        (whole, own_qk),
        (later, qk_one),
        (later, qk_two),
        (whole, own_vo),
        (later, vo_one),
        (later, vo_two),
    ]
    q, k, v, weights, context, hidden_low, normed_one, scale_one = call(
        partial(attention_kernel, pairs),
        mp,
        "attention",
        32,
        [
            (whole, x),
            *head_args,
            (per_step, smalls),
            (whole, key_valid),
            (whole, vectors),
        ],
        [
            (per_step, heads_low),
            (per_step, heads_low),
            (per_step, heads_low),
            (per_step, shape((mp, pairs, cols // HEAD * slots, slots), F32)),
            (per_step, heads_low),
            (whole, low_shape),
            (whole, rows_shape),
            (whole, shape((rows, 1), F32)),
        ],
        [pltpu.VMEM((rows, width), F32)],
        here,
        range(5),
    )
    got, hidden_low, cot_blocks = tie(got, hidden_low, cot_blocks)
    ffn.take(ffn.steps - 1, got)
    in_one, down_one = ffn.halves()
    in_two, down_two = flip(in_one, "dp", 1), flip(down_one, "dp", 1)
    in_two, down_two, hidden_low = tie(in_two, down_two, hidden_low)

    column_mine = pl.BlockSpec((width, half_units), lambda s, h: (0, h[0]))
    column_other = pl.BlockSpec((width, half_units), lambda s, h: (0, 1 - h[0]))
    in_args = [(column_mine, w_in), (column_other, w_in), (later, in_one), (later, in_two)]
    half = shape((mp, half_units, width), BF16)
    pre_shape = shape((mp, rows, units), BF16)
    vmem = lambda a: pltpu.VMEM(a.shape, a.dtype)
    results = call(
        partial(ffn_kernel, mp),
        1,
        "ffn",
        44,
        [
            (where_it_is, hidden_low),
            (where_it_is, normed_one),
            (where_it_is, w_in),
            (in_vmem, in_one),
            (in_vmem, in_two),
            (where_it_is, w_down),
            (in_vmem, down_one),
            (in_vmem, down_two),
            (whole, smalls),
            (whole, vectors),
            *[(where_it_is, c) for c in cot_blocks],
        ],
        [
            *[(whole, block_shape)] * mp,
            (where_it_is, rows_shape),
            (where_it_is, pre_shape),
            (where_it_is, half),
            (where_it_is, half),
            (where_it_is, half),
            (where_it_is, half),
            (whole, shape((mp, 1, units), F32)),
            (whole, sums_shape),
        ],
        [
            vmem(low_shape),
            vmem(rows_shape),
            pltpu.VMEM((width, units), BF16),
            pltpu.VMEM((units, width), BF16),
            pltpu.VMEM((mp,) + block_shape.shape, BF16),
            vmem(pre_shape),
            pltpu.VMEM(pre_shape.shape, F32),
            vmem(rows_shape),
            vmem(rows_shape),
            vmem(pre_shape),
            vmem(half),
            vmem(half),
            vmem(half),
            vmem(half),
            pltpu.SemaphoreType.DMA((3 + 1 + mp + 1 + 5 * mp,)),
        ],
        here,
        range(mp + 6),
    )
    out_blocks = results[:mp]
    delta_ffn, pre_grad, in_keep, in_send, down_keep, down_send, sum_in, sums_two = results[mp:]
    in_got, down_got = flip(in_send, "dp", 1), flip(down_send, "dp", 1)
    delta_attn, attn_low, sums_one = call(
        ffn_back_kernel,
        mp,
        "ffn_back",
        32,
        [
            (per_step, pre_grad),
            *in_args,
            (whole, delta_ffn),
            (whole, normed_one),
            (whole, scale_one),
            (whole, vectors),
        ],
        [(whole, rows_shape), (whole, low_shape), (whole, sums_shape)],
        [pltpu.VMEM((rows, width), F32)],
        here,
    )
    in_got, down_got, out_blocks, attn_low = tie(in_got, down_got, out_blocks, attn_low)
    ffn = Reduce([in_keep, down_keep], [in_got, down_got])
    packs = ffn.pack(0)
    packs, attn_low, out_blocks = tie(packs, attn_low, out_blocks)
    got = ffn.send(0, packs)
    out_got = [out_blocks[0]] + [flip(out_blocks[k], "mp", k) for k in range(1, mp)]
    small_half = shape((mp, cols, width), BF16)
    results = call(
        partial(attention_back_kernel, pairs),
        mp,
        "attention_back",
        40,
        [
            (whole, x),
            (whole, attn_low),
            (whole, delta_attn),
            *head_args,
            (per_step, q),
            (per_step, k),
            (per_step, v),
            (per_step, weights),
            (per_step, context),
            (whole, sums_one),
            (whole, sums_two),
            (whole, sum_in),
        ],
        [
            (per_step, small_half),
            (per_step, small_half),
            (
                pl.BlockSpec((2, 1, cols, width), lambda s, h: (0, s, 0, 0)),
                shape((2, mp, cols, width), BF16),
            ),
            (whole, shape((16 + 2 * mp, width), F32)),
            *[(whole, block_shape)] * mp,
        ],
        [pltpu.VMEM((rows, cols), BF16)] * 3 + [pltpu.VMEM((rows, width), F32)],
        here,
        (0, 1, 2) + tuple(range(4, 4 + mp)),
    )
    qk_keep, vo_keep, att_send, sums = results[:4]
    row_sends = results[4:]
    got, out_got, att_send, row_sends, sums = tie(got, out_got, att_send, row_sends, sums)
    for step in range(1, ffn.steps):
        ffn.take(got)
        packs = ffn.pack(step)
        got = ffn.send(step, packs)
        if step == 1:
            att_got = flip(att_send, "dp", 1)
            row_three = flip(row_sends[3], "mp", 3)
        got, att_got, row_three, row_sends = tie(got, att_got, row_three, row_sends)
    place = lambda blocks, dtype: call(
        partial(place_kernel, pairs),
        1,
        "place",
        16,
        [(whole, b) for b in blocks],
        [(whole, shape((mp * pairs, rows_local, width), dtype))],
        [],
        here,
    )[0]
    layer_out = place(out_got, BF16)
    ffn.take(got)
    ffn_parts = ffn.finish()
    ffn_odd = jnp.concatenate([p[1::2] for p in ffn_parts], axis=1)
    ffn_even = jnp.concatenate([p[0::2] for p in ffn_parts], axis=1)
    att = Reduce([qk_keep, vo_keep], [att_got[0], att_got[1]])
    ffn_odd, ffn_even, sums = tie(ffn_odd, ffn_even, sums)
    got = att.send(0, att.pack(0))
    ffn_got = flip(ffn_odd, "mp", 1)
    sums_got = flip(sums, "dp", 1)
    row_two = flip(row_sends[2], "mp", 2)
    got, ffn_got, sums_got, row_two, row_sends, layer_out = tie(
        got, ffn_got, sums_got, row_two, row_sends, layer_out
    )
    sums = sums + sums_got
    for mask in [1 << b for b in range(2, dp.bit_length() - 2)]:
        sums = sums + flip(sums, "dp", mask)
    ffn_two = add_parts(ffn_even[1], ffn_got[1])
    for step in range(1, att.steps):
        att.take(got)
        packs = att.pack(step)
        got = att.send(step, packs)
        if step == 1:
            ffn_last = flip(ffn_two, "mp", 2)
            row_one = flip(row_sends[1], "mp", 1)
            sums_got = flip(sums, "dp", 2)
        got, ffn_last, row_one, sums_got, row_sends = tie(got, ffn_last, row_one, sums_got, row_sends)
    att.take(got)
    sums = sums + sums_got
    att_parts = att.finish()
    att_odd = jnp.concatenate([p[1::2] for p in att_parts], axis=1)
    att_even = jnp.concatenate([p[0::2] for p in att_parts], axis=1)
    ffn_sum = add_parts(ffn_even[0], ffn_got[0], ffn_last)
    ffn = Gather([ffn_sum[None, :ffn_part], ffn_sum[None, ffn_part:]])
    ffn.held, att_odd, att_even, sums = tie(ffn.held, att_odd, att_even, sums)
    got = ffn.send(0)
    att_got = flip(att_odd, "mp", 1)
    sums_got = flip(sums, "dp", dp // 2)
    got, att_got, sums_got, row_one = tie(got, att_got, sums_got, row_one)
    grad_input = place([row_sends[0], row_one, row_two, row_three], F32)
    sums = sums + sums_got
    att_two = add_parts(att_even[1], att_got[1])
    for step in range(1, ffn.steps):
        ffn.take(step - 1, got)
        got = ffn.send(step)
        if step == 1:
            att_last = flip(att_two, "mp", 2)
            sums_got = flip(sums, "mp", 1)
        got, att_last, sums_got, grad_input = tie(got, att_last, sums_got, grad_input)
    ffn.take(ffn.steps - 1, got)
    sums = sums + sums_got
    att_sum = add_parts(att_even[0], att_got[0], att_last)
    ffn_halves = ffn.halves()
    core_got = [flip(h, "dp", 1) for h in ffn_halves]
    att = Pieces([att_sum[:att_part], att_sum[att_part:]])
    got = att.send(0)
    core_got, got, sums = tie(core_got, got, sums)
    for step in range(1, att.steps):
        att.take(step - 1, got)
        got = att.send(step)
        if step == 1:
            sums_got = flip(sums, "mp", 2)
        if step < att.steps - 1:
            got = tie(*got)
    grad_in, grad_down = call(
        unit_grads_kernel,
        1,
        "unit_grads",
        24,
        [(whole, a) for a in ffn_halves + core_got],
        [(whole, shape((width, units), F32)), (whole, shape((units, width), F32))],
        [],
        here,
    )
    grad_in, grad_down, got, sums_got = tie(grad_in, grad_down, got, sums_got)
    sums = sums + sums_got
    att.take(att.steps - 1, got)
    core_got = [flip(h, "dp", 1) for h in att.held]
    grad_qkv, grad_out = call(
        partial(head_grads_kernel, att.indices),
        1,
        "head_grads",
        24,
        [(whole, a) for a in att.held + core_got],
        [
            (whole, shape((3, cols // att_part, att_part, width), F32)),
            (whole, shape((cols // att_part, att_part, width), F32)),
        ],
        [],
        here,
    )
    sum_in_bias = lax.dynamic_index_in_dim(sums, 16 + mi, 0, keepdims=False)
    sum_qv = lax.dynamic_index_in_dim(sums, 16 + mp + mi, 0, keepdims=False)
    sum_qv = jnp.stack([sum_qv[:cols], sum_qv[2 * cols : 3 * cols]])
    return (
        layer_out,
        grad_input,
        grad_qkv.reshape(3, cols, width).transpose(0, 2, 1),
        sum_qv,
        grad_out.reshape(cols, width),
        sums[0],
        sums[1],
        sums[2],
        grad_in,
        sum_in_bias,
        grad_down,
        sums[10],
        sums[8],
        sums[9],
    )


def solution(mesh):
    in_specs = (
        P("dp", "mp", None),
        P("dp"),
        P("dp"),
        P(None, None, "mp"),
        P(None, "mp"),
        P("mp", None),
        P(),
        P(),
        P(),
        P(None, "mp"),
        P("mp"),
        P("mp", None),
        P(),
        P(),
        P(),
        P("dp", "mp", None),
    )
    out_specs = (
        P("dp", "mp", None),
        P("dp", "mp", None),
        P(None, None, "mp"),
        P(None, "mp"),
        P("mp", None),
        P(),
        P(),
        P(),
        P(None, "mp"),
        P("mp"),
        P("mp", None),
        P(),
        P(),
        P(),
    )
    return jax.shard_map(shards, mesh=mesh, in_specs=in_specs, out_specs=out_specs, check_vma=False)
```

```python
from functools import partial

import jax
import jax.numpy as jnp
from jax import lax
from jax.experimental import pallas as pl
from jax.experimental.pallas import tpu as pltpu
from jax.sharding import PartitionSpec as P

HEAD = 64
WORDS = 60
EPSILON = 1e-05
SQRT_HALF = 0.7071067811865476
DENSITY = 0.3989422804014327
F32 = jnp.float32
BF16 = jnp.bfloat16
MIB = 1024 * 1024


def dot(one, two, one_axis, two_axis):
    return lax.dot_general(
        one, two, (((one_axis,), (two_axis,)), ((), ())), preferred_element_type=F32
    )


def normalize(total, gain, shift):
    centered = total - jnp.mean(total, axis=-1, keepdims=True)
    inv_scale = lax.rsqrt(jnp.mean(centered * centered, axis=-1, keepdims=True) + EPSILON)
    normed = centered * inv_scale
    return normed * gain + shift, normed, inv_scale


def normalize_back(upstream, normed, inv_scale, gain):
    scaled_up = upstream * gain
    mean_one = jnp.mean(scaled_up, axis=-1, keepdims=True)
    mean_two = jnp.mean(scaled_up * normed, axis=-1, keepdims=True)
    return inv_scale * (scaled_up - mean_one - normed * mean_two)


def column_sum(array):
    return jnp.sum(array, axis=0, keepdims=True)


def head_stack(array, heads):
    head = lax.broadcasted_iota(jnp.int32, array.shape, 1) // HEAD
    zero = jnp.zeros_like(array)
    return jnp.concatenate([jnp.where(head == h, array, zero) for h in range(heads)], axis=0)


def head_pick(stacked, heads):
    rows = stacked.shape[0] // heads
    head = lax.broadcasted_iota(jnp.int32, (rows, stacked.shape[1]), 1) // HEAD
    total = stacked[:rows]
    for h in range(1, heads):
        total = jnp.where(head == h, stacked[h * rows : (h + 1) * rows], total)
    return total


def head_weights(first, here_ref, own_ref, one_ref, two_ref):
    low = here_ref[0] == 0
    half = one_ref.shape[1]
    one, two = one_ref[0], two_ref[0]
    return (
        jnp.where(first, own_ref[:half], jnp.where(low, one, two)),
        jnp.where(first, own_ref[half:], jnp.where(low, two, one)),
    )


def attention_kernel(
    pairs, here_ref, x_ref, own_qk, qk_one, qk_two, own_vo, vo_one, vo_two, small_ref, valid_ref, vectors_ref,
    q_ref, k_ref, v_ref, weights_ref, context_ref, low_ref, normed_ref, scale_ref, total_ref,
):
    step = pl.program_id(0)
    cols = q_ref.shape[2]
    heads = cols // HEAD
    slots = x_ref.shape[0] // pairs
    x = x_ref[...]
    w_q, w_k = head_weights(step == 0, here_ref, own_qk, qk_one, qk_two)
    w_v, w_o = head_weights(step == 0, here_ref, own_vo, vo_one, vo_two)
    q_ref[0] = (dot(x, w_q, 1, 1) + small_ref[0, 0:1, :cols]).astype(BF16)
    k_ref[0] = dot(x, w_k, 1, 1).astype(BF16)
    v_ref[0] = (dot(x, w_v, 1, 1) + small_ref[0, 1:2, :cols]).astype(BF16)
    for p in range(pairs):
        rows = slice(p * slots, (p + 1) * slots)
        scores = dot(head_stack(q_ref[0, rows], heads), k_ref[0, rows], 1, 1) * HEAD ** (-0.5)
        scores = jnp.where(valid_ref[p] > 0.5, scores, -1e30)
        exp_scores = jnp.exp(scores - jnp.max(scores, axis=-1, keepdims=True))
        weights = exp_scores / jnp.sum(exp_scores, axis=-1, keepdims=True)
        weights_ref[0, p] = weights
        mixed = dot(weights.astype(BF16), v_ref[0, rows], 1, 0)
        context_ref[0, rows] = head_pick(mixed, heads).astype(BF16)
    branch = dot(context_ref[0], w_o, 1, 0)

    @pl.when(step == 0)
    def _():
        total_ref[...] = branch

    @pl.when(step > 0)
    def _():
        total_ref[...] += branch

    @pl.when(step == pl.num_programs(0) - 1)
    def _():
        first_sum = total_ref[...] + vectors_ref[0:1] + x.astype(F32)
        hidden, normed, scale = normalize(first_sum, vectors_ref[1:2], vectors_ref[2:3])
        low_ref[...] = hidden.astype(BF16)
        normed_ref[...] = normed
        scale_ref[...] = scale


def unit_rows(one, two, start, stop):
    half = one.shape[1]
    parts = []
    if start < half:
        parts.append(one[0, start : min(stop, half)])
    if stop > half:
        parts.append(two[0, max(start - half, 0) : stop - half])
    return parts[0] if len(parts) == 1 else jnp.concatenate(parts, axis=0)


def unit_columns(one, two, start, stop):
    half = one.shape[1]
    parts = []
    if start < half:
        parts.append(one[:, start : min(stop, half)])
    if stop > half:
        parts.append(two[:, max(start - half, 0) : stop - half])
    return parts[0] if len(parts) == 1 else jnp.concatenate(parts, axis=1)


def blocks_of(units):
    size = min(256, units)
    return [(start, start + size) for start in range(0, units, size)]


def join_rows(refs):
    pairs = refs[0].shape[0]
    return jnp.concatenate([ref[p].astype(F32) for p in range(pairs) for ref in refs], axis=0)


def leave_rows(array, refs):
    pairs, rows = refs[0].shape[:2]
    for p in range(pairs):
        for j, ref in enumerate(refs):
            start = (p * len(refs) + j) * rows
            ref[p] = array[start : start + rows].astype(BF16)


def ffn_kernel(
    count, here_ref, low_hbm, normed_hbm, w_in_hbm, in_one, in_two, w_down_hbm, down_one, down_two, small_ref,
    vectors_ref, *refs,
):
    cot_hbm, out_refs = refs[:count], refs[count : 2 * count]
    (
        delta_hbm, pre_grad_hbm, in_keep_hbm, in_send_hbm, down_keep_hbm, down_send_hbm, sum_in_ref, sums_ref,
        low_ref, normed_ref, w_in_ref, w_down_ref, cot_ref, act_ref, slope_ref, total_ref, delta_ref, pre_grad_ref,
        in_keep_ref, in_send_ref, down_keep_ref, down_send_ref, sems,
    ) = refs[2 * count :]
    core = here_ref[0]
    half = in_one.shape[1]
    started = [0]

    def start(*pairs):
        copies = []
        for source, target in pairs:
            copies.append(pltpu.make_async_copy(source, target, sems.at[started[0]]))
            copies[-1].start()
            started[0] += 1
        return copies

    def wait(copies):
        for copy in copies:
            copy.wait()

    def halves(start_, stop):
        parts = []
        if start_ < half:
            parts.append((0, start_, min(stop, half)))
        if stop > half:
            parts.append((1, max(start_ - half, 0), stop - half))
        return parts

    def own(which, first, last):
        side = core if which == 0 else 1 - core
        return pl.ds(pl.multiple_of(side * half + first, 128), last - first)

    def down_rows(slot, start_, stop):
        if slot == 0:
            parts = [w_down_ref[own(w, a, b)] for w, a, b in halves(start_, stop)]
        else:
            parts = [(down_one, down_two)[w][slot - 1, a:b] for w, a, b in halves(start_, stop)]
        return jnp.concatenate(parts, axis=0)

    def forward(slot):
        low = low_ref[...]
        branch = None
        for first, last in blocks_of(2 * half):
            parts = halves(first, last)
            if slot == 0:
                w_in = jnp.concatenate([w_in_ref[:, own(*p)] for p in parts], axis=1)
                pre_act = dot(low, w_in, 1, 0)
            else:
                w_in = jnp.concatenate([(in_one, in_two)[w][slot - 1, a:b] for w, a, b in parts], axis=0)
                pre_act = dot(low, w_in, 1, 1)
            bias = jnp.concatenate([small_ref[slot, 2:3, own(*p)] for p in parts], axis=1)
            pre_act = pre_act + bias
            share = 0.5 * (1.0 + lax.erf(pre_act * SQRT_HALF))
            act = (pre_act * share).astype(BF16)
            act_ref[slot, :, first:last] = act
            slope_ref[slot, :, first:last] = share + pre_act * (DENSITY * jnp.exp(-0.5 * pre_act * pre_act))
            term = dot(act, down_rows(slot, first, last), 1, 0)
            branch = term if branch is None else branch + term
        if slot == 1:
            total_ref[...] = branch
        else:
            total_ref[...] += branch

    low_copies = start((low_hbm, low_ref))
    own_copies = start((w_in_hbm, w_in_ref), (w_down_hbm, w_down_ref))
    later_copies = start((normed_hbm, normed_ref), *[(cot_hbm[k], cot_ref.at[k]) for k in range(count)])
    wait(low_copies)
    for slot in range(1, count):
        forward(slot)
    wait(own_copies)
    forward(0)
    wait(later_copies)

    hidden = normed_ref[...] * vectors_ref[1:2] + vectors_ref[2:3]
    second = total_ref[...] + vectors_ref[3:4] + hidden
    gain = vectors_ref[4:5]
    output, normed, scale = normalize(second, gain, vectors_ref[5:6])
    leave_rows(output, out_refs)
    upstream = join_rows([cot_ref.at[k] for k in range(count)])
    delta = normalize_back(upstream, normed, scale, gain)
    delta_ref[...] = delta
    leaving = start((delta_ref, delta_hbm))
    sums_ref[...] = jnp.zeros_like(sums_ref)
    sums_ref[0:1] = column_sum(upstream * normed)
    sums_ref[1:2] = column_sum(upstream)
    sums_ref[2:3] = column_sum(delta)
    ffn_low = delta.astype(BF16)
    low = low_ref[...]
    for slot in range(count):
        for first, last in blocks_of(2 * half):
            act_grad = dot(ffn_low, down_rows(slot, first, last), 1, 1)
            pre_grad_ref[slot, :, first:last] = (act_grad * slope_ref[slot, :, first:last]).astype(BF16)
        leaving += start((pre_grad_ref.at[slot], pre_grad_hbm.at[slot]))
        down_send_ref[slot] = dot(act_ref[slot, :, half:], ffn_low, 0, 0).astype(BF16)
        leaving += start((down_send_ref.at[slot], down_send_hbm.at[slot]))
        down_keep_ref[slot] = dot(act_ref[slot, :, :half], ffn_low, 0, 0).astype(BF16)
        leaving += start((down_keep_ref.at[slot], down_keep_hbm.at[slot]))
        one, two = pre_grad_ref[slot, :, :half], pre_grad_ref[slot, :, half:]
        in_send_ref[slot] = dot(two, low, 0, 0).astype(BF16)
        leaving += start((in_send_ref.at[slot], in_send_hbm.at[slot]))
        in_keep_ref[slot] = dot(one, low, 0, 0).astype(BF16)
        leaving += start((in_keep_ref.at[slot], in_keep_hbm.at[slot]))
        natural = slot ^ here_ref[1]
        sum_in_ref[natural, :, own(0, 0, half)] = column_sum(one.astype(F32))
        sum_in_ref[natural, :, own(1, 0, half)] = column_sum(two.astype(F32))
    wait(leaving)


def ffn_back_kernel(
    here_ref, pre_grad_ref, own_in_one, own_in_two, in_one, in_two, delta_ref, normed_ref, scale_ref, vectors_ref,
    delta_attn_ref, attn_low_ref, sums_ref, total_ref,
):
    step = pl.program_id(0)

    def body(first):
        branch = None
        for start, stop in blocks_of(pre_grad_ref.shape[2]):
            pre_grad = pre_grad_ref[0, :, start:stop]
            if first:
                term = dot(pre_grad, unit_columns(own_in_one, own_in_two, start, stop), 1, 1)
            else:
                term = dot(pre_grad, unit_rows(in_one, in_two, start, stop), 1, 0)
            branch = term if branch is None else branch + term
        if first:
            total_ref[...] = branch
        else:
            total_ref[...] += branch

    pl.when(step == 0)(partial(body, True))
    pl.when(step > 0)(partial(body, False))

    @pl.when(step == pl.num_programs(0) - 1)
    def _():
        hidden_grad = total_ref[...] + delta_ref[...]
        normed = normed_ref[...]
        delta = normalize_back(hidden_grad, normed, scale_ref[...], vectors_ref[1:2])
        delta_attn_ref[...] = delta
        attn_low_ref[...] = delta.astype(BF16)
        sums_ref[...] = jnp.zeros_like(sums_ref)
        sums_ref[0:1] = column_sum(delta)
        sums_ref[1:2] = column_sum(hidden_grad * normed)
        sums_ref[2:3] = column_sum(hidden_grad)


def attention_back_kernel(
    pairs, here_ref, x_ref, attn_low_ref, delta_ref, own_qk, qk_one, qk_two, own_vo, vo_one, vo_two, q_ref, k_ref,
    v_ref, weights_ref, context_ref, sums_one_ref, sums_two_ref, sum_in_ref,
    qk_keep_ref, vo_keep_ref, send_ref, sums_ref, *refs,
):
    step = pl.program_id(0)
    shards_ = pl.num_programs(0)
    out_refs = refs[:shards_]
    dq_ref, dk_ref, dv_ref, total_ref = refs[shards_:]

    @pl.when(step == 0)
    def _():
        total_ref[...] = delta_ref[...]
        sums_ref[...] = jnp.zeros_like(sums_ref)
        sums_ref[0:3] = sums_one_ref[0:3]
        sums_ref[3:6] = sums_two_ref[0:3]
        for j in range(shards_):
            sums_ref[6 + j : 7 + j] = sum_in_ref[j]

    core = here_ref[0]
    cols = q_ref.shape[2]
    heads = cols // HEAD
    slots = x_ref.shape[0] // pairs
    scale = HEAD ** (-0.5)
    x = x_ref[...]
    attn_low = attn_low_ref[...]
    w_q, w_k = head_weights(step == 0, here_ref, own_qk, qk_one, qk_two)
    w_v, w_o = head_weights(step == 0, here_ref, own_vo, vo_one, vo_two)
    context_grad = dot(attn_low, w_o, 1, 1).astype(BF16)
    grad_out = dot(context_ref[0], attn_low, 0, 0).astype(BF16)
    for p in range(pairs):
        rows = slice(p * slots, (p + 1) * slots)
        up = head_stack(context_grad[rows], heads)
        weights = weights_ref[0, p]
        prob_grad = dot(up, v_ref[0, rows], 1, 1)
        inner = jnp.sum(prob_grad * weights, axis=-1, keepdims=True)
        score_grad = (weights * (prob_grad - inner)).astype(BF16)
        dv_ref[rows] = dot(weights.astype(BF16), up, 0, 0).astype(BF16)
        query_grad = head_pick(dot(score_grad, k_ref[0, rows], 1, 0), heads)
        dq_ref[rows] = (query_grad * scale).astype(BF16)
        key_grad = dot(score_grad, head_stack(q_ref[0, rows], heads), 0, 0)
        dk_ref[rows] = (key_grad * scale).astype(BF16)
    dq, dk, dv = dq_ref[...], dk_ref[...], dv_ref[...]
    row = pl.ds(6 + shards_ + (step ^ here_ref[1]), 1)
    sums_ref[row, :cols] = column_sum(dq.astype(F32))
    sums_ref[row, 2 * cols : 3 * cols] = column_sum(dv.astype(F32))
    grad_q = dot(dq, x, 0, 0).astype(BF16)
    grad_k = dot(dk, x, 0, 0).astype(BF16)
    grad_v = dot(dv, x, 0, 0).astype(BF16)

    @pl.when(core == 0)
    def _():
        qk_keep_ref[0], send_ref[0, 0] = grad_q, grad_k
        vo_keep_ref[0], send_ref[1, 0] = grad_v, grad_out

    @pl.when(core != 0)
    def _():
        qk_keep_ref[0], send_ref[0, 0] = grad_k, grad_q
        vo_keep_ref[0], send_ref[1, 0] = grad_out, grad_v

    total_ref[...] += dot(dq, w_q, 1, 0) + dot(dk, w_k, 1, 0) + dot(dv, w_v, 1, 0)

    @pl.when(step == shards_ - 1)
    def _():
        leave_rows(total_ref[...], out_refs)


def place_kernel(pairs, here_ref, *refs):
    out_ref = refs[-1]
    for k, ref in enumerate(refs[:-1]):
        out_ref[pl.ds((here_ref[1] ^ k) * pairs, pairs)] = ref[...].astype(out_ref.dtype)


def head_grads_kernel(order, here_ref, mine_ref, other_ref, grad_qkv_ref, grad_out_ref):
    core = here_ref[0]
    part = grad_out_ref.shape[1]
    for side, ref in ((core, mine_ref), (1 - core, other_ref)):
        for k, index in enumerate(order):
            place = here_ref[2] ^ index
            piece = ref[k].astype(F32)
            grad_qkv_ref[side, place] = piece[:part]

            @pl.when(side == 0)
            def _():
                grad_qkv_ref[2, place] = piece[part:]

            @pl.when(side != 0)
            def _():
                grad_out_ref[place] = piece[part:]


def unit_grads_kernel(here_ref, in_ref, down_ref, in_other, down_other, grad_in_ref, grad_down_ref):
    half = in_ref.shape[1]
    mine = pl.multiple_of(here_ref[0] * half, half)
    other = pl.multiple_of((1 - here_ref[0]) * half, half)
    grad_in_ref[:, pl.ds(mine, half)] = in_ref[0].astype(F32).T
    grad_in_ref[:, pl.ds(other, half)] = in_other[0].astype(F32).T
    grad_down_ref[pl.ds(mine, half)] = down_ref[0].astype(F32)
    grad_down_ref[pl.ds(other, half)] = down_other[0].astype(F32)


def whole(array):
    return pl.BlockSpec(array.shape, lambda *_: (0,) * len(array.shape))


def per_step(array):
    return pl.BlockSpec((1,) + array.shape[1:], lambda s, *_: (s,) + (0,) * (len(array.shape) - 1))


def where_it_is(array):
    return pl.BlockSpec(memory_space=pl.ANY)


def in_vmem(array):
    return pl.BlockSpec(memory_space=pltpu.VMEM)


def call(kernel, steps, name, vmem, inputs, outputs, scratch, scalar, kept=()):
    spec = pltpu.PrefetchScalarGridSpec(
        num_scalar_prefetch=1,
        grid=(steps,),
        in_specs=[make if isinstance(make, pl.BlockSpec) else make(a) for make, a in inputs],
        out_specs=[make if isinstance(make, pl.BlockSpec) else make(a) for make, a in outputs],
        scratch_shapes=scratch,
    )
    return pl.pallas_call(
        kernel,
        grid_spec=spec,
        out_shape=[pltpu.HBM(a.shape, a.dtype) if i in kept else a for i, (_, a) in enumerate(outputs)],
        name=name,
        cost_estimate=pl.CostEstimate(flops=0, bytes_accessed=0, transcendentals=0),
        compiler_params=pltpu.CompilerParams(vmem_limit_bytes=vmem * MIB),
    )(scalar, *[a if make is in_vmem else in_place(a) for make, a in inputs])


def shape(dims, dtype):
    return jax.ShapeDtypeStruct(dims, dtype)


def in_place(array):
    if array.size * array.dtype.itemsize < MIB:
        return array
    return pltpu.with_memory_space_constraint(array, pltpu.HBM)


def add_kernel(counts, *refs):
    refs = refs[1:]
    out_refs = refs[sum(counts) :]
    for count, out_ref in zip(counts, out_refs):
        total = refs[0][...].astype(F32)
        for ref in refs[1:count]:
            total = total + ref[...].astype(F32)
        out_ref[...] = total.astype(BF16)
        refs = refs[count:]


def add_terms(sides, me):
    in_specs, out_specs, arrays, outs, lefts = [], [], [], [], []

    def place(own_bits, fixed, left):
        def index(g, me_ref):
            at = 0
            for b in own_bits:
                if b in fixed:
                    value = (me_ref[0] >> b) & 1
                    value = value if fixed[b] else 1 - value
                else:
                    value = (g >> (len(left) - 1 - left.index(b))) & 1
                at = at * 2 + value
            return (0, at, 0, 0)

        return index

    for terms, fixed in sides:
        first, bits = terms[0]
        left = [b for b in bits if b not in fixed]
        n, _, rows, cols = first.shape
        in_specs += [pl.BlockSpec((n, 1, rows, cols), place(b, fixed, left)) for _, b in terms]
        out_specs.append(pl.BlockSpec((n, 1, rows, cols), lambda g, _: (0, g, 0, 0)))
        arrays += [a for a, _ in terms]
        outs.append(shape((n, 1 << len(left), rows, cols), BF16))
        lefts.append(left)
    results = pl.pallas_call(
        partial(add_kernel, [len(terms) for terms, _ in sides]),
        grid_spec=pltpu.PrefetchScalarGridSpec(
            num_scalar_prefetch=1, grid=(1 << len(lefts[0]),), in_specs=in_specs, out_specs=out_specs
        ),
        out_shape=outs,
        name="add",
        cost_estimate=pl.CostEstimate(flops=0, bytes_accessed=0, transcendentals=0),
        compiler_params=pltpu.CompilerParams(vmem_limit_bytes=24 * MIB),
    )(me, *arrays)
    return results, lefts


def flip(array, axis, mask):
    size = lax.axis_size(axis)
    return lax.ppermute(array, axis, [(i, i ^ mask) for i in range(size)])


def tie(*arrays):
    return lax.optimization_barrier(arrays)


def pick(array, axis, index):
    return lax.dynamic_index_in_dim(array, index, axis, keepdims=False)


def outer_bits():
    bits = list(range(1, lax.axis_size("dp").bit_length() - 1))
    return bits, (bits, bits[::-1])


def share_of():
    me = lax.axis_index("dp")
    return (me & 1) * (lax.axis_size("dp") // 2) + (me >> 1)


class Gather:
    def __init__(self, pair):
        self.bits, self.orders = outer_bits()
        self.steps = len(self.bits)
        self.n, _, self.cols = pair[0].shape
        self.held = [
            a.reshape((self.n,) + (1,) * self.steps + a.shape[1:]) for a in pair
        ]

    def send(self, step):
        return [flip(h, "dp", 1 << order[step]) for h, order in zip(self.held, self.orders)]

    def take(self, step, got):
        me = lax.axis_index("dp")
        merged = []
        for mine, theirs, order in zip(self.held, got, self.orders):
            bit = order[step]
            low = ((me >> bit) & 1) == 0
            parts = [jnp.where(low, mine, theirs), jnp.where(low, theirs, mine)]
            merged.append(jnp.concatenate(parts, axis=1 + self.steps - bit))
        self.held = merged

    def halves(self):
        return [h.reshape(self.n, -1, self.cols) for h in self.held]


class Reduce:
    def __init__(self, keeps, gots):
        self.bits, self.orders = outer_bits()
        self.steps = len(self.bits)
        self.me = lax.axis_index("dp").astype(jnp.int32).reshape(1)
        high_first = self.bits[::-1]
        n, rows, cols = keeps[0].shape
        form = (n, 1 << self.steps, rows >> self.steps, cols)
        self.terms = [
            [(k.reshape(form), high_first), (g.reshape(form), high_first)]
            for k, g in zip(keeps, gots)
        ]
        self.left = [None, None]

    def pack(self, step):
        sides = []
        for terms, order in zip(self.terms, self.orders):
            fixed = {b: True for b in order[:step]}
            fixed[order[step]] = False
            sides.append((terms, fixed))
        sends, self.left = add_terms(sides, self.me)
        return sends

    def send(self, step, packs):
        return [flip(p, "dp", 1 << order[step]) for p, order in zip(packs, self.orders)]

    def take(self, got):
        for side in range(2):
            self.terms[side].append((got[side], self.left[side]))

    def finish(self):
        fixed = {b: True for b in self.bits}
        sums, _ = add_terms([(t, fixed) for t in self.terms], self.me)
        return [a[:, 0] for a in sums]


def gather_stack(piece):
    bits, _ = outer_bits()
    order = list(range(1 << len(bits)))
    if len(order) <= 4:
        return [piece] + [flip(piece, "dp", 2 * k) for k in order[1:]], order
    held = piece[None]
    for bit in bits:
        held = jnp.concatenate([held, flip(held, "dp", 1 << bit)])
    return [held[k] for k in order], order


def add_parts(*parts):
    total = parts[0].astype(F32)
    for part in parts[1:]:
        total = total + part.astype(F32)
    return total.astype(BF16)


def shards(
    tokens,
    word_len,
    region_count,
    w_qkv,
    qv_bias,
    w_out,
    out_bias,
    norm1_gain,
    norm1_bias,
    w_in,
    in_bias,
    w_down,
    down_bias,
    norm2_gain,
    norm2_bias,
    cotangent,
):
    mp = lax.axis_size("mp")
    dp = lax.axis_size("dp")
    mi = lax.axis_index("mp")
    width = tokens.shape[2]
    rows_local = tokens.shape[1]
    slots = rows_local * mp
    pairs = tokens.shape[0] // mp
    rows = pairs * slots
    cols = w_qkv.shape[2]
    units = w_in.shape[1]
    half_units = units // 2
    order = jnp.arange(mp) ^ mi
    here = jnp.stack([lax.axis_index("dp") & 1, mi, lax.axis_index("dp") >> 1]).astype(jnp.int32)
    share = share_of()

    turned = w_qkv.transpose(0, 2, 1).reshape(3 * cols, width)
    own_qk = turned[: 2 * cols]
    own_vo = jnp.concatenate([turned[2 * cols :], w_out], axis=0)
    att_part, ffn_part = 2 * cols // dp, units // dp
    first = share * att_part
    rows_of = lambda array, start, size: lax.dynamic_slice_in_dim(array, start, size, 0)
    vo_piece = jnp.where(
        first < cols,
        rows_of(turned, 2 * cols + jnp.minimum(first, cols - att_part), att_part),
        rows_of(w_out, jnp.maximum(first - cols, 0), att_part),
    )

    def row_blocks(array):
        blocks = array.reshape((mp, pairs) + array.shape[1:])
        return [pick(blocks, 0, mi ^ k) for k in range(mp)]

    def join(blocks):
        return jnp.concatenate(blocks, axis=1).reshape(rows, width)

    fill = lambda v: jnp.pad(v, ((0, 0), (0, width - v.shape[1])))
    small = jnp.concatenate([fill(qv_bias), in_bias.reshape(1, units), jnp.zeros((5, width), BF16)])
    att_send = jnp.concatenate([rows_of(turned, first, att_part), vo_piece], axis=0)
    ffn_send = jnp.concatenate(
        [rows_of(w_in.T, share * ffn_part, ffn_part), rows_of(w_down, share * ffn_part, ffn_part), small],
        axis=0,
    )
    tok = row_blocks(tokens)
    cot = row_blocks(cotangent)
    vectors = jnp.stack(
        [out_bias, norm1_gain, norm1_bias, down_bias, norm2_gain, norm2_bias, out_bias, out_bias]
    ).astype(F32)
    words = lax.dynamic_slice_in_dim(word_len, mi * pairs, pairs, 0)
    regions = lax.dynamic_slice_in_dim(region_count, mi * pairs, pairs, 0)
    slot_index = (order[:, None] * rows_local + jnp.arange(rows_local)[None, :]).reshape(-1)
    key_valid = jnp.where(
        slot_index[None, :] < WORDS,
        slot_index[None, :] < words[:, None],
        slot_index[None, :] - WORDS < regions[:, None],
    ).astype(F32)[:, None, :]

    att_got = [flip(att_send, "mp", k) for k in range(1, mp)]
    att_got, ffn_send, tok, vectors, key_valid, here, own_qk, own_vo = tie(
        att_got, ffn_send, tok, vectors, key_valid, here, own_qk, own_vo
    )
    att = Gather(
        [
            jnp.stack([g[:att_part] for g in att_got]),
            jnp.stack([g[att_part:] for g in att_got]),
        ]
    )
    ffn_two = flip(ffn_send, "mp", 2)
    got = att.send(0)
    tok_one = flip(tok[1], "mp", 1)
    ffn_two, got, tok_one, ffn_send, tok = tie(ffn_two, got, tok_one, ffn_send, tok)
    for step in range(1, att.steps):
        att.take(step - 1, got)
        got = att.send(step)
        if step == 1:
            ffn_odd = flip(jnp.stack([ffn_send, ffn_two]), "mp", 1)
            tok_three = flip(tok[3], "mp", 3)
        got, ffn_odd, tok_three, tok = tie(got, ffn_odd, tok_three, tok)
    att.take(att.steps - 1, got)
    ffn_got = [ffn_odd[0], ffn_two, ffn_odd[1]]
    ffn = Gather(
        [
            jnp.stack([g[:ffn_part] for g in ffn_got]),
            jnp.stack([g[ffn_part : 2 * ffn_part] for g in ffn_got]),
        ]
    )
    got = ffn.send(0)
    qk_one, vo_one = att.halves()
    qk_two, vo_two = flip(qk_one, "dp", 1), flip(vo_one, "dp", 1)
    tok_two = flip(tok[2], "mp", 2)
    smalls = jnp.stack([small] + [g[2 * ffn_part :] for g in ffn_got]).astype(F32)
    got, qk_two, vo_two, tok_two, cot, smalls = tie(got, qk_two, vo_two, tok_two, cot, smalls)
    heads_low = shape((mp, rows, cols), BF16)
    low_shape = shape((rows, width), BF16)
    rows_shape = shape((rows, width), F32)
    sums_shape = shape((8, width), F32)
    block_shape = shape((pairs, rows_local, width), BF16)
    for step in range(1, ffn.steps):
        ffn.take(step - 1, got)
        got = ffn.send(step)
        if step == 1:
            cot_blocks = [cot[0]] + [flip(cot[k], "mp", k) for k in range(1, mp)]
        if step < ffn.steps - 1:
            got = tie(*got)
    x = join([tok[0], tok_one, tok_two, tok_three])
    later = lambda a: pl.BlockSpec((1,) + a.shape[1:], lambda s, h: (jnp.clip(s - 1, 0, mp - 2), 0, 0))
    head_args = [
        (whole, own_qk),
        (later, qk_one),
        (later, qk_two),
        (whole, own_vo),
        (later, vo_one),
        (later, vo_two),
    ]
    q, k, v, weights, context, hidden_low, normed_one, scale_one = call(
        partial(attention_kernel, pairs),
        mp,
        "attention",
        32,
        [
            (whole, x),
            *head_args,
            (per_step, smalls),
            (whole, key_valid),
            (whole, vectors),
        ],
        [
            (per_step, heads_low),
            (per_step, heads_low),
            (per_step, heads_low),
            (per_step, shape((mp, pairs, cols // HEAD * slots, slots), F32)),
            (per_step, heads_low),
            (whole, low_shape),
            (whole, rows_shape),
            (whole, shape((rows, 1), F32)),
        ],
        [pltpu.VMEM((rows, width), F32)],
        here,
        range(5),
    )
    got, hidden_low, cot_blocks = tie(got, hidden_low, cot_blocks)
    ffn.take(ffn.steps - 1, got)
    in_one, down_one = ffn.halves()
    in_two, down_two = flip(in_one, "dp", 1), flip(down_one, "dp", 1)
    in_two, down_two, hidden_low = tie(in_two, down_two, hidden_low)

    column_mine = pl.BlockSpec((width, half_units), lambda s, h: (0, h[0]))
    column_other = pl.BlockSpec((width, half_units), lambda s, h: (0, 1 - h[0]))
    in_args = [(column_mine, w_in), (column_other, w_in), (later, in_one), (later, in_two)]
    half = shape((mp, half_units, width), BF16)
    pre_shape = shape((mp, rows, units), BF16)
    vmem = lambda a: pltpu.VMEM(a.shape, a.dtype)
    results = call(
        partial(ffn_kernel, mp),
        1,
        "ffn",
        44,
        [
            (where_it_is, hidden_low),
            (where_it_is, normed_one),
            (where_it_is, w_in),
            (in_vmem, in_one),
            (in_vmem, in_two),
            (where_it_is, w_down),
            (in_vmem, down_one),
            (in_vmem, down_two),
            (whole, smalls),
            (whole, vectors),
            *[(where_it_is, c) for c in cot_blocks],
        ],
        [
            *[(whole, block_shape)] * mp,
            (where_it_is, rows_shape),
            (where_it_is, pre_shape),
            (where_it_is, half),
            (where_it_is, half),
            (where_it_is, half),
            (where_it_is, half),
            (whole, shape((mp, 1, units), F32)),
            (whole, sums_shape),
        ],
        [
            vmem(low_shape),
            vmem(rows_shape),
            pltpu.VMEM((width, units), BF16),
            pltpu.VMEM((units, width), BF16),
            pltpu.VMEM((mp,) + block_shape.shape, BF16),
            vmem(pre_shape),
            pltpu.VMEM(pre_shape.shape, F32),
            vmem(rows_shape),
            vmem(rows_shape),
            vmem(pre_shape),
            vmem(half),
            vmem(half),
            vmem(half),
            vmem(half),
            pltpu.SemaphoreType.DMA((3 + 1 + mp + 1 + 5 * mp,)),
        ],
        here,
        range(mp + 6),
    )
    out_blocks = results[:mp]
    delta_ffn, pre_grad, in_keep, in_send, down_keep, down_send, sum_in, sums_two = results[mp:]
    in_got, down_got = flip(in_send, "dp", 1), flip(down_send, "dp", 1)
    delta_attn, attn_low, sums_one = call(
        ffn_back_kernel,
        mp,
        "ffn_back",
        32,
        [
            (per_step, pre_grad),
            *in_args,
            (whole, delta_ffn),
            (whole, normed_one),
            (whole, scale_one),
            (whole, vectors),
        ],
        [(whole, rows_shape), (whole, low_shape), (whole, sums_shape)],
        [pltpu.VMEM((rows, width), F32)],
        here,
        (0,),
    )
    in_got, down_got, out_blocks, attn_low = tie(in_got, down_got, out_blocks, attn_low)
    ffn = Reduce([in_keep, down_keep], [in_got, down_got])
    packs = ffn.pack(0)
    packs, attn_low, out_blocks = tie(packs, attn_low, out_blocks)
    got = ffn.send(0, packs)
    out_got = [out_blocks[0]] + [flip(out_blocks[k], "mp", k) for k in range(1, mp)]
    small_half = shape((mp, cols, width), BF16)
    results = call(
        partial(attention_back_kernel, pairs),
        mp,
        "attention_back",
        40,
        [
            (whole, x),
            (whole, attn_low),
            (whole, delta_attn),
            *head_args,
            (per_step, q),
            (per_step, k),
            (per_step, v),
            (per_step, weights),
            (per_step, context),
            (whole, sums_one),
            (whole, sums_two),
            (whole, sum_in),
        ],
        [
            (per_step, small_half),
            (per_step, small_half),
            (
                pl.BlockSpec((2, 1, cols, width), lambda s, h: (0, s, 0, 0)),
                shape((2, mp, cols, width), BF16),
            ),
            (whole, shape((-(-(6 + 2 * mp) // 8) * 8, width), F32)),
            *[(whole, block_shape)] * mp,
        ],
        [pltpu.VMEM((rows, cols), BF16)] * 3 + [pltpu.VMEM((rows, width), F32)],
        here,
        (0, 1, 2) + tuple(range(4, 4 + mp)),
    )
    qk_keep, vo_keep, att_send, sums = results[:4]
    row_sends = results[4:]
    got, out_got, att_send, row_sends, sums = tie(got, out_got, att_send, row_sends, sums)
    for step in range(1, ffn.steps):
        ffn.take(got)
        packs = ffn.pack(step)
        got = ffn.send(step, packs)
        if step == 1:
            att_got = flip(att_send, "dp", 1)
            row_three = flip(row_sends[3], "mp", 3)
            sums_got = flip(sums, "mp", 2)
        got, att_got, row_three, sums_got, row_sends = tie(got, att_got, row_three, sums_got, row_sends)
    sums = sums + sums_got
    place = lambda blocks, dtype: call(
        partial(place_kernel, pairs),
        1,
        "place",
        16,
        [(whole, b) for b in blocks],
        [(whole, shape((mp * pairs, rows_local, width), dtype))],
        [],
        here,
    )[0]
    layer_out = place(out_got, BF16)
    ffn.take(got)
    ffn_parts = ffn.finish()
    ffn_odd = jnp.concatenate([p[1::2] for p in ffn_parts], axis=1)
    ffn_even = jnp.concatenate([p[0::2] for p in ffn_parts], axis=1)
    att = Reduce([qk_keep, vo_keep], [att_got[0], att_got[1]])
    ffn_odd, ffn_even, sums = tie(ffn_odd, ffn_even, sums)
    got = att.send(0, att.pack(0))
    ffn_got = flip(ffn_odd, "mp", 1)
    sums_got = flip(sums, "dp", 2)
    row_two = flip(row_sends[2], "mp", 2)
    got, ffn_got, sums_got, row_two, row_sends, layer_out = tie(
        got, ffn_got, sums_got, row_two, row_sends, layer_out
    )
    sums = sums + sums_got
    for mask in [1 << b for b in range(2, dp.bit_length() - 2)]:
        sums = sums + flip(sums, "dp", mask)
    ffn_two = add_parts(ffn_even[1], ffn_got[1])
    for step in range(1, att.steps):
        att.take(got)
        packs = att.pack(step)
        got = att.send(step, packs)
        if step == 1:
            ffn_last = flip(ffn_two, "mp", 2)
            row_one = flip(row_sends[1], "mp", 1)
            sums_got = flip(sums, "dp", dp // 2)
        got, ffn_last, row_one, sums_got, row_sends = tie(got, ffn_last, row_one, sums_got, row_sends)
    att.take(got)
    sums = sums + sums_got
    att_parts = att.finish()
    att_odd = jnp.concatenate([p[1::2] for p in att_parts], axis=1)
    att_even = jnp.concatenate([p[0::2] for p in att_parts], axis=1)
    ffn_sum = add_parts(ffn_even[0], ffn_got[0], ffn_last)
    ffn = Gather([ffn_sum[None, :ffn_part], ffn_sum[None, ffn_part:]])
    ffn.held, att_odd, att_even, sums = tie(ffn.held, att_odd, att_even, sums)
    got = ffn.send(0)
    att_got = flip(att_odd, "mp", 1)
    sums_got = flip(sums, "dp", 1)
    got, att_got, sums_got, row_one = tie(got, att_got, sums_got, row_one)
    grad_input = place([row_sends[0], row_one, row_two, row_three], F32)
    sums = sums + sums_got
    att_two = add_parts(att_even[1], att_got[1])
    for step in range(1, ffn.steps):
        ffn.take(step - 1, got)
        got = ffn.send(step)
        if step == 1:
            att_last = flip(att_two, "mp", 2)
            sums_got = flip(sums, "mp", 1)
        got, att_last, sums_got, grad_input = tie(got, att_last, sums_got, grad_input)
    ffn.take(ffn.steps - 1, got)
    sums = sums + sums_got
    att_sum = add_parts(att_even[0], att_got[0], att_last)
    ffn_halves = ffn.halves()
    core_got = [flip(h, "dp", 1) for h in ffn_halves]
    att_mine, att_order = gather_stack(att_sum)
    grad_in, grad_down = call(
        unit_grads_kernel,
        1,
        "unit_grads",
        24,
        [(whole, a) for a in ffn_halves + core_got],
        [(whole, shape((width, units), F32)), (whole, shape((units, width), F32))],
        [],
        here,
    )
    att_mine, grad_in, grad_down, sums = tie(att_mine, grad_in, grad_down, sums)
    att_mine = jnp.stack(att_mine)
    att_other = flip(att_mine, "dp", 1)
    grad_qkv, grad_out = call(
        partial(head_grads_kernel, att_order),
        1,
        "head_grads",
        24,
        [(whole, att_mine), (whole, att_other)],
        [
            (whole, shape((3, cols // att_part, att_part, width), F32)),
            (whole, shape((cols // att_part, att_part, width), F32)),
        ],
        [],
        here,
    )
    sum_in_bias = lax.dynamic_index_in_dim(sums, 6 + mi, 0, keepdims=False)
    sum_qv = lax.dynamic_index_in_dim(sums, 6 + mp + mi, 0, keepdims=False)
    sum_qv = jnp.stack([sum_qv[:cols], sum_qv[2 * cols : 3 * cols]])
    return (
        layer_out,
        grad_input,
        grad_qkv.reshape(3, cols, width).transpose(0, 2, 1),
        sum_qv,
        grad_out.reshape(cols, width),
        sums[0],
        sums[1],
        sums[2],
        grad_in,
        sum_in_bias,
        grad_down,
        sums[5],
        sums[3],
        sums[4],
    )


def solution(mesh):
    in_specs = (
        P("dp", "mp", None),
        P("dp"),
        P("dp"),
        P(None, None, "mp"),
        P(None, "mp"),
        P("mp", None),
        P(),
        P(),
        P(),
        P(None, "mp"),
        P("mp"),
        P("mp", None),
        P(),
        P(),
        P(),
        P("dp", "mp", None),
    )
    out_specs = (
        P("dp", "mp", None),
        P("dp", "mp", None),
        P(None, None, "mp"),
        P(None, "mp"),
        P("mp", None),
        P(),
        P(),
        P(),
        P(None, "mp"),
        P("mp"),
        P("mp", None),
        P(),
        P(),
        P(),
    )
    return jax.shard_map(shards, mesh=mesh, in_specs=in_specs, out_specs=out_specs, check_vma=False)
```

```python
from functools import partial

import jax
import jax.numpy as jnp
from jax import lax
from jax.experimental import pallas as pl
from jax.experimental.pallas import tpu as pltpu
from jax.sharding import PartitionSpec as P

HEAD = 64
WORDS = 60
EPSILON = 1e-05
SQRT_HALF = 0.7071067811865476
DENSITY = 0.3989422804014327
F32 = jnp.float32
BF16 = jnp.bfloat16
MIB = 1024 * 1024


def dot(one, two, one_axis, two_axis):
    return lax.dot_general(
        one, two, (((one_axis,), (two_axis,)), ((), ())), preferred_element_type=F32
    )


def normalize(total, gain, shift):
    centered = total - jnp.mean(total, axis=-1, keepdims=True)
    inv_scale = lax.rsqrt(jnp.mean(centered * centered, axis=-1, keepdims=True) + EPSILON)
    normed = centered * inv_scale
    return normed * gain + shift, normed, inv_scale


def normalize_back(upstream, normed, inv_scale, gain):
    scaled_up = upstream * gain
    mean_one = jnp.mean(scaled_up, axis=-1, keepdims=True)
    mean_two = jnp.mean(scaled_up * normed, axis=-1, keepdims=True)
    return inv_scale * (scaled_up - mean_one - normed * mean_two)


def column_sum(array):
    return jnp.sum(array, axis=0, keepdims=True)


def head_stack(array, heads):
    head = lax.broadcasted_iota(jnp.int32, array.shape, 1) // HEAD
    zero = jnp.zeros_like(array)
    return jnp.concatenate([jnp.where(head == h, array, zero) for h in range(heads)], axis=0)


def head_pick(stacked, heads):
    rows = stacked.shape[0] // heads
    head = lax.broadcasted_iota(jnp.int32, (rows, stacked.shape[1]), 1) // HEAD
    total = stacked[:rows]
    for h in range(1, heads):
        total = jnp.where(head == h, stacked[h * rows : (h + 1) * rows], total)
    return total


def head_weights(first, here_ref, own_ref, one_ref, two_ref):
    low = here_ref[0] == 0
    half = one_ref.shape[1]
    one, two = one_ref[0], two_ref[0]
    return (
        jnp.where(first, own_ref[:half], jnp.where(low, one, two)),
        jnp.where(first, own_ref[half:], jnp.where(low, two, one)),
    )


def attention_kernel(
    pairs, here_ref, x_ref, own_qk, qk_one, qk_two, own_vo, vo_one, vo_two, small_ref, valid_ref, vectors_ref,
    q_ref, k_ref, v_ref, weights_ref, context_ref, low_ref, normed_ref, scale_ref, total_ref,
):
    step = pl.program_id(0)
    cols = q_ref.shape[2]
    heads = cols // HEAD
    slots = x_ref.shape[0] // pairs
    x = x_ref[...]
    w_q, w_k = head_weights(step == 0, here_ref, own_qk, qk_one, qk_two)
    w_v, w_o = head_weights(step == 0, here_ref, own_vo, vo_one, vo_two)
    q_ref[0] = (dot(x, w_q, 1, 1) + small_ref[0, 0:1, :cols]).astype(BF16)
    k_ref[0] = dot(x, w_k, 1, 1).astype(BF16)
    v_ref[0] = (dot(x, w_v, 1, 1) + small_ref[0, 1:2, :cols]).astype(BF16)
    for p in range(pairs):
        rows = slice(p * slots, (p + 1) * slots)
        scores = dot(head_stack(q_ref[0, rows], heads), k_ref[0, rows], 1, 1) * HEAD ** (-0.5)
        scores = jnp.where(valid_ref[p] > 0.5, scores, -1e30)
        exp_scores = jnp.exp(scores - jnp.max(scores, axis=-1, keepdims=True))
        weights = exp_scores / jnp.sum(exp_scores, axis=-1, keepdims=True)
        weights_ref[0, p] = weights
        mixed = dot(weights.astype(BF16), v_ref[0, rows], 1, 0)
        context_ref[0, rows] = head_pick(mixed, heads).astype(BF16)
    branch = dot(context_ref[0], w_o, 1, 0)

    @pl.when(step == 0)
    def _():
        total_ref[...] = branch

    @pl.when(step > 0)
    def _():
        total_ref[...] += branch

    @pl.when(step == pl.num_programs(0) - 1)
    def _():
        first_sum = total_ref[...] + vectors_ref[0:1] + x.astype(F32)
        hidden, normed, scale = normalize(first_sum, vectors_ref[1:2], vectors_ref[2:3])
        low_ref[...] = hidden.astype(BF16)
        normed_ref[...] = normed
        scale_ref[...] = scale


def blocks_of(units):
    size = min(256, units)
    return [(start, min(start + size, units)) for start in range(0, units, size)]


class Copies:
    def __init__(self, sems):
        self.sems, self.used = sems, 0

    def start(self, *pairs):
        copies = []
        for source, target in pairs:
            copies.append(pltpu.make_async_copy(source, target, self.sems.at[self.used]))
            copies[-1].start()
            self.used += 1
        return copies


def wait_all(copies):
    for copy in copies:
        copy.wait()


def halves_of(half, start, stop):
    parts = []
    if start < half:
        parts.append((0, start, min(stop, half)))
    if stop > half:
        parts.append((1, max(start - half, 0), stop - half))
    return parts


def own_units(core, half, which, first, last):
    side = core if which == 0 else 1 - core
    return pl.ds(pl.multiple_of(side * half + first, 128), last - first)


def join_rows(refs):
    pairs = refs[0].shape[0]
    return jnp.concatenate([ref[p].astype(F32) for p in range(pairs) for ref in refs], axis=0)


def leave_rows(array, refs):
    pairs, rows = refs[0].shape[:2]
    for p in range(pairs):
        for j, ref in enumerate(refs):
            start = (p * len(refs) + j) * rows
            ref[p] = array[start : start + rows].astype(BF16)


def ffn_kernel(
    count, here_ref, low_hbm, normed_hbm, w_in_hbm, in_one, in_two, w_down_hbm, down_one, down_two, small_ref,
    vectors_ref, *refs,
):
    cot_hbm, out_refs = refs[:count], refs[count : 2 * count]
    (
        delta_hbm, pre_grad_hbm, in_keep_hbm, in_send_hbm, down_keep_hbm, down_send_hbm, sum_in_ref, sums_ref,
        low_ref, normed_ref, w_in_ref, w_down_ref, cot_ref, act_ref, slope_ref, total_ref, delta_ref, pre_grad_ref,
        in_keep_ref, in_send_ref, down_keep_ref, down_send_ref, sems,
    ) = refs[2 * count :]
    core = here_ref[0]
    half = in_one.shape[1]
    copies_ = Copies(sems)
    start, wait = copies_.start, wait_all

    halves = partial(halves_of, half)
    own = partial(own_units, core, half)

    def down_rows(slot, start_, stop):
        if slot == 0:
            parts = [w_down_ref[own(w, a, b)] for w, a, b in halves(start_, stop)]
        else:
            parts = [(down_one, down_two)[w][slot - 1, a:b] for w, a, b in halves(start_, stop)]
        return jnp.concatenate(parts, axis=0)

    def forward(slot):
        low = low_ref[...]
        branch = None
        for first, last in blocks_of(2 * half):
            parts = halves(first, last)
            if slot == 0:
                w_in = jnp.concatenate([w_in_ref[:, own(*p)] for p in parts], axis=1)
                pre_act = dot(low, w_in, 1, 0)
            else:
                w_in = jnp.concatenate([(in_one, in_two)[w][slot - 1, a:b] for w, a, b in parts], axis=0)
                pre_act = dot(low, w_in, 1, 1)
            bias = jnp.concatenate([small_ref[slot, 2:3, own(*p)] for p in parts], axis=1)
            pre_act = pre_act + bias
            share = 0.5 * (1.0 + lax.erf(pre_act * SQRT_HALF))
            act = (pre_act * share).astype(BF16)
            act_ref[slot, :, first:last] = act
            slope_ref[slot, :, first:last] = share + pre_act * (DENSITY * jnp.exp(-0.5 * pre_act * pre_act))
            term = dot(act, down_rows(slot, first, last), 1, 0)
            branch = term if branch is None else branch + term
        if slot == 1:
            total_ref[...] = branch
        else:
            total_ref[...] += branch

    low_copies = start((low_hbm, low_ref))
    own_copies = start((w_in_hbm, w_in_ref), (w_down_hbm, w_down_ref))
    later_copies = start((normed_hbm, normed_ref), *[(cot_hbm[k], cot_ref.at[k]) for k in range(count)])
    wait(low_copies)
    for slot in range(1, count):
        forward(slot)
    wait(own_copies)
    forward(0)
    wait(later_copies)

    hidden = normed_ref[...] * vectors_ref[1:2] + vectors_ref[2:3]
    second = total_ref[...] + vectors_ref[3:4] + hidden
    gain = vectors_ref[4:5]
    output, normed, scale = normalize(second, gain, vectors_ref[5:6])
    leave_rows(output, out_refs)
    upstream = join_rows([cot_ref.at[k] for k in range(count)])
    delta = normalize_back(upstream, normed, scale, gain)
    delta_ref[...] = delta
    leaving = start((delta_ref, delta_hbm))
    sums_ref[...] = jnp.zeros_like(sums_ref)
    sums_ref[0:1] = column_sum(upstream * normed)
    sums_ref[1:2] = column_sum(upstream)
    sums_ref[2:3] = column_sum(delta)
    ffn_low = delta.astype(BF16)
    low = low_ref[...]
    for slot in range(count):
        for first, last in blocks_of(2 * half):
            act_grad = dot(ffn_low, down_rows(slot, first, last), 1, 1)
            pre_grad_ref[slot, :, first:last] = (act_grad * slope_ref[slot, :, first:last]).astype(BF16)
        leaving += start((pre_grad_ref.at[slot], pre_grad_hbm.at[slot]))
        down_send_ref[slot] = dot(act_ref[slot, :, half:], ffn_low, 0, 0).astype(BF16)
        leaving += start((down_send_ref.at[slot], down_send_hbm.at[slot]))
        down_keep_ref[slot] = dot(act_ref[slot, :, :half], ffn_low, 0, 0).astype(BF16)
        leaving += start((down_keep_ref.at[slot], down_keep_hbm.at[slot]))
        one, two = pre_grad_ref[slot, :, :half], pre_grad_ref[slot, :, half:]
        in_send_ref[slot] = dot(two, low, 0, 0).astype(BF16)
        leaving += start((in_send_ref.at[slot], in_send_hbm.at[slot]))
        in_keep_ref[slot] = dot(one, low, 0, 0).astype(BF16)
        leaving += start((in_keep_ref.at[slot], in_keep_hbm.at[slot]))
        natural = slot ^ here_ref[1]
        sum_in_ref[natural, :, own(0, 0, half)] = column_sum(one.astype(F32))
        sum_in_ref[natural, :, own(1, 0, half)] = column_sum(two.astype(F32))
    wait(leaving)


def ffn_back_kernel(
    count, here_ref, pre_grad_hbm, w_in_hbm, in_one, in_two, delta_hbm, normed_hbm, scale_ref, vectors_ref,
    delta_attn_hbm, attn_low_ref, sums_ref, pre_grad_ref, w_in_ref, delta_ref, normed_ref, total_ref, sems,
):
    core = here_ref[0]
    half = in_one.shape[1]
    copies = Copies(sems)
    slots = list(range(1, count)) + [0]
    pre_copies = {slot: copies.start((pre_grad_hbm.at[slot], pre_grad_ref.at[slot])) for slot in slots}
    w_copies = copies.start((w_in_hbm, w_in_ref))
    norm_copies = copies.start((delta_hbm, delta_ref), (normed_hbm, normed_ref))
    branch = None
    for slot in slots:
        wait_all(pre_copies[slot])
        if slot == 0:
            wait_all(w_copies)
        for a, b in blocks_of(2 * half):
            pre_grad = pre_grad_ref[slot, :, a:b]
            parts = halves_of(half, a, b)
            if slot == 0:
                w_in = jnp.concatenate([w_in_ref[:, own_units(core, half, *p)] for p in parts], axis=1)
                term = dot(pre_grad, w_in, 1, 1)
            else:
                w_in = jnp.concatenate([(in_one, in_two)[w][slot - 1, c:d] for w, c, d in parts], axis=0)
                term = dot(pre_grad, w_in, 1, 0)
            branch = term if branch is None else branch + term
    wait_all(norm_copies)
    hidden_grad = branch + delta_ref[...]
    normed = normed_ref[...]
    delta = normalize_back(hidden_grad, normed, scale_ref[...], vectors_ref[1:2])
    total_ref[...] = delta
    leaving = copies.start((total_ref, delta_attn_hbm))
    attn_low_ref[...] = delta.astype(BF16)
    sums_ref[...] = jnp.zeros_like(sums_ref)
    sums_ref[0:1] = column_sum(delta)
    sums_ref[1:2] = column_sum(hidden_grad * normed)
    sums_ref[2:3] = column_sum(hidden_grad)
    wait_all(leaving)


def attention_back_kernel(
    pairs, here_ref, x_ref, attn_low_ref, delta_ref, own_qk, qk_one, qk_two, own_vo, vo_one, vo_two, q_ref, k_ref,
    v_ref, weights_ref, context_ref, sums_one_ref, sums_two_ref, sum_in_ref,
    qk_keep_ref, vo_keep_ref, send_ref, sums_ref, *refs,
):
    step = pl.program_id(0)
    shards_ = pl.num_programs(0)
    out_refs = refs[:shards_]
    dq_ref, dk_ref, dv_ref, total_ref = refs[shards_:]

    @pl.when(step == 0)
    def _():
        total_ref[...] = delta_ref[...]
        sums_ref[...] = jnp.zeros_like(sums_ref)
        sums_ref[0:3] = sums_one_ref[0:3]
        sums_ref[3:6] = sums_two_ref[0:3]
        for j in range(shards_):
            sums_ref[6 + j : 7 + j] = sum_in_ref[j]

    core = here_ref[0]
    cols = q_ref.shape[2]
    heads = cols // HEAD
    slots = x_ref.shape[0] // pairs
    scale = HEAD ** (-0.5)
    x = x_ref[...]
    attn_low = attn_low_ref[...]
    w_q, w_k = head_weights(step == 0, here_ref, own_qk, qk_one, qk_two)
    w_v, w_o = head_weights(step == 0, here_ref, own_vo, vo_one, vo_two)
    context_grad = dot(attn_low, w_o, 1, 1).astype(BF16)
    grad_out = dot(context_ref[0], attn_low, 0, 0).astype(BF16)
    for p in range(pairs):
        rows = slice(p * slots, (p + 1) * slots)
        up = head_stack(context_grad[rows], heads)
        weights = weights_ref[0, p]
        prob_grad = dot(up, v_ref[0, rows], 1, 1)
        inner = jnp.sum(prob_grad * weights, axis=-1, keepdims=True)
        score_grad = (weights * (prob_grad - inner)).astype(BF16)
        dv_ref[rows] = dot(weights.astype(BF16), up, 0, 0).astype(BF16)
        query_grad = head_pick(dot(score_grad, k_ref[0, rows], 1, 0), heads)
        dq_ref[rows] = (query_grad * scale).astype(BF16)
        key_grad = dot(score_grad, head_stack(q_ref[0, rows], heads), 0, 0)
        dk_ref[rows] = (key_grad * scale).astype(BF16)
    dq, dk, dv = dq_ref[...], dk_ref[...], dv_ref[...]
    row = pl.ds(6 + shards_ + (step ^ here_ref[1]), 1)
    sums_ref[row, :cols] = column_sum(dq.astype(F32))
    sums_ref[row, 2 * cols : 3 * cols] = column_sum(dv.astype(F32))
    grad_q = dot(dq, x, 0, 0).astype(BF16)
    grad_k = dot(dk, x, 0, 0).astype(BF16)
    grad_v = dot(dv, x, 0, 0).astype(BF16)

    @pl.when(core == 0)
    def _():
        qk_keep_ref[0], send_ref[0, 0] = grad_q, grad_k
        vo_keep_ref[0], send_ref[1, 0] = grad_v, grad_out

    @pl.when(core != 0)
    def _():
        qk_keep_ref[0], send_ref[0, 0] = grad_k, grad_q
        vo_keep_ref[0], send_ref[1, 0] = grad_out, grad_v

    total_ref[...] += dot(dq, w_q, 1, 0) + dot(dk, w_k, 1, 0) + dot(dv, w_v, 1, 0)

    @pl.when(step == shards_ - 1)
    def _():
        leave_rows(total_ref[...], out_refs)


def place_kernel(pairs, here_ref, *refs):
    out_ref = refs[-1]
    for k, ref in enumerate(refs[:-1]):
        out_ref[pl.ds((here_ref[1] ^ k) * pairs, pairs)] = ref[...].astype(out_ref.dtype)


def head_grads_kernel(order, here_ref, mine_ref, other_ref, grad_qkv_ref, grad_out_ref):
    core = here_ref[0]
    part = grad_out_ref.shape[1]
    for side, ref in ((core, mine_ref), (1 - core, other_ref)):
        for k, index in enumerate(order):
            place = here_ref[2] ^ index
            piece = ref[k].astype(F32)
            grad_qkv_ref[side, place] = piece[:part]

            @pl.when(side == 0)
            def _():
                grad_qkv_ref[2, place] = piece[part:]

            @pl.when(side != 0)
            def _():
                grad_out_ref[place] = piece[part:]


def unit_grads_kernel(here_ref, in_ref, down_ref, in_other, down_other, grad_in_ref, grad_down_ref):
    half = in_ref.shape[1]
    mine = pl.multiple_of(here_ref[0] * half, half)
    other = pl.multiple_of((1 - here_ref[0]) * half, half)
    grad_in_ref[:, pl.ds(mine, half)] = in_ref[0].astype(F32).T
    grad_in_ref[:, pl.ds(other, half)] = in_other[0].astype(F32).T
    grad_down_ref[pl.ds(mine, half)] = down_ref[0].astype(F32)
    grad_down_ref[pl.ds(other, half)] = down_other[0].astype(F32)


def whole(array):
    return pl.BlockSpec(array.shape, lambda *_: (0,) * len(array.shape))


def per_step(array):
    return pl.BlockSpec((1,) + array.shape[1:], lambda s, *_: (s,) + (0,) * (len(array.shape) - 1))


def where_it_is(array):
    return pl.BlockSpec(memory_space=pl.ANY)


def in_vmem(array):
    return pl.BlockSpec(memory_space=pltpu.VMEM)


def call(kernel, steps, name, vmem, inputs, outputs, scratch, scalar, kept=()):
    spec = pltpu.PrefetchScalarGridSpec(
        num_scalar_prefetch=1,
        grid=(steps,),
        in_specs=[make if isinstance(make, pl.BlockSpec) else make(a) for make, a in inputs],
        out_specs=[make if isinstance(make, pl.BlockSpec) else make(a) for make, a in outputs],
        scratch_shapes=scratch,
    )
    return pl.pallas_call(
        kernel,
        grid_spec=spec,
        out_shape=[pltpu.HBM(a.shape, a.dtype) if i in kept else a for i, (_, a) in enumerate(outputs)],
        name=name,
        cost_estimate=pl.CostEstimate(flops=0, bytes_accessed=0, transcendentals=0),
        compiler_params=pltpu.CompilerParams(vmem_limit_bytes=vmem * MIB),
    )(scalar, *[a if make is in_vmem else in_place(a) for make, a in inputs])


def shape(dims, dtype):
    return jax.ShapeDtypeStruct(dims, dtype)


def in_place(array):
    if array.size * array.dtype.itemsize < MIB:
        return array
    return pltpu.with_memory_space_constraint(array, pltpu.HBM)


def add_kernel(counts, *refs):
    refs = refs[1:]
    out_refs = refs[sum(counts) :]
    for count, out_ref in zip(counts, out_refs):
        total = refs[0][...].astype(F32)
        for ref in refs[1:count]:
            total = total + ref[...].astype(F32)
        out_ref[...] = total.astype(BF16)
        refs = refs[count:]


def add_terms(sides, me):
    in_specs, out_specs, arrays, outs, lefts = [], [], [], [], []

    def place(own_bits, fixed, left):
        def index(g, me_ref):
            at = 0
            for b in own_bits:
                if b in fixed:
                    value = (me_ref[0] >> b) & 1
                    value = value if fixed[b] else 1 - value
                else:
                    value = (g >> (len(left) - 1 - left.index(b))) & 1
                at = at * 2 + value
            return (0, at, 0, 0)

        return index

    for terms, fixed in sides:
        first, bits = terms[0]
        left = [b for b in bits if b not in fixed]
        n, _, rows, cols = first.shape
        in_specs += [pl.BlockSpec((n, 1, rows, cols), place(b, fixed, left)) for _, b in terms]
        out_specs.append(pl.BlockSpec((n, 1, rows, cols), lambda g, _: (0, g, 0, 0)))
        arrays += [a for a, _ in terms]
        outs.append(shape((n, 1 << len(left), rows, cols), BF16))
        lefts.append(left)
    results = pl.pallas_call(
        partial(add_kernel, [len(terms) for terms, _ in sides]),
        grid_spec=pltpu.PrefetchScalarGridSpec(
            num_scalar_prefetch=1, grid=(1 << len(lefts[0]),), in_specs=in_specs, out_specs=out_specs
        ),
        out_shape=outs,
        name="add",
        cost_estimate=pl.CostEstimate(flops=0, bytes_accessed=0, transcendentals=0),
        compiler_params=pltpu.CompilerParams(vmem_limit_bytes=24 * MIB),
    )(me, *arrays)
    return results, lefts


def flip(array, axis, mask):
    size = lax.axis_size(axis)
    return lax.ppermute(array, axis, [(i, i ^ mask) for i in range(size)])


def tie(*arrays):
    return lax.optimization_barrier(arrays)


def pick(array, axis, index):
    return lax.dynamic_index_in_dim(array, index, axis, keepdims=False)


def outer_bits():
    bits = list(range(1, lax.axis_size("dp").bit_length() - 1))
    return bits, (bits, bits[::-1])


def share_of():
    me = lax.axis_index("dp")
    return (me & 1) * (lax.axis_size("dp") // 2) + (me >> 1)


class Gather:
    def __init__(self, pair):
        self.bits, self.orders = outer_bits()
        self.steps = len(self.bits)
        self.n, _, self.cols = pair[0].shape
        self.held = [
            a.reshape((self.n,) + (1,) * self.steps + a.shape[1:]) for a in pair
        ]

    def send(self, step):
        return [flip(h, "dp", 1 << order[step]) for h, order in zip(self.held, self.orders)]

    def merge(self, step, mine, theirs):
        me = lax.axis_index("dp")
        merged = []
        for one, two, order in zip(mine, theirs, self.orders):
            bit = order[step]
            low = ((me >> bit) & 1) == 0
            parts = [jnp.where(low, one, two), jnp.where(low, two, one)]
            merged.append(jnp.concatenate(parts, axis=1 + self.steps - bit))
        return merged

    def take(self, step, got):
        self.held = self.merge(step, self.held, got)

    def halves(self):
        return self.flat(self.held)

    def flat(self, arrays):
        return [a.reshape(self.n, -1, self.cols) for a in arrays]


class Reduce:
    def __init__(self, keeps, gots):
        self.bits, self.orders = outer_bits()
        self.steps = len(self.bits)
        self.me = lax.axis_index("dp").astype(jnp.int32).reshape(1)
        high_first = self.bits[::-1]
        n, rows, cols = keeps[0].shape
        form = (n, 1 << self.steps, rows >> self.steps, cols)
        self.terms = [
            [(k.reshape(form), high_first), (g.reshape(form), high_first)]
            for k, g in zip(keeps, gots)
        ]
        self.left = [None, None]

    def pack(self, step):
        sides = []
        for terms, order in zip(self.terms, self.orders):
            fixed = {b: True for b in order[:step]}
            fixed[order[step]] = False
            sides.append((terms, fixed))
        sends, self.left = add_terms(sides, self.me)
        return sends

    def send(self, step, packs):
        return [flip(p, "dp", 1 << order[step]) for p, order in zip(packs, self.orders)]

    def take(self, got):
        for side in range(2):
            self.terms[side].append((got[side], self.left[side]))

    def finish(self):
        fixed = {b: True for b in self.bits}
        sums, _ = add_terms([(t, fixed) for t in self.terms], self.me)
        return [a[:, 0] for a in sums]


def gather_stack(piece):
    bits, _ = outer_bits()
    order = list(range(1 << len(bits)))
    if len(order) <= 4:
        return [piece] + [flip(piece, "dp", 2 * k) for k in order[1:]], order
    held = piece[None]
    for bit in bits:
        held = jnp.concatenate([held, flip(held, "dp", 1 << bit)])
    return [held[k] for k in order], order


def add_parts(*parts):
    total = parts[0].astype(F32)
    for part in parts[1:]:
        total = total + part.astype(F32)
    return total.astype(BF16)


def shards(
    tokens,
    word_len,
    region_count,
    w_qkv,
    qv_bias,
    w_out,
    out_bias,
    norm1_gain,
    norm1_bias,
    w_in,
    in_bias,
    w_down,
    down_bias,
    norm2_gain,
    norm2_bias,
    cotangent,
):
    mp = lax.axis_size("mp")
    dp = lax.axis_size("dp")
    mi = lax.axis_index("mp")
    width = tokens.shape[2]
    rows_local = tokens.shape[1]
    slots = rows_local * mp
    pairs = tokens.shape[0] // mp
    rows = pairs * slots
    cols = w_qkv.shape[2]
    units = w_in.shape[1]
    half_units = units // 2
    order = jnp.arange(mp) ^ mi
    here = jnp.stack([lax.axis_index("dp") & 1, mi, lax.axis_index("dp") >> 1]).astype(jnp.int32)
    share = share_of()

    turned = w_qkv.transpose(0, 2, 1).reshape(3 * cols, width)
    own_qk = turned[: 2 * cols]
    own_vo = jnp.concatenate([turned[2 * cols :], w_out], axis=0)
    att_part, ffn_part = 2 * cols // dp, units // dp
    first = share * att_part
    rows_of = lambda array, start, size: lax.dynamic_slice_in_dim(array, start, size, 0)
    vo_piece = jnp.where(
        first < cols,
        rows_of(turned, 2 * cols + jnp.minimum(first, cols - att_part), att_part),
        rows_of(w_out, jnp.maximum(first - cols, 0), att_part),
    )

    def row_blocks(array):
        blocks = array.reshape((mp, pairs) + array.shape[1:])
        return [pick(blocks, 0, mi ^ k) for k in range(mp)]

    def join(blocks):
        return jnp.concatenate(blocks, axis=1).reshape(rows, width)

    fill = lambda v: jnp.pad(v, ((0, 0), (0, width - v.shape[1])))
    small = jnp.concatenate([fill(qv_bias), in_bias.reshape(1, units), jnp.zeros((5, width), BF16)])
    att_send = jnp.concatenate([rows_of(turned, first, att_part), vo_piece], axis=0)
    ffn_send = jnp.concatenate(
        [rows_of(w_in.T, share * ffn_part, ffn_part), rows_of(w_down, share * ffn_part, ffn_part), small],
        axis=0,
    )
    tok = row_blocks(tokens)
    cot = row_blocks(cotangent)
    vectors = jnp.stack(
        [out_bias, norm1_gain, norm1_bias, down_bias, norm2_gain, norm2_bias, out_bias, out_bias]
    ).astype(F32)
    words = lax.dynamic_slice_in_dim(word_len, mi * pairs, pairs, 0)
    regions = lax.dynamic_slice_in_dim(region_count, mi * pairs, pairs, 0)
    slot_index = (order[:, None] * rows_local + jnp.arange(rows_local)[None, :]).reshape(-1)
    key_valid = jnp.where(
        slot_index[None, :] < WORDS,
        slot_index[None, :] < words[:, None],
        slot_index[None, :] - WORDS < regions[:, None],
    ).astype(F32)[:, None, :]

    att_got = {k: flip(att_send, "mp", k) for k in (3, 2, 1)}
    att_got = [att_got[k] for k in (1, 2, 3)]
    att_got, ffn_send, tok, vectors, key_valid, here, own_qk, own_vo = tie(
        att_got, ffn_send, tok, vectors, key_valid, here, own_qk, own_vo
    )
    att = Gather(
        [
            jnp.stack([g[:att_part] for g in att_got]),
            jnp.stack([g[att_part:] for g in att_got]),
        ]
    )
    ffn_two = flip(ffn_send, "mp", 2)
    got = att.send(0)
    tok_one = flip(tok[1], "mp", 1)
    ffn_two, got, tok_one, ffn_send, tok = tie(ffn_two, got, tok_one, ffn_send, tok)
    for step in range(1, att.steps):
        att.take(step - 1, got)
        got = att.send(step)
        if step == 1:
            ffn_odd = flip(jnp.stack([ffn_send, ffn_two]), "mp", 1)
            tok_three = flip(tok[3], "mp", 3)
        got, ffn_odd, tok_three, tok = tie(got, ffn_odd, tok_three, tok)
    att.take(att.steps - 1, got)
    ffn_got = [ffn_odd[0], ffn_two, ffn_odd[1]]
    ffn = Gather(
        [
            jnp.stack([g[:ffn_part] for g in ffn_got]),
            jnp.stack([g[ffn_part : 2 * ffn_part] for g in ffn_got]),
        ]
    )
    got = ffn.send(0)
    qk_one, vo_one = att.halves()
    qk_two, vo_two = flip(qk_one, "dp", 1), flip(vo_one, "dp", 1)
    tok_two = flip(tok[2], "mp", 2)
    smalls = jnp.stack([small] + [g[2 * ffn_part :] for g in ffn_got]).astype(F32)
    got, qk_two, vo_two, tok_two, cot, smalls = tie(got, qk_two, vo_two, tok_two, cot, smalls)
    heads_low = shape((mp, rows, cols), BF16)
    low_shape = shape((rows, width), BF16)
    rows_shape = shape((rows, width), F32)
    sums_shape = shape((8, width), F32)
    block_shape = shape((pairs, rows_local, width), BF16)
    for step in range(1, ffn.steps):
        ffn.take(step - 1, got)
        got = ffn.send(step)
        if step < ffn.steps - 1:
            got = tie(*got)
    early = [flip(h, "dp", 1) for h in ffn.held]
    early, cot, x = tie(early, cot, join([tok[0], tok_one, tok_two, tok_three]))
    cot_blocks = [cot[0]] + [flip(cot[k], "mp", k) for k in range(1, mp)]
    later = lambda a: pl.BlockSpec((1,) + a.shape[1:], lambda s, h: (jnp.clip(s - 1, 0, mp - 2), 0, 0))
    head_args = [
        (whole, own_qk),
        (later, qk_one),
        (later, qk_two),
        (whole, own_vo),
        (later, vo_one),
        (later, vo_two),
    ]
    q, k, v, weights, context, hidden_low, normed_one, scale_one = call(
        partial(attention_kernel, pairs),
        mp,
        "attention",
        32,
        [
            (whole, x),
            *head_args,
            (per_step, smalls),
            (whole, key_valid),
            (whole, vectors),
        ],
        [
            (per_step, heads_low),
            (per_step, heads_low),
            (per_step, heads_low),
            (per_step, shape((mp, pairs, cols // HEAD * slots, slots), F32)),
            (per_step, heads_low),
            (whole, low_shape),
            (whole, rows_shape),
            (whole, shape((rows, 1), F32)),
        ],
        [pltpu.VMEM((rows, width), F32)],
        here,
        range(5),
    )
    got, early, hidden_low, cot_blocks = tie(got, early, hidden_low, cot_blocks)
    ffn.take(ffn.steps - 1, got)
    in_one, down_one = ffn.halves()
    late = [flip(g, "dp", 1) for g in got]
    late, hidden_low = tie(late, hidden_low)
    in_two, down_two = ffn.flat(ffn.merge(ffn.steps - 1, early, late))

    half = shape((mp, half_units, width), BF16)
    pre_shape = shape((mp, rows, units), BF16)
    vmem = lambda a: pltpu.VMEM(a.shape, a.dtype)
    results = call(
        partial(ffn_kernel, mp),
        1,
        "ffn",
        44,
        [
            (where_it_is, hidden_low),
            (where_it_is, normed_one),
            (where_it_is, w_in),
            (in_vmem, in_one),
            (in_vmem, in_two),
            (where_it_is, w_down),
            (in_vmem, down_one),
            (in_vmem, down_two),
            (whole, smalls),
            (whole, vectors),
            *[(where_it_is, c) for c in cot_blocks],
        ],
        [
            *[(whole, block_shape)] * mp,
            (where_it_is, rows_shape),
            (where_it_is, pre_shape),
            (where_it_is, half),
            (where_it_is, half),
            (where_it_is, half),
            (where_it_is, half),
            (whole, shape((mp, 1, units), F32)),
            (whole, sums_shape),
        ],
        [
            vmem(low_shape),
            vmem(rows_shape),
            pltpu.VMEM((width, units), BF16),
            pltpu.VMEM((units, width), BF16),
            pltpu.VMEM((mp,) + block_shape.shape, BF16),
            vmem(pre_shape),
            pltpu.VMEM(pre_shape.shape, F32),
            vmem(rows_shape),
            vmem(rows_shape),
            vmem(pre_shape),
            vmem(half),
            vmem(half),
            vmem(half),
            vmem(half),
            pltpu.SemaphoreType.DMA((3 + 1 + mp + 1 + 5 * mp,)),
        ],
        here,
        range(mp + 6),
    )
    out_blocks = results[:mp]
    delta_ffn, pre_grad, in_keep, in_send, down_keep, down_send, sum_in, sums_two = results[mp:]
    in_got, down_got = flip(in_send, "dp", 1), flip(down_send, "dp", 1)
    delta_attn, attn_low, sums_one = call(
        partial(ffn_back_kernel, mp),
        1,
        "ffn_back",
        28,
        [
            (where_it_is, pre_grad),
            (where_it_is, w_in),
            (in_vmem, in_one),
            (in_vmem, in_two),
            (where_it_is, delta_ffn),
            (where_it_is, normed_one),
            (whole, scale_one),
            (whole, vectors),
        ],
        [(where_it_is, rows_shape), (whole, low_shape), (whole, sums_shape)],
        [
            vmem(pre_shape),
            pltpu.VMEM((width, units), BF16),
            vmem(rows_shape),
            vmem(rows_shape),
            vmem(rows_shape),
            pltpu.SemaphoreType.DMA((mp + 1 + 2 + 1,)),
        ],
        here,
        (0,),
    )
    in_got, down_got, out_blocks, attn_low = tie(in_got, down_got, out_blocks, attn_low)
    ffn = Reduce([in_keep, down_keep], [in_got, down_got])
    packs = ffn.pack(0)
    packs, attn_low, out_blocks = tie(packs, attn_low, out_blocks)
    got = ffn.send(0, packs)
    out_got = [out_blocks[0]] + [flip(out_blocks[k], "mp", k) for k in range(1, mp)]
    small_half = shape((mp, cols, width), BF16)
    results = call(
        partial(attention_back_kernel, pairs),
        mp,
        "attention_back",
        40,
        [
            (whole, x),
            (whole, attn_low),
            (whole, delta_attn),
            *head_args,
            (per_step, q),
            (per_step, k),
            (per_step, v),
            (per_step, weights),
            (per_step, context),
            (whole, sums_one),
            (whole, sums_two),
            (whole, sum_in),
        ],
        [
            (per_step, small_half),
            (per_step, small_half),
            (
                pl.BlockSpec((2, 1, cols, width), lambda s, h: (0, s, 0, 0)),
                shape((2, mp, cols, width), BF16),
            ),
            (whole, shape((-(-(6 + 2 * mp) // 8) * 8, width), F32)),
            *[(whole, block_shape)] * mp,
        ],
        [pltpu.VMEM((rows, cols), BF16)] * 3 + [pltpu.VMEM((rows, width), F32)],
        here,
        (0, 1, 2) + tuple(range(4, 4 + mp)),
    )
    qk_keep, vo_keep, att_send, sums = results[:4]
    row_sends = results[4:]
    got, out_got, att_send, row_sends, sums = tie(got, out_got, att_send, row_sends, sums)
    for step in range(1, ffn.steps):
        ffn.take(got)
        packs = ffn.pack(step)
        got = ffn.send(step, packs)
        if step == 1:
            att_got = flip(att_send, "dp", 1)
            row_three = flip(row_sends[3], "mp", 3)
            sums_got = flip(sums, "mp", 2)
        got, att_got, row_three, sums_got, row_sends = tie(got, att_got, row_three, sums_got, row_sends)
    sums = sums + sums_got
    place = lambda blocks, dtype: call(
        partial(place_kernel, pairs),
        1,
        "place",
        16,
        [(whole, b) for b in blocks],
        [(whole, shape((mp * pairs, rows_local, width), dtype))],
        [],
        here,
    )[0]
    layer_out = place(out_got, BF16)
    ffn.take(got)
    ffn_parts = ffn.finish()
    ffn_odd = jnp.concatenate([p[1::2] for p in ffn_parts], axis=1)
    ffn_even = jnp.concatenate([p[0::2] for p in ffn_parts], axis=1)
    att = Reduce([qk_keep, vo_keep], [att_got[0], att_got[1]])
    ffn_odd, ffn_even, sums = tie(ffn_odd, ffn_even, sums)
    got = att.send(0, att.pack(0))
    ffn_got = flip(ffn_odd, "mp", 1)
    sums_got = flip(sums, "dp", 2)
    row_two = flip(row_sends[2], "mp", 2)
    got, ffn_got, sums_got, row_two, row_sends, layer_out = tie(
        got, ffn_got, sums_got, row_two, row_sends, layer_out
    )
    sums = sums + sums_got
    for mask in [1 << b for b in range(2, dp.bit_length() - 2)]:
        sums = sums + flip(sums, "dp", mask)
    ffn_two = add_parts(ffn_even[1], ffn_got[1])
    for step in range(1, att.steps):
        att.take(got)
        packs = att.pack(step)
        got = att.send(step, packs)
        if step == 1:
            ffn_last = flip(ffn_two, "mp", 2)
            row_one = flip(row_sends[1], "mp", 1)
            sums_got = flip(sums, "dp", dp // 2)
        got, ffn_last, row_one, sums_got, row_sends = tie(got, ffn_last, row_one, sums_got, row_sends)
    att.take(got)
    sums = sums + sums_got
    att_parts = att.finish()
    att_odd = jnp.concatenate([p[1::2] for p in att_parts], axis=1)
    att_even = jnp.concatenate([p[0::2] for p in att_parts], axis=1)
    ffn_sum = add_parts(ffn_even[0], ffn_got[0], ffn_last)
    ffn = Gather([ffn_sum[None, :ffn_part], ffn_sum[None, ffn_part:]])
    ffn.held, att_odd, att_even, sums = tie(ffn.held, att_odd, att_even, sums)
    got = ffn.send(0)
    att_got = flip(att_odd, "mp", 1)
    sums_got = flip(sums, "dp", 1)
    got, att_got, sums_got, row_one = tie(got, att_got, sums_got, row_one)
    grad_input = place([row_sends[0], row_one, row_two, row_three], F32)
    sums = sums + sums_got
    att_two = add_parts(att_even[1], att_got[1])
    for step in range(1, ffn.steps):
        ffn.take(step - 1, got)
        got = ffn.send(step)
        if step == 1:
            att_last = flip(att_two, "mp", 2)
            sums_got = flip(sums, "mp", 1)
        got, att_last, sums_got, grad_input = tie(got, att_last, sums_got, grad_input)
    ffn.take(ffn.steps - 1, got)
    sums = sums + sums_got
    att_sum = add_parts(att_even[0], att_got[0], att_last)
    ffn_halves = ffn.halves()
    core_got = [flip(h, "dp", 1) for h in ffn_halves]
    att_mine, att_order = gather_stack(att_sum)
    grad_in, grad_down = call(
        unit_grads_kernel,
        1,
        "unit_grads",
        24,
        [(whole, a) for a in ffn_halves + core_got],
        [(whole, shape((width, units), F32)), (whole, shape((units, width), F32))],
        [],
        here,
    )
    att_mine, grad_in, grad_down, sums = tie(att_mine, grad_in, grad_down, sums)
    att_mine = jnp.stack(att_mine)
    att_other = flip(att_mine, "dp", 1)
    grad_qkv, grad_out = call(
        partial(head_grads_kernel, att_order),
        1,
        "head_grads",
        24,
        [(whole, att_mine), (whole, att_other)],
        [
            (whole, shape((3, cols // att_part, att_part, width), F32)),
            (whole, shape((cols // att_part, att_part, width), F32)),
        ],
        [],
        here,
    )
    sum_in_bias = lax.dynamic_index_in_dim(sums, 6 + mi, 0, keepdims=False)
    sum_qv = lax.dynamic_index_in_dim(sums, 6 + mp + mi, 0, keepdims=False)
    sum_qv = jnp.stack([sum_qv[:cols], sum_qv[2 * cols : 3 * cols]])
    return (
        layer_out,
        grad_input,
        grad_qkv.reshape(3, cols, width).transpose(0, 2, 1),
        sum_qv,
        grad_out.reshape(cols, width),
        sums[0],
        sums[1],
        sums[2],
        grad_in,
        sum_in_bias,
        grad_down,
        sums[5],
        sums[3],
        sums[4],
    )


def solution(mesh):
    in_specs = (
        P("dp", "mp", None),
        P("dp"),
        P("dp"),
        P(None, None, "mp"),
        P(None, "mp"),
        P("mp", None),
        P(),
        P(),
        P(),
        P(None, "mp"),
        P("mp"),
        P("mp", None),
        P(),
        P(),
        P(),
        P("dp", "mp", None),
    )
    out_specs = (
        P("dp", "mp", None),
        P("dp", "mp", None),
        P(None, None, "mp"),
        P(None, "mp"),
        P("mp", None),
        P(),
        P(),
        P(),
        P(None, "mp"),
        P("mp"),
        P("mp", None),
        P(),
        P(),
        P(),
    )
    return jax.shard_map(shards, mesh=mesh, in_specs=in_specs, out_specs=out_specs, check_vma=False)
```

```python
from functools import partial

import jax
import jax.numpy as jnp
from jax import lax
from jax.experimental import pallas as pl
from jax.experimental.pallas import tpu as pltpu
from jax.sharding import PartitionSpec as P

HEAD = 64
WORDS = 60
EPSILON = 1e-05
SQRT_HALF = 0.7071067811865476
DENSITY = 0.3989422804014327
F32 = jnp.float32
BF16 = jnp.bfloat16
MIB = 1024 * 1024


def dot(one, two, one_axis, two_axis):
    return lax.dot_general(
        one, two, (((one_axis,), (two_axis,)), ((), ())), preferred_element_type=F32
    )


def normalize(total, gain, shift):
    centered = total - jnp.mean(total, axis=-1, keepdims=True)
    inv_scale = lax.rsqrt(jnp.mean(centered * centered, axis=-1, keepdims=True) + EPSILON)
    normed = centered * inv_scale
    return normed * gain + shift, normed, inv_scale


def normalize_back(upstream, normed, inv_scale, gain):
    scaled_up = upstream * gain
    mean_one = jnp.mean(scaled_up, axis=-1, keepdims=True)
    mean_two = jnp.mean(scaled_up * normed, axis=-1, keepdims=True)
    return inv_scale * (scaled_up - mean_one - normed * mean_two)


def column_sum(array):
    return jnp.sum(array, axis=0, keepdims=True)


def head_stack(array, heads):
    head = lax.broadcasted_iota(jnp.int32, array.shape, 1) // HEAD
    zero = jnp.zeros_like(array)
    return jnp.concatenate([jnp.where(head == h, array, zero) for h in range(heads)], axis=0)


def head_pick(stacked, heads):
    rows = stacked.shape[0] // heads
    head = lax.broadcasted_iota(jnp.int32, (rows, stacked.shape[1]), 1) // HEAD
    total = stacked[:rows]
    for h in range(1, heads):
        total = jnp.where(head == h, stacked[h * rows : (h + 1) * rows], total)
    return total


def head_weights(first, here_ref, own_ref, one_ref, two_ref):
    low = here_ref[0] == 0
    half = one_ref.shape[1]
    one, two = one_ref[0], two_ref[0]
    return (
        jnp.where(first, own_ref[:half], jnp.where(low, one, two)),
        jnp.where(first, own_ref[half:], jnp.where(low, two, one)),
    )


def attention_kernel(
    pairs, here_ref, x_ref, own_qk, qk_one, qk_two, own_vo, vo_one, vo_two, small_ref, valid_ref, vectors_ref,
    q_ref, k_ref, v_ref, weights_ref, context_ref, low_ref, normed_ref, scale_ref, total_ref,
):
    step = pl.program_id(0)
    cols = q_ref.shape[2]
    heads = cols // HEAD
    slots = x_ref.shape[0] // pairs
    x = x_ref[...]
    w_q, w_k = head_weights(step == 0, here_ref, own_qk, qk_one, qk_two)
    w_v, w_o = head_weights(step == 0, here_ref, own_vo, vo_one, vo_two)
    q_ref[0] = (dot(x, w_q, 1, 1) + small_ref[0, 0:1, :cols]).astype(BF16)
    k_ref[0] = dot(x, w_k, 1, 1).astype(BF16)
    v_ref[0] = (dot(x, w_v, 1, 1) + small_ref[0, 1:2, :cols]).astype(BF16)
    for p in range(pairs):
        rows = slice(p * slots, (p + 1) * slots)
        scores = dot(head_stack(q_ref[0, rows], heads), k_ref[0, rows], 1, 1) * HEAD ** (-0.5)
        scores = jnp.where(valid_ref[p] > 0.5, scores, -1e30)
        exp_scores = jnp.exp(scores - jnp.max(scores, axis=-1, keepdims=True))
        weights = exp_scores / jnp.sum(exp_scores, axis=-1, keepdims=True)
        weights_ref[0, p] = weights
        mixed = dot(weights.astype(BF16), v_ref[0, rows], 1, 0)
        context_ref[0, rows] = head_pick(mixed, heads).astype(BF16)
    branch = dot(context_ref[0], w_o, 1, 0)

    @pl.when(step == 0)
    def _():
        total_ref[...] = branch

    @pl.when(step > 0)
    def _():
        total_ref[...] += branch

    @pl.when(step == pl.num_programs(0) - 1)
    def _():
        first_sum = total_ref[...] + vectors_ref[0:1] + x.astype(F32)
        hidden, normed, scale = normalize(first_sum, vectors_ref[1:2], vectors_ref[2:3])
        low_ref[...] = hidden.astype(BF16)
        normed_ref[...] = normed
        scale_ref[...] = scale


def blocks_of(units):
    size = min(256, units)
    return [(start, min(start + size, units)) for start in range(0, units, size)]


class Copies:
    def __init__(self, sems):
        self.sems, self.used = sems, 0

    def start(self, *pairs):
        copies = []
        for source, target in pairs:
            copies.append(pltpu.make_async_copy(source, target, self.sems.at[self.used]))
            copies[-1].start()
            self.used += 1
        return copies


def wait_all(copies):
    for copy in copies:
        copy.wait()


def halves_of(half, start, stop):
    parts = []
    if start < half:
        parts.append((0, start, min(stop, half)))
    if stop > half:
        parts.append((1, max(start - half, 0), stop - half))
    return parts


def own_units(core, half, which, first, last):
    side = core if which == 0 else 1 - core
    return pl.ds(pl.multiple_of(side * half + first, 128), last - first)


def join_rows(refs):
    pairs = refs[0].shape[0]
    return jnp.concatenate([ref[p].astype(F32) for p in range(pairs) for ref in refs], axis=0)


def leave_rows(array, refs):
    pairs, rows = refs[0].shape[:2]
    for p in range(pairs):
        for j, ref in enumerate(refs):
            start = (p * len(refs) + j) * rows
            ref[p] = array[start : start + rows].astype(BF16)


def ffn_kernel(
    count, here_ref, low_hbm, normed_hbm, w_in_hbm, in_one, in_two, w_down_hbm, down_one, down_two, small_ref,
    vectors_ref, *refs,
):
    cot_hbm, out_refs = refs[:count], refs[count : 2 * count]
    (
        delta_hbm, pre_grad_hbm, in_keep_hbm, in_send_hbm, down_keep_hbm, down_send_hbm, sum_in_ref, sums_ref,
        low_ref, normed_ref, w_in_ref, w_down_ref, cot_ref, act_ref, slope_ref, total_ref, delta_ref, pre_grad_ref,
        in_keep_ref, in_send_ref, down_keep_ref, down_send_ref, ffn_low_ref, sems,
    ) = refs[2 * count :]
    core = here_ref[0]
    half = in_one.shape[1]
    copies_ = Copies(sems)
    start, wait = copies_.start, wait_all

    halves = partial(halves_of, half)
    own = partial(own_units, core, half)

    def down_rows(slot, first, start_, stop):
        if first:
            parts = [w_down_ref[own(w, a, b)] for w, a, b in halves(start_, stop)]
        else:
            parts = [(down_one, down_two)[w][slot - 1, a:b] for w, a, b in halves(start_, stop)]
        return jnp.concatenate(parts, axis=0)

    def forward(slot, mine):
        low = low_ref[...]
        branch = None
        for first, last in blocks_of(2 * half):
            parts = halves(first, last)
            if mine:
                w_in = jnp.concatenate([w_in_ref[:, own(*p)] for p in parts], axis=1)
                pre_act = dot(low, w_in, 1, 0)
            else:
                w_in = jnp.concatenate([(in_one, in_two)[w][slot - 1, a:b] for w, a, b in parts], axis=0)
                pre_act = dot(low, w_in, 1, 1)
            bias = jnp.concatenate([small_ref[slot, 2:3, own(*p)] for p in parts], axis=1)
            pre_act = pre_act + bias
            share = 0.5 * (1.0 + lax.erf(pre_act * SQRT_HALF))
            act = (pre_act * share).astype(BF16)
            act_ref[slot, :, first:last] = act
            slope_ref[slot, :, first:last] = share + pre_act * (DENSITY * jnp.exp(-0.5 * pre_act * pre_act))
            term = dot(act, down_rows(slot, mine, first, last), 1, 0)
            branch = term if branch is None else branch + term
        total_ref[...] += branch

    low_copies = start((low_hbm, low_ref))
    own_copies = start((w_in_hbm, w_in_ref), (w_down_hbm, w_down_ref))
    later_copies = start((normed_hbm, normed_ref), *[(cot_hbm[k], cot_ref.at[k]) for k in range(count)])
    total_ref[...] = jnp.zeros_like(total_ref)
    wait(low_copies)
    for slot in range(1, count):
        forward(slot, False)
    wait(own_copies)
    forward(0, True)
    wait(later_copies)

    hidden = normed_ref[...] * vectors_ref[1:2] + vectors_ref[2:3]
    second = total_ref[...] + vectors_ref[3:4] + hidden
    gain = vectors_ref[4:5]
    output, normed, scale = normalize(second, gain, vectors_ref[5:6])
    leave_rows(output, out_refs)
    upstream = join_rows([cot_ref.at[k] for k in range(count)])
    delta = normalize_back(upstream, normed, scale, gain)
    delta_ref[...] = delta
    leaving = start((delta_ref, delta_hbm))
    sums_ref[...] = jnp.zeros_like(sums_ref)
    sums_ref[0:1] = column_sum(upstream * normed)
    sums_ref[1:2] = column_sum(upstream)
    sums_ref[2:3] = column_sum(delta)
    ffn_low_ref[...] = delta.astype(BF16)
    leavers = (
        (pre_grad_ref, pre_grad_hbm),
        (down_send_ref, down_send_hbm),
        (down_keep_ref, down_keep_hbm),
        (in_send_ref, in_send_hbm),
        (in_keep_ref, in_keep_hbm),
    )
    base = copies_.used

    def leave(slot, i):
        source, target = leavers[i]
        return pltpu.make_async_copy(source.at[slot], target.at[slot], sems.at[base + len(leavers) * slot + i])

    def backward(slot, mine):
        ffn_low, low = ffn_low_ref[...], low_ref[...]
        for first, last in blocks_of(2 * half):
            act_grad = dot(ffn_low, down_rows(slot, mine, first, last), 1, 1)
            pre_grad_ref[slot, :, first:last] = (act_grad * slope_ref[slot, :, first:last]).astype(BF16)
        leave(slot, 0).start()
        down_send_ref[slot] = dot(act_ref[slot, :, half:], ffn_low, 0, 0).astype(BF16)
        leave(slot, 1).start()
        down_keep_ref[slot] = dot(act_ref[slot, :, :half], ffn_low, 0, 0).astype(BF16)
        leave(slot, 2).start()
        one, two = pre_grad_ref[slot, :, :half], pre_grad_ref[slot, :, half:]
        in_send_ref[slot] = dot(two, low, 0, 0).astype(BF16)
        leave(slot, 3).start()
        in_keep_ref[slot] = dot(one, low, 0, 0).astype(BF16)
        leave(slot, 4).start()
        natural = slot ^ here_ref[1]
        sum_in_ref[natural, :, own(0, 0, half)] = column_sum(one.astype(F32))
        sum_in_ref[natural, :, own(1, 0, half)] = column_sum(two.astype(F32))

    backward(0, True)
    lax.fori_loop(1, count, lambda slot, _: (backward(slot, False), 0)[1], 0)
    wait(leaving)
    for slot in range(count):
        for i in range(len(leavers)):
            leave(slot, i).wait()


def ffn_back_kernel(
    count, here_ref, pre_grad_hbm, w_in_hbm, in_one, in_two, delta_hbm, normed_hbm, scale_ref, vectors_ref,
    delta_attn_hbm, attn_low_ref, sums_ref, pre_grad_ref, w_in_ref, delta_ref, normed_ref, total_ref, sems,
):
    core = here_ref[0]
    half = in_one.shape[1]
    copies = Copies(sems)
    base = copies.used
    copies.used += count

    def load(slot):
        return pltpu.make_async_copy(pre_grad_hbm.at[slot], pre_grad_ref.at[slot], sems.at[base + slot])

    for slot in list(range(1, count)) + [0]:
        load(slot).start()
    w_copies = copies.start((w_in_hbm, w_in_ref))
    norm_copies = copies.start((delta_hbm, delta_ref), (normed_hbm, normed_ref))

    def add(slot, mine):
        load(slot).wait()
        branch = None
        for a, b in blocks_of(2 * half):
            pre_grad = pre_grad_ref[slot, :, a:b]
            parts = halves_of(half, a, b)
            if mine:
                w_in = jnp.concatenate([w_in_ref[:, own_units(core, half, *p)] for p in parts], axis=1)
                term = dot(pre_grad, w_in, 1, 1)
            else:
                w_in = jnp.concatenate([(in_one, in_two)[w][slot - 1, c:d] for w, c, d in parts], axis=0)
                term = dot(pre_grad, w_in, 1, 0)
            branch = term if branch is None else branch + term
        total_ref[...] += branch

    total_ref[...] = jnp.zeros_like(total_ref)
    lax.fori_loop(1, count, lambda slot, _: (add(slot, False), 0)[1], 0)
    wait_all(w_copies)
    add(0, True)
    wait_all(norm_copies)
    hidden_grad = total_ref[...] + delta_ref[...]
    normed = normed_ref[...]
    delta = normalize_back(hidden_grad, normed, scale_ref[...], vectors_ref[1:2])
    total_ref[...] = delta
    leaving = copies.start((total_ref, delta_attn_hbm))
    attn_low_ref[...] = delta.astype(BF16)
    sums_ref[...] = jnp.zeros_like(sums_ref)
    sums_ref[0:1] = column_sum(delta)
    sums_ref[1:2] = column_sum(hidden_grad * normed)
    sums_ref[2:3] = column_sum(hidden_grad)
    wait_all(leaving)


def attention_back_kernel(
    pairs, here_ref, x_ref, attn_low_ref, delta_ref, own_qk, qk_one, qk_two, own_vo, vo_one, vo_two, q_ref, k_ref,
    v_ref, weights_ref, context_ref, sums_one_ref, sums_two_ref, sum_in_ref,
    qk_keep_ref, vo_keep_ref, send_ref, sums_ref, *refs,
):
    step = pl.program_id(0)
    shards_ = pl.num_programs(0)
    out_refs = refs[:shards_]
    dq_ref, dk_ref, dv_ref, total_ref = refs[shards_:]

    @pl.when(step == 0)
    def _():
        total_ref[...] = delta_ref[...]
        sums_ref[...] = jnp.zeros_like(sums_ref)
        sums_ref[0:3] = sums_one_ref[0:3]
        sums_ref[3:6] = sums_two_ref[0:3]
        for j in range(shards_):
            sums_ref[6 + j : 7 + j] = sum_in_ref[j]

    core = here_ref[0]
    cols = q_ref.shape[2]
    heads = cols // HEAD
    slots = x_ref.shape[0] // pairs
    scale = HEAD ** (-0.5)
    x = x_ref[...]
    attn_low = attn_low_ref[...]
    w_q, w_k = head_weights(step == 0, here_ref, own_qk, qk_one, qk_two)
    w_v, w_o = head_weights(step == 0, here_ref, own_vo, vo_one, vo_two)
    context_grad = dot(attn_low, w_o, 1, 1).astype(BF16)
    grad_out = dot(context_ref[0], attn_low, 0, 0).astype(BF16)
    for p in range(pairs):
        rows = slice(p * slots, (p + 1) * slots)
        up = head_stack(context_grad[rows], heads)
        weights = weights_ref[0, p]
        prob_grad = dot(up, v_ref[0, rows], 1, 1)
        inner = jnp.sum(prob_grad * weights, axis=-1, keepdims=True)
        score_grad = (weights * (prob_grad - inner)).astype(BF16)
        dv_ref[rows] = dot(weights.astype(BF16), up, 0, 0).astype(BF16)
        query_grad = head_pick(dot(score_grad, k_ref[0, rows], 1, 0), heads)
        dq_ref[rows] = (query_grad * scale).astype(BF16)
        key_grad = dot(score_grad, head_stack(q_ref[0, rows], heads), 0, 0)
        dk_ref[rows] = (key_grad * scale).astype(BF16)
    dq, dk, dv = dq_ref[...], dk_ref[...], dv_ref[...]
    row = pl.ds(6 + shards_ + (step ^ here_ref[1]), 1)
    sums_ref[row, :cols] = column_sum(dq.astype(F32))
    sums_ref[row, 2 * cols : 3 * cols] = column_sum(dv.astype(F32))
    grad_q = dot(dq, x, 0, 0).astype(BF16)
    grad_k = dot(dk, x, 0, 0).astype(BF16)
    grad_v = dot(dv, x, 0, 0).astype(BF16)

    @pl.when(core == 0)
    def _():
        qk_keep_ref[0], send_ref[0, 0] = grad_q, grad_k
        vo_keep_ref[0], send_ref[1, 0] = grad_v, grad_out

    @pl.when(core != 0)
    def _():
        qk_keep_ref[0], send_ref[0, 0] = grad_k, grad_q
        vo_keep_ref[0], send_ref[1, 0] = grad_out, grad_v

    total_ref[...] += dot(dq, w_q, 1, 0) + dot(dk, w_k, 1, 0) + dot(dv, w_v, 1, 0)

    @pl.when(step == shards_ - 1)
    def _():
        leave_rows(total_ref[...], out_refs)


def place_kernel(pairs, here_ref, *refs):
    out_ref = refs[-1]
    for k, ref in enumerate(refs[:-1]):
        out_ref[pl.ds((here_ref[1] ^ k) * pairs, pairs)] = ref[...].astype(out_ref.dtype)


def head_grads_kernel(order, here_ref, mine_ref, other_ref, grad_qkv_ref, grad_out_ref):
    core = here_ref[0]
    part = grad_out_ref.shape[1]
    for side, ref in ((core, mine_ref), (1 - core, other_ref)):
        for k, index in enumerate(order):
            place = here_ref[2] ^ index
            piece = ref[k].astype(F32)
            grad_qkv_ref[side, place] = piece[:part]

            @pl.when(side == 0)
            def _():
                grad_qkv_ref[2, place] = piece[part:]

            @pl.when(side != 0)
            def _():
                grad_out_ref[place] = piece[part:]


def unit_grads_kernel(here_ref, in_ref, down_ref, in_other, down_other, grad_in_ref, grad_down_ref):
    half = in_ref.shape[1]
    mine = pl.multiple_of(here_ref[0] * half, half)
    other = pl.multiple_of((1 - here_ref[0]) * half, half)
    grad_in_ref[:, pl.ds(mine, half)] = in_ref[0].astype(F32).T
    grad_in_ref[:, pl.ds(other, half)] = in_other[0].astype(F32).T
    grad_down_ref[pl.ds(mine, half)] = down_ref[0].astype(F32)
    grad_down_ref[pl.ds(other, half)] = down_other[0].astype(F32)


def whole(array):
    return pl.BlockSpec(array.shape, lambda *_: (0,) * len(array.shape))


def per_step(array):
    return pl.BlockSpec((1,) + array.shape[1:], lambda s, *_: (s,) + (0,) * (len(array.shape) - 1))


def where_it_is(array):
    return pl.BlockSpec(memory_space=pl.ANY)


def in_vmem(array):
    return pl.BlockSpec(memory_space=pltpu.VMEM)


def call(kernel, steps, name, vmem, inputs, outputs, scratch, scalar, kept=()):
    spec = pltpu.PrefetchScalarGridSpec(
        num_scalar_prefetch=1,
        grid=(steps,),
        in_specs=[make if isinstance(make, pl.BlockSpec) else make(a) for make, a in inputs],
        out_specs=[make if isinstance(make, pl.BlockSpec) else make(a) for make, a in outputs],
        scratch_shapes=scratch,
    )
    return pl.pallas_call(
        kernel,
        grid_spec=spec,
        out_shape=[pltpu.HBM(a.shape, a.dtype) if i in kept else a for i, (_, a) in enumerate(outputs)],
        name=name,
        cost_estimate=pl.CostEstimate(flops=0, bytes_accessed=0, transcendentals=0),
        compiler_params=pltpu.CompilerParams(vmem_limit_bytes=vmem * MIB),
    )(scalar, *[a if make is in_vmem else in_place(a) for make, a in inputs])


def shape(dims, dtype):
    return jax.ShapeDtypeStruct(dims, dtype)


def in_place(array):
    if array.size * array.dtype.itemsize < MIB:
        return array
    return pltpu.with_memory_space_constraint(array, pltpu.HBM)


def add_kernel(counts, *refs):
    refs = refs[1:]
    out_refs = refs[sum(counts) :]
    for count, out_ref in zip(counts, out_refs):
        total = refs[0][...].astype(F32)
        for ref in refs[1:count]:
            total = total + ref[...].astype(F32)
        out_ref[...] = total.astype(BF16)
        refs = refs[count:]


def add_terms(sides, me):
    in_specs, out_specs, arrays, outs, lefts = [], [], [], [], []

    def place(own_bits, fixed, left):
        def index(g, me_ref):
            at = 0
            for b in own_bits:
                if b in fixed:
                    value = (me_ref[0] >> b) & 1
                    value = value if fixed[b] else 1 - value
                else:
                    value = (g >> (len(left) - 1 - left.index(b))) & 1
                at = at * 2 + value
            return (0, at, 0, 0)

        return index

    for terms, fixed in sides:
        first, bits = terms[0]
        left = [b for b in bits if b not in fixed]
        n, _, rows, cols = first.shape
        in_specs += [pl.BlockSpec((n, 1, rows, cols), place(b, fixed, left)) for _, b in terms]
        out_specs.append(pl.BlockSpec((n, 1, rows, cols), lambda g, _: (0, g, 0, 0)))
        arrays += [a for a, _ in terms]
        outs.append(shape((n, 1 << len(left), rows, cols), BF16))
        lefts.append(left)
    results = pl.pallas_call(
        partial(add_kernel, [len(terms) for terms, _ in sides]),
        grid_spec=pltpu.PrefetchScalarGridSpec(
            num_scalar_prefetch=1, grid=(1 << len(lefts[0]),), in_specs=in_specs, out_specs=out_specs
        ),
        out_shape=outs,
        name="add",
        cost_estimate=pl.CostEstimate(flops=0, bytes_accessed=0, transcendentals=0),
        compiler_params=pltpu.CompilerParams(vmem_limit_bytes=24 * MIB),
    )(me, *arrays)
    return results, lefts


def flip(array, axis, mask):
    size = lax.axis_size(axis)
    return lax.ppermute(array, axis, [(i, i ^ mask) for i in range(size)])


def tie(*arrays):
    return lax.optimization_barrier(arrays)


def pick(array, axis, index):
    return lax.dynamic_index_in_dim(array, index, axis, keepdims=False)


def outer_bits():
    bits = list(range(1, lax.axis_size("dp").bit_length() - 1))
    return bits, (bits, bits[::-1])


def share_of():
    me = lax.axis_index("dp")
    return (me & 1) * (lax.axis_size("dp") // 2) + (me >> 1)


class Gather:
    def __init__(self, pair):
        self.bits, self.orders = outer_bits()
        self.steps = len(self.bits)
        self.n, _, self.cols = pair[0].shape
        self.held = [
            a.reshape((self.n,) + (1,) * self.steps + a.shape[1:]) for a in pair
        ]

    def send(self, step):
        return [flip(h, "dp", 1 << order[step]) for h, order in zip(self.held, self.orders)]

    def merge(self, step, mine, theirs):
        me = lax.axis_index("dp")
        merged = []
        for one, two, order in zip(mine, theirs, self.orders):
            bit = order[step]
            low = ((me >> bit) & 1) == 0
            parts = [jnp.where(low, one, two), jnp.where(low, two, one)]
            merged.append(jnp.concatenate(parts, axis=1 + self.steps - bit))
        return merged

    def take(self, step, got):
        self.held = self.merge(step, self.held, got)

    def halves(self):
        return self.flat(self.held)

    def flat(self, arrays):
        return [a.reshape(self.n, -1, self.cols) for a in arrays]


class Reduce:
    def __init__(self, keeps, gots):
        self.bits, self.orders = outer_bits()
        self.steps = len(self.bits)
        self.me = lax.axis_index("dp").astype(jnp.int32).reshape(1)
        high_first = self.bits[::-1]
        n, rows, cols = keeps[0].shape
        form = (n, 1 << self.steps, rows >> self.steps, cols)
        self.terms = [
            [(k.reshape(form), high_first), (g.reshape(form), high_first)]
            for k, g in zip(keeps, gots)
        ]
        self.left = [None, None]

    def pack(self, step):
        sides = []
        for terms, order in zip(self.terms, self.orders):
            fixed = {b: True for b in order[:step]}
            fixed[order[step]] = False
            sides.append((terms, fixed))
        sends, self.left = add_terms(sides, self.me)
        return sends

    def send(self, step, packs):
        return [flip(p, "dp", 1 << order[step]) for p, order in zip(packs, self.orders)]

    def take(self, got):
        for side in range(2):
            self.terms[side].append((got[side], self.left[side]))

    def finish(self):
        fixed = {b: True for b in self.bits}
        sums, _ = add_terms([(t, fixed) for t in self.terms], self.me)
        return [a[:, 0] for a in sums]


def gather_stack(piece):
    bits, _ = outer_bits()
    order = list(range(1 << len(bits)))
    if len(order) <= 4:
        return [piece] + [flip(piece, "dp", 2 * k) for k in order[1:]], order
    held = piece[None]
    for bit in bits:
        held = jnp.concatenate([held, flip(held, "dp", 1 << bit)])
    return [held[k] for k in order], order


def add_parts(*parts):
    total = parts[0].astype(F32)
    for part in parts[1:]:
        total = total + part.astype(F32)
    return total.astype(BF16)


def shards(
    tokens,
    word_len,
    region_count,
    w_qkv,
    qv_bias,
    w_out,
    out_bias,
    norm1_gain,
    norm1_bias,
    w_in,
    in_bias,
    w_down,
    down_bias,
    norm2_gain,
    norm2_bias,
    cotangent,
):
    mp = lax.axis_size("mp")
    dp = lax.axis_size("dp")
    mi = lax.axis_index("mp")
    width = tokens.shape[2]
    rows_local = tokens.shape[1]
    slots = rows_local * mp
    pairs = tokens.shape[0] // mp
    rows = pairs * slots
    cols = w_qkv.shape[2]
    units = w_in.shape[1]
    half_units = units // 2
    order = jnp.arange(mp) ^ mi
    here = jnp.stack([lax.axis_index("dp") & 1, mi, lax.axis_index("dp") >> 1]).astype(jnp.int32)
    share = share_of()

    turned = w_qkv.transpose(0, 2, 1).reshape(3 * cols, width)
    own_qk = turned[: 2 * cols]
    own_vo = jnp.concatenate([turned[2 * cols :], w_out], axis=0)
    att_part, ffn_part = 2 * cols // dp, units // dp
    first = share * att_part
    rows_of = lambda array, start, size: lax.dynamic_slice_in_dim(array, start, size, 0)
    vo_piece = jnp.where(
        first < cols,
        rows_of(turned, 2 * cols + jnp.minimum(first, cols - att_part), att_part),
        rows_of(w_out, jnp.maximum(first - cols, 0), att_part),
    )

    def row_blocks(array):
        blocks = array.reshape((mp, pairs) + array.shape[1:])
        return [pick(blocks, 0, mi ^ k) for k in range(mp)]

    def join(blocks):
        return jnp.concatenate(blocks, axis=1).reshape(rows, width)

    fill = lambda v: jnp.pad(v, ((0, 0), (0, width - v.shape[1])))
    small = jnp.concatenate([fill(qv_bias), in_bias.reshape(1, units), jnp.zeros((5, width), BF16)])
    att_send = jnp.concatenate([rows_of(turned, first, att_part), vo_piece], axis=0)
    ffn_send = jnp.concatenate(
        [rows_of(w_in.T, share * ffn_part, ffn_part), rows_of(w_down, share * ffn_part, ffn_part), small],
        axis=0,
    )
    tok = row_blocks(tokens)
    cot = row_blocks(cotangent)
    vectors = jnp.stack(
        [out_bias, norm1_gain, norm1_bias, down_bias, norm2_gain, norm2_bias, out_bias, out_bias]
    ).astype(F32)
    words = lax.dynamic_slice_in_dim(word_len, mi * pairs, pairs, 0)
    regions = lax.dynamic_slice_in_dim(region_count, mi * pairs, pairs, 0)
    slot_index = (order[:, None] * rows_local + jnp.arange(rows_local)[None, :]).reshape(-1)
    key_valid = jnp.where(
        slot_index[None, :] < WORDS,
        slot_index[None, :] < words[:, None],
        slot_index[None, :] - WORDS < regions[:, None],
    ).astype(F32)[:, None, :]

    att_got = {k: flip(att_send, "mp", k) for k in (3, 2, 1)}
    att_got = [att_got[k] for k in (1, 2, 3)]
    att_got, ffn_send, tok, vectors, key_valid, here, own_qk, own_vo = tie(
        att_got, ffn_send, tok, vectors, key_valid, here, own_qk, own_vo
    )
    att = Gather(
        [
            jnp.stack([g[:att_part] for g in att_got]),
            jnp.stack([g[att_part:] for g in att_got]),
        ]
    )
    ffn_two = flip(ffn_send, "mp", 2)
    got = att.send(0)
    tok_one = flip(tok[1], "mp", 1)
    ffn_two, got, tok_one, ffn_send, tok = tie(ffn_two, got, tok_one, ffn_send, tok)
    for step in range(1, att.steps):
        att.take(step - 1, got)
        got = att.send(step)
        if step == 1:
            ffn_odd = flip(jnp.stack([ffn_send, ffn_two]), "mp", 1)
            tok_three = flip(tok[3], "mp", 3)
        got, ffn_odd, tok_three, tok = tie(got, ffn_odd, tok_three, tok)
    att.take(att.steps - 1, got)
    ffn_got = [ffn_odd[0], ffn_two, ffn_odd[1]]
    ffn = Gather(
        [
            jnp.stack([g[:ffn_part] for g in ffn_got]),
            jnp.stack([g[ffn_part : 2 * ffn_part] for g in ffn_got]),
        ]
    )
    got = ffn.send(0)
    qk_one, vo_one = att.halves()
    qk_two, vo_two = flip(qk_one, "dp", 1), flip(vo_one, "dp", 1)
    tok_two = flip(tok[2], "mp", 2)
    smalls = jnp.stack([small] + [g[2 * ffn_part :] for g in ffn_got]).astype(F32)
    got, qk_two, vo_two, tok_two, cot, smalls = tie(got, qk_two, vo_two, tok_two, cot, smalls)
    heads_low = shape((mp, rows, cols), BF16)
    low_shape = shape((rows, width), BF16)
    rows_shape = shape((rows, width), F32)
    sums_shape = shape((8, width), F32)
    block_shape = shape((pairs, rows_local, width), BF16)
    for step in range(1, ffn.steps):
        ffn.take(step - 1, got)
        got = ffn.send(step)
        if step < ffn.steps - 1:
            got = tie(*got)
    early = [flip(h, "dp", 1) for h in ffn.held]
    early, cot, x = tie(early, cot, join([tok[0], tok_one, tok_two, tok_three]))
    cot_blocks = [cot[0]] + [flip(cot[k], "mp", k) for k in range(1, mp)]
    later = lambda a: pl.BlockSpec((1,) + a.shape[1:], lambda s, h: (jnp.clip(s - 1, 0, mp - 2), 0, 0))
    head_args = [
        (whole, own_qk),
        (later, qk_one),
        (later, qk_two),
        (whole, own_vo),
        (later, vo_one),
        (later, vo_two),
    ]
    q, k, v, weights, context, hidden_low, normed_one, scale_one = call(
        partial(attention_kernel, pairs),
        mp,
        "attention",
        32,
        [
            (whole, x),
            *head_args,
            (per_step, smalls),
            (whole, key_valid),
            (whole, vectors),
        ],
        [
            (per_step, heads_low),
            (per_step, heads_low),
            (per_step, heads_low),
            (per_step, shape((mp, pairs, cols // HEAD * slots, slots), F32)),
            (per_step, heads_low),
            (whole, low_shape),
            (whole, rows_shape),
            (whole, shape((rows, 1), F32)),
        ],
        [pltpu.VMEM((rows, width), F32)],
        here,
        range(5),
    )
    got, early, hidden_low, cot_blocks = tie(got, early, hidden_low, cot_blocks)
    ffn.take(ffn.steps - 1, got)
    in_one, down_one = ffn.halves()
    late = [flip(g, "dp", 1) for g in got]
    late, hidden_low = tie(late, hidden_low)
    in_two, down_two = ffn.flat(ffn.merge(ffn.steps - 1, early, late))

    half = shape((mp, half_units, width), BF16)
    pre_shape = shape((mp, rows, units), BF16)
    vmem = lambda a: pltpu.VMEM(a.shape, a.dtype)
    results = call(
        partial(ffn_kernel, mp),
        1,
        "ffn",
        44,
        [
            (where_it_is, hidden_low),
            (where_it_is, normed_one),
            (where_it_is, w_in),
            (in_vmem, in_one),
            (in_vmem, in_two),
            (where_it_is, w_down),
            (in_vmem, down_one),
            (in_vmem, down_two),
            (whole, smalls),
            (whole, vectors),
            *[(where_it_is, c) for c in cot_blocks],
        ],
        [
            *[(whole, block_shape)] * mp,
            (where_it_is, rows_shape),
            (where_it_is, pre_shape),
            (where_it_is, half),
            (where_it_is, half),
            (where_it_is, half),
            (where_it_is, half),
            (whole, shape((mp, 1, units), F32)),
            (whole, sums_shape),
        ],
        [
            vmem(low_shape),
            vmem(rows_shape),
            pltpu.VMEM((width, units), BF16),
            pltpu.VMEM((units, width), BF16),
            pltpu.VMEM((mp,) + block_shape.shape, BF16),
            vmem(pre_shape),
            pltpu.VMEM(pre_shape.shape, F32),
            vmem(rows_shape),
            vmem(rows_shape),
            vmem(pre_shape),
            vmem(half),
            vmem(half),
            vmem(half),
            vmem(half),
            vmem(low_shape),
            pltpu.SemaphoreType.DMA((3 + 1 + mp + 1 + 5 * mp,)),
        ],
        here,
        range(mp + 6),
    )
    out_blocks = results[:mp]
    delta_ffn, pre_grad, in_keep, in_send, down_keep, down_send, sum_in, sums_two = results[mp:]
    in_got, down_got = flip(in_send, "dp", 1), flip(down_send, "dp", 1)
    delta_attn, attn_low, sums_one = call(
        partial(ffn_back_kernel, mp),
        1,
        "ffn_back",
        28,
        [
            (where_it_is, pre_grad),
            (where_it_is, w_in),
            (in_vmem, in_one),
            (in_vmem, in_two),
            (where_it_is, delta_ffn),
            (where_it_is, normed_one),
            (whole, scale_one),
            (whole, vectors),
        ],
        [(where_it_is, rows_shape), (whole, low_shape), (whole, sums_shape)],
        [
            vmem(pre_shape),
            pltpu.VMEM((width, units), BF16),
            vmem(rows_shape),
            vmem(rows_shape),
            vmem(rows_shape),
            pltpu.SemaphoreType.DMA((mp + 1 + 2 + 1,)),
        ],
        here,
        (0,),
    )
    in_got, down_got, out_blocks, attn_low = tie(in_got, down_got, out_blocks, attn_low)
    ffn = Reduce([in_keep, down_keep], [in_got, down_got])
    packs = ffn.pack(0)
    packs, attn_low, out_blocks = tie(packs, attn_low, out_blocks)
    got = ffn.send(0, packs)
    out_got = [out_blocks[0]] + [flip(out_blocks[k], "mp", k) for k in range(1, mp)]
    small_half = shape((mp, cols, width), BF16)
    results = call(
        partial(attention_back_kernel, pairs),
        mp,
        "attention_back",
        40,
        [
            (whole, x),
            (whole, attn_low),
            (whole, delta_attn),
            *head_args,
            (per_step, q),
            (per_step, k),
            (per_step, v),
            (per_step, weights),
            (per_step, context),
            (whole, sums_one),
            (whole, sums_two),
            (whole, sum_in),
        ],
        [
            (per_step, small_half),
            (per_step, small_half),
            (
                pl.BlockSpec((2, 1, cols, width), lambda s, h: (0, s, 0, 0)),
                shape((2, mp, cols, width), BF16),
            ),
            (whole, shape((-(-(6 + 2 * mp) // 8) * 8, width), F32)),
            *[(whole, block_shape)] * mp,
        ],
        [pltpu.VMEM((rows, cols), BF16)] * 3 + [pltpu.VMEM((rows, width), F32)],
        here,
        (0, 1, 2) + tuple(range(4, 4 + mp)),
    )
    qk_keep, vo_keep, att_send, sums = results[:4]
    row_sends = results[4:]
    got, out_got, att_send, row_sends, sums = tie(got, out_got, att_send, row_sends, sums)
    for step in range(1, ffn.steps):
        ffn.take(got)
        packs = ffn.pack(step)
        got = ffn.send(step, packs)
        if step == 1:
            att_got = flip(att_send, "dp", 1)
            row_three = flip(row_sends[3], "mp", 3)
            sums_got = flip(sums, "mp", 2)
        got, att_got, row_three, sums_got, row_sends = tie(got, att_got, row_three, sums_got, row_sends)
    sums = sums + sums_got
    place = lambda blocks, dtype: call(
        partial(place_kernel, pairs),
        1,
        "place",
        16,
        [(whole, b) for b in blocks],
        [(whole, shape((mp * pairs, rows_local, width), dtype))],
        [],
        here,
    )[0]
    layer_out = place(out_got, BF16)
    ffn.take(got)
    ffn_parts = ffn.finish()
    ffn_odd = jnp.concatenate([p[1::2] for p in ffn_parts], axis=1)
    ffn_even = jnp.concatenate([p[0::2] for p in ffn_parts], axis=1)
    att = Reduce([qk_keep, vo_keep], [att_got[0], att_got[1]])
    ffn_odd, ffn_even, sums = tie(ffn_odd, ffn_even, sums)
    got = att.send(0, att.pack(0))
    ffn_got = flip(ffn_odd, "mp", 1)
    sums_got = flip(sums, "dp", 2)
    row_two = flip(row_sends[2], "mp", 2)
    got, ffn_got, sums_got, row_two, row_sends, layer_out = tie(
        got, ffn_got, sums_got, row_two, row_sends, layer_out
    )
    sums = sums + sums_got
    for mask in [1 << b for b in range(2, dp.bit_length() - 2)]:
        sums = sums + flip(sums, "dp", mask)
    ffn_two = add_parts(ffn_even[1], ffn_got[1])
    for step in range(1, att.steps):
        att.take(got)
        packs = att.pack(step)
        got = att.send(step, packs)
        if step == 1:
            ffn_last = flip(ffn_two, "mp", 2)
            row_one = flip(row_sends[1], "mp", 1)
            sums_got = flip(sums, "dp", dp // 2)
        got, ffn_last, row_one, sums_got, row_sends = tie(got, ffn_last, row_one, sums_got, row_sends)
    att.take(got)
    sums = sums + sums_got
    att_parts = att.finish()
    att_odd = jnp.concatenate([p[1::2] for p in att_parts], axis=1)
    att_even = jnp.concatenate([p[0::2] for p in att_parts], axis=1)
    ffn_sum = add_parts(ffn_even[0], ffn_got[0], ffn_last)
    ffn = Gather([ffn_sum[None, :ffn_part], ffn_sum[None, ffn_part:]])
    ffn.held, att_odd, att_even, sums = tie(ffn.held, att_odd, att_even, sums)
    got = ffn.send(0)
    att_got = flip(att_odd, "mp", 1)
    sums_got = flip(sums, "dp", 1)
    got, att_got, sums_got, row_one = tie(got, att_got, sums_got, row_one)
    grad_input = place([row_sends[0], row_one, row_two, row_three], F32)
    sums = sums + sums_got
    att_two = add_parts(att_even[1], att_got[1])
    for step in range(1, ffn.steps):
        ffn.take(step - 1, got)
        got = ffn.send(step)
        if step == 1:
            att_last = flip(att_two, "mp", 2)
            sums_got = flip(sums, "mp", 1)
        got, att_last, sums_got, grad_input = tie(got, att_last, sums_got, grad_input)
    ffn.take(ffn.steps - 1, got)
    sums = sums + sums_got
    att_sum = add_parts(att_even[0], att_got[0], att_last)
    ffn_halves = ffn.halves()
    core_got = [flip(h, "dp", 1) for h in ffn_halves]
    att_mine, att_order = gather_stack(att_sum)
    grad_in, grad_down = call(
        unit_grads_kernel,
        1,
        "unit_grads",
        24,
        [(whole, a) for a in ffn_halves + core_got],
        [(whole, shape((width, units), F32)), (whole, shape((units, width), F32))],
        [],
        here,
    )
    att_mine, grad_in, grad_down, sums = tie(att_mine, grad_in, grad_down, sums)
    att_mine = jnp.stack(att_mine)
    att_other = flip(att_mine, "dp", 1)
    grad_qkv, grad_out = call(
        partial(head_grads_kernel, att_order),
        1,
        "head_grads",
        24,
        [(whole, att_mine), (whole, att_other)],
        [
            (whole, shape((3, cols // att_part, att_part, width), F32)),
            (whole, shape((cols // att_part, att_part, width), F32)),
        ],
        [],
        here,
    )
    sum_in_bias = lax.dynamic_index_in_dim(sums, 6 + mi, 0, keepdims=False)
    sum_qv = lax.dynamic_index_in_dim(sums, 6 + mp + mi, 0, keepdims=False)
    sum_qv = jnp.stack([sum_qv[:cols], sum_qv[2 * cols : 3 * cols]])
    return (
        layer_out,
        grad_input,
        grad_qkv.reshape(3, cols, width).transpose(0, 2, 1),
        sum_qv,
        grad_out.reshape(cols, width),
        sums[0],
        sums[1],
        sums[2],
        grad_in,
        sum_in_bias,
        grad_down,
        sums[5],
        sums[3],
        sums[4],
    )


def solution(mesh):
    in_specs = (
        P("dp", "mp", None),
        P("dp"),
        P("dp"),
        P(None, None, "mp"),
        P(None, "mp"),
        P("mp", None),
        P(),
        P(),
        P(),
        P(None, "mp"),
        P("mp"),
        P("mp", None),
        P(),
        P(),
        P(),
        P("dp", "mp", None),
    )
    out_specs = (
        P("dp", "mp", None),
        P("dp", "mp", None),
        P(None, None, "mp"),
        P(None, "mp"),
        P("mp", None),
        P(),
        P(),
        P(),
        P(None, "mp"),
        P("mp"),
        P("mp", None),
        P(),
        P(),
        P(),
    )
    return jax.shard_map(shards, mesh=mesh, in_specs=in_specs, out_specs=out_specs, check_vma=False)
```

```python
from functools import partial

import jax
import jax.numpy as jnp
from jax import lax
from jax.experimental import pallas as pl
from jax.experimental.pallas import tpu as pltpu
from jax.sharding import PartitionSpec as P

HEAD = 64
WORDS = 60
EPSILON = 1e-05
SQRT_HALF = 0.7071067811865476
DENSITY = 0.3989422804014327
F32 = jnp.float32
BF16 = jnp.bfloat16
MIB = 1024 * 1024


def dot(one, two, one_axis, two_axis):
    return lax.dot_general(
        one, two, (((one_axis,), (two_axis,)), ((), ())), preferred_element_type=F32
    )


def normalize(total, gain, shift):
    centered = total - jnp.mean(total, axis=-1, keepdims=True)
    inv_scale = lax.rsqrt(jnp.mean(centered * centered, axis=-1, keepdims=True) + EPSILON)
    normed = centered * inv_scale
    return normed * gain + shift, normed, inv_scale


def normalize_back(upstream, normed, inv_scale, gain):
    scaled_up = upstream * gain
    mean_one = jnp.mean(scaled_up, axis=-1, keepdims=True)
    mean_two = jnp.mean(scaled_up * normed, axis=-1, keepdims=True)
    return inv_scale * (scaled_up - mean_one - normed * mean_two)


def column_sum(array):
    return jnp.sum(array, axis=0, keepdims=True)


def head_stack(array, heads):
    head = lax.broadcasted_iota(jnp.int32, array.shape, 1) // HEAD
    zero = jnp.zeros_like(array)
    return jnp.concatenate([jnp.where(head == h, array, zero) for h in range(heads)], axis=0)


def head_pick(stacked, heads):
    rows = stacked.shape[0] // heads
    head = lax.broadcasted_iota(jnp.int32, (rows, stacked.shape[1]), 1) // HEAD
    total = stacked[:rows]
    for h in range(1, heads):
        total = jnp.where(head == h, stacked[h * rows : (h + 1) * rows], total)
    return total


def head_weights(first, here_ref, own_ref, one_ref, two_ref):
    low = here_ref[0] == 0
    half = one_ref.shape[1]
    one, two = one_ref[0], two_ref[0]
    return (
        jnp.where(first, own_ref[:half], jnp.where(low, one, two)),
        jnp.where(first, own_ref[half:], jnp.where(low, two, one)),
    )


def attention_kernel(
    pairs, here_ref, x_ref, own_qk, qk_one, qk_two, own_vo, vo_one, vo_two, small_ref, valid_ref, vectors_ref,
    q_ref, k_ref, v_ref, weights_ref, context_ref, low_ref, normed_ref, scale_ref, total_ref,
):
    step = pl.program_id(0)
    cols = q_ref.shape[2]
    heads = cols // HEAD
    slots = x_ref.shape[0] // pairs
    x = x_ref[...]
    w_q, w_k = head_weights(step == 0, here_ref, own_qk, qk_one, qk_two)
    w_v, w_o = head_weights(step == 0, here_ref, own_vo, vo_one, vo_two)
    q_ref[0] = (dot(x, w_q, 1, 1) + small_ref[0, 0:1, :cols]).astype(BF16)
    k_ref[0] = dot(x, w_k, 1, 1).astype(BF16)
    v_ref[0] = (dot(x, w_v, 1, 1) + small_ref[0, 1:2, :cols]).astype(BF16)
    for p in range(pairs):
        rows = slice(p * slots, (p + 1) * slots)
        scores = dot(head_stack(q_ref[0, rows], heads), k_ref[0, rows], 1, 1) * HEAD ** (-0.5)
        scores = jnp.where(valid_ref[p] > 0.5, scores, -1e30)
        exp_scores = jnp.exp(scores - jnp.max(scores, axis=-1, keepdims=True))
        weights = exp_scores / jnp.sum(exp_scores, axis=-1, keepdims=True)
        weights_ref[0, p] = weights
        mixed = dot(weights.astype(BF16), v_ref[0, rows], 1, 0)
        context_ref[0, rows] = head_pick(mixed, heads).astype(BF16)
    branch = dot(context_ref[0], w_o, 1, 0)

    @pl.when(step == 0)
    def _():
        total_ref[...] = branch

    @pl.when(step > 0)
    def _():
        total_ref[...] += branch

    @pl.when(step == pl.num_programs(0) - 1)
    def _():
        first_sum = total_ref[...] + vectors_ref[0:1] + x.astype(F32)
        hidden, normed, scale = normalize(first_sum, vectors_ref[1:2], vectors_ref[2:3])
        low_ref[...] = hidden.astype(BF16)
        normed_ref[...] = normed
        scale_ref[...] = scale


def blocks_of(units):
    size = min(256, units)
    return [(start, min(start + size, units)) for start in range(0, units, size)]


class Copies:
    def __init__(self, sems):
        self.sems, self.used = sems, 0

    def start(self, *pairs):
        copies = []
        for source, target in pairs:
            copies.append(pltpu.make_async_copy(source, target, self.sems.at[self.used]))
            copies[-1].start()
            self.used += 1
        return copies


def wait_all(copies):
    for copy in copies:
        copy.wait()


def halves_of(half, start, stop):
    parts = []
    if start < half:
        parts.append((0, start, min(stop, half)))
    if stop > half:
        parts.append((1, max(start - half, 0), stop - half))
    return parts


def own_units(core, half, which, first, last):
    side = core if which == 0 else 1 - core
    return pl.ds(pl.multiple_of(side * half + first, 128), last - first)


def join_rows(refs):
    pairs = refs[0].shape[0]
    return jnp.concatenate([ref[p].astype(F32) for p in range(pairs) for ref in refs], axis=0)


def leave_rows(array, refs):
    pairs, rows = refs[0].shape[:2]
    for p in range(pairs):
        for j, ref in enumerate(refs):
            start = (p * len(refs) + j) * rows
            ref[p] = array[start : start + rows].astype(BF16)


def ffn_kernel(
    count, here_ref, low_hbm, normed_hbm, w_in_hbm, in_one, in_two, w_down_hbm, down_one, down_two, small_ref,
    vectors_ref, *refs,
):
    cot_hbm, out_refs = refs[:count], refs[count : 2 * count]
    (
        delta_hbm, pre_grad_hbm, in_keep_hbm, in_send_hbm, down_keep_hbm, down_send_hbm, sum_in_ref, sums_ref,
        low_ref, normed_ref, w_in_ref, w_down_ref, cot_ref, act_ref, slope_ref, total_ref, delta_ref, pre_grad_ref,
        in_keep_ref, in_send_ref, down_keep_ref, down_send_ref, ffn_low_ref, sems,
    ) = refs[2 * count :]
    core = here_ref[0]
    half = in_one.shape[1]
    copies_ = Copies(sems)
    start, wait = copies_.start, wait_all

    halves = partial(halves_of, half)
    own = partial(own_units, core, half)

    def down_rows(slot, first, start_, stop):
        if first:
            parts = [w_down_ref[own(w, a, b)] for w, a, b in halves(start_, stop)]
        else:
            parts = [(down_one, down_two)[w][slot - 1, a:b] for w, a, b in halves(start_, stop)]
        return jnp.concatenate(parts, axis=0)

    def forward(slot, mine):
        low = low_ref[...]
        branch = None
        for first, last in blocks_of(2 * half):
            parts = halves(first, last)
            if mine:
                w_in = jnp.concatenate([w_in_ref[:, own(*p)] for p in parts], axis=1)
                pre_act = dot(low, w_in, 1, 0)
            else:
                w_in = jnp.concatenate([(in_one, in_two)[w][slot - 1, a:b] for w, a, b in parts], axis=0)
                pre_act = dot(low, w_in, 1, 1)
            bias = jnp.concatenate([small_ref[slot, 2:3, own(*p)] for p in parts], axis=1)
            pre_act = pre_act + bias
            share = 0.5 * (1.0 + lax.erf(pre_act * SQRT_HALF))
            act = (pre_act * share).astype(BF16)
            act_ref[slot, :, first:last] = act
            slope_ref[slot, :, first:last] = share + pre_act * (DENSITY * jnp.exp(-0.5 * pre_act * pre_act))
            term = dot(act, down_rows(slot, mine, first, last), 1, 0)
            branch = term if branch is None else branch + term
        total_ref[...] += branch

    low_copies = start((low_hbm, low_ref))
    own_copies = start((w_in_hbm, w_in_ref), (w_down_hbm, w_down_ref))
    later_copies = start((normed_hbm, normed_ref), *[(cot_hbm[k], cot_ref.at[k]) for k in range(count)])
    total_ref[...] = jnp.zeros_like(total_ref)
    wait(low_copies)
    for slot in range(1, count):
        forward(slot, False)
    wait(own_copies)
    forward(0, True)
    wait(later_copies)

    hidden = normed_ref[...] * vectors_ref[1:2] + vectors_ref[2:3]
    second = total_ref[...] + vectors_ref[3:4] + hidden
    gain = vectors_ref[4:5]
    output, normed, scale = normalize(second, gain, vectors_ref[5:6])
    leave_rows(output, out_refs)
    upstream = join_rows([cot_ref.at[k] for k in range(count)])
    delta = normalize_back(upstream, normed, scale, gain)
    delta_ref[...] = delta
    leaving = start((delta_ref, delta_hbm))
    sums_ref[...] = jnp.zeros_like(sums_ref)
    sums_ref[0:1] = column_sum(upstream * normed)
    sums_ref[1:2] = column_sum(upstream)
    sums_ref[2:3] = column_sum(delta)
    ffn_low_ref[...] = delta.astype(BF16)
    leavers = (
        (pre_grad_ref, pre_grad_hbm),
        (down_send_ref, down_send_hbm),
        (down_keep_ref, down_keep_hbm),
        (in_send_ref, in_send_hbm),
        (in_keep_ref, in_keep_hbm),
    )
    base = copies_.used

    def leave(slot, i):
        source, target = leavers[i]
        return pltpu.make_async_copy(source.at[slot], target.at[slot], sems.at[base + len(leavers) * slot + i])

    def backward(slot, mine):
        ffn_low, low = ffn_low_ref[...], low_ref[...]
        for first, last in blocks_of(2 * half):
            act_grad = dot(ffn_low, down_rows(slot, mine, first, last), 1, 1)
            pre_grad_ref[slot, :, first:last] = (act_grad * slope_ref[slot, :, first:last]).astype(BF16)
        leave(slot, 0).start()
        down_send_ref[slot] = dot(act_ref[slot, :, half:], ffn_low, 0, 0).astype(BF16)
        leave(slot, 1).start()
        down_keep_ref[slot] = dot(act_ref[slot, :, :half], ffn_low, 0, 0).astype(BF16)
        leave(slot, 2).start()
        one, two = pre_grad_ref[slot, :, :half], pre_grad_ref[slot, :, half:]
        in_send_ref[slot] = dot(two, low, 0, 0).astype(BF16)
        leave(slot, 3).start()
        in_keep_ref[slot] = dot(one, low, 0, 0).astype(BF16)
        leave(slot, 4).start()
        natural = slot ^ here_ref[1]
        sum_in_ref[natural, :, own(0, 0, half)] = column_sum(one.astype(F32))
        sum_in_ref[natural, :, own(1, 0, half)] = column_sum(two.astype(F32))

    backward(0, True)
    lax.fori_loop(1, count, lambda slot, _: (backward(slot, False), 0)[1], 0)
    wait(leaving)
    for slot in range(count):
        for i in range(len(leavers)):
            leave(slot, i).wait()


def ffn_back_kernel(
    count, here_ref, pre_grad_hbm, w_in_hbm, in_one, in_two, delta_hbm, normed_hbm, scale_ref, vectors_ref,
    delta_attn_hbm, attn_low_ref, sums_ref, pre_grad_ref, w_in_ref, delta_ref, normed_ref, total_ref, sems,
):
    core = here_ref[0]
    half = in_one.shape[1]
    copies = Copies(sems)
    base = copies.used
    copies.used += count

    def load(slot):
        return pltpu.make_async_copy(pre_grad_hbm.at[slot], pre_grad_ref.at[slot], sems.at[base + slot])

    for slot in list(range(1, count)) + [0]:
        load(slot).start()
    w_copies = copies.start((w_in_hbm, w_in_ref))
    norm_copies = copies.start((delta_hbm, delta_ref), (normed_hbm, normed_ref))

    def add(slot, mine):
        load(slot).wait()
        branch = None
        for a, b in blocks_of(2 * half):
            pre_grad = pre_grad_ref[slot, :, a:b]
            parts = halves_of(half, a, b)
            if mine:
                w_in = jnp.concatenate([w_in_ref[:, own_units(core, half, *p)] for p in parts], axis=1)
                term = dot(pre_grad, w_in, 1, 1)
            else:
                w_in = jnp.concatenate([(in_one, in_two)[w][slot - 1, c:d] for w, c, d in parts], axis=0)
                term = dot(pre_grad, w_in, 1, 0)
            branch = term if branch is None else branch + term
        total_ref[...] += branch

    total_ref[...] = jnp.zeros_like(total_ref)
    lax.fori_loop(1, count, lambda slot, _: (add(slot, False), 0)[1], 0)
    wait_all(w_copies)
    add(0, True)
    wait_all(norm_copies)
    hidden_grad = total_ref[...] + delta_ref[...]
    normed = normed_ref[...]
    delta = normalize_back(hidden_grad, normed, scale_ref[...], vectors_ref[1:2])
    total_ref[...] = delta
    leaving = copies.start((total_ref, delta_attn_hbm))
    attn_low_ref[...] = delta.astype(BF16)
    sums_ref[...] = jnp.zeros_like(sums_ref)
    sums_ref[0:1] = column_sum(delta)
    sums_ref[1:2] = column_sum(hidden_grad * normed)
    sums_ref[2:3] = column_sum(hidden_grad)
    wait_all(leaving)


def attention_back_kernel(
    pairs, here_ref, x_ref, attn_low_ref, delta_ref, own_qk, qk_one, qk_two, own_vo, vo_one, vo_two, q_ref, k_ref,
    v_ref, weights_ref, context_ref, sums_one_ref, sums_two_ref, sum_in_ref,
    qk_keep_ref, vo_keep_ref, send_ref, sums_ref, *refs,
):
    step = pl.program_id(0)
    shards_ = pl.num_programs(0)
    out_refs = refs[:shards_]
    dq_ref, dk_ref, dv_ref, total_ref = refs[shards_:]

    @pl.when(step == 0)
    def _():
        total_ref[...] = delta_ref[...]
        sums_ref[...] = jnp.zeros_like(sums_ref)
        sums_ref[0:3] = sums_one_ref[0:3]
        sums_ref[3:6] = sums_two_ref[0:3]
        for j in range(shards_):
            sums_ref[6 + j : 7 + j] = sum_in_ref[j]

    core = here_ref[0]
    cols = q_ref.shape[2]
    heads = cols // HEAD
    slots = x_ref.shape[0] // pairs
    scale = HEAD ** (-0.5)
    x = x_ref[...]
    attn_low = attn_low_ref[...]
    w_q, w_k = head_weights(step == 0, here_ref, own_qk, qk_one, qk_two)
    w_v, w_o = head_weights(step == 0, here_ref, own_vo, vo_one, vo_two)
    context_grad = dot(attn_low, w_o, 1, 1).astype(BF16)
    grad_out = dot(context_ref[0], attn_low, 0, 0).astype(BF16)
    for p in range(pairs):
        rows = slice(p * slots, (p + 1) * slots)
        up = head_stack(context_grad[rows], heads)
        weights = weights_ref[0, p]
        prob_grad = dot(up, v_ref[0, rows], 1, 1)
        inner = jnp.sum(prob_grad * weights, axis=-1, keepdims=True)
        score_grad = (weights * (prob_grad - inner)).astype(BF16)
        dv_ref[rows] = dot(weights.astype(BF16), up, 0, 0).astype(BF16)
        query_grad = head_pick(dot(score_grad, k_ref[0, rows], 1, 0), heads)
        dq_ref[rows] = (query_grad * scale).astype(BF16)
        key_grad = dot(score_grad, head_stack(q_ref[0, rows], heads), 0, 0)
        dk_ref[rows] = (key_grad * scale).astype(BF16)
    dq, dk, dv = dq_ref[...], dk_ref[...], dv_ref[...]
    row = pl.ds(6 + shards_ + (step ^ here_ref[1]), 1)
    sums_ref[row, :cols] = column_sum(dq.astype(F32))
    sums_ref[row, 2 * cols : 3 * cols] = column_sum(dv.astype(F32))
    grad_q = dot(dq, x, 0, 0).astype(BF16)
    grad_k = dot(dk, x, 0, 0).astype(BF16)
    grad_v = dot(dv, x, 0, 0).astype(BF16)

    @pl.when(core == 0)
    def _():
        qk_keep_ref[0], send_ref[0, 0] = grad_q, grad_k
        vo_keep_ref[0], send_ref[1, 0] = grad_v, grad_out

    @pl.when(core != 0)
    def _():
        qk_keep_ref[0], send_ref[0, 0] = grad_k, grad_q
        vo_keep_ref[0], send_ref[1, 0] = grad_out, grad_v

    total_ref[...] += dot(dq, w_q, 1, 0) + dot(dk, w_k, 1, 0) + dot(dv, w_v, 1, 0)

    @pl.when(step == shards_ - 1)
    def _():
        leave_rows(total_ref[...], out_refs)


def place_kernel(pairs, here_ref, *refs):
    out_ref = refs[-1]
    for k, ref in enumerate(refs[:-1]):
        out_ref[pl.ds((here_ref[1] ^ k) * pairs, pairs)] = ref[...].astype(out_ref.dtype)


def head_grads_kernel(order, here_ref, mine_ref, other_ref, grad_qkv_ref, grad_out_ref):
    core = here_ref[0]
    part = grad_out_ref.shape[1]
    for side, ref in ((core, mine_ref), (1 - core, other_ref)):
        for k, index in enumerate(order):
            place = here_ref[2] ^ index
            piece = ref[k].astype(F32)
            grad_qkv_ref[side, place] = piece[:part]

            @pl.when(side == 0)
            def _():
                grad_qkv_ref[2, place] = piece[part:]

            @pl.when(side != 0)
            def _():
                grad_out_ref[place] = piece[part:]


def unit_grads_kernel(here_ref, in_ref, down_ref, in_other, down_other, grad_in_ref, grad_down_ref):
    half = in_ref.shape[1]
    mine = pl.multiple_of(here_ref[0] * half, half)
    other = pl.multiple_of((1 - here_ref[0]) * half, half)
    grad_in_ref[:, pl.ds(mine, half)] = in_ref[0].astype(F32).T
    grad_in_ref[:, pl.ds(other, half)] = in_other[0].astype(F32).T
    grad_down_ref[pl.ds(mine, half)] = down_ref[0].astype(F32)
    grad_down_ref[pl.ds(other, half)] = down_other[0].astype(F32)


def whole(array):
    return pl.BlockSpec(array.shape, lambda *_: (0,) * len(array.shape))


def per_step(array):
    return pl.BlockSpec((1,) + array.shape[1:], lambda s, *_: (s,) + (0,) * (len(array.shape) - 1))


def where_it_is(array):
    return pl.BlockSpec(memory_space=pl.ANY)


def in_vmem(array):
    return pl.BlockSpec(memory_space=pltpu.VMEM)


def call(kernel, steps, name, vmem, inputs, outputs, scratch, scalar, kept=()):
    spec = pltpu.PrefetchScalarGridSpec(
        num_scalar_prefetch=1,
        grid=(steps,),
        in_specs=[make if isinstance(make, pl.BlockSpec) else make(a) for make, a in inputs],
        out_specs=[make if isinstance(make, pl.BlockSpec) else make(a) for make, a in outputs],
        scratch_shapes=scratch,
    )
    return pl.pallas_call(
        kernel,
        grid_spec=spec,
        out_shape=[pltpu.HBM(a.shape, a.dtype) if i in kept else a for i, (_, a) in enumerate(outputs)],
        name=name,
        cost_estimate=pl.CostEstimate(flops=0, bytes_accessed=0, transcendentals=0),
        compiler_params=pltpu.CompilerParams(vmem_limit_bytes=vmem * MIB),
    )(scalar, *[a if make is in_vmem else in_place(a) for make, a in inputs])


def shape(dims, dtype):
    return jax.ShapeDtypeStruct(dims, dtype)


def in_place(array):
    if array.size * array.dtype.itemsize < MIB:
        return array
    return pltpu.with_memory_space_constraint(array, pltpu.HBM)


def add_kernel(counts, *refs):
    refs = refs[1:]
    out_refs = refs[sum(counts) :]
    for count, out_ref in zip(counts, out_refs):
        total = refs[0][...].astype(F32)
        for ref in refs[1:count]:
            total = total + ref[...].astype(F32)
        out_ref[...] = total.astype(BF16)
        refs = refs[count:]


def add_terms(sides, me):
    in_specs, out_specs, arrays, outs, lefts = [], [], [], [], []

    def place(own_bits, fixed, left):
        def index(g, me_ref):
            at = 0
            for b in own_bits:
                if b in fixed:
                    value = (me_ref[0] >> b) & 1
                    value = value if fixed[b] else 1 - value
                else:
                    value = (g >> (len(left) - 1 - left.index(b))) & 1
                at = at * 2 + value
            return (0, at, 0, 0)

        return index

    for terms, fixed in sides:
        first, bits = terms[0]
        left = [b for b in bits if b not in fixed]
        n, _, rows, cols = first.shape
        in_specs += [pl.BlockSpec((n, 1, rows, cols), place(b, fixed, left)) for _, b in terms]
        out_specs.append(pl.BlockSpec((n, 1, rows, cols), lambda g, _: (0, g, 0, 0)))
        arrays += [a for a, _ in terms]
        outs.append(shape((n, 1 << len(left), rows, cols), BF16))
        lefts.append(left)
    results = pl.pallas_call(
        partial(add_kernel, [len(terms) for terms, _ in sides]),
        grid_spec=pltpu.PrefetchScalarGridSpec(
            num_scalar_prefetch=1, grid=(1 << len(lefts[0]),), in_specs=in_specs, out_specs=out_specs
        ),
        out_shape=outs,
        name="add",
        cost_estimate=pl.CostEstimate(flops=0, bytes_accessed=0, transcendentals=0),
        compiler_params=pltpu.CompilerParams(vmem_limit_bytes=24 * MIB),
    )(me, *arrays)
    return results, lefts


def flip(array, axis, mask):
    size = lax.axis_size(axis)
    return lax.ppermute(array, axis, [(i, i ^ mask) for i in range(size)])


def tie(*arrays):
    return lax.optimization_barrier(arrays)


def pick(array, axis, index):
    return lax.dynamic_index_in_dim(array, index, axis, keepdims=False)


def outer_bits():
    bits = list(range(1, lax.axis_size("dp").bit_length() - 1))
    return bits, (bits, bits[::-1])


def share_of():
    me = lax.axis_index("dp")
    return (me & 1) * (lax.axis_size("dp") // 2) + (me >> 1)


class Gather:
    def __init__(self, pair):
        self.bits, self.orders = outer_bits()
        self.steps = len(self.bits)
        self.n, _, self.cols = pair[0].shape
        self.held = [
            a.reshape((self.n,) + (1,) * self.steps + a.shape[1:]) for a in pair
        ]

    def send(self, step):
        return [flip(h, "dp", 1 << order[step]) for h, order in zip(self.held, self.orders)]

    def merge(self, step, mine, theirs):
        me = lax.axis_index("dp")
        merged = []
        for one, two, order in zip(mine, theirs, self.orders):
            bit = order[step]
            low = ((me >> bit) & 1) == 0
            parts = [jnp.where(low, one, two), jnp.where(low, two, one)]
            merged.append(jnp.concatenate(parts, axis=1 + self.steps - bit))
        return merged

    def take(self, step, got):
        self.held = self.merge(step, self.held, got)

    def halves(self):
        return self.flat(self.held)

    def flat(self, arrays):
        return [a.reshape(self.n, -1, self.cols) for a in arrays]


class Reduce:
    def __init__(self, keeps, gots):
        self.bits, self.orders = outer_bits()
        self.steps = len(self.bits)
        self.me = lax.axis_index("dp").astype(jnp.int32).reshape(1)
        high_first = self.bits[::-1]
        n, rows, cols = keeps[0].shape
        form = (n, 1 << self.steps, rows >> self.steps, cols)
        self.terms = [
            [(k.reshape(form), high_first), (g.reshape(form), high_first)]
            for k, g in zip(keeps, gots)
        ]
        self.left = [None, None]

    def pack(self, step):
        sides = []
        for terms, order in zip(self.terms, self.orders):
            fixed = {b: True for b in order[:step]}
            fixed[order[step]] = False
            sides.append((terms, fixed))
        sends, self.left = add_terms(sides, self.me)
        return sends

    def send(self, step, packs):
        return [flip(p, "dp", 1 << order[step]) for p, order in zip(packs, self.orders)]

    def take(self, got):
        for side in range(2):
            self.terms[side].append((got[side], self.left[side]))

    def finish(self):
        fixed = {b: True for b in self.bits}
        sums, _ = add_terms([(t, fixed) for t in self.terms], self.me)
        return [a[:, 0] for a in sums]


def gather_stack(piece):
    bits, _ = outer_bits()
    order = list(range(1 << len(bits)))
    if len(order) <= 4:
        order = order[:1] + order[:0:-1]
        return [piece] + [flip(piece, "dp", 2 * k) for k in order[1:]], order
    held = piece[None]
    for bit in bits:
        held = jnp.concatenate([held, flip(held, "dp", 1 << bit)])
    return [held[k] for k in order], order


def add_parts(*parts):
    total = parts[0].astype(F32)
    for part in parts[1:]:
        total = total + part.astype(F32)
    return total.astype(BF16)


def shards(
    tokens,
    word_len,
    region_count,
    w_qkv,
    qv_bias,
    w_out,
    out_bias,
    norm1_gain,
    norm1_bias,
    w_in,
    in_bias,
    w_down,
    down_bias,
    norm2_gain,
    norm2_bias,
    cotangent,
):
    mp = lax.axis_size("mp")
    dp = lax.axis_size("dp")
    mi = lax.axis_index("mp")
    width = tokens.shape[2]
    rows_local = tokens.shape[1]
    slots = rows_local * mp
    pairs = tokens.shape[0] // mp
    rows = pairs * slots
    cols = w_qkv.shape[2]
    units = w_in.shape[1]
    half_units = units // 2
    order = jnp.arange(mp) ^ mi
    here = jnp.stack([lax.axis_index("dp") & 1, mi, lax.axis_index("dp") >> 1]).astype(jnp.int32)
    share = share_of()

    turned = w_qkv.transpose(0, 2, 1).reshape(3 * cols, width)
    own_qk = turned[: 2 * cols]
    own_vo = jnp.concatenate([turned[2 * cols :], w_out], axis=0)
    att_part, ffn_part = 2 * cols // dp, units // dp
    first = share * att_part
    rows_of = lambda array, start, size: lax.dynamic_slice_in_dim(array, start, size, 0)
    vo_piece = jnp.where(
        first < cols,
        rows_of(turned, 2 * cols + jnp.minimum(first, cols - att_part), att_part),
        rows_of(w_out, jnp.maximum(first - cols, 0), att_part),
    )

    def row_blocks(array):
        blocks = array.reshape((mp, pairs) + array.shape[1:])
        return [pick(blocks, 0, mi ^ k) for k in range(mp)]

    def join(blocks):
        return jnp.concatenate(blocks, axis=1).reshape(rows, width)

    fill = lambda v: jnp.pad(v, ((0, 0), (0, width - v.shape[1])))
    small = jnp.concatenate([fill(qv_bias), in_bias.reshape(1, units), jnp.zeros((5, width), BF16)])
    att_send = jnp.concatenate([rows_of(turned, first, att_part), vo_piece], axis=0)
    ffn_send = jnp.concatenate(
        [rows_of(w_in.T, share * ffn_part, ffn_part), rows_of(w_down, share * ffn_part, ffn_part), small],
        axis=0,
    )
    tok = row_blocks(tokens)
    cot = row_blocks(cotangent)
    vectors = jnp.stack(
        [out_bias, norm1_gain, norm1_bias, down_bias, norm2_gain, norm2_bias, out_bias, out_bias]
    ).astype(F32)
    words = lax.dynamic_slice_in_dim(word_len, mi * pairs, pairs, 0)
    regions = lax.dynamic_slice_in_dim(region_count, mi * pairs, pairs, 0)
    slot_index = (order[:, None] * rows_local + jnp.arange(rows_local)[None, :]).reshape(-1)
    key_valid = jnp.where(
        slot_index[None, :] < WORDS,
        slot_index[None, :] < words[:, None],
        slot_index[None, :] - WORDS < regions[:, None],
    ).astype(F32)[:, None, :]

    att_got = {k: flip(att_send, "mp", k) for k in (3, 2, 1)}
    att_got = [att_got[k] for k in (1, 2, 3)]
    att_got, ffn_send, tok, vectors, key_valid, here, own_qk, own_vo = tie(
        att_got, ffn_send, tok, vectors, key_valid, here, own_qk, own_vo
    )
    att = Gather(
        [
            jnp.stack([g[:att_part] for g in att_got]),
            jnp.stack([g[att_part:] for g in att_got]),
        ]
    )
    ffn_two = flip(ffn_send, "mp", 2)
    got = att.send(0)
    tok_one = flip(tok[1], "mp", 1)
    ffn_two, got, tok_one, ffn_send, tok = tie(ffn_two, got, tok_one, ffn_send, tok)
    for step in range(1, att.steps):
        att.take(step - 1, got)
        got = att.send(step)
        if step == 1:
            ffn_odd = flip(jnp.stack([ffn_send, ffn_two]), "mp", 1)
            tok_three = flip(tok[3], "mp", 3)
        got, ffn_odd, tok_three, tok = tie(got, ffn_odd, tok_three, tok)
    att.take(att.steps - 1, got)
    ffn_got = [ffn_odd[0], ffn_two, ffn_odd[1]]
    ffn = Gather(
        [
            jnp.stack([g[:ffn_part] for g in ffn_got]),
            jnp.stack([g[ffn_part : 2 * ffn_part] for g in ffn_got]),
        ]
    )
    got = ffn.send(0)
    qk_one, vo_one = att.halves()
    qk_two, vo_two = flip(qk_one, "dp", 1), flip(vo_one, "dp", 1)
    tok_two = flip(tok[2], "mp", 2)
    smalls = jnp.stack([small] + [g[2 * ffn_part :] for g in ffn_got]).astype(F32)
    got, qk_two, vo_two, tok_two, cot, smalls = tie(got, qk_two, vo_two, tok_two, cot, smalls)
    heads_low = shape((mp, rows, cols), BF16)
    low_shape = shape((rows, width), BF16)
    rows_shape = shape((rows, width), F32)
    sums_shape = shape((8, width), F32)
    block_shape = shape((pairs, rows_local, width), BF16)
    for step in range(1, ffn.steps):
        ffn.take(step - 1, got)
        got = ffn.send(step)
        if step < ffn.steps - 1:
            got = tie(*got)
    early = [flip(h, "dp", 1) for h in ffn.held]
    early, cot, x = tie(early, cot, join([tok[0], tok_one, tok_two, tok_three]))
    cot_blocks = [cot[0]] + [flip(cot[k], "mp", k) for k in range(1, mp)]
    later = lambda a: pl.BlockSpec((1,) + a.shape[1:], lambda s, h: (jnp.clip(s - 1, 0, mp - 2), 0, 0))
    head_args = [
        (whole, own_qk),
        (later, qk_one),
        (later, qk_two),
        (whole, own_vo),
        (later, vo_one),
        (later, vo_two),
    ]
    q, k, v, weights, context, hidden_low, normed_one, scale_one = call(
        partial(attention_kernel, pairs),
        mp,
        "attention",
        24,
        [
            (whole, x),
            *head_args,
            (per_step, smalls),
            (whole, key_valid),
            (whole, vectors),
        ],
        [
            (per_step, heads_low),
            (per_step, heads_low),
            (per_step, heads_low),
            (per_step, shape((mp, pairs, cols // HEAD * slots, slots), F32)),
            (per_step, heads_low),
            (whole, low_shape),
            (whole, rows_shape),
            (whole, shape((rows, 1), F32)),
        ],
        [pltpu.VMEM((rows, width), F32)],
        here,
        range(5),
    )
    got, early, hidden_low, cot_blocks = tie(got, early, hidden_low, cot_blocks)
    ffn.take(ffn.steps - 1, got)
    in_one, down_one = ffn.halves()
    late = [flip(g, "dp", 1) for g in got]
    late, hidden_low = tie(late, hidden_low)
    in_two, down_two = ffn.flat(ffn.merge(ffn.steps - 1, early, late))

    half = shape((mp, half_units, width), BF16)
    pre_shape = shape((mp, rows, units), BF16)
    vmem = lambda a: pltpu.VMEM(a.shape, a.dtype)
    results = call(
        partial(ffn_kernel, mp),
        1,
        "ffn",
        42,
        [
            (where_it_is, hidden_low),
            (where_it_is, normed_one),
            (where_it_is, w_in),
            (in_vmem, in_one),
            (in_vmem, in_two),
            (where_it_is, w_down),
            (in_vmem, down_one),
            (in_vmem, down_two),
            (whole, smalls),
            (whole, vectors),
            *[(where_it_is, c) for c in cot_blocks],
        ],
        [
            *[(whole, block_shape)] * mp,
            (where_it_is, rows_shape),
            (where_it_is, pre_shape),
            (where_it_is, half),
            (where_it_is, half),
            (where_it_is, half),
            (where_it_is, half),
            (whole, shape((mp, 1, units), F32)),
            (whole, sums_shape),
        ],
        [
            vmem(low_shape),
            vmem(rows_shape),
            pltpu.VMEM((width, units), BF16),
            pltpu.VMEM((units, width), BF16),
            pltpu.VMEM((mp,) + block_shape.shape, BF16),
            vmem(pre_shape),
            pltpu.VMEM(pre_shape.shape, F32),
            vmem(rows_shape),
            vmem(rows_shape),
            vmem(pre_shape),
            vmem(half),
            vmem(half),
            vmem(half),
            vmem(half),
            vmem(low_shape),
            pltpu.SemaphoreType.DMA((3 + 1 + mp + 1 + 5 * mp,)),
        ],
        here,
        range(mp + 6),
    )
    out_blocks = results[:mp]
    delta_ffn, pre_grad, in_keep, in_send, down_keep, down_send, sum_in, sums_two = results[mp:]
    in_got, down_got = flip(in_send, "dp", 1), flip(down_send, "dp", 1)
    delta_attn, attn_low, sums_one = call(
        partial(ffn_back_kernel, mp),
        1,
        "ffn_back",
        18,
        [
            (where_it_is, pre_grad),
            (where_it_is, w_in),
            (in_vmem, in_one),
            (in_vmem, in_two),
            (where_it_is, delta_ffn),
            (where_it_is, normed_one),
            (whole, scale_one),
            (whole, vectors),
        ],
        [(where_it_is, rows_shape), (whole, low_shape), (whole, sums_shape)],
        [
            vmem(pre_shape),
            pltpu.VMEM((width, units), BF16),
            vmem(rows_shape),
            vmem(rows_shape),
            vmem(rows_shape),
            pltpu.SemaphoreType.DMA((mp + 1 + 2 + 1,)),
        ],
        here,
        (0,),
    )
    in_got, down_got, out_blocks, attn_low = tie(in_got, down_got, out_blocks, attn_low)
    ffn = Reduce([in_keep, down_keep], [in_got, down_got])
    packs = ffn.pack(0)
    packs, attn_low, out_blocks = tie(packs, attn_low, out_blocks)
    got = ffn.send(0, packs)
    out_got = [out_blocks[0]] + [flip(out_blocks[k], "mp", k) for k in range(1, mp)]
    small_half = shape((mp, cols, width), BF16)
    results = call(
        partial(attention_back_kernel, pairs),
        mp,
        "attention_back",
        28,
        [
            (whole, x),
            (whole, attn_low),
            (whole, delta_attn),
            *head_args,
            (per_step, q),
            (per_step, k),
            (per_step, v),
            (per_step, weights),
            (per_step, context),
            (whole, sums_one),
            (whole, sums_two),
            (whole, sum_in),
        ],
        [
            (per_step, small_half),
            (per_step, small_half),
            (
                pl.BlockSpec((2, 1, cols, width), lambda s, h: (0, s, 0, 0)),
                shape((2, mp, cols, width), BF16),
            ),
            (whole, shape((-(-(6 + 2 * mp) // 8) * 8, width), F32)),
            *[(whole, block_shape)] * mp,
        ],
        [pltpu.VMEM((rows, cols), BF16)] * 3 + [pltpu.VMEM((rows, width), F32)],
        here,
        (0, 1, 2) + tuple(range(4, 4 + mp)),
    )
    qk_keep, vo_keep, att_send, sums = results[:4]
    row_sends = results[4:]
    got, out_got, att_send, row_sends, sums = tie(got, out_got, att_send, row_sends, sums)
    place = lambda blocks, dtype: call(
        partial(place_kernel, pairs),
        1,
        "place",
        16,
        [(whole, b) for b in blocks],
        [(whole, shape((mp * pairs, rows_local, width), dtype))],
        [],
        here,
    )[0]
    for step in range(1, ffn.steps):
        ffn.take(got)
        packs = ffn.pack(step)
        got = ffn.send(step, packs)
        if step == 1:
            att_got = flip(att_send, "dp", 1)
            row_three = flip(row_sends[3], "mp", 3)
            sums_got = flip(sums, "mp", 2)
            att = Reduce([qk_keep, vo_keep], [att_got[0], att_got[1]])
            att_packs = att.pack(0)
            layer_out = place(out_got, BF16)
        got, att_packs, row_three, sums_got, row_sends, layer_out = tie(
            got, att_packs, row_three, sums_got, row_sends, layer_out
        )
    sums = sums + sums_got
    ffn.take(got)
    ffn_parts = ffn.finish()
    ffn_odd = jnp.concatenate([p[1::2] for p in ffn_parts], axis=1)
    ffn_even = jnp.concatenate([p[0::2] for p in ffn_parts], axis=1)
    got = att.send(0, att_packs)
    ffn_got = flip(ffn_odd, "mp", 1)
    sums_got = flip(sums, "dp", 2)
    row_two = flip(row_sends[2], "mp", 2)
    got, ffn_got, sums_got, row_two, row_sends = tie(got, ffn_got, sums_got, row_two, row_sends)
    sums = sums + sums_got
    for mask in [1 << b for b in range(2, dp.bit_length() - 2)]:
        sums = sums + flip(sums, "dp", mask)
    ffn_two = add_parts(ffn_even[1], ffn_got[1])
    for step in range(1, att.steps):
        att.take(got)
        packs = att.pack(step)
        got = att.send(step, packs)
        if step == 1:
            ffn_last = flip(ffn_two, "mp", 2)
            row_one = flip(row_sends[1], "mp", 1)
            sums_got = flip(sums, "dp", dp // 2)
        got, ffn_last, row_one, sums_got, row_sends = tie(got, ffn_last, row_one, sums_got, row_sends)
    att.take(got)
    sums = sums + sums_got
    att_parts = att.finish()
    att_odd = jnp.concatenate([p[1::2] for p in att_parts], axis=1)
    att_even = jnp.concatenate([p[0::2] for p in att_parts], axis=1)
    ffn_sum = add_parts(ffn_even[0], ffn_got[0], ffn_last)
    ffn = Gather([ffn_sum[None, :ffn_part], ffn_sum[None, ffn_part:]])
    ffn.held, att_odd, att_even, sums = tie(ffn.held, att_odd, att_even, sums)
    got = ffn.send(0)
    att_got = flip(att_odd, "mp", 1)
    sums_got = flip(sums, "dp", 1)
    got, att_got, sums_got, row_one = tie(got, att_got, sums_got, row_one)
    grad_input = place([row_sends[0], row_one, row_two, row_three], F32)
    sums = sums + sums_got
    att_two = add_parts(att_even[1], att_got[1])
    for step in range(1, ffn.steps):
        ffn.take(step - 1, got)
        got = ffn.send(step)
        if step == 1:
            att_last = flip(att_two, "mp", 2)
            sums_got = flip(sums, "mp", 1)
        got, att_last, sums_got, grad_input = tie(got, att_last, sums_got, grad_input)
    ffn.take(ffn.steps - 1, got)
    sums = sums + sums_got
    att_sum = add_parts(att_even[0], att_got[0], att_last)
    ffn_halves = ffn.halves()
    core_got = [flip(h, "dp", 1) for h in ffn_halves]
    att_mine, att_order = gather_stack(att_sum)
    grad_in, grad_down = call(
        unit_grads_kernel,
        1,
        "unit_grads",
        24,
        [(whole, a) for a in ffn_halves + core_got],
        [(whole, shape((width, units), F32)), (whole, shape((units, width), F32))],
        [],
        here,
    )
    att_mine, grad_in, grad_down, sums = tie(att_mine, grad_in, grad_down, sums)
    att_mine = jnp.stack(att_mine)
    att_other = flip(att_mine, "dp", 1)
    grad_qkv, grad_out = call(
        partial(head_grads_kernel, att_order),
        1,
        "head_grads",
        24,
        [(whole, att_mine), (whole, att_other)],
        [
            (whole, shape((3, cols // att_part, att_part, width), F32)),
            (whole, shape((cols // att_part, att_part, width), F32)),
        ],
        [],
        here,
    )
    sum_in_bias = lax.dynamic_index_in_dim(sums, 6 + mi, 0, keepdims=False)
    sum_qv = lax.dynamic_index_in_dim(sums, 6 + mp + mi, 0, keepdims=False)
    sum_qv = jnp.stack([sum_qv[:cols], sum_qv[2 * cols : 3 * cols]])
    return (
        layer_out,
        grad_input,
        grad_qkv.reshape(3, cols, width).transpose(0, 2, 1),
        sum_qv,
        grad_out.reshape(cols, width),
        sums[0],
        sums[1],
        sums[2],
        grad_in,
        sum_in_bias,
        grad_down,
        sums[5],
        sums[3],
        sums[4],
    )


def solution(mesh):
    in_specs = (
        P("dp", "mp", None),
        P("dp"),
        P("dp"),
        P(None, None, "mp"),
        P(None, "mp"),
        P("mp", None),
        P(),
        P(),
        P(),
        P(None, "mp"),
        P("mp"),
        P("mp", None),
        P(),
        P(),
        P(),
        P("dp", "mp", None),
    )
    out_specs = (
        P("dp", "mp", None),
        P("dp", "mp", None),
        P(None, None, "mp"),
        P(None, "mp"),
        P("mp", None),
        P(),
        P(),
        P(),
        P(None, "mp"),
        P("mp"),
        P("mp", None),
        P(),
        P(),
        P(),
    )
    return jax.shard_map(shards, mesh=mesh, in_specs=in_specs, out_specs=out_specs, check_vma=False)
```

```python
from functools import partial

import jax
import jax.numpy as jnp
from jax import lax
from jax.experimental import pallas as pl
from jax.experimental.pallas import tpu as pltpu
from jax.sharding import PartitionSpec as P

HEAD = 64
WORDS = 60
EPSILON = 1e-05
SQRT_HALF = 0.7071067811865476
DENSITY = 0.3989422804014327
F32 = jnp.float32
BF16 = jnp.bfloat16
MIB = 1024 * 1024


def dot(one, two, one_axis, two_axis):
    return lax.dot_general(
        one, two, (((one_axis,), (two_axis,)), ((), ())), preferred_element_type=F32
    )


def normalize(total, gain, shift):
    centered = total - jnp.mean(total, axis=-1, keepdims=True)
    inv_scale = lax.rsqrt(jnp.mean(centered * centered, axis=-1, keepdims=True) + EPSILON)
    normed = centered * inv_scale
    return normed * gain + shift, normed, inv_scale


def normalize_back(upstream, normed, inv_scale, gain):
    scaled_up = upstream * gain
    mean_one = jnp.mean(scaled_up, axis=-1, keepdims=True)
    mean_two = jnp.mean(scaled_up * normed, axis=-1, keepdims=True)
    return inv_scale * (scaled_up - mean_one - normed * mean_two)


def column_sum(array):
    return jnp.sum(array, axis=0, keepdims=True)


def head_stack(array, heads):
    head = lax.broadcasted_iota(jnp.int32, array.shape, 1) // HEAD
    zero = jnp.zeros_like(array)
    return jnp.concatenate([jnp.where(head == h, array, zero) for h in range(heads)], axis=0)


def head_pick(stacked, heads):
    rows = stacked.shape[0] // heads
    head = lax.broadcasted_iota(jnp.int32, (rows, stacked.shape[1]), 1) // HEAD
    total = stacked[:rows]
    for h in range(1, heads):
        total = jnp.where(head == h, stacked[h * rows : (h + 1) * rows], total)
    return total


def head_weights(first, here_ref, own_ref, one_ref, two_ref):
    low = here_ref[0] == 0
    half = one_ref.shape[1]
    one, two = one_ref[0], two_ref[0]
    return (
        jnp.where(first, own_ref[:half], jnp.where(low, one, two)),
        jnp.where(first, own_ref[half:], jnp.where(low, two, one)),
    )


def attention_kernel(
    pairs, here_ref, x_ref, own_qk, qk_one, qk_two, own_vo, vo_one, vo_two, small_ref, valid_ref, vectors_ref,
    q_ref, k_ref, v_ref, weights_ref, context_ref, low_ref, normed_ref, scale_ref, total_ref,
):
    step = pl.program_id(0)
    cols = q_ref.shape[2]
    heads = cols // HEAD
    slots = x_ref.shape[0] // pairs
    x = x_ref[...]
    w_q, w_k = head_weights(step == 0, here_ref, own_qk, qk_one, qk_two)
    w_v, w_o = head_weights(step == 0, here_ref, own_vo, vo_one, vo_two)
    q_ref[0] = (dot(x, w_q, 1, 1) + small_ref[0, 0:1, :cols]).astype(BF16)
    k_ref[0] = dot(x, w_k, 1, 1).astype(BF16)
    v_ref[0] = (dot(x, w_v, 1, 1) + small_ref[0, 1:2, :cols]).astype(BF16)
    for p in range(pairs):
        rows = slice(p * slots, (p + 1) * slots)
        scores = dot(head_stack(q_ref[0, rows], heads), k_ref[0, rows], 1, 1) * HEAD ** (-0.5)
        scores = jnp.where(valid_ref[p] > 0.5, scores, -1e30)
        exp_scores = jnp.exp(scores - jnp.max(scores, axis=-1, keepdims=True))
        weights = exp_scores / jnp.sum(exp_scores, axis=-1, keepdims=True)
        weights_ref[0, p] = weights
        mixed = dot(weights.astype(BF16), v_ref[0, rows], 1, 0)
        context_ref[0, rows] = head_pick(mixed, heads).astype(BF16)
    branch = dot(context_ref[0], w_o, 1, 0)

    @pl.when(step == 0)
    def _():
        total_ref[...] = branch

    @pl.when(step > 0)
    def _():
        total_ref[...] += branch

    @pl.when(step == pl.num_programs(0) - 1)
    def _():
        first_sum = total_ref[...] + vectors_ref[0:1] + x.astype(F32)
        hidden, normed, scale = normalize(first_sum, vectors_ref[1:2], vectors_ref[2:3])
        low_ref[...] = hidden.astype(BF16)
        normed_ref[...] = normed
        scale_ref[...] = scale


def blocks_of(units):
    size = min(256, units)
    return [(start, min(start + size, units)) for start in range(0, units, size)]


class Copies:
    def __init__(self, sems):
        self.sems, self.used = sems, 0

    def start(self, *pairs):
        copies = []
        for source, target in pairs:
            copies.append(pltpu.make_async_copy(source, target, self.sems.at[self.used]))
            copies[-1].start()
            self.used += 1
        return copies


def wait_all(copies):
    for copy in copies:
        copy.wait()


def halves_of(half, start, stop):
    parts = []
    if start < half:
        parts.append((0, start, min(stop, half)))
    if stop > half:
        parts.append((1, max(start - half, 0), stop - half))
    return parts


def own_units(core, half, which, first, last):
    side = core if which == 0 else 1 - core
    return pl.ds(pl.multiple_of(side * half + first, 128), last - first)


def join_rows(refs):
    pairs = refs[0].shape[0]
    return jnp.concatenate([ref[p].astype(F32) for p in range(pairs) for ref in refs], axis=0)


def leave_rows(array, refs):
    pairs, rows = refs[0].shape[:2]
    for p in range(pairs):
        for j, ref in enumerate(refs):
            start = (p * len(refs) + j) * rows
            ref[p] = array[start : start + rows].astype(BF16)


def ffn_kernel(
    count, here_ref, low_hbm, normed_hbm, w_in_hbm, in_one, in_two, w_down_hbm, down_one, down_two, small_ref,
    vectors_ref, *refs,
):
    cot_hbm, out_refs = refs[:count], refs[count : 2 * count]
    (
        delta_hbm, pre_grad_hbm, in_keep_hbm, in_send_hbm, down_keep_hbm, down_send_hbm, sum_in_ref, sums_ref,
        low_ref, normed_ref, w_in_ref, w_down_ref, cot_ref, act_ref, slope_ref, total_ref, delta_ref, pre_grad_ref,
        in_keep_ref, in_send_ref, down_keep_ref, down_send_ref, ffn_low_ref, sems,
    ) = refs[2 * count :]
    core = here_ref[0]
    half = in_one.shape[1]
    copies_ = Copies(sems)
    start, wait = copies_.start, wait_all

    halves = partial(halves_of, half)
    own = partial(own_units, core, half)

    def down_rows(slot, first, start_, stop):
        if first:
            parts = [w_down_ref[own(w, a, b)] for w, a, b in halves(start_, stop)]
        else:
            parts = [(down_one, down_two)[w][slot - 1, a:b] for w, a, b in halves(start_, stop)]
        return jnp.concatenate(parts, axis=0)

    def forward(slot, mine):
        low = low_ref[...]
        branch = None
        for first, last in blocks_of(2 * half):
            parts = halves(first, last)
            if mine:
                w_in = jnp.concatenate([w_in_ref[:, own(*p)] for p in parts], axis=1)
                pre_act = dot(low, w_in, 1, 0)
            else:
                w_in = jnp.concatenate([(in_one, in_two)[w][slot - 1, a:b] for w, a, b in parts], axis=0)
                pre_act = dot(low, w_in, 1, 1)
            bias = jnp.concatenate([small_ref[slot, 2:3, own(*p)] for p in parts], axis=1)
            pre_act = pre_act + bias
            share = 0.5 * (1.0 + lax.erf(pre_act * SQRT_HALF))
            act = (pre_act * share).astype(BF16)
            act_ref[slot, :, first:last] = act
            slope_ref[slot, :, first:last] = share + pre_act * (DENSITY * jnp.exp(-0.5 * pre_act * pre_act))
            term = dot(act, down_rows(slot, mine, first, last), 1, 0)
            branch = term if branch is None else branch + term
        total_ref[...] += branch

    low_copies = start((low_hbm, low_ref))
    own_copies = start((w_in_hbm, w_in_ref), (w_down_hbm, w_down_ref))
    later_copies = start((normed_hbm, normed_ref), *[(cot_hbm[k], cot_ref.at[k]) for k in range(count)])
    total_ref[...] = jnp.zeros_like(total_ref)
    wait(low_copies)
    for slot in range(1, count):
        forward(slot, False)
    wait(own_copies)
    forward(0, True)
    wait(later_copies)

    hidden = normed_ref[...] * vectors_ref[1:2] + vectors_ref[2:3]
    second = total_ref[...] + vectors_ref[3:4] + hidden
    gain = vectors_ref[4:5]
    output, normed, scale = normalize(second, gain, vectors_ref[5:6])
    leave_rows(output, out_refs)
    upstream = join_rows([cot_ref.at[k] for k in range(count)])
    delta = normalize_back(upstream, normed, scale, gain)
    delta_ref[...] = delta
    leaving = start((delta_ref, delta_hbm))
    sums_ref[...] = jnp.zeros_like(sums_ref)
    sums_ref[0:1] = column_sum(upstream * normed)
    sums_ref[1:2] = column_sum(upstream)
    sums_ref[2:3] = column_sum(delta)
    ffn_low_ref[...] = delta.astype(BF16)
    leavers = (
        (pre_grad_ref, pre_grad_hbm),
        (down_send_ref, down_send_hbm),
        (down_keep_ref, down_keep_hbm),
        (in_send_ref, in_send_hbm),
        (in_keep_ref, in_keep_hbm),
    )
    base = copies_.used

    def leave(slot, i):
        source, target = leavers[i]
        return pltpu.make_async_copy(source.at[slot], target.at[slot], sems.at[base + len(leavers) * slot + i])

    def backward(slot, mine):
        ffn_low, low = ffn_low_ref[...], low_ref[...]
        for first, last in blocks_of(2 * half):
            act_grad = dot(ffn_low, down_rows(slot, mine, first, last), 1, 1)
            pre_grad_ref[slot, :, first:last] = (act_grad * slope_ref[slot, :, first:last]).astype(BF16)
        leave(slot, 0).start()
        down_send_ref[slot] = dot(act_ref[slot, :, half:], ffn_low, 0, 0).astype(BF16)
        leave(slot, 1).start()
        down_keep_ref[slot] = dot(act_ref[slot, :, :half], ffn_low, 0, 0).astype(BF16)
        leave(slot, 2).start()
        one, two = pre_grad_ref[slot, :, :half], pre_grad_ref[slot, :, half:]
        in_send_ref[slot] = dot(two, low, 0, 0).astype(BF16)
        leave(slot, 3).start()
        in_keep_ref[slot] = dot(one, low, 0, 0).astype(BF16)
        leave(slot, 4).start()
        natural = slot ^ here_ref[1]
        sum_in_ref[natural, :, own(0, 0, half)] = column_sum(one.astype(F32))
        sum_in_ref[natural, :, own(1, 0, half)] = column_sum(two.astype(F32))

    backward(0, True)
    lax.fori_loop(1, count, lambda slot, _: (backward(slot, False), 0)[1], 0)
    wait(leaving)
    for slot in range(count):
        for i in range(len(leavers)):
            leave(slot, i).wait()


def ffn_back_kernel(
    count, here_ref, pre_grad_hbm, w_in_hbm, in_one, in_two, delta_hbm, normed_hbm, scale_ref, vectors_ref,
    delta_attn_hbm, attn_low_ref, sums_ref, pre_grad_ref, w_in_ref, delta_ref, normed_ref, total_ref, sems,
):
    core = here_ref[0]
    half = in_one.shape[1]
    copies = Copies(sems)
    base = copies.used
    copies.used += count

    def load(slot):
        return pltpu.make_async_copy(pre_grad_hbm.at[slot], pre_grad_ref.at[slot], sems.at[base + slot])

    for slot in list(range(1, count)) + [0]:
        load(slot).start()
    w_copies = copies.start((w_in_hbm, w_in_ref))
    norm_copies = copies.start((delta_hbm, delta_ref), (normed_hbm, normed_ref))

    def add(slot, mine):
        load(slot).wait()
        branch = None
        for a, b in blocks_of(2 * half):
            pre_grad = pre_grad_ref[slot, :, a:b]
            parts = halves_of(half, a, b)
            if mine:
                w_in = jnp.concatenate([w_in_ref[:, own_units(core, half, *p)] for p in parts], axis=1)
                term = dot(pre_grad, w_in, 1, 1)
            else:
                w_in = jnp.concatenate([(in_one, in_two)[w][slot - 1, c:d] for w, c, d in parts], axis=0)
                term = dot(pre_grad, w_in, 1, 0)
            branch = term if branch is None else branch + term
        total_ref[...] += branch

    total_ref[...] = jnp.zeros_like(total_ref)
    lax.fori_loop(1, count, lambda slot, _: (add(slot, False), 0)[1], 0)
    wait_all(w_copies)
    add(0, True)
    wait_all(norm_copies)
    hidden_grad = total_ref[...] + delta_ref[...]
    normed = normed_ref[...]
    delta = normalize_back(hidden_grad, normed, scale_ref[...], vectors_ref[1:2])
    total_ref[...] = delta
    leaving = copies.start((total_ref, delta_attn_hbm))
    attn_low_ref[...] = delta.astype(BF16)
    sums_ref[...] = jnp.zeros_like(sums_ref)
    sums_ref[0:1] = column_sum(delta)
    sums_ref[1:2] = column_sum(hidden_grad * normed)
    sums_ref[2:3] = column_sum(hidden_grad)
    wait_all(leaving)


def attention_back_kernel(
    pairs, here_ref, x_ref, attn_low_ref, delta_ref, own_qk, qk_one, qk_two, own_vo, vo_one, vo_two, q_ref, k_ref,
    v_ref, weights_ref, context_ref, sums_one_ref, sums_two_ref, sum_in_ref,
    qk_keep_ref, vo_keep_ref, send_ref, sums_ref, *refs,
):
    step = pl.program_id(0)
    shards_ = pl.num_programs(0)
    out_refs = refs[:shards_]
    dq_ref, dk_ref, dv_ref, total_ref = refs[shards_:]

    @pl.when(step == 0)
    def _():
        total_ref[...] = delta_ref[...]
        sums_ref[...] = jnp.zeros_like(sums_ref)
        sums_ref[0:3] = sums_one_ref[0:3]
        sums_ref[3:6] = sums_two_ref[0:3]
        for j in range(shards_):
            sums_ref[6 + j : 7 + j] = sum_in_ref[j]

    core = here_ref[0]
    cols = q_ref.shape[2]
    heads = cols // HEAD
    slots = x_ref.shape[0] // pairs
    scale = HEAD ** (-0.5)
    x = x_ref[...]
    attn_low = attn_low_ref[...]
    w_q, w_k = head_weights(step == 0, here_ref, own_qk, qk_one, qk_two)
    w_v, w_o = head_weights(step == 0, here_ref, own_vo, vo_one, vo_two)
    context_grad = dot(attn_low, w_o, 1, 1).astype(BF16)
    grad_out = dot(context_ref[0], attn_low, 0, 0).astype(BF16)
    for p in range(pairs):
        rows = slice(p * slots, (p + 1) * slots)
        up = head_stack(context_grad[rows], heads)
        weights = weights_ref[0, p]
        prob_grad = dot(up, v_ref[0, rows], 1, 1)
        inner = jnp.sum(prob_grad * weights, axis=-1, keepdims=True)
        score_grad = (weights * (prob_grad - inner)).astype(BF16)
        dv_ref[rows] = dot(weights.astype(BF16), up, 0, 0).astype(BF16)
        query_grad = head_pick(dot(score_grad, k_ref[0, rows], 1, 0), heads)
        dq_ref[rows] = (query_grad * scale).astype(BF16)
        key_grad = dot(score_grad, head_stack(q_ref[0, rows], heads), 0, 0)
        dk_ref[rows] = (key_grad * scale).astype(BF16)
    dq, dk, dv = dq_ref[...], dk_ref[...], dv_ref[...]
    row = pl.ds(6 + shards_ + (step ^ here_ref[1]), 1)
    sums_ref[row, :cols] = column_sum(dq.astype(F32))
    sums_ref[row, 2 * cols : 3 * cols] = column_sum(dv.astype(F32))
    grad_q = dot(dq, x, 0, 0).astype(BF16)
    grad_k = dot(dk, x, 0, 0).astype(BF16)
    grad_v = dot(dv, x, 0, 0).astype(BF16)

    @pl.when(core == 0)
    def _():
        qk_keep_ref[0], send_ref[0, 0] = grad_q, grad_k
        vo_keep_ref[0], send_ref[1, 0] = grad_v, grad_out

    @pl.when(core != 0)
    def _():
        qk_keep_ref[0], send_ref[0, 0] = grad_k, grad_q
        vo_keep_ref[0], send_ref[1, 0] = grad_out, grad_v

    total_ref[...] += dot(dq, w_q, 1, 0) + dot(dk, w_k, 1, 0) + dot(dv, w_v, 1, 0)

    @pl.when(step == shards_ - 1)
    def _():
        leave_rows(total_ref[...], out_refs)


def place_kernel(pairs, here_ref, *refs):
    out_ref = refs[-1]
    for k, ref in enumerate(refs[:-1]):
        out_ref[pl.ds((here_ref[1] ^ k) * pairs, pairs)] = ref[...].astype(out_ref.dtype)


def head_grads_kernel(order, here_ref, mine_ref, other_ref, grad_qkv_ref, grad_out_ref):
    core = here_ref[0]
    part = grad_out_ref.shape[1]
    for side, ref in ((core, mine_ref), (1 - core, other_ref)):
        for k, index in enumerate(order):
            place = here_ref[2] ^ index
            piece = ref[k].astype(F32)
            grad_qkv_ref[side, place] = piece[:part]

            @pl.when(side == 0)
            def _():
                grad_qkv_ref[2, place] = piece[part:]

            @pl.when(side != 0)
            def _():
                grad_out_ref[place] = piece[part:]


def unit_grads_kernel(here_ref, in_ref, down_ref, in_other, down_other, grad_in_ref, grad_down_ref):
    half = in_ref.shape[1]
    mine = pl.multiple_of(here_ref[0] * half, half)
    other = pl.multiple_of((1 - here_ref[0]) * half, half)
    grad_in_ref[:, pl.ds(mine, half)] = in_ref[0].astype(F32).T
    grad_in_ref[:, pl.ds(other, half)] = in_other[0].astype(F32).T
    grad_down_ref[pl.ds(mine, half)] = down_ref[0].astype(F32)
    grad_down_ref[pl.ds(other, half)] = down_other[0].astype(F32)


def whole(array):
    return pl.BlockSpec(array.shape, lambda *_: (0,) * len(array.shape))


def per_step(array):
    return pl.BlockSpec((1,) + array.shape[1:], lambda s, *_: (s,) + (0,) * (len(array.shape) - 1))


def where_it_is(array):
    return pl.BlockSpec(memory_space=pl.ANY)


def in_vmem(array):
    return pl.BlockSpec(memory_space=pltpu.VMEM)


def call(kernel, steps, name, vmem, inputs, outputs, scratch, scalar, kept=()):
    spec = pltpu.PrefetchScalarGridSpec(
        num_scalar_prefetch=1,
        grid=(steps,),
        in_specs=[make if isinstance(make, pl.BlockSpec) else make(a) for make, a in inputs],
        out_specs=[make if isinstance(make, pl.BlockSpec) else make(a) for make, a in outputs],
        scratch_shapes=scratch,
    )
    return pl.pallas_call(
        kernel,
        grid_spec=spec,
        out_shape=[pltpu.HBM(a.shape, a.dtype) if i in kept else a for i, (_, a) in enumerate(outputs)],
        name=name,
        cost_estimate=pl.CostEstimate(flops=0, bytes_accessed=0, transcendentals=0),
        compiler_params=pltpu.CompilerParams(vmem_limit_bytes=vmem * MIB),
    )(scalar, *[a if make is in_vmem else in_place(a) for make, a in inputs])


def shape(dims, dtype):
    return jax.ShapeDtypeStruct(dims, dtype)


def in_place(array):
    if array.size * array.dtype.itemsize < MIB:
        return array
    return pltpu.with_memory_space_constraint(array, pltpu.HBM)


def add_kernel(counts, *refs):
    refs = refs[1:]
    out_refs = refs[sum(counts) :]
    for count, out_ref in zip(counts, out_refs):
        total = refs[0][...].astype(F32)
        for ref in refs[1:count]:
            total = total + ref[...].astype(F32)
        out_ref[...] = total.astype(BF16)
        refs = refs[count:]


def add_terms(sides, me):
    in_specs, out_specs, arrays, outs, lefts = [], [], [], [], []

    def place(own_bits, fixed, left):
        def index(g, me_ref):
            at = 0
            for b in own_bits:
                if b in fixed:
                    value = (me_ref[0] >> b) & 1
                    value = value if fixed[b] else 1 - value
                else:
                    value = (g >> (len(left) - 1 - left.index(b))) & 1
                at = at * 2 + value
            return (0, at, 0, 0)

        return index

    for terms, fixed in sides:
        first, bits = terms[0]
        left = [b for b in bits if b not in fixed]
        n, _, rows, cols = first.shape
        in_specs += [pl.BlockSpec((n, 1, rows, cols), place(b, fixed, left)) for _, b in terms]
        out_specs.append(pl.BlockSpec((n, 1, rows, cols), lambda g, _: (0, g, 0, 0)))
        arrays += [a for a, _ in terms]
        outs.append(shape((n, 1 << len(left), rows, cols), BF16))
        lefts.append(left)
    results = pl.pallas_call(
        partial(add_kernel, [len(terms) for terms, _ in sides]),
        grid_spec=pltpu.PrefetchScalarGridSpec(
            num_scalar_prefetch=1, grid=(1 << len(lefts[0]),), in_specs=in_specs, out_specs=out_specs
        ),
        out_shape=outs,
        name="add",
        cost_estimate=pl.CostEstimate(flops=0, bytes_accessed=0, transcendentals=0),
        compiler_params=pltpu.CompilerParams(vmem_limit_bytes=24 * MIB),
    )(me, *arrays)
    return results, lefts


def flip(array, axis, mask):
    size = lax.axis_size(axis)
    return lax.ppermute(array, axis, [(i, i ^ mask) for i in range(size)])


def tie(*arrays):
    return lax.optimization_barrier(arrays)


def pick(array, axis, index):
    return lax.dynamic_index_in_dim(array, index, axis, keepdims=False)


def outer_bits():
    bits = list(range(1, lax.axis_size("dp").bit_length() - 1))
    return bits, (bits, bits[::-1])


def share_of():
    me = lax.axis_index("dp")
    return (me & 1) * (lax.axis_size("dp") // 2) + (me >> 1)


def flip_core(arrays):
    form = (arrays[0].shape[0], -1, arrays[0].shape[-1])
    got = flip(jnp.stack([a.reshape(form) for a in arrays]), "dp", 1)
    return [got[i].reshape(a.shape) for i, a in enumerate(arrays)]


class Gather:
    def __init__(self, pair):
        self.bits, self.orders = outer_bits()
        self.steps = len(self.bits)
        self.n, _, self.cols = pair[0].shape
        self.held = [
            a.reshape((self.n,) + (1,) * self.steps + a.shape[1:]) for a in pair
        ]

    def send(self, step):
        return [flip(h, "dp", 1 << order[step]) for h, order in zip(self.held, self.orders)]

    def merge(self, step, mine, theirs):
        me = lax.axis_index("dp")
        merged = []
        for one, two, order in zip(mine, theirs, self.orders):
            bit = order[step]
            low = ((me >> bit) & 1) == 0
            parts = [jnp.where(low, one, two), jnp.where(low, two, one)]
            merged.append(jnp.concatenate(parts, axis=1 + self.steps - bit))
        return merged

    def take(self, step, got):
        self.held = self.merge(step, self.held, got)

    def halves(self):
        return self.flat(self.held)

    def flat(self, arrays):
        return [a.reshape(self.n, -1, self.cols) for a in arrays]


class Reduce:
    def __init__(self, keeps, gots):
        self.bits, self.orders = outer_bits()
        self.steps = len(self.bits)
        self.me = lax.axis_index("dp").astype(jnp.int32).reshape(1)
        high_first = self.bits[::-1]
        n, rows, cols = keeps[0].shape
        form = (n, 1 << self.steps, rows >> self.steps, cols)
        self.terms = [
            [(k.reshape(form), high_first), (g.reshape(form), high_first)]
            for k, g in zip(keeps, gots)
        ]
        self.left = [None, None]

    def pack(self, step):
        sides = []
        for terms, order in zip(self.terms, self.orders):
            fixed = {b: True for b in order[:step]}
            fixed[order[step]] = False
            sides.append((terms, fixed))
        sends, self.left = add_terms(sides, self.me)
        return sends

    def send(self, step, packs):
        return [flip(p, "dp", 1 << order[step]) for p, order in zip(packs, self.orders)]

    def take(self, got):
        for side in range(2):
            self.terms[side].append((got[side], self.left[side]))

    def finish(self):
        fixed = {b: True for b in self.bits}
        sums, _ = add_terms([(t, fixed) for t in self.terms], self.me)
        return [a[:, 0] for a in sums]


def gather_stack(piece):
    bits, _ = outer_bits()
    order = list(range(1 << len(bits)))
    if len(order) <= 4:
        order = order[:1] + order[:0:-1]
        return [piece] + [flip(piece, "dp", 2 * k) for k in order[1:]], order
    held = piece[None]
    for bit in bits:
        held = jnp.concatenate([held, flip(held, "dp", 1 << bit)])
    return [held[k] for k in order], order


def add_parts(*parts):
    total = parts[0].astype(F32)
    for part in parts[1:]:
        total = total + part.astype(F32)
    return total.astype(BF16)


def shards(
    tokens,
    word_len,
    region_count,
    w_qkv,
    qv_bias,
    w_out,
    out_bias,
    norm1_gain,
    norm1_bias,
    w_in,
    in_bias,
    w_down,
    down_bias,
    norm2_gain,
    norm2_bias,
    cotangent,
):
    mp = lax.axis_size("mp")
    dp = lax.axis_size("dp")
    mi = lax.axis_index("mp")
    width = tokens.shape[2]
    rows_local = tokens.shape[1]
    slots = rows_local * mp
    pairs = tokens.shape[0] // mp
    rows = pairs * slots
    cols = w_qkv.shape[2]
    units = w_in.shape[1]
    half_units = units // 2
    order = jnp.arange(mp) ^ mi
    here = jnp.stack([lax.axis_index("dp") & 1, mi, lax.axis_index("dp") >> 1]).astype(jnp.int32)
    share = share_of()

    turned = w_qkv.transpose(0, 2, 1).reshape(3 * cols, width)
    own_qk = turned[: 2 * cols]
    own_vo = jnp.concatenate([turned[2 * cols :], w_out], axis=0)
    att_part, ffn_part = 2 * cols // dp, units // dp
    first = share * att_part
    rows_of = lambda array, start, size: lax.dynamic_slice_in_dim(array, start, size, 0)
    vo_piece = jnp.where(
        first < cols,
        rows_of(turned, 2 * cols + jnp.minimum(first, cols - att_part), att_part),
        rows_of(w_out, jnp.maximum(first - cols, 0), att_part),
    )

    def row_blocks(array):
        blocks = array.reshape((mp, pairs) + array.shape[1:])
        return [pick(blocks, 0, mi ^ k) for k in range(mp)]

    def join(blocks):
        return jnp.concatenate(blocks, axis=1).reshape(rows, width)

    fill = lambda v: jnp.pad(v, ((0, 0), (0, width - v.shape[1])))
    small = jnp.concatenate([fill(qv_bias), in_bias.reshape(1, units), jnp.zeros((5, width), BF16)])
    att_send = jnp.concatenate([rows_of(turned, first, att_part), vo_piece], axis=0)
    ffn_send = jnp.concatenate(
        [rows_of(w_in.T, share * ffn_part, ffn_part), rows_of(w_down, share * ffn_part, ffn_part), small],
        axis=0,
    )
    tok = row_blocks(tokens)
    cot = row_blocks(cotangent)
    vectors = jnp.stack(
        [out_bias, norm1_gain, norm1_bias, down_bias, norm2_gain, norm2_bias, out_bias, out_bias]
    ).astype(F32)
    words = lax.dynamic_slice_in_dim(word_len, mi * pairs, pairs, 0)
    regions = lax.dynamic_slice_in_dim(region_count, mi * pairs, pairs, 0)
    slot_index = (order[:, None] * rows_local + jnp.arange(rows_local)[None, :]).reshape(-1)
    key_valid = jnp.where(
        slot_index[None, :] < WORDS,
        slot_index[None, :] < words[:, None],
        slot_index[None, :] - WORDS < regions[:, None],
    ).astype(F32)[:, None, :]

    att_got = {k: flip(att_send, "mp", k) for k in (3, 2, 1)}
    att_got = [att_got[k] for k in (1, 2, 3)]
    att_got, ffn_send, tok, vectors, key_valid, here, own_qk, own_vo = tie(
        att_got, ffn_send, tok, vectors, key_valid, here, own_qk, own_vo
    )
    att = Gather(
        [
            jnp.stack([g[:att_part] for g in att_got]),
            jnp.stack([g[att_part:] for g in att_got]),
        ]
    )
    ffn_two = flip(ffn_send, "mp", 2)
    got = att.send(0)
    tok_one = flip(tok[1], "mp", 1)
    ffn_two, got, tok_one, ffn_send, tok = tie(ffn_two, got, tok_one, ffn_send, tok)
    for step in range(1, att.steps):
        att.take(step - 1, got)
        got = att.send(step)
        if step == 1:
            ffn_odd = flip(jnp.stack([ffn_send, ffn_two]), "mp", 1)
            tok_three = flip(tok[3], "mp", 3)
        got, ffn_odd, tok_three, tok = tie(got, ffn_odd, tok_three, tok)
    att.take(att.steps - 1, got)
    ffn_got = [ffn_odd[0], ffn_two, ffn_odd[1]]
    ffn = Gather(
        [
            jnp.stack([g[:ffn_part] for g in ffn_got]),
            jnp.stack([g[ffn_part : 2 * ffn_part] for g in ffn_got]),
        ]
    )
    got = ffn.send(0)
    qk_one, vo_one = att.halves()
    qk_two, vo_two = flip(qk_one, "dp", 1), flip(vo_one, "dp", 1)
    tok_two = flip(tok[2], "mp", 2)
    smalls = jnp.stack([small] + [g[2 * ffn_part :] for g in ffn_got]).astype(F32)
    got, qk_two, vo_two, tok_two, cot, smalls = tie(got, qk_two, vo_two, tok_two, cot, smalls)
    heads_low = shape((mp, rows, cols), BF16)
    low_shape = shape((rows, width), BF16)
    rows_shape = shape((rows, width), F32)
    sums_shape = shape((8, width), F32)
    block_shape = shape((pairs, rows_local, width), BF16)
    for step in range(1, ffn.steps):
        ffn.take(step - 1, got)
        got = ffn.send(step)
        if step < ffn.steps - 1:
            got = tie(*got)
    early = flip_core(ffn.held)
    early, cot, x = tie(early, cot, join([tok[0], tok_one, tok_two, tok_three]))
    cot_blocks = [cot[0]] + [flip(cot[k], "mp", k) for k in range(1, mp)]
    later = lambda a: pl.BlockSpec((1,) + a.shape[1:], lambda s, h: (jnp.clip(s - 1, 0, mp - 2), 0, 0))
    head_args = [
        (whole, own_qk),
        (later, qk_one),
        (later, qk_two),
        (whole, own_vo),
        (later, vo_one),
        (later, vo_two),
    ]
    q, k, v, weights, context, hidden_low, normed_one, scale_one = call(
        partial(attention_kernel, pairs),
        mp,
        "attention",
        24,
        [
            (whole, x),
            *head_args,
            (per_step, smalls),
            (whole, key_valid),
            (whole, vectors),
        ],
        [
            (per_step, heads_low),
            (per_step, heads_low),
            (per_step, heads_low),
            (per_step, shape((mp, pairs, cols // HEAD * slots, slots), F32)),
            (per_step, heads_low),
            (whole, low_shape),
            (whole, rows_shape),
            (whole, shape((rows, 1), F32)),
        ],
        [pltpu.VMEM((rows, width), F32)],
        here,
        range(5),
    )
    got, early, hidden_low, cot_blocks = tie(got, early, hidden_low, cot_blocks)
    ffn.take(ffn.steps - 1, got)
    in_one, down_one = ffn.halves()
    late = [flip(g, "dp", 1) for g in got]
    late, hidden_low = tie(late, hidden_low)
    in_two, down_two = ffn.flat(ffn.merge(ffn.steps - 1, early, late))

    half = shape((mp, half_units, width), BF16)
    pre_shape = shape((mp, rows, units), BF16)
    vmem = lambda a: pltpu.VMEM(a.shape, a.dtype)
    results = call(
        partial(ffn_kernel, mp),
        1,
        "ffn",
        42,
        [
            (where_it_is, hidden_low),
            (where_it_is, normed_one),
            (where_it_is, w_in),
            (in_vmem, in_one),
            (in_vmem, in_two),
            (where_it_is, w_down),
            (in_vmem, down_one),
            (in_vmem, down_two),
            (whole, smalls),
            (whole, vectors),
            *[(where_it_is, c) for c in cot_blocks],
        ],
        [
            *[(whole, block_shape)] * mp,
            (where_it_is, rows_shape),
            (where_it_is, pre_shape),
            (where_it_is, half),
            (where_it_is, half),
            (where_it_is, half),
            (where_it_is, half),
            (whole, shape((mp, 1, units), F32)),
            (whole, sums_shape),
        ],
        [
            vmem(low_shape),
            vmem(rows_shape),
            pltpu.VMEM((width, units), BF16),
            pltpu.VMEM((units, width), BF16),
            pltpu.VMEM((mp,) + block_shape.shape, BF16),
            vmem(pre_shape),
            pltpu.VMEM(pre_shape.shape, F32),
            vmem(rows_shape),
            vmem(rows_shape),
            vmem(pre_shape),
            vmem(half),
            vmem(half),
            vmem(half),
            vmem(half),
            vmem(low_shape),
            pltpu.SemaphoreType.DMA((3 + 1 + mp + 1 + 5 * mp,)),
        ],
        here,
        range(mp + 6),
    )
    out_blocks = results[:mp]
    delta_ffn, pre_grad, in_keep, in_send, down_keep, down_send, sum_in, sums_two = results[mp:]
    in_got, down_got = flip(in_send, "dp", 1), flip(down_send, "dp", 1)
    delta_attn, attn_low, sums_one = call(
        partial(ffn_back_kernel, mp),
        1,
        "ffn_back",
        18,
        [
            (where_it_is, pre_grad),
            (where_it_is, w_in),
            (in_vmem, in_one),
            (in_vmem, in_two),
            (where_it_is, delta_ffn),
            (where_it_is, normed_one),
            (whole, scale_one),
            (whole, vectors),
        ],
        [(where_it_is, rows_shape), (whole, low_shape), (whole, sums_shape)],
        [
            vmem(pre_shape),
            pltpu.VMEM((width, units), BF16),
            vmem(rows_shape),
            vmem(rows_shape),
            vmem(rows_shape),
            pltpu.SemaphoreType.DMA((mp + 1 + 2 + 1,)),
        ],
        here,
        (0,),
    )
    in_got, down_got, out_blocks, attn_low = tie(in_got, down_got, out_blocks, attn_low)
    ffn = Reduce([in_keep, down_keep], [in_got, down_got])
    packs = ffn.pack(0)
    packs, attn_low, out_blocks = tie(packs, attn_low, out_blocks)
    got = ffn.send(0, packs)
    out_got = [out_blocks[0]] + [flip(out_blocks[k], "mp", k) for k in range(1, mp)]
    small_half = shape((mp, cols, width), BF16)
    results = call(
        partial(attention_back_kernel, pairs),
        mp,
        "attention_back",
        28,
        [
            (whole, x),
            (whole, attn_low),
            (whole, delta_attn),
            *head_args,
            (per_step, q),
            (per_step, k),
            (per_step, v),
            (per_step, weights),
            (per_step, context),
            (whole, sums_one),
            (whole, sums_two),
            (whole, sum_in),
        ],
        [
            (per_step, small_half),
            (per_step, small_half),
            (
                pl.BlockSpec((2, 1, cols, width), lambda s, h: (0, s, 0, 0)),
                shape((2, mp, cols, width), BF16),
            ),
            (whole, shape((-(-(6 + 2 * mp) // 8) * 8, width), F32)),
            *[(whole, block_shape)] * mp,
        ],
        [pltpu.VMEM((rows, cols), BF16)] * 3 + [pltpu.VMEM((rows, width), F32)],
        here,
        (0, 1, 2) + tuple(range(4, 4 + mp)),
    )
    qk_keep, vo_keep, att_send, sums = results[:4]
    row_sends = results[4:]
    got, out_got, att_send, row_sends, sums = tie(got, out_got, att_send, row_sends, sums)
    place = lambda blocks, dtype: call(
        partial(place_kernel, pairs),
        1,
        "place",
        16,
        [(whole, b) for b in blocks],
        [(whole, shape((mp * pairs, rows_local, width), dtype))],
        [],
        here,
    )[0]
    for step in range(1, ffn.steps):
        ffn.take(got)
        packs = ffn.pack(step)
        got = ffn.send(step, packs)
        if step == 1:
            att_got = flip(att_send, "dp", 1)
            row_three = flip(row_sends[3], "mp", 3)
            sums_got = flip(sums, "mp", 2)
            att = Reduce([qk_keep, vo_keep], [att_got[0], att_got[1]])
            att_packs = att.pack(0)
            layer_out = place(out_got, BF16)
        got, att_packs, row_three, sums_got, row_sends, layer_out = tie(
            got, att_packs, row_three, sums_got, row_sends, layer_out
        )
    sums = sums + sums_got
    ffn.take(got)
    ffn_parts = ffn.finish()
    ffn_odd = jnp.concatenate([p[1::2] for p in ffn_parts], axis=1)
    ffn_even = jnp.concatenate([p[0::2] for p in ffn_parts], axis=1)
    got = att.send(0, att_packs)
    ffn_got = flip(ffn_odd, "mp", 1)
    sums_got = flip(sums, "dp", 2)
    row_two = flip(row_sends[2], "mp", 2)
    got, ffn_got, sums_got, row_two, row_sends = tie(got, ffn_got, sums_got, row_two, row_sends)
    sums = sums + sums_got
    for mask in [1 << b for b in range(2, dp.bit_length() - 2)]:
        sums = sums + flip(sums, "dp", mask)
    ffn_two = add_parts(ffn_even[1], ffn_got[1])
    for step in range(1, att.steps):
        att.take(got)
        packs = att.pack(step)
        got = att.send(step, packs)
        if step == 1:
            ffn_last = flip(ffn_two, "mp", 2)
            row_one = flip(row_sends[1], "mp", 1)
            sums_got = flip(sums, "dp", dp // 2)
        got, ffn_last, row_one, sums_got, row_sends = tie(got, ffn_last, row_one, sums_got, row_sends)
    att.take(got)
    sums = sums + sums_got
    att_parts = att.finish()
    att_odd = jnp.concatenate([p[1::2] for p in att_parts], axis=1)
    att_even = jnp.concatenate([p[0::2] for p in att_parts], axis=1)
    ffn_sum = add_parts(ffn_even[0], ffn_got[0], ffn_last)
    ffn = Gather([ffn_sum[None, :ffn_part], ffn_sum[None, ffn_part:]])
    ffn.held, att_odd, att_even, sums = tie(ffn.held, att_odd, att_even, sums)
    got = ffn.send(0)
    att_got = flip(att_odd, "mp", 1)
    sums_got = flip(sums, "dp", 1)
    got, att_got, sums_got, row_one = tie(got, att_got, sums_got, row_one)
    grad_input = place([row_sends[0], row_one, row_two, row_three], F32)
    sums = sums + sums_got
    att_two = add_parts(att_even[1], att_got[1])
    for step in range(1, ffn.steps):
        ffn.take(step - 1, got)
        got = ffn.send(step)
        if step == 1:
            att_last = flip(att_two, "mp", 2)
            sums_got = flip(sums, "mp", 1)
        got, att_last, sums_got, grad_input = tie(got, att_last, sums_got, grad_input)
    ffn.take(ffn.steps - 1, got)
    sums = sums + sums_got
    att_sum = add_parts(att_even[0], att_got[0], att_last)
    ffn_halves = ffn.halves()
    core_got = flip_core(ffn_halves)
    att_mine, att_order = gather_stack(att_sum)
    grad_in, grad_down = call(
        unit_grads_kernel,
        1,
        "unit_grads",
        24,
        [(whole, a) for a in ffn_halves + core_got],
        [(whole, shape((width, units), F32)), (whole, shape((units, width), F32))],
        [],
        here,
    )
    att_mine, grad_in, grad_down, sums = tie(att_mine, grad_in, grad_down, sums)
    att_mine = jnp.stack(att_mine)
    att_other = flip(att_mine, "dp", 1)
    grad_qkv, grad_out = call(
        partial(head_grads_kernel, att_order),
        1,
        "head_grads",
        24,
        [(whole, att_mine), (whole, att_other)],
        [
            (whole, shape((3, cols // att_part, att_part, width), F32)),
            (whole, shape((cols // att_part, att_part, width), F32)),
        ],
        [],
        here,
    )
    sum_in_bias = lax.dynamic_index_in_dim(sums, 6 + mi, 0, keepdims=False)
    sum_qv = lax.dynamic_index_in_dim(sums, 6 + mp + mi, 0, keepdims=False)
    sum_qv = jnp.stack([sum_qv[:cols], sum_qv[2 * cols : 3 * cols]])
    return (
        layer_out,
        grad_input,
        grad_qkv.reshape(3, cols, width).transpose(0, 2, 1),
        sum_qv,
        grad_out.reshape(cols, width),
        sums[0],
        sums[1],
        sums[2],
        grad_in,
        sum_in_bias,
        grad_down,
        sums[5],
        sums[3],
        sums[4],
    )


def solution(mesh):
    in_specs = (
        P("dp", "mp", None),
        P("dp"),
        P("dp"),
        P(None, None, "mp"),
        P(None, "mp"),
        P("mp", None),
        P(),
        P(),
        P(),
        P(None, "mp"),
        P("mp"),
        P("mp", None),
        P(),
        P(),
        P(),
        P("dp", "mp", None),
    )
    out_specs = (
        P("dp", "mp", None),
        P("dp", "mp", None),
        P(None, None, "mp"),
        P(None, "mp"),
        P("mp", None),
        P(),
        P(),
        P(),
        P(None, "mp"),
        P("mp"),
        P("mp", None),
        P(),
        P(),
        P(),
    )
    return jax.shard_map(shards, mesh=mesh, in_specs=in_specs, out_specs=out_specs, check_vma=False)
```

```python
from functools import partial

import jax
import jax.numpy as jnp
from jax import lax
from jax.experimental import pallas as pl
from jax.experimental.pallas import tpu as pltpu
from jax.sharding import PartitionSpec as P

HEAD = 64
WORDS = 60
EPSILON = 1e-05
SQRT_HALF = 0.7071067811865476
DENSITY = 0.3989422804014327
F32 = jnp.float32
BF16 = jnp.bfloat16
MIB = 1024 * 1024


def dot(one, two, one_axis, two_axis):
    return lax.dot_general(
        one, two, (((one_axis,), (two_axis,)), ((), ())), preferred_element_type=F32
    )


def normalize(total, gain, shift):
    centered = total - jnp.mean(total, axis=-1, keepdims=True)
    inv_scale = lax.rsqrt(jnp.mean(centered * centered, axis=-1, keepdims=True) + EPSILON)
    normed = centered * inv_scale
    return normed * gain + shift, normed, inv_scale


def normalize_back(upstream, normed, inv_scale, gain):
    scaled_up = upstream * gain
    mean_one = jnp.mean(scaled_up, axis=-1, keepdims=True)
    mean_two = jnp.mean(scaled_up * normed, axis=-1, keepdims=True)
    return inv_scale * (scaled_up - mean_one - normed * mean_two)


def column_sum(array):
    return jnp.sum(array, axis=0, keepdims=True)


def head_stack(array, heads):
    head = lax.broadcasted_iota(jnp.int32, array.shape, 1) // HEAD
    zero = jnp.zeros_like(array)
    return jnp.concatenate([jnp.where(head == h, array, zero) for h in range(heads)], axis=0)


def head_pick(stacked, heads):
    rows = stacked.shape[0] // heads
    head = lax.broadcasted_iota(jnp.int32, (rows, stacked.shape[1]), 1) // HEAD
    total = stacked[:rows]
    for h in range(1, heads):
        total = jnp.where(head == h, stacked[h * rows : (h + 1) * rows], total)
    return total


def head_weights(first, here_ref, own_ref, one_ref, two_ref):
    low = here_ref[0] == 0
    half = one_ref.shape[1]
    one, two = one_ref[0], two_ref[0]
    return (
        jnp.where(first, own_ref[:half], jnp.where(low, one, two)),
        jnp.where(first, own_ref[half:], jnp.where(low, two, one)),
    )


def attention_kernel(
    pairs, here_ref, x_ref, own_qk, qk_one, qk_two, own_vo, vo_one, vo_two, small_ref, valid_ref, vectors_ref,
    q_ref, k_ref, v_ref, weights_ref, context_ref, low_ref, normed_ref, scale_ref, total_ref,
):
    step = pl.program_id(0)
    cols = q_ref.shape[2]
    heads = cols // HEAD
    slots = x_ref.shape[0] // pairs
    x = x_ref[...]
    w_q, w_k = head_weights(step == 0, here_ref, own_qk, qk_one, qk_two)
    w_v, w_o = head_weights(step == 0, here_ref, own_vo, vo_one, vo_two)
    q_ref[0] = (dot(x, w_q, 1, 1) + small_ref[0, 0:1, :cols]).astype(BF16)
    k_ref[0] = dot(x, w_k, 1, 1).astype(BF16)
    v_ref[0] = (dot(x, w_v, 1, 1) + small_ref[0, 1:2, :cols]).astype(BF16)
    for p in range(pairs):
        rows = slice(p * slots, (p + 1) * slots)
        scores = dot(head_stack(q_ref[0, rows], heads), k_ref[0, rows], 1, 1) * HEAD ** (-0.5)
        scores = jnp.where(valid_ref[p] > 0.5, scores, -1e30)
        exp_scores = jnp.exp(scores - jnp.max(scores, axis=-1, keepdims=True))
        weights = exp_scores / jnp.sum(exp_scores, axis=-1, keepdims=True)
        weights_ref[0, p] = weights
        mixed = dot(weights.astype(BF16), v_ref[0, rows], 1, 0)
        context_ref[0, rows] = head_pick(mixed, heads).astype(BF16)
    branch = dot(context_ref[0], w_o, 1, 0)

    @pl.when(step == 0)
    def _():
        total_ref[...] = branch

    @pl.when(step > 0)
    def _():
        total_ref[...] += branch

    @pl.when(step == pl.num_programs(0) - 1)
    def _():
        first_sum = total_ref[...] + vectors_ref[0:1] + x.astype(F32)
        hidden, normed, scale = normalize(first_sum, vectors_ref[1:2], vectors_ref[2:3])
        low_ref[...] = hidden.astype(BF16)
        normed_ref[...] = normed
        scale_ref[...] = scale


def blocks_of(units):
    size = min(256, units)
    return [(start, min(start + size, units)) for start in range(0, units, size)]


class Copies:
    def __init__(self, sems):
        self.sems, self.used = sems, 0

    def start(self, *pairs):
        copies = []
        for source, target in pairs:
            copies.append(pltpu.make_async_copy(source, target, self.sems.at[self.used]))
            copies[-1].start()
            self.used += 1
        return copies


def wait_all(copies):
    for copy in copies:
        copy.wait()


def halves_of(half, start, stop):
    parts = []
    if start < half:
        parts.append((0, start, min(stop, half)))
    if stop > half:
        parts.append((1, max(start - half, 0), stop - half))
    return parts


def own_units(core, half, which, first, last):
    side = core if which == 0 else 1 - core
    return pl.ds(pl.multiple_of(side * half + first, 128), last - first)


def join_rows(refs):
    pairs = refs[0].shape[0]
    return jnp.concatenate([ref[p].astype(F32) for p in range(pairs) for ref in refs], axis=0)


def leave_rows(array, refs):
    pairs, rows = refs[0].shape[:2]
    for p in range(pairs):
        for j, ref in enumerate(refs):
            start = (p * len(refs) + j) * rows
            ref[p] = array[start : start + rows].astype(BF16)


def ffn_kernel(
    count, here_ref, low_hbm, normed_hbm, w_in_hbm, in_one, in_two, w_down_hbm, down_one, down_two, small_ref,
    vectors_ref, *refs,
):
    cot_hbm, out_refs = refs[:count], refs[count : 2 * count]
    (
        delta_hbm, pre_grad_hbm, in_keep_hbm, in_send_hbm, down_keep_hbm, down_send_hbm, sum_in_ref, sums_ref,
        low_ref, normed_ref, w_in_ref, w_down_ref, cot_ref, act_ref, slope_ref, total_ref, delta_ref, pre_grad_ref,
        in_keep_ref, in_send_ref, down_keep_ref, down_send_ref, ffn_low_ref, sems,
    ) = refs[2 * count :]
    core = here_ref[0]
    half = in_one.shape[1]
    copies_ = Copies(sems)
    start, wait = copies_.start, wait_all

    halves = partial(halves_of, half)
    own = partial(own_units, core, half)

    def down_rows(slot, first, start_, stop):
        if first:
            parts = [w_down_ref[own(w, a, b)] for w, a, b in halves(start_, stop)]
        else:
            parts = [(down_one, down_two)[w][slot - 1, a:b] for w, a, b in halves(start_, stop)]
        return jnp.concatenate(parts, axis=0)

    def forward(slot, mine):
        low = low_ref[...]
        branch = None
        for first, last in blocks_of(2 * half):
            parts = halves(first, last)
            if mine:
                w_in = jnp.concatenate([w_in_ref[:, own(*p)] for p in parts], axis=1)
                pre_act = dot(low, w_in, 1, 0)
            else:
                w_in = jnp.concatenate([(in_one, in_two)[w][slot - 1, a:b] for w, a, b in parts], axis=0)
                pre_act = dot(low, w_in, 1, 1)
            bias = jnp.concatenate([small_ref[slot, 2:3, own(*p)] for p in parts], axis=1)
            pre_act = pre_act + bias
            share = 0.5 * (1.0 + lax.erf(pre_act * SQRT_HALF))
            act = (pre_act * share).astype(BF16)
            act_ref[slot, :, first:last] = act
            slope_ref[slot, :, first:last] = share + pre_act * (DENSITY * jnp.exp(-0.5 * pre_act * pre_act))
            term = dot(act, down_rows(slot, mine, first, last), 1, 0)
            branch = term if branch is None else branch + term
        total_ref[...] += branch

    low_copies = start((low_hbm, low_ref))
    own_copies = start((w_in_hbm, w_in_ref), (w_down_hbm, w_down_ref))
    later_copies = start((normed_hbm, normed_ref), *[(cot_hbm[k], cot_ref.at[k]) for k in range(count)])
    total_ref[...] = jnp.zeros_like(total_ref)
    wait(low_copies)
    for slot in range(1, count):
        forward(slot, False)
    wait(own_copies)
    forward(0, True)
    wait(later_copies)

    hidden = normed_ref[...] * vectors_ref[1:2] + vectors_ref[2:3]
    second = total_ref[...] + vectors_ref[3:4] + hidden
    gain = vectors_ref[4:5]
    output, normed, scale = normalize(second, gain, vectors_ref[5:6])
    leave_rows(output, out_refs)
    upstream = join_rows([cot_ref.at[k] for k in range(count)])
    delta = normalize_back(upstream, normed, scale, gain)
    delta_ref[...] = delta
    leaving = start((delta_ref, delta_hbm))
    sums_ref[...] = jnp.zeros_like(sums_ref)
    sums_ref[0:1] = column_sum(upstream * normed)
    sums_ref[1:2] = column_sum(upstream)
    sums_ref[2:3] = column_sum(delta)
    ffn_low_ref[...] = delta.astype(BF16)
    leavers = (
        (pre_grad_ref, pre_grad_hbm),
        (down_send_ref, down_send_hbm),
        (down_keep_ref, down_keep_hbm),
        (in_send_ref, in_send_hbm),
        (in_keep_ref, in_keep_hbm),
    )
    base = copies_.used

    def leave(slot, i):
        source, target = leavers[i]
        return pltpu.make_async_copy(source.at[slot], target.at[slot], sems.at[base + len(leavers) * slot + i])

    def backward(slot, mine):
        ffn_low, low = ffn_low_ref[...], low_ref[...]
        for first, last in blocks_of(2 * half):
            act_grad = dot(ffn_low, down_rows(slot, mine, first, last), 1, 1)
            pre_grad_ref[slot, :, first:last] = (act_grad * slope_ref[slot, :, first:last]).astype(BF16)
        leave(slot, 0).start()
        down_send_ref[slot] = dot(act_ref[slot, :, half:], ffn_low, 0, 0).astype(BF16)
        leave(slot, 1).start()
        down_keep_ref[slot] = dot(act_ref[slot, :, :half], ffn_low, 0, 0).astype(BF16)
        leave(slot, 2).start()
        one, two = pre_grad_ref[slot, :, :half], pre_grad_ref[slot, :, half:]
        in_send_ref[slot] = dot(two, low, 0, 0).astype(BF16)
        leave(slot, 3).start()
        in_keep_ref[slot] = dot(one, low, 0, 0).astype(BF16)
        leave(slot, 4).start()
        natural = slot ^ here_ref[1]
        sum_in_ref[natural, :, own(0, 0, half)] = column_sum(one.astype(F32))
        sum_in_ref[natural, :, own(1, 0, half)] = column_sum(two.astype(F32))

    backward(0, True)
    lax.fori_loop(1, count, lambda slot, _: (backward(slot, False), 0)[1], 0)
    wait(leaving)
    for slot in range(count):
        for i in range(len(leavers)):
            leave(slot, i).wait()


def ffn_back_kernel(
    count, here_ref, pre_grad_hbm, w_in_hbm, in_one, in_two, delta_hbm, normed_hbm, scale_ref, vectors_ref,
    delta_attn_hbm, attn_low_ref, sums_ref, pre_grad_ref, w_in_ref, delta_ref, normed_ref, total_ref, sems,
):
    core = here_ref[0]
    half = in_one.shape[1]
    copies = Copies(sems)
    base = copies.used
    copies.used += count

    def load(slot):
        return pltpu.make_async_copy(pre_grad_hbm.at[slot], pre_grad_ref.at[slot], sems.at[base + slot])

    for slot in list(range(1, count)) + [0]:
        load(slot).start()
    w_copies = copies.start((w_in_hbm, w_in_ref))
    norm_copies = copies.start((delta_hbm, delta_ref), (normed_hbm, normed_ref))

    def add(slot, mine):
        load(slot).wait()
        branch = None
        for a, b in blocks_of(2 * half):
            pre_grad = pre_grad_ref[slot, :, a:b]
            parts = halves_of(half, a, b)
            if mine:
                w_in = jnp.concatenate([w_in_ref[:, own_units(core, half, *p)] for p in parts], axis=1)
                term = dot(pre_grad, w_in, 1, 1)
            else:
                w_in = jnp.concatenate([(in_one, in_two)[w][slot - 1, c:d] for w, c, d in parts], axis=0)
                term = dot(pre_grad, w_in, 1, 0)
            branch = term if branch is None else branch + term
        total_ref[...] += branch

    total_ref[...] = jnp.zeros_like(total_ref)
    lax.fori_loop(1, count, lambda slot, _: (add(slot, False), 0)[1], 0)
    wait_all(w_copies)
    add(0, True)
    wait_all(norm_copies)
    hidden_grad = total_ref[...] + delta_ref[...]
    normed = normed_ref[...]
    delta = normalize_back(hidden_grad, normed, scale_ref[...], vectors_ref[1:2])
    total_ref[...] = delta
    leaving = copies.start((total_ref, delta_attn_hbm))
    attn_low_ref[...] = delta.astype(BF16)
    sums_ref[...] = jnp.zeros_like(sums_ref)
    sums_ref[0:1] = column_sum(delta)
    sums_ref[1:2] = column_sum(hidden_grad * normed)
    sums_ref[2:3] = column_sum(hidden_grad)
    wait_all(leaving)


def attention_back_kernel(
    pairs, here_ref, x_ref, attn_low_ref, delta_ref, own_qk, qk_one, qk_two, own_vo, vo_one, vo_two, q_ref, k_ref,
    v_ref, weights_ref, context_ref, sums_one_ref, sums_two_ref, sum_in_ref,
    qk_keep_ref, vo_keep_ref, send_ref, sums_ref, *refs,
):
    step = pl.program_id(0)
    shards_ = pl.num_programs(0)
    out_refs = refs[:shards_]
    dq_ref, dk_ref, dv_ref, total_ref = refs[shards_:]

    @pl.when(step == 0)
    def _():
        total_ref[...] = delta_ref[...]
        sums_ref[...] = jnp.zeros_like(sums_ref)
        sums_ref[0:3] = sums_one_ref[0:3]
        sums_ref[3:6] = sums_two_ref[0:3]
        for j in range(shards_):
            sums_ref[6 + j : 7 + j] = sum_in_ref[j]

    core = here_ref[0]
    cols = q_ref.shape[2]
    heads = cols // HEAD
    slots = x_ref.shape[0] // pairs
    scale = HEAD ** (-0.5)
    x = x_ref[...]
    attn_low = attn_low_ref[...]
    w_q, w_k = head_weights(step == 0, here_ref, own_qk, qk_one, qk_two)
    w_v, w_o = head_weights(step == 0, here_ref, own_vo, vo_one, vo_two)
    context_grad = dot(attn_low, w_o, 1, 1).astype(BF16)
    grad_out = dot(context_ref[0], attn_low, 0, 0).astype(BF16)
    for p in range(pairs):
        rows = slice(p * slots, (p + 1) * slots)
        up = head_stack(context_grad[rows], heads)
        weights = weights_ref[0, p]
        prob_grad = dot(up, v_ref[0, rows], 1, 1)
        inner = jnp.sum(prob_grad * weights, axis=-1, keepdims=True)
        score_grad = (weights * (prob_grad - inner)).astype(BF16)
        dv_ref[rows] = dot(weights.astype(BF16), up, 0, 0).astype(BF16)
        query_grad = head_pick(dot(score_grad, k_ref[0, rows], 1, 0), heads)
        dq_ref[rows] = (query_grad * scale).astype(BF16)
        key_grad = dot(score_grad, head_stack(q_ref[0, rows], heads), 0, 0)
        dk_ref[rows] = (key_grad * scale).astype(BF16)
    dq, dk, dv = dq_ref[...], dk_ref[...], dv_ref[...]
    row = pl.ds(6 + shards_ + (step ^ here_ref[1]), 1)
    sums_ref[row, :cols] = column_sum(dq.astype(F32))
    sums_ref[row, 2 * cols : 3 * cols] = column_sum(dv.astype(F32))
    grad_q = dot(dq, x, 0, 0).astype(BF16)
    grad_k = dot(dk, x, 0, 0).astype(BF16)
    grad_v = dot(dv, x, 0, 0).astype(BF16)

    @pl.when(core == 0)
    def _():
        qk_keep_ref[0], send_ref[0, 0] = grad_q, grad_k
        vo_keep_ref[0], send_ref[1, 0] = grad_v, grad_out

    @pl.when(core != 0)
    def _():
        qk_keep_ref[0], send_ref[0, 0] = grad_k, grad_q
        vo_keep_ref[0], send_ref[1, 0] = grad_out, grad_v

    total_ref[...] += dot(dq, w_q, 1, 0) + dot(dk, w_k, 1, 0) + dot(dv, w_v, 1, 0)

    @pl.when(step == shards_ - 1)
    def _():
        leave_rows(total_ref[...], out_refs)


def place_kernel(pairs, here_ref, *refs):
    out_ref = refs[-1]
    for k, ref in enumerate(refs[:-1]):
        out_ref[pl.ds((here_ref[1] ^ k) * pairs, pairs)] = ref[...].astype(out_ref.dtype)


def head_grads_kernel(order, here_ref, mine_ref, other_ref, grad_qkv_ref, grad_out_ref):
    core = here_ref[0]
    part = grad_out_ref.shape[1]
    for side, ref in ((core, mine_ref), (1 - core, other_ref)):
        for k, index in enumerate(order):
            place = here_ref[2] ^ index
            piece = ref[k].astype(F32)
            grad_qkv_ref[side, place] = piece[:part]

            @pl.when(side == 0)
            def _():
                grad_qkv_ref[2, place] = piece[part:]

            @pl.when(side != 0)
            def _():
                grad_out_ref[place] = piece[part:]


def unit_grads_kernel(here_ref, in_ref, down_ref, in_other, down_other, grad_in_ref, grad_down_ref):
    half = in_ref.shape[1]
    mine = pl.multiple_of(here_ref[0] * half, half)
    other = pl.multiple_of((1 - here_ref[0]) * half, half)
    grad_in_ref[:, pl.ds(mine, half)] = in_ref[0].astype(F32).T
    grad_in_ref[:, pl.ds(other, half)] = in_other[0].astype(F32).T
    grad_down_ref[pl.ds(mine, half)] = down_ref[0].astype(F32)
    grad_down_ref[pl.ds(other, half)] = down_other[0].astype(F32)


def whole(array):
    return pl.BlockSpec(array.shape, lambda *_: (0,) * len(array.shape))


def per_step(array):
    return pl.BlockSpec((1,) + array.shape[1:], lambda s, *_: (s,) + (0,) * (len(array.shape) - 1))


def where_it_is(array):
    return pl.BlockSpec(memory_space=pl.ANY)


def in_vmem(array):
    return pl.BlockSpec(memory_space=pltpu.VMEM)


def call(kernel, steps, name, vmem, inputs, outputs, scratch, scalar, kept=()):
    spec = pltpu.PrefetchScalarGridSpec(
        num_scalar_prefetch=1,
        grid=(steps,),
        in_specs=[make if isinstance(make, pl.BlockSpec) else make(a) for make, a in inputs],
        out_specs=[make if isinstance(make, pl.BlockSpec) else make(a) for make, a in outputs],
        scratch_shapes=scratch,
    )
    return pl.pallas_call(
        kernel,
        grid_spec=spec,
        out_shape=[pltpu.HBM(a.shape, a.dtype) if i in kept else a for i, (_, a) in enumerate(outputs)],
        name=name,
        cost_estimate=pl.CostEstimate(flops=0, bytes_accessed=0, transcendentals=0),
        compiler_params=pltpu.CompilerParams(vmem_limit_bytes=vmem * MIB),
    )(scalar, *[a if make is in_vmem else in_place(a) for make, a in inputs])


def shape(dims, dtype):
    return jax.ShapeDtypeStruct(dims, dtype)


def in_place(array):
    if array.size * array.dtype.itemsize < MIB:
        return array
    return pltpu.with_memory_space_constraint(array, pltpu.HBM)


def add_kernel(counts, *refs):
    refs = refs[1:]
    out_refs = refs[sum(counts) :]
    for count, out_ref in zip(counts, out_refs):
        total = refs[0][...].astype(F32)
        for ref in refs[1:count]:
            total = total + ref[...].astype(F32)
        out_ref[...] = total.astype(BF16)
        refs = refs[count:]


def add_terms(sides, me):
    in_specs, out_specs, arrays, outs, lefts = [], [], [], [], []

    def place(own_bits, fixed, left):
        def index(g, me_ref):
            at = 0
            for b in own_bits:
                if b in fixed:
                    value = (me_ref[0] >> b) & 1
                    value = value if fixed[b] else 1 - value
                else:
                    value = (g >> (len(left) - 1 - left.index(b))) & 1
                at = at * 2 + value
            return (0, at, 0, 0)

        return index

    for terms, fixed in sides:
        first, bits = terms[0]
        left = [b for b in bits if b not in fixed]
        n, _, rows, cols = first.shape
        in_specs += [pl.BlockSpec((n, 1, rows, cols), place(b, fixed, left)) for _, b in terms]
        out_specs.append(pl.BlockSpec((n, 1, rows, cols), lambda g, _: (0, g, 0, 0)))
        arrays += [a for a, _ in terms]
        outs.append(shape((n, 1 << len(left), rows, cols), BF16))
        lefts.append(left)
    results = pl.pallas_call(
        partial(add_kernel, [len(terms) for terms, _ in sides]),
        grid_spec=pltpu.PrefetchScalarGridSpec(
            num_scalar_prefetch=1, grid=(1 << len(lefts[0]),), in_specs=in_specs, out_specs=out_specs
        ),
        out_shape=outs,
        name="add",
        cost_estimate=pl.CostEstimate(flops=0, bytes_accessed=0, transcendentals=0),
        compiler_params=pltpu.CompilerParams(vmem_limit_bytes=24 * MIB),
    )(me, *arrays)
    return results, lefts


def flip(array, axis, mask):
    size = lax.axis_size(axis)
    return lax.ppermute(array, axis, [(i, i ^ mask) for i in range(size)])


def tie(*arrays):
    return lax.optimization_barrier(arrays)


def pick(array, axis, index):
    return lax.dynamic_index_in_dim(array, index, axis, keepdims=False)


def outer_bits():
    bits = list(range(1, lax.axis_size("dp").bit_length() - 1))
    return bits, (bits, bits[::-1])


def share_of():
    me = lax.axis_index("dp")
    return (me & 1) * (lax.axis_size("dp") // 2) + (me >> 1)


def flip_core(arrays):
    form = (arrays[0].shape[0], -1, arrays[0].shape[-1])
    got = flip(jnp.stack([a.reshape(form) for a in arrays]), "dp", 1)
    return [got[i].reshape(a.shape) for i, a in enumerate(arrays)]


class Gather:
    def __init__(self, pair):
        self.bits, self.orders = outer_bits()
        self.steps = len(self.bits)
        self.n, _, self.cols = pair[0].shape
        self.held = [
            a.reshape((self.n,) + (1,) * self.steps + a.shape[1:]) for a in pair
        ]

    def send(self, step):
        return [flip(h, "dp", 1 << order[step]) for h, order in zip(self.held, self.orders)]

    def merge(self, step, mine, theirs):
        me = lax.axis_index("dp")
        merged = []
        for one, two, order in zip(mine, theirs, self.orders):
            bit = order[step]
            low = ((me >> bit) & 1) == 0
            parts = [jnp.where(low, one, two), jnp.where(low, two, one)]
            merged.append(jnp.concatenate(parts, axis=1 + self.steps - bit))
        return merged

    def take(self, step, got):
        self.held = self.merge(step, self.held, got)

    def halves(self):
        return self.flat(self.held)

    def flat(self, arrays):
        return [a.reshape(self.n, -1, self.cols) for a in arrays]


class Reduce:
    def __init__(self, keeps, gots):
        self.bits, self.orders = outer_bits()
        self.steps = len(self.bits)
        self.me = lax.axis_index("dp").astype(jnp.int32).reshape(1)
        high_first = self.bits[::-1]
        n, rows, cols = keeps[0].shape
        form = (n, 1 << self.steps, rows >> self.steps, cols)
        self.terms = [
            [(k.reshape(form), high_first), (g.reshape(form), high_first)]
            for k, g in zip(keeps, gots)
        ]
        self.left = [None, None]

    def pack(self, step):
        sides = []
        for terms, order in zip(self.terms, self.orders):
            fixed = {b: True for b in order[:step]}
            fixed[order[step]] = False
            sides.append((terms, fixed))
        sends, self.left = add_terms(sides, self.me)
        return sends

    def send(self, step, packs):
        return [flip(p, "dp", 1 << order[step]) for p, order in zip(packs, self.orders)]

    def take(self, got):
        for side in range(2):
            self.terms[side].append((got[side], self.left[side]))

    def finish(self):
        fixed = {b: True for b in self.bits}
        sums, _ = add_terms([(t, fixed) for t in self.terms], self.me)
        return [a[:, 0] for a in sums]


def gather_stack(piece):
    bits, _ = outer_bits()
    order = list(range(1 << len(bits)))
    if len(order) <= 4:
        order = order[:1] + order[:0:-1]
        return [piece] + [flip(piece, "dp", 2 * k) for k in order[1:]], order
    held = piece[None]
    for bit in bits:
        held = jnp.concatenate([held, flip(held, "dp", 1 << bit)])
    return [held[k] for k in order], order


def add_parts(*parts):
    total = parts[0].astype(F32)
    for part in parts[1:]:
        total = total + part.astype(F32)
    return total.astype(BF16)


def shards(
    tokens,
    word_len,
    region_count,
    w_qkv,
    qv_bias,
    w_out,
    out_bias,
    norm1_gain,
    norm1_bias,
    w_in,
    in_bias,
    w_down,
    down_bias,
    norm2_gain,
    norm2_bias,
    cotangent,
):
    mp = lax.axis_size("mp")
    dp = lax.axis_size("dp")
    mi = lax.axis_index("mp")
    width = tokens.shape[2]
    rows_local = tokens.shape[1]
    slots = rows_local * mp
    pairs = tokens.shape[0] // mp
    rows = pairs * slots
    cols = w_qkv.shape[2]
    units = w_in.shape[1]
    half_units = units // 2
    order = jnp.arange(mp) ^ mi
    here = jnp.stack([lax.axis_index("dp") & 1, mi, lax.axis_index("dp") >> 1]).astype(jnp.int32)
    share = share_of()

    turned = w_qkv.transpose(0, 2, 1).reshape(3 * cols, width)
    own_qk = turned[: 2 * cols]
    own_vo = jnp.concatenate([turned[2 * cols :], w_out], axis=0)
    att_part, ffn_part = 2 * cols // dp, units // dp
    first = share * att_part
    rows_of = lambda array, start, size: lax.dynamic_slice_in_dim(array, start, size, 0)
    vo_piece = jnp.where(
        first < cols,
        rows_of(turned, 2 * cols + jnp.minimum(first, cols - att_part), att_part),
        rows_of(w_out, jnp.maximum(first - cols, 0), att_part),
    )

    def row_blocks(array):
        blocks = array.reshape((mp, pairs) + array.shape[1:])
        return [pick(blocks, 0, mi ^ k) for k in range(mp)]

    def join(blocks):
        return jnp.concatenate(blocks, axis=1).reshape(rows, width)

    fill = lambda v: jnp.pad(v, ((0, 0), (0, width - v.shape[1])))
    small = jnp.concatenate([fill(qv_bias), in_bias.reshape(1, units), jnp.zeros((5, width), BF16)])
    att_send = jnp.concatenate([rows_of(turned, first, att_part), vo_piece], axis=0)
    ffn_send = jnp.concatenate(
        [rows_of(w_in.T, share * ffn_part, ffn_part), rows_of(w_down, share * ffn_part, ffn_part), small],
        axis=0,
    )
    tok = row_blocks(tokens)
    cot = row_blocks(cotangent)
    vectors = jnp.stack(
        [out_bias, norm1_gain, norm1_bias, down_bias, norm2_gain, norm2_bias, out_bias, out_bias]
    ).astype(F32)
    words = lax.dynamic_slice_in_dim(word_len, mi * pairs, pairs, 0)
    regions = lax.dynamic_slice_in_dim(region_count, mi * pairs, pairs, 0)
    slot_index = (order[:, None] * rows_local + jnp.arange(rows_local)[None, :]).reshape(-1)
    key_valid = jnp.where(
        slot_index[None, :] < WORDS,
        slot_index[None, :] < words[:, None],
        slot_index[None, :] - WORDS < regions[:, None],
    ).astype(F32)[:, None, :]

    att_got = {k: flip(att_send, "mp", k) for k in (3, 2, 1)}
    att_got = [att_got[k] for k in (1, 2, 3)]
    att_got, ffn_send, tok, vectors, key_valid, here, own_qk, own_vo = tie(
        att_got, ffn_send, tok, vectors, key_valid, here, own_qk, own_vo
    )
    att = Gather(
        [
            jnp.stack([g[:att_part] for g in att_got]),
            jnp.stack([g[att_part:] for g in att_got]),
        ]
    )
    ffn_two = flip(ffn_send, "mp", 2)
    got = att.send(0)
    tok_one = flip(tok[1], "mp", 1)
    ffn_two, got, tok_one, ffn_send, tok = tie(ffn_two, got, tok_one, ffn_send, tok)
    for step in range(1, att.steps):
        att.take(step - 1, got)
        got = att.send(step)
        if step == 1:
            ffn_odd = flip(jnp.stack([ffn_send, ffn_two]), "mp", 1)
            tok_three = flip(tok[3], "mp", 3)
        got, ffn_odd, tok_three, tok = tie(got, ffn_odd, tok_three, tok)
    att.take(att.steps - 1, got)
    ffn_got = [ffn_odd[0], ffn_two, ffn_odd[1]]
    ffn = Gather(
        [
            jnp.stack([g[:ffn_part] for g in ffn_got]),
            jnp.stack([g[ffn_part : 2 * ffn_part] for g in ffn_got]),
        ]
    )
    got = ffn.send(0)
    qk_one, vo_one = att.halves()
    qk_two, vo_two = flip(qk_one, "dp", 1), flip(vo_one, "dp", 1)
    tok_two = flip(tok[2], "mp", 2)
    smalls = jnp.stack([small] + [g[2 * ffn_part :] for g in ffn_got]).astype(F32)
    got, qk_two, vo_two, tok_two, cot, smalls = tie(got, qk_two, vo_two, tok_two, cot, smalls)
    heads_low = shape((mp, rows, cols), BF16)
    low_shape = shape((rows, width), BF16)
    rows_shape = shape((rows, width), F32)
    sums_shape = shape((8, width), F32)
    block_shape = shape((pairs, rows_local, width), BF16)
    for step in range(1, ffn.steps):
        ffn.take(step - 1, got)
        got = ffn.send(step)
        if step < ffn.steps - 1:
            got = tie(*got)
    early = flip_core(ffn.held)
    early, cot, x = tie(early, cot, join([tok[0], tok_one, tok_two, tok_three]))
    cot_blocks = [cot[0]] + [flip(cot[k], "mp", k) for k in range(1, mp)]
    later = lambda a: pl.BlockSpec((1,) + a.shape[1:], lambda s, h: (jnp.clip(s - 1, 0, mp - 2), 0, 0))
    head_args = [
        (whole, own_qk),
        (later, qk_one),
        (later, qk_two),
        (whole, own_vo),
        (later, vo_one),
        (later, vo_two),
    ]
    q, k, v, weights, context, hidden_low, normed_one, scale_one = call(
        partial(attention_kernel, pairs),
        mp,
        "attention",
        24,
        [
            (whole, x),
            *head_args,
            (per_step, smalls),
            (whole, key_valid),
            (whole, vectors),
        ],
        [
            (per_step, heads_low),
            (per_step, heads_low),
            (per_step, heads_low),
            (per_step, shape((mp, pairs, cols // HEAD * slots, slots), F32)),
            (per_step, heads_low),
            (whole, low_shape),
            (whole, rows_shape),
            (whole, shape((rows, 1), F32)),
        ],
        [pltpu.VMEM((rows, width), F32)],
        here,
        range(5),
    )
    got, early, hidden_low, cot_blocks = tie(got, early, hidden_low, cot_blocks)
    ffn.take(ffn.steps - 1, got)
    in_one, down_one = ffn.halves()
    late = [flip(g, "dp", 1) for g in got]
    late, hidden_low = tie(late, hidden_low)
    in_two, down_two = ffn.flat(ffn.merge(ffn.steps - 1, early, late))

    half = shape((mp, half_units, width), BF16)
    pre_shape = shape((mp, rows, units), BF16)
    vmem = lambda a: pltpu.VMEM(a.shape, a.dtype)
    results = call(
        partial(ffn_kernel, mp),
        1,
        "ffn",
        42,
        [
            (where_it_is, hidden_low),
            (where_it_is, normed_one),
            (where_it_is, w_in),
            (in_vmem, in_one),
            (in_vmem, in_two),
            (where_it_is, w_down),
            (in_vmem, down_one),
            (in_vmem, down_two),
            (whole, smalls),
            (whole, vectors),
            *[(where_it_is, c) for c in cot_blocks],
        ],
        [
            *[(whole, block_shape)] * mp,
            (where_it_is, rows_shape),
            (where_it_is, pre_shape),
            (where_it_is, half),
            (where_it_is, half),
            (where_it_is, half),
            (where_it_is, half),
            (whole, shape((mp, 1, units), F32)),
            (whole, sums_shape),
        ],
        [
            vmem(low_shape),
            vmem(rows_shape),
            pltpu.VMEM((width, units), BF16),
            pltpu.VMEM((units, width), BF16),
            pltpu.VMEM((mp,) + block_shape.shape, BF16),
            vmem(pre_shape),
            pltpu.VMEM(pre_shape.shape, F32),
            vmem(rows_shape),
            vmem(rows_shape),
            vmem(pre_shape),
            vmem(half),
            vmem(half),
            vmem(half),
            vmem(half),
            vmem(low_shape),
            pltpu.SemaphoreType.DMA((3 + 1 + mp + 1 + 5 * mp,)),
        ],
        here,
        range(mp + 6),
    )
    out_blocks = results[:mp]
    delta_ffn, pre_grad, in_keep, in_send, down_keep, down_send, sum_in, sums_two = results[mp:]
    in_got, down_got = flip(in_send, "dp", 1), flip(down_send, "dp", 1)
    delta_attn, attn_low, sums_one = call(
        partial(ffn_back_kernel, mp),
        1,
        "ffn_back",
        18,
        [
            (where_it_is, pre_grad),
            (where_it_is, w_in),
            (in_vmem, in_one),
            (in_vmem, in_two),
            (where_it_is, delta_ffn),
            (where_it_is, normed_one),
            (whole, scale_one),
            (whole, vectors),
        ],
        [(where_it_is, rows_shape), (whole, low_shape), (whole, sums_shape)],
        [
            vmem(pre_shape),
            pltpu.VMEM((width, units), BF16),
            vmem(rows_shape),
            vmem(rows_shape),
            vmem(rows_shape),
            pltpu.SemaphoreType.DMA((mp + 1 + 2 + 1,)),
        ],
        here,
        (0,),
    )
    in_got, down_got, out_blocks, attn_low = tie(in_got, down_got, out_blocks, attn_low)
    ffn = Reduce([in_keep, down_keep], [in_got, down_got])
    packs = ffn.pack(0)
    packs, attn_low, out_blocks = tie(packs, attn_low, out_blocks)
    got = ffn.send(0, packs)
    out_got = [out_blocks[0]] + [flip(out_blocks[k], "mp", k) for k in range(1, mp)]
    small_half = shape((mp, cols, width), BF16)
    results = call(
        partial(attention_back_kernel, pairs),
        mp,
        "attention_back",
        28,
        [
            (whole, x),
            (whole, attn_low),
            (whole, delta_attn),
            *head_args,
            (per_step, q),
            (per_step, k),
            (per_step, v),
            (per_step, weights),
            (per_step, context),
            (whole, sums_one),
            (whole, sums_two),
            (whole, sum_in),
        ],
        [
            (per_step, small_half),
            (per_step, small_half),
            (
                pl.BlockSpec((2, 1, cols, width), lambda s, h: (0, s, 0, 0)),
                shape((2, mp, cols, width), BF16),
            ),
            (whole, shape((-(-(6 + 2 * mp) // 8) * 8, width), F32)),
            *[(whole, block_shape)] * mp,
        ],
        [pltpu.VMEM((rows, cols), BF16)] * 3 + [pltpu.VMEM((rows, width), F32)],
        here,
        (0, 1, 2) + tuple(range(4, 4 + mp)),
    )
    qk_keep, vo_keep, att_send, sums = results[:4]
    row_sends = results[4:]
    got, out_got, att_send, row_sends, sums = tie(got, out_got, att_send, row_sends, sums)
    place = lambda blocks, dtype: call(
        partial(place_kernel, pairs),
        1,
        "place",
        16,
        [(whole, b) for b in blocks],
        [(whole, shape((mp * pairs, rows_local, width), dtype))],
        [],
        here,
    )[0]
    for step in range(1, ffn.steps):
        ffn.take(got)
        packs = ffn.pack(step)
        got = ffn.send(step, packs)
        if step == 1:
            att_got = flip(att_send, "dp", 1)
            row_three = flip(row_sends[3], "mp", 3)
            row_one = flip(row_sends[1], "mp", 1)
            sums_got = flip(sums, "mp", 2)
            att = Reduce([qk_keep, vo_keep], [att_got[0], att_got[1]])
            att_packs = att.pack(0)
            layer_out = place(out_got, BF16)
        got, att_packs, row_one, row_three, sums_got, row_sends, layer_out = tie(
            got, att_packs, row_one, row_three, sums_got, row_sends, layer_out
        )
    sums = sums + sums_got
    ffn.take(got)
    ffn_parts = ffn.finish()
    ffn_odd = jnp.concatenate([p[1::2] for p in ffn_parts], axis=1)
    ffn_even = jnp.concatenate([p[0::2] for p in ffn_parts], axis=1)
    got = att.send(0, att_packs)
    ffn_got = flip(ffn_odd, "mp", 1)
    sums_got = flip(sums, "dp", 2)
    row_two = flip(row_sends[2], "mp", 2)
    got, ffn_got, sums_got, row_two, row_sends = tie(got, ffn_got, sums_got, row_two, row_sends)
    sums = sums + sums_got
    for mask in [1 << b for b in range(2, dp.bit_length() - 2)]:
        sums = sums + flip(sums, "dp", mask)
    ffn_two = add_parts(ffn_even[1], ffn_got[1])
    for step in range(1, att.steps):
        att.take(got)
        packs = att.pack(step)
        got = att.send(step, packs)
        if step == 1:
            ffn_last = flip(ffn_two, "mp", 2)
            sums_got = flip(sums, "dp", dp // 2)
        got, ffn_last, sums_got, row_sends = tie(got, ffn_last, sums_got, row_sends)
    att.take(got)
    sums = sums + sums_got
    att_parts = att.finish()
    att_odd = jnp.concatenate([p[1::2] for p in att_parts], axis=1)
    att_even = jnp.concatenate([p[0::2] for p in att_parts], axis=1)
    ffn_sum = add_parts(ffn_even[0], ffn_got[0], ffn_last)
    ffn = Gather([ffn_sum[None, :ffn_part], ffn_sum[None, ffn_part:]])
    ffn.held, att_odd, att_even, sums = tie(ffn.held, att_odd, att_even, sums)
    got = ffn.send(0)
    att_got = flip(att_odd, "mp", 1)
    sums_got = flip(sums, "dp", 1)
    got, att_got, sums_got, row_one = tie(got, att_got, sums_got, row_one)
    grad_input = place([row_sends[0], row_one, row_two, row_three], F32)
    sums = sums + sums_got
    att_two = add_parts(att_even[1], att_got[1])
    for step in range(1, ffn.steps):
        ffn.take(step - 1, got)
        got = ffn.send(step)
        if step == 1:
            att_last = flip(att_two, "mp", 2)
            sums_got = flip(sums, "mp", 1)
        got, att_last, sums_got, grad_input = tie(got, att_last, sums_got, grad_input)
    ffn.take(ffn.steps - 1, got)
    sums = sums + sums_got
    att_sum = add_parts(att_even[0], att_got[0], att_last)
    ffn_halves = ffn.halves()
    core_got = flip_core(ffn_halves)
    att_mine, att_order = gather_stack(att_sum)
    grad_in, grad_down = call(
        unit_grads_kernel,
        1,
        "unit_grads",
        24,
        [(whole, a) for a in ffn_halves + core_got],
        [(whole, shape((width, units), F32)), (whole, shape((units, width), F32))],
        [],
        here,
    )
    att_mine, grad_in, grad_down, sums = tie(att_mine, grad_in, grad_down, sums)
    att_mine = jnp.stack(att_mine)
    att_other = flip(att_mine, "dp", 1)
    grad_qkv, grad_out = call(
        partial(head_grads_kernel, att_order),
        1,
        "head_grads",
        24,
        [(whole, att_mine), (whole, att_other)],
        [
            (whole, shape((3, cols // att_part, att_part, width), F32)),
            (whole, shape((cols // att_part, att_part, width), F32)),
        ],
        [],
        here,
    )
    sum_in_bias = lax.dynamic_index_in_dim(sums, 6 + mi, 0, keepdims=False)
    sum_qv = lax.dynamic_index_in_dim(sums, 6 + mp + mi, 0, keepdims=False)
    sum_qv = jnp.stack([sum_qv[:cols], sum_qv[2 * cols : 3 * cols]])
    return (
        layer_out,
        grad_input,
        grad_qkv.reshape(3, cols, width).transpose(0, 2, 1),
        sum_qv,
        grad_out.reshape(cols, width),
        sums[0],
        sums[1],
        sums[2],
        grad_in,
        sum_in_bias,
        grad_down,
        sums[5],
        sums[3],
        sums[4],
    )


def solution(mesh):
    in_specs = (
        P("dp", "mp", None),
        P("dp"),
        P("dp"),
        P(None, None, "mp"),
        P(None, "mp"),
        P("mp", None),
        P(),
        P(),
        P(),
        P(None, "mp"),
        P("mp"),
        P("mp", None),
        P(),
        P(),
        P(),
        P("dp", "mp", None),
    )
    out_specs = (
        P("dp", "mp", None),
        P("dp", "mp", None),
        P(None, None, "mp"),
        P(None, "mp"),
        P("mp", None),
        P(),
        P(),
        P(),
        P(None, "mp"),
        P("mp"),
        P("mp", None),
        P(),
        P(),
        P(),
    )
    return jax.shard_map(shards, mesh=mesh, in_specs=in_specs, out_specs=out_specs, check_vma=False)
```
